32 devices in a mesh: dp: 8 (over z, y), mp: 4 (over x, core).
Axes of the slice: x: 2, y: 2, z: 4, core: 2. Of those that a mesh axis runs over, the one named last changes fastest.
Arguments:
- tokens: bfloat16 [16, 1024, 768], P('dp', 'mp'), may hold values from -6 to 6
- w_query: bfloat16 [768, 768], P('dp', 'mp'), may hold values from -0.21875 to 0.21875
- w_key: bfloat16 [768, 768], P('dp', 'mp'), may hold values from -0.21875 to 0.21875
- w_value: bfloat16 [768, 768], P('dp', 'mp'), may hold values from -0.21875 to 0.21875
- w_out: bfloat16 [768, 768], P('mp', 'dp'), may hold values from -3 to 3
- w_up: bfloat16 [768, 3072], P('dp', 'mp'), may hold values from -0.21875 to 0.21875
- w_down: bfloat16 [3072, 768], P('mp', 'dp'), may hold values from -0.109375 to 0.109375
- gain_attn: float32 [768], replicated, may hold values from 0.5 to 1.5
- bias_attn: float32 [768], replicated, may hold values from -1.25 to 1.25
- gain_ffn: float32 [768], replicated, may hold values from 0.5 to 1.5
- bias_ffn: float32 [768], replicated, may hold values from -1.25 to 1.25
- lengths: int32 [16], P('dp'), may hold values from 256 to 1024, as said below
- random_blocks: int32 [12, 16, 3], replicated, may hold values from 0 to 15
- cotangent: bfloat16 [16, 1024, 768], P('dp', 'mp'), may hold values from -6 to 6
Outputs:
- output: bfloat16 [16, 1024, 768], P('dp', 'mp')
- grad_tokens: float32 [16, 1024, 768], P('dp', 'mp')
- grad_query: float32 [768, 768], P('dp', 'mp')
- grad_key: float32 [768, 768], P('dp', 'mp')
- grad_value: float32 [768, 768], P('dp', 'mp')
- grad_out: float32 [768, 768], P('mp', 'dp')
- grad_up: float32 [768, 3072], P('dp', 'mp')
- grad_down: float32 [3072, 768], P('mp', 'dp')
- grad_gain_attn: float32 [768], replicated
- grad_bias_attn: float32 [768], replicated
- grad_gain_ffn: float32 [768], replicated
- grad_bias_ffn: float32 [768], replicated
The draws below stay inside these ranges and needn't reach their ends.
Inputs may be any that keep to these rules, and one draw needn't show every extreme that they name: `lengths`: in each group of 2 slots that share an index of dp, one slot has length exactly 1024.
All inputs are finite; a program needn't handle non-finite values.
Results may differ from the reference program's by a relative error of at most 0.017.
Values may be sent and summed in bfloat16 or wider, within the bound.
No kernel may reach another device: no remote copies, remote signals or barrier semaphores. Data moves between devices by JAX's collectives and lax.ppermute only.
A program may use at most 128 MiB of HBM per device.

```python
from functools import partial
import jax
import jax.numpy as jnp
from jax import lax

D = 768
H = 12
HD = 64
FF = 3072
BLOCK = 64
RAND = 3
SEQ = 1024
SLOT_GRP = 2
SLOTS = 16
NB = 16
LMIN = 256
N_DP = 8


def draw_lengths(key, part):
    key = jax.random.fold_in(key, 11)
    key_lengths, key_choice = jax.random.split(key)
    drawn = jax.random.randint(key_lengths, (SLOTS,), LMIN, SEQ + 1)
    picked = jax.random.randint(key_choice, (N_DP, 1), 0, SLOT_GRP)
    full_rows = (jnp.arange(SLOT_GRP)[None, :] == picked).reshape(SLOTS)
    return jnp.where(full_rows, SEQ, drawn).astype(jnp.int32)


def set_ends(entries, own_key, low, largest):
    index_at = [jax.random.randint(jax.random.fold_in(own_key, axis), (), 0, length) for axis, length in enumerate(entries.shape)]
    main_axis = entries.shape.index(max(entries.shape))
    next_to = index_at[:main_axis] + [(index_at[main_axis] + 1) % entries.shape[main_axis]] + index_at[main_axis + 1:]
    return entries.at[tuple(index_at)].set(low).at[tuple(next_to)].set(largest)


def steps_of(rng, shape, pieces, smallest, top_value):
    loudness, own = 1.0, jax.random.fold_in(rng, 6)
    for dim, parts in pieces:
        heights = jnp.exp(jax.random.uniform(jax.random.fold_in(own, dim), (parts,), jnp.float32, smallest / len(pieces), top_value / len(pieces)))
        loudness = loudness * jnp.repeat(heights, shape[dim] // parts).reshape([-1 if axis == dim else 1 for axis in range(len(shape))])
    return loudness


def normal_values(key, dims, scale, limit, pieces=(), held_as=jnp.bfloat16):
    result = jax.random.normal(key, dims, jnp.float32) * scale
    if len(pieces) > 0:
        result = steps_of(key, dims, pieces, -0.22, 0.18) * result
    return jnp.clip(result, min=-limit, max=limit).astype(held_as)


def setup_inputs(seed: int = 0) -> dict:
    streams_of = jax.random.split(jax.random.key(seed), 15)
    return {
        "tokens": normal_values(streams_of[0], (SLOTS, SEQ, D), 1.0, 6.0, ((0, 8), (1, 4))),
        "w_query": normal_values(streams_of[1], (D, D), D ** -0.5, 0.21875, ((0, 8), (1, 4))),
        "w_key": normal_values(streams_of[2], (D, D), D ** -0.5, 0.21875, ((0, 8), (1, 4))),
        "w_value": normal_values(streams_of[3], (D, D), D ** -0.5, 0.21875, ((0, 8), (1, 4))),
        "w_out": normal_values(streams_of[4], (D, D), 4 ** -0.5, 3.0, ((0, 4), (1, 8))),
        "w_up": normal_values(streams_of[5], (D, FF), D ** -0.5, 0.21875, ((0, 8), (1, 4))),
        "w_down": normal_values(streams_of[6], (FF, D), FF ** -0.5, 0.109375, ((0, 4), (1, 8))),
        "gain_attn": jnp.clip(1.0 + 0.1 * jax.random.normal(streams_of[7], (D,), jnp.float32), 0.5, 1.5),
        "bias_attn": normal_values(streams_of[8], (D,), 0.2, 1.25, (), jnp.float32),
        "gain_ffn": jnp.clip(1.0 + 0.1 * jax.random.normal(streams_of[9], (D,), jnp.float32), 0.5, 1.5),
        "bias_ffn": normal_values(streams_of[10], (D,), 0.2, 1.25, (), jnp.float32),
        "lengths": draw_lengths(jax.random.fold_in(streams_of[14], 71), 0),
        "random_blocks": set_ends(jax.random.randint(streams_of[12], (H, NB, RAND), 0, NB), jax.random.fold_in(streams_of[12], 1), 0, NB - 1).astype(jnp.int32),
        "cotangent": normal_values(streams_of[13], (SLOTS, SEQ, D), 1.0, 6.0, ((0, 8), (1, 4))),
    }


@jax.custom_vjp
def low(v):
    return lax.optimization_barrier(v.astype(jnp.bfloat16)).astype(jnp.float32)

@jax.custom_vjp
def low_back(v):
    return v

def low_keep(v):
    return (low(v), None)

def low_pass(kept, grad):
    return (grad,)

def back_keep(v):
    return (v, None)

def back_low(kept, grad):
    return (low(grad),)
low.defvjp(low_keep, low_pass)
low_back.defvjp(back_keep, back_low)
EPSILON = 1e-12
SCALE = 0.125
NEGATIVE = -1e+30

def layer_norm(values, gain_vec, bias_vec):
    center = lax.optimization_barrier(jnp.mean(values, axis=-1, keepdims=True))
    shifted = values - center
    spread = lax.optimization_barrier(jnp.mean(shifted * shifted, axis=-1, keepdims=True))
    return shifted * lax.rsqrt(spread + EPSILON) * gain_vec + bias_vec

def product(left_side, right_side):
    return jnp.dot(left_side, right_side, precision=lax.Precision.HIGHEST, preferred_element_type=jnp.float32)

def split_heads(flat_rows):
    return flat_rows.reshape(SEQ, H, HD).transpose(1, 0, 2)

def forward(allowed, inputs, w_query, w_key, w_value, w_out, w_up, w_down, gain_attn, bias_attn, gain_ffn, bias_ffn):
    queries = split_heads(low(low_back(product(inputs, w_query))))
    key_rows = split_heads(low(low_back(product(inputs, w_key))))
    value_rows = split_heads(low(low_back(product(inputs, w_value))))
    scores = low_back(jnp.einsum('hqd,hkd->hqk', queries, key_rows, precision=lax.Precision.HIGHEST) * SCALE)
    scores = jnp.where(allowed, scores, NEGATIVE)
    probabilities = low(jax.nn.softmax(scores, axis=-1))
    context = jnp.einsum('hqk,hkd->hqd', probabilities, value_rows, precision=lax.Precision.HIGHEST)
    context = low(low_back(context.transpose(1, 0, 2).reshape(SEQ, H * HD)))
    attended = low_back(product(context, w_out))
    normed = low(layer_norm(inputs + attended, gain_attn, bias_attn))
    upper_in = low_back(product(normed, w_up))
    active = low(jax.nn.gelu(upper_in, approximate=False))
    mixed_out = low_back(product(active, w_down))
    return layer_norm(normed + mixed_out, gain_ffn, bias_ffn)

def reference(tokens, w_query, w_key, w_value, w_out, w_up, w_down, gain_attn, bias_attn, gain_ffn, bias_ffn, lengths, random_blocks, cotangent):
    params = tuple((weight_arg.astype(jnp.float32) for weight_arg in (w_query, w_key, w_value, w_out, w_up, w_down, gain_attn, bias_attn, gain_ffn, bias_ffn)))
    nblocks = SEQ // BLOCK
    blocks = jnp.arange(nblocks)
    nearby = jnp.abs(blocks[:, None] - blocks[None, :]) <= 1
    edge_blocks = (blocks == 0) | (blocks == nblocks - 1)
    fixed_part = nearby | edge_blocks[:, None] | edge_blocks[None, :]
    chosen = jnp.any(random_blocks[:, :, :, None] == blocks[None, None, None, :], axis=2)
    block_mask = fixed_part[None] | chosen
    token_mask = jnp.repeat(jnp.repeat(block_mask, BLOCK, axis=1), BLOCK, axis=2)
    positions = jnp.arange(SEQ)

    def per_slot(running, sample):
        slot_tokens, slot_cotangent, slot_length = sample
        key_valid = positions < slot_length
        allowed = token_mask & key_valid[None, None, :]
        outputs, backward = jax.vjp(partial(forward, allowed), slot_tokens.astype(jnp.float32), *params)
        gradients = backward(slot_cotangent.astype(jnp.float32) * key_valid.astype(jnp.float32)[:, None])
        running = tuple((summed + addend for summed, addend in zip(running, gradients[1:])))
        return (running, (outputs.astype(jnp.bfloat16), gradients[0]))
    start = tuple((jnp.zeros_like(weight_arg) for weight_arg in params))
    summed, (layer_out, grad_tokens) = lax.scan(per_slot, start, (tokens, cotangent, lengths))
    return (layer_out, grad_tokens, summed[0], summed[1], summed[2], summed[3], summed[4], summed[5], summed[6], summed[7], summed[8], summed[9])
```

```python
import functools

import jax
import jax.numpy as jnp
from jax import lax
from jax.experimental import pallas as pl
from jax.experimental.pallas import tpu as pltpu
from jax.sharding import PartitionSpec as P

HD = 64
BLOCK = 64
LANES = 128
TILE = 256
EPSILON = 1e-12
SCALE = 0.125
LOG2E = 1.4426950408889634
LN2 = 0.6931471805599453
NEGATIVE = -1e30
F32 = jnp.float32
BF16 = jnp.bfloat16

ERFCX_STEP = 0.45
ERFCX = (
    -8.220994855312894e-06,
    0.2540684902923417,
    0.25234751996246985,
    0.23373082558517694,
    0.1739141918052578,
    0.06370751405215419,
    0.18661300519520473,
    -0.22870513112792096,
    0.06433208636936971,
)

CORE_SWAP = [(0, 1), (1, 0), (2, 3), (3, 2)]
CHIP_SWAP = [(0, 2), (2, 0), (1, 3), (3, 1)]


def nn(a, b):
    return lax.dot_general(a, b, (((1,), (0,)), ((), ())), preferred_element_type=F32)


def nt(a, b):
    return lax.dot_general(a, b, (((1,), (1,)), ((), ())), preferred_element_type=F32)


def tn(a, b):
    return lax.dot_general(a, b, (((0,), (0,)), ((), ())), preferred_element_type=F32)


def vmem():
    return pl.BlockSpec(memory_space=pltpu.VMEM)


def smem():
    return pl.BlockSpec(memory_space=pltpu.SMEM)


def rows(width):
    return pl.BlockSpec((TILE, width), lambda i: (i, 0))


def whole(shape):
    return pl.BlockSpec(shape, lambda i: (0,) * len(shape))


def cost(flops, moved, exps=0):
    return pl.CostEstimate(flops=int(flops), bytes_accessed=int(moved), transcendentals=int(exps))


def params(mib):
    return pltpu.CompilerParams(vmem_limit_bytes=mib * 2**20)


def place(order, me, w_ref, dst_ref):
    count, height, _ = w_ref.shape
    for j in range(count):
        at = 0 if count == 1 else pl.multiple_of((me ^ order[j]) * height, height)
        dst_ref[pl.ds(at, height), :] = w_ref[j]


def pick(order, me, fulls, out_ref):
    count, height, _ = out_ref.shape
    for j in range(count):
        at = 0 if count == 1 else pl.multiple_of((me ^ order[j]) * height, height)
        both = [full[pl.ds(at, height), :] for full in fulls]
        out_ref[j] = jnp.concatenate(both, axis=1).astype(BF16)


def attend_kernel(order, has_prior, info, tok, w, mask, *rest):
    if has_prior:
        prior, qa, ka, va, ctx, part, wfull = rest
    else:
        qa, ka, va, ctx, part, wfull = rest
        prior = None
    seq = tok.shape[0]
    heads = qa.shape[0]
    span = heads * HD
    place(order, info[0], w, wfull)
    lane = lax.broadcasted_iota(jnp.int32, (TILE, LANES), 1)
    row0 = lax.broadcasted_iota(jnp.int32, (TILE, LANES), 0)
    for t in range(seq // TILE):
        at = pl.ds(t * TILE, TILE)
        row = row0 + t * TILE
        made = nn(tok[at, :], wfull[:, : 3 * span])
        onehot = jnp.where(lane - HD == row // BLOCK, 1.0, 0.0)[:, HD:]
        position = row + info[4]
        position = jnp.where(position >= seq, position - seq, position)
        dead = (position >= info[3]) & (lane >= HD) & (lane < HD + 16)
        for h in range(heads):
            q = made[:, h * HD : (h + 1) * HD] * (SCALE * LOG2E)
            k = made[:, span + h * HD : span + (h + 1) * HD]
            v = made[:, 2 * span + h * HD : 2 * span + (h + 1) * HD]
            qa[h, at, :] = jnp.concatenate([q, onehot], axis=1).astype(BF16)
            per = TILE // BLOCK
            table = jnp.concatenate(
                [
                    jnp.broadcast_to(mask[h, t * per + b : t * per + b + 1, :], (BLOCK, LANES))
                    for b in range(per)
                ],
                axis=0,
            )
            table = jnp.where(dead, NEGATIVE, table)
            ka[h, at, :] = jnp.concatenate([k, table[:, HD:]], axis=1).astype(BF16)
            va[h, at, :] = jnp.concatenate([v, jnp.full((TILE, HD), -1.0, F32)], axis=1).astype(BF16)
    for t in range(seq // TILE):
        at = pl.ds(t * TILE, TILE)
        pieces = []
        for h in range(heads):
            q = qa[h, at, :]
            s = nt(q, ka[h])
            top = jnp.max(s, axis=1, keepdims=True)
            p = jnp.exp2(s - top).astype(BF16)
            got = nn(p, va[h])
            total = -got[:, HD:]
            pieces.append(got[:, :HD] / total)
            log = top + jnp.log2(-got)
            hi = log.astype(BF16).astype(F32)
            mid = (log - hi).astype(BF16).astype(F32)
            low = log - hi - mid
            new = jnp.where(
                lane == HD + 16,
                hi,
                jnp.where(lane == HD + 17, mid, jnp.where(lane == HD + 18, low, q.astype(F32))),
            )
            qa[h, at, :] = new.astype(BF16)
        c = jnp.concatenate(pieces, axis=1).astype(BF16)
        ctx[at, :] = c
        out = nt(c, wfull[:, 3 * span :])
        if prior is not None:
            out = out + prior[at, :]
        part[at, :] = out.astype(part.dtype)


def attend(order, info, tok, w, mask, prior):
    seq, width = tok.shape
    heads = mask.shape[0]
    span = heads * HD
    aug = jax.ShapeDtypeStruct((heads, seq, LANES), BF16)
    last = BF16 if prior is not None else F32
    args = (info, tok, w, mask) + (() if prior is None else (prior,))
    return pl.pallas_call(
        functools.partial(attend_kernel, order, prior is not None),
        out_shape=(
            aug,
            aug,
            aug,
            jax.ShapeDtypeStruct((seq, span), BF16),
            jax.ShapeDtypeStruct((seq, width), last),
        ),
        in_specs=[smem()] + [vmem()] * (len(args) - 1),
        out_specs=tuple(vmem() for _ in range(5)),
        scratch_shapes=[pltpu.VMEM((width, 4 * span), BF16)],
        compiler_params=params(40),
        cost_estimate=cost(
            8 * seq * width * span + 4 * heads * seq * seq * LANES, 12e6, heads * seq * seq
        ),
        name="attend",
    )(*args)


def attend_back_kernel(order, has_prior, info, dz, w, qa, ka, va, ctx, *rest):
    if has_prior:
        prior, dqkv, back, wfull, da, parts = rest
    else:
        dqkv, back, wfull, da, parts = rest
        prior = None
    seq = dz.shape[0]
    heads = qa.shape[0]
    span = heads * HD
    place(order, info[0], w, wfull)
    lane = lax.broadcasted_iota(jnp.int32, (TILE, LANES), 1)
    for t in range(seq // TILE):
        at = pl.ds(t * TILE, TILE)
        dctx = nn(dz[at, :], wfull[:, 3 * span :]).astype(BF16).astype(F32)
        both = dctx * ctx[at, :].astype(F32)
        for h in range(heads):
            inner = jnp.sum(both[:, h * HD : (h + 1) * HD], axis=1, keepdims=True)
            hi = inner.astype(BF16).astype(F32)
            mid = (inner - hi).astype(BF16).astype(F32)
            low = inner - hi - mid
            one = jnp.concatenate(
                [dctx[:, h * HD : (h + 1) * HD], jnp.zeros((TILE, HD), F32)], axis=1
            )
            one = jnp.where(lane == HD, hi, one)
            one = jnp.where(lane == HD + 1, mid, one)
            one = jnp.where(lane == HD + 2, low, one)
            da[h, at, :] = one.astype(BF16)
    for h in range(heads):
        k_turned = jnp.transpose(ka[h].astype(F32)).astype(BF16)
        dq_turned = None
        for t in range(seq // TILE):
            at = pl.ds(t * TILE, TILE)
            p = jnp.exp2(nt(ka[h, at, :], qa[h]))
            ds = (p * nt(va[h, at, :], da[h])).astype(BF16)
            parts[2 * heads + h, at, :] = nn(p.astype(BF16), da[h])
            parts[heads + h, at, :] = nn(ds, qa[h]) * LN2
            more = nn(k_turned[:, t * TILE : (t + 1) * TILE], ds)
            dq_turned = more if dq_turned is None else dq_turned + more
        parts[h] = jnp.transpose(dq_turned) * SCALE
    for t in range(seq // TILE):
        at = pl.ds(t * TILE, TILE)
        grads = jnp.concatenate([parts[i, at, :][:, :HD] for i in range(3 * heads)], axis=1)
        grads = grads.astype(BF16)
        dqkv[at, :] = grads
        out = nt(grads, wfull[:, : 3 * span])
        if prior is not None:
            out = out + prior[at, :]
        back[at, :] = out.astype(back.dtype)


def attend_back(order, info, dz, w, qa, ka, va, ctx, prior):
    seq, width = dz.shape
    heads = qa.shape[0]
    span = heads * HD
    last = BF16 if prior is not None else F32
    args = (info, dz, w, qa, ka, va, ctx) + (() if prior is None else (prior,))
    return pl.pallas_call(
        functools.partial(attend_back_kernel, order, prior is not None),
        out_shape=(
            jax.ShapeDtypeStruct((seq, 3 * span), BF16),
            jax.ShapeDtypeStruct((seq, width), last),
        ),
        in_specs=[smem()] + [vmem()] * (len(args) - 1),
        out_specs=(vmem(), vmem()),
        scratch_shapes=[
            pltpu.VMEM((width, 4 * span), BF16),
            pltpu.VMEM((heads, seq, LANES), BF16),
            pltpu.VMEM((3 * heads, seq, LANES), F32),
        ],
        compiler_params=params(48),
        cost_estimate=cost(
            8 * seq * width * span + 10 * heads * seq * seq * LANES, 14e6, heads * seq * seq
        ),
        name="attend_back",
    )(*args)


def center(z):
    mean = jnp.mean(z, axis=1, keepdims=True)
    moved = z - mean
    spread = jnp.mean(moved * moved, axis=1, keepdims=True)
    scale = lax.rsqrt(spread + EPSILON)
    return moved * scale, scale


def norm_back(n, scale, gy, gain):
    dn = gy * gain
    return scale * (
        dn - jnp.mean(dn, axis=1, keepdims=True) - n * jnp.mean(dn * n, axis=1, keepdims=True)
    )


def add_sums(info, gy, n, sums):
    i = pl.program_id(0)

    @pl.when(i == 0)
    def _():
        sums[...] = jnp.zeros_like(sums)

    @pl.when((i & 1) == info[2])
    def _():
        sums[0:1, :] += jnp.sum(gy * n, axis=0, keepdims=True)
        sums[1:2, :] += jnp.sum(gy, axis=0, keepdims=True)


def norm_one_kernel(tok, p0, p1, gain, bias, z, hn):
    value = tok[...].astype(F32) + (p0[...].astype(F32) + p1[...].astype(F32))
    z[...] = value
    n, _ = center(value)
    hn[...] = (n * gain[...] + bias[...]).astype(BF16)


def norm_one(tok, p0, p1, gain, bias):
    seq, width = tok.shape
    return pl.pallas_call(
        norm_one_kernel,
        grid=(seq // TILE,),
        out_shape=(
            jax.ShapeDtypeStruct((seq, width), F32),
            jax.ShapeDtypeStruct((seq, width), BF16),
        ),
        in_specs=[rows(width)] * 3 + [whole((1, width))] * 2,
        out_specs=(rows(width), rows(width)),
        cost_estimate=cost(seq * width * 10, 9e6),
        name="norm_one",
    )(tok, p0, p1, gain, bias)


def norm_two_kernel(info, hn, m0, m1, cot, gain, bias, out, dz, dzb, sums):
    value = hn[...].astype(F32) + (m0[...].astype(F32) + m1[...].astype(F32))
    n, scale = center(value)
    out[...] = (n * gain[...] + bias[...]).astype(BF16)
    row = lax.broadcasted_iota(jnp.int32, value.shape, 0) + pl.program_id(0) * TILE
    seq = pl.num_programs(0) * TILE
    position = row + info[4]
    position = jnp.where(position >= seq, position - seq, position)
    gy = jnp.where(position < info[3], cot[...].astype(F32), 0.0)
    grad = norm_back(n, scale, gy, gain[...])
    dz[...] = grad
    dzb[...] = grad.astype(BF16)
    add_sums(info, gy, n, sums)


def norm_two(info, hn, m0, m1, cot, gain, bias):
    seq, width = hn.shape
    return pl.pallas_call(
        norm_two_kernel,
        grid=(seq // TILE,),
        out_shape=(
            jax.ShapeDtypeStruct((seq, width), BF16),
            jax.ShapeDtypeStruct((seq, width), F32),
            jax.ShapeDtypeStruct((seq, width), BF16),
            jax.ShapeDtypeStruct((2, width), F32),
        ),
        in_specs=[smem()] + [rows(width)] * 4 + [whole((1, width))] * 2,
        out_specs=(rows(width), rows(width), rows(width), whole((2, width))),
        cost_estimate=cost(seq * width * 30, 13e6),
        name="norm_two",
    )(info, hn, m0, m1, cot, gain, bias)


def norm_one_back_kernel(info, z, dz2, p0, p1, gain, dz, dzb, sums):
    n, scale = center(z[...])
    gy = dz2[...] + (p0[...].astype(F32) + p1[...].astype(F32))
    grad = norm_back(n, scale, gy, gain[...])
    dz[...] = grad
    dzb[...] = grad.astype(BF16)
    add_sums(info, gy, n, sums)


def norm_one_back(info, z, dz2, p0, p1, gain):
    seq, width = z.shape
    return pl.pallas_call(
        norm_one_back_kernel,
        grid=(seq // TILE,),
        out_shape=(
            jax.ShapeDtypeStruct((seq, width), F32),
            jax.ShapeDtypeStruct((seq, width), BF16),
            jax.ShapeDtypeStruct((2, width), F32),
        ),
        in_specs=[smem()] + [rows(width)] * 4 + [whole((1, width))],
        out_specs=(rows(width), rows(width), whole((2, width))),
        cost_estimate=cost(seq * width * 30, 14e6),
        name="norm_one_back",
    )(info, z, dz2, p0, p1, gain)


def gelu_pair(u):
    z = jnp.abs(u) * 0.7071067811865476
    t = 1.0 / (1.0 + ERFCX_STEP * z)
    poly = jnp.full_like(t, ERFCX[-1])
    for coefficient in ERFCX[-2::-1]:
        poly = poly * t + coefficient
    e = jnp.exp(-z * z)
    tail = 0.5 * (poly * e)
    phi = jnp.where(u >= 0, 1.0 - tail, tail)
    return u * phi, phi + u * (e * 0.3989422804014327)


def feed_kernel(order, has_prior, info, hn, w, *rest):
    if has_prior:
        prior, active, slope, part, wfull = rest
    else:
        active, slope, part, wfull = rest
        prior = None

    @pl.when(pl.program_id(0) == 0)
    def _():
        place(order, info[0], w, wfull)

    units = active.shape[1]
    u = nn(hn[...], wfull[:, :units])
    a, g = gelu_pair(u)
    a = a.astype(BF16)
    active[...] = a
    slope[...] = g.astype(BF16)
    out = nt(a, wfull[:, units:])
    if prior is not None:
        out = out + prior[...]
    part[...] = out.astype(part.dtype)


def feed(order, info, hn, w, prior):
    seq, width = hn.shape
    units = w.shape[2] // 2
    last = BF16 if prior is not None else F32
    args = (info, hn, w) + (() if prior is None else (prior,))
    return pl.pallas_call(
        functools.partial(feed_kernel, order, prior is not None),
        grid=(seq // TILE,),
        out_shape=(
            jax.ShapeDtypeStruct((seq, units), BF16),
            jax.ShapeDtypeStruct((seq, units), BF16),
            jax.ShapeDtypeStruct((seq, width), last),
        ),
        in_specs=[smem(), rows(width), whole(w.shape)] + [rows(width)] * (len(args) - 3),
        out_specs=(rows(units), rows(units), rows(width)),
        scratch_shapes=[pltpu.VMEM((width, 2 * units), BF16)],
        compiler_params=params(32),
        cost_estimate=cost(4 * seq * width * units, 12e6, seq * units),
        name="feed",
    )(*args)


def feed_back_kernel(order, has_prior, info, dzb, slope, w, *rest):
    if has_prior:
        prior, du, part, wfull = rest
    else:
        du, part, wfull = rest
        prior = None

    @pl.when(pl.program_id(0) == 0)
    def _():
        place(order, info[0], w, wfull)

    units = du.shape[1]
    da = nn(dzb[...], wfull[:, units:])
    grad = (da * slope[...].astype(F32)).astype(BF16)
    du[...] = grad
    out = nt(grad, wfull[:, :units])
    if prior is not None:
        out = out + prior[...]
    part[...] = out.astype(part.dtype)


def feed_back(order, info, dzb, slope, w, prior):
    seq, width = dzb.shape
    units = slope.shape[1]
    last = BF16 if prior is not None else F32
    args = (info, dzb, slope, w) + (() if prior is None else (prior,))
    return pl.pallas_call(
        functools.partial(feed_back_kernel, order, prior is not None),
        grid=(seq // TILE,),
        out_shape=(
            jax.ShapeDtypeStruct((seq, units), BF16),
            jax.ShapeDtypeStruct((seq, width), last),
        ),
        in_specs=[smem(), rows(width), rows(units), whole(w.shape)]
        + [rows(width)] * (len(args) - 4),
        out_specs=(rows(units), rows(width)),
        scratch_shapes=[pltpu.VMEM((width, 2 * units), BF16)],
        compiler_params=params(32),
        cost_estimate=cost(4 * seq * width * units, 12e6),
        name="feed_back",
    )(*args)


def weight_grad_kernel(order, info, a, da, b, db, out, full_a, full_b):
    full_a[...] = tn(a[...], da[...])
    full_b[...] = tn(b[...], db[...])
    pick(order, info[0], (full_a, full_b), out)


def weight_grad(order, info, a, da, b, db):
    seq, width = a.shape
    total = da.shape[1] + db.shape[1]
    count = len(order)
    return pl.pallas_call(
        functools.partial(weight_grad_kernel, order),
        out_shape=jax.ShapeDtypeStruct((count, width // count, total), BF16),
        in_specs=[smem()] + [vmem()] * 4,
        out_specs=vmem(),
        scratch_shapes=[
            pltpu.VMEM((width, da.shape[1]), F32),
            pltpu.VMEM((width, db.shape[1]), F32),
        ],
        compiler_params=params(40),
        cost_estimate=cost(2 * seq * width * total, 9e6),
        name="weight_grad",
    )(info, a, da, b, db)


def across(values, axis, pairs):
    return lax.ppermute(values, axis, pairs)


def dp_pairs(size, bit):
    return [(i, i ^ (1 << bit)) for i in range(size)]


def gather_rows(piece, size, order):
    if len(order) == 1:
        return lax.all_gather(piece, "dp", axis=0, tiled=True)[None]
    held = piece[None]
    for bit in reversed(range(size.bit_length() - 1)):
        held = jnp.concatenate([held, across(held, "dp", dp_pairs(size, bit))], axis=0)
    return held


def sum_rows(own, other, size, order):
    got = across(other, "mp", CHIP_SWAP)
    total = own.astype(F32) + got.astype(F32)
    if len(order) == 1:
        return lax.psum_scatter(total[0], "dp", scatter_dimension=0, tiled=True)
    for bit in range(size.bit_length() - 1):
        half = total.shape[0] // 2
        sent = across(total[half:].astype(BF16), "dp", dp_pairs(size, bit))
        total = total[:half] + sent.astype(F32)
    return total[0]


def by_chip(x, own, other):
    return jnp.where(x == 0, jnp.stack([own, other]), jnp.stack([other, own]))


def local(
    tokens,
    w_query,
    w_key,
    w_value,
    w_out,
    w_up,
    w_down,
    gain_attn,
    bias_attn,
    gain_ffn,
    bias_ffn,
    lengths,
    random_blocks,
    cotangent,
):
    size = lax.axis_size("dp")
    rank = lax.axis_index("mp")
    me = lax.axis_index("dp")
    x, core = rank // 2, rank % 2
    _, quarter, features = tokens.shape
    seq = 4 * quarter
    height = w_query.shape[0]
    span = w_query.shape[1]
    heads = span // HD
    nblocks = seq // BLOCK
    order = (0,)
    if height % 16 == 0:
        for bit in reversed(range(size.bit_length() - 1)):
            order = order + tuple(i + (1 << bit) for i in order)

    length = lax.dynamic_index_in_dim(lengths, x, 0, keepdims=False)
    shift = x * (seq // 2)
    info = jnp.stack([me, x, core, length, shift]).astype(jnp.int32)

    piece = jnp.concatenate([w_query, w_key, w_value, w_out.T], axis=1)
    attn_own = gather_rows(piece, size, order)
    attn_other = across(attn_own, "mp", CHIP_SWAP)
    piece = jnp.concatenate([w_up, w_down.T], axis=1)
    feed_own = gather_rows(piece, size, order)
    feed_other = across(feed_own, "mp", CHIP_SWAP)

    def slot_rows(values):
        mine = lax.dynamic_index_in_dim(values, x, 0, keepdims=False)
        theirs = lax.dynamic_index_in_dim(values, 1 - x, 0, keepdims=False)
        pair = jnp.stack([mine, across(theirs, "mp", CHIP_SWAP)])
        sent = across(pair, "mp", CORE_SWAP)
        full = jnp.where(
            core == 0, jnp.stack([pair, sent], axis=1), jnp.stack([sent, pair], axis=1)
        )
        return full.reshape(seq, features)

    tok = slot_rows(tokens)
    cot = slot_rows(cotangent)

    blocks = (jnp.arange(nblocks) + x * (nblocks // 2)) % nblocks
    near = jnp.abs(blocks[:, None] - blocks[None, :]) <= 1
    edge = (blocks == 0) | (blocks == nblocks - 1)
    fixed = near | edge[:, None] | edge[None, :]

    def table(shard):
        chosen = lax.dynamic_slice_in_dim(random_blocks, shard * heads, heads, 0)
        chosen = jnp.roll(chosen, -x * (nblocks // 2), axis=1)
        hit = jnp.any(chosen[:, None, :, :] == blocks[None, :, None, None], axis=3)
        bias = jnp.where(fixed.T[None] | hit, 0.0, NEGATIVE)
        return jnp.concatenate(
            [
                jnp.zeros((heads, nblocks, HD), F32),
                bias,
                jnp.full((heads, nblocks, 3), -1.0, F32),
                jnp.zeros((heads, nblocks, HD - 3 - nblocks), F32),
            ],
            axis=2,
        )

    mask_own, mask_other = table(rank), table(rank ^ 2)
    g_one, b_one = gain_attn[None], bias_attn[None]
    g_two, b_two = gain_ffn[None], bias_ffn[None]

    qa0, ka0, va0, ctx0, attn_part = attend(order, info, tok, attn_own, mask_own, None)
    qa1, ka1, va1, ctx1, attn_part = attend(order, info, tok, attn_other, mask_other, attn_part)
    z_one, hn = norm_one(tok, attn_part, across(attn_part, "mp", CORE_SWAP), g_one, b_one)

    act0, slope0, mixed = feed(order, info, hn, feed_own, None)
    act1, slope1, mixed = feed(order, info, hn, feed_other, mixed)
    out, dz_two, dzb_two, sums_two = norm_two(
        info, hn, mixed, across(mixed, "mp", CORE_SWAP), cot, g_two, b_two
    )
    out = out.reshape(2, 2, quarter, features)
    out = lax.dynamic_index_in_dim(out, core, 1, keepdims=False)
    output = by_chip(x, out[0], across(out[1], "mp", CHIP_SWAP))

    du1, back = feed_back(order, info, dzb_two, slope1, feed_other, None)
    du0, back = feed_back(order, info, dzb_two, slope0, feed_own, back)
    back_got = across(back, "mp", CORE_SWAP)
    grad_feed1 = weight_grad(order, info, hn, du1, dzb_two, act1)
    grad_feed0 = weight_grad(order, info, hn, du0, dzb_two, act0)
    grad_feed = sum_rows(grad_feed0, grad_feed1, size, order)

    dz_one, dzb_one, sums_one = norm_one_back(info, z_one, dz_two, back, back_got, g_one)
    sums = jnp.concatenate([sums_one, sums_two], axis=0)
    sums = sums + across(sums, "mp", CORE_SWAP)
    sums = sums + across(sums, "mp", CHIP_SWAP)
    for bit in range(size.bit_length() - 1):
        sums = sums + across(sums, "dp", dp_pairs(size, bit))

    dqkv1, back = attend_back(order, info, dzb_one, attn_other, qa1, ka1, va1, ctx1, None)
    grad_attn1 = weight_grad(order, info, tok, dqkv1, dzb_one, ctx1)
    dqkv0, back = attend_back(order, info, dzb_one, attn_own, qa0, ka0, va0, ctx0, back)
    grad_attn0 = weight_grad(order, info, tok, dqkv0, dzb_one, ctx0)

    back = back.reshape(2, 2, quarter, features)
    mine = lax.dynamic_index_in_dim(back, core, 1, keepdims=False)
    sent = lax.dynamic_index_in_dim(back, 1 - core, 1, keepdims=False)
    kept = lax.dynamic_index_in_dim(
        dz_one.reshape(2, 2, quarter, features), core, 1, keepdims=False
    )
    final = kept + mine.astype(F32) + across(sent, "mp", CORE_SWAP).astype(F32)
    grad_tokens = by_chip(
        x, final[0], across(final[1].astype(BF16), "mp", CHIP_SWAP).astype(F32)
    )
    grad_attn = sum_rows(grad_attn0, grad_attn1, size, order)

    units = w_up.shape[1]
    return (
        output,
        grad_tokens,
        grad_attn[:, :span],
        grad_attn[:, span : 2 * span],
        grad_attn[:, 2 * span : 3 * span],
        grad_attn[:, 3 * span :].T,
        grad_feed[:, :units],
        grad_feed[:, units:].T,
        sums[0],
        sums[1],
        sums[2],
        sums[3],
    )


def solution(mesh):
    return jax.shard_map(
        local,
        mesh=mesh,
        in_specs=(
            P("dp", "mp", None),
            P("dp", "mp"),
            P("dp", "mp"),
            P("dp", "mp"),
            P("mp", "dp"),
            P("dp", "mp"),
            P("mp", "dp"),
            P(),
            P(),
            P(),
            P(),
            P("dp"),
            P(),
            P("dp", "mp", None),
        ),
        out_specs=(
            P("dp", "mp", None),
            P("dp", "mp", None),
            P("dp", "mp"),
            P("dp", "mp"),
            P("dp", "mp"),
            P("mp", "dp"),
            P("dp", "mp"),
            P("mp", "dp"),
            P(),
            P(),
            P(),
            P(),
        ),
        check_vma=False,
    )
```

```python
import functools

import jax
import jax.numpy as jnp
from jax import lax
from jax.experimental import pallas as pl
from jax.experimental.pallas import tpu as pltpu
from jax.sharding import PartitionSpec as P

HD = 64
BLOCK = 64
LANES = 128
TILE = 256
EPSILON = 1e-12
SCALE = 0.125
LOG2E = 1.4426950408889634
LN2 = 0.6931471805599453
NEGATIVE = -1e30
F32 = jnp.float32
BF16 = jnp.bfloat16

ERFCX_STEP = 0.45
ERFCX = (
    -8.220994855312894e-06,
    0.2540684902923417,
    0.25234751996246985,
    0.23373082558517694,
    0.1739141918052578,
    0.06370751405215419,
    0.18661300519520473,
    -0.22870513112792096,
    0.06433208636936971,
)

CORE_SWAP = [(0, 1), (1, 0), (2, 3), (3, 2)]
CHIP_SWAP = [(0, 2), (2, 0), (1, 3), (3, 1)]


def nn(a, b):
    return lax.dot_general(a, b, (((1,), (0,)), ((), ())), preferred_element_type=F32)


def nt(a, b):
    return lax.dot_general(a, b, (((1,), (1,)), ((), ())), preferred_element_type=F32)


def tn(a, b):
    return lax.dot_general(a, b, (((0,), (0,)), ((), ())), preferred_element_type=F32)


def vmem():
    return pl.BlockSpec(memory_space=pltpu.VMEM)


def smem():
    return pl.BlockSpec(memory_space=pltpu.SMEM)


def anywhere():
    return pl.BlockSpec(memory_space=pl.ANY)


def rows(width):
    return pl.BlockSpec((TILE, width), lambda i: (i, 0))


def whole(shape):
    return pl.BlockSpec(shape, lambda i: (0,) * len(shape))


def array(shape, dtype):
    return jax.ShapeDtypeStruct(shape, dtype)


def run(kernel, name, args, specs, outs, out_specs, scratch=(), mib=32, flops=0, moved=0, grid=(), after=()):
    given, extra = len(args), len(after)

    def body(*refs):
        kernel(*refs[:given], *refs[given + extra :])

    return pl.pallas_call(
        body,
        grid=grid,
        out_shape=tuple(outs),
        in_specs=list(specs) + [anywhere()] * extra,
        out_specs=tuple(out_specs),
        scratch_shapes=list(scratch),
        compiler_params=pltpu.CompilerParams(vmem_limit_bytes=mib * 2**20),
        cost_estimate=pl.CostEstimate(flops=1, bytes_accessed=1, transcendentals=0),
        name=name,
    )(*args, *after)


def place(me, refs, slots, dst_ref, first=0, last=None):
    for ref, of in zip(refs, slots):
        height, width = ref.shape[1], ref.shape[2]
        end = width if last is None else last
        for e, (chip, j) in enumerate(of):
            at = 0 if height == dst_ref.shape[0] else pl.multiple_of((me ^ j) * height, height)
            to = chip * (end - first)
            dst_ref[pl.ds(at, height), pl.ds(to, end - first)] = ref[e, :, first:end]


def pick(me, full_ref, out_ref, slots, width):
    height = out_ref.shape[1]
    for e, (chip, j) in enumerate(slots):
        at = 0 if height == full_ref.shape[0] else pl.multiple_of((me ^ j) * height, height)
        out_ref[e] = full_ref[pl.ds(at, height), pl.ds(chip * width, width)].astype(BF16)


def attend_kernel(slots, info, tok, mask, *rest):
    refs, (qa, ka, va, ctx, wfull) = rest[: len(slots)], rest[len(slots) :]
    seq = tok.shape[0]
    heads = qa.shape[0]
    width = wfull.shape[1]
    first = 0 if heads == 2 else HD
    span = heads * HD
    place(info[0], refs, slots, wfull, refs[0].shape[2] - width)
    lane = lax.broadcasted_iota(jnp.int32, (TILE, LANES), 1)
    row0 = lax.broadcasted_iota(jnp.int32, (TILE, LANES), 0)
    for t in range(seq // TILE):
        at = pl.ds(t * TILE, TILE)
        row = row0 + t * TILE
        made = nn(tok[at, :], wfull[...])
        onehot = jnp.where(lane - HD == row // BLOCK, 1.0, 0.0)[:, HD:]
        position = row + info[4]
        position = jnp.where(position >= seq, position - seq, position)
        dead = (position >= info[3]) & (lane >= HD) & (lane < HD + 16)
        for h in range(heads):
            q_at = first + h * HD
            q = made[:, q_at : q_at + HD] * (SCALE * LOG2E)
            k = made[:, q_at + span : q_at + span + HD]
            v = made[:, q_at + 2 * span : q_at + 2 * span + HD]
            qa[h, at, :] = jnp.concatenate([q, onehot], axis=1).astype(BF16)
            per = TILE // BLOCK
            table = jnp.concatenate(
                [
                    jnp.broadcast_to(mask[h, t * per + b : t * per + b + 1, :], (BLOCK, LANES))
                    for b in range(per)
                ],
                axis=0,
            )
            table = jnp.where(dead, NEGATIVE, table)
            ka[h, at, :] = jnp.concatenate([k, table[:, HD:]], axis=1).astype(BF16)
            va[h, at, :] = jnp.concatenate([v, jnp.full((TILE, HD), -1.0, F32)], axis=1).astype(BF16)
    for t in range(seq // TILE):
        at = pl.ds(t * TILE, TILE)
        pieces = []
        for h in range(heads):
            q = qa[h, at, :]
            s = nt(q, ka[h])
            top = jnp.max(s, axis=1, keepdims=True)
            p = jnp.exp2(s - top).astype(BF16)
            got = nn(p, va[h])
            total = -got[:, HD:]
            pieces.append(got[:, :HD] / total)
            log = top + jnp.log2(-got)
            hi = log.astype(BF16).astype(F32)
            mid = (log - hi).astype(BF16).astype(F32)
            low = log - hi - mid
            new = jnp.where(
                lane == HD + 16,
                hi,
                jnp.where(lane == HD + 17, mid, jnp.where(lane == HD + 18, low, q.astype(F32))),
            )
            qa[h, at, :] = new.astype(BF16)
        if heads == 1:
            pieces.append(jnp.zeros((TILE, HD), F32))
        ctx[at, :] = jnp.concatenate(pieces, axis=1).astype(BF16)


def attend(info, tok, gathered, mask, after=()):
    arrays, slots = gathered
    seq, width = tok.shape
    heads = mask.shape[0]
    cols = 6 * HD if heads == 2 else 4 * HD
    aug = array((heads, seq, LANES), BF16)
    return run(
        functools.partial(attend_kernel, slots),
        "attend",
        (info, tok, mask) + arrays,
        [smem()] + [vmem()] * (2 + len(arrays)),
        (aug, aug, aug, array((seq, LANES), BF16)),
        [vmem()] * 4,
        [pltpu.VMEM((width, cols), BF16)],
        40,
        2 * seq * width * cols + 4 * heads * seq * seq * LANES,
        4e6,
        after=after,
    )


def project_kernel(slots, info, c01a, c2a, c01b, c2b, *rest):
    refs, (part, wfull) = rest[: len(slots)], rest[len(slots) :]

    @pl.when(pl.program_id(0) == 0)
    def _():
        place(info[0], refs, slots, wfull, 0, 4 * HD)

    both = jnp.concatenate([c01a[...], c2a[...], c01b[...], c2b[...]], axis=1)
    part[...] = nt(both, wfull[...]).astype(BF16)


def project(info, contexts, gathered, width, after=()):
    arrays, slots = gathered
    seq = contexts[0].shape[0]
    return run(
        functools.partial(project_kernel, slots),
        "project",
        (info,) + contexts + arrays,
        [smem()] + [rows(LANES)] * 4 + [whole(a.shape) for a in arrays],
        (array((seq, width), BF16),),
        [rows(width)],
        [pltpu.VMEM((width, 8 * HD), BF16)],
        32,
        2 * seq * width * 8 * HD,
        4e6,
        (seq // TILE,),
        after,
    )[0]


def attend_back_kernel(slots, info, dz, qa, ka, va, ctx, *rest):
    refs, (dqkv, wfull, da, parts) = rest[: len(slots)], rest[len(slots) :]
    seq = dz.shape[0]
    heads = qa.shape[0]
    first = 0 if heads == 2 else LANES
    place(info[0], refs, slots, wfull, first, first + LANES)
    lane = lax.broadcasted_iota(jnp.int32, (TILE, LANES), 1)
    for t in range(seq // TILE):
        at = pl.ds(t * TILE, TILE)
        dctx = nn(dz[at, :], wfull[...]).astype(BF16).astype(F32)
        both = dctx * ctx[at, :].astype(F32)
        for h in range(heads):
            inner = jnp.sum(both[:, h * HD : (h + 1) * HD], axis=1, keepdims=True)
            hi = inner.astype(BF16).astype(F32)
            mid = (inner - hi).astype(BF16).astype(F32)
            low = inner - hi - mid
            one = jnp.concatenate(
                [dctx[:, h * HD : (h + 1) * HD], jnp.zeros((TILE, HD), F32)], axis=1
            )
            one = jnp.where(lane == HD, hi, one)
            one = jnp.where(lane == HD + 1, mid, one)
            one = jnp.where(lane == HD + 2, low, one)
            da[h, at, :] = one.astype(BF16)
    for h in range(heads):
        k_turned = jnp.transpose(ka[h].astype(F32)).astype(BF16)
        dq_turned = None
        for t in range(seq // TILE):
            at = pl.ds(t * TILE, TILE)
            p = jnp.exp2(nt(ka[h, at, :], qa[h]))
            ds = (p * nt(va[h, at, :], da[h])).astype(BF16)
            parts[2 * heads + h, at, :] = nn(p.astype(BF16), da[h])
            parts[heads + h, at, :] = nn(ds, qa[h]) * LN2
            more = nn(k_turned[:, t * TILE : (t + 1) * TILE], ds)
            dq_turned = more if dq_turned is None else dq_turned + more
        parts[h] = jnp.transpose(dq_turned) * SCALE
    for t in range(seq // TILE):
        at = pl.ds(t * TILE, TILE)
        pieces = [] if heads == 2 else [jnp.zeros((TILE, HD), F32)]
        pieces += [parts[i, at, :][:, :HD] for i in range(3 * heads)]
        dqkv[at, :] = jnp.concatenate(pieces, axis=1).astype(BF16)


def attend_back(info, dz, gathered, saved, after=()):
    arrays, slots = gathered
    qa, ka, va, ctx = saved
    seq, width = dz.shape
    heads = qa.shape[0]
    cols = 6 * HD if heads == 2 else 4 * HD
    return run(
        functools.partial(attend_back_kernel, slots),
        "attend_back",
        (info, dz, qa, ka, va, ctx) + arrays,
        [smem()] + [vmem()] * (5 + len(arrays)),
        (array((seq, cols), BF16),),
        [vmem()],
        [
            pltpu.VMEM((width, LANES), BF16),
            pltpu.VMEM((heads, seq, LANES), BF16),
            pltpu.VMEM((3 * heads, seq, LANES), F32),
        ],
        48,
        2 * seq * width * LANES + 10 * heads * seq * seq * LANES,
        6e6,
        after=after,
    )[0]


def input_back_kernel(slots1, slots2, info, d01a, d2a, d01b, d2b, *rest):
    n1, n2 = len(slots1), len(slots2)
    refs1, refs2, (back, w1, w2) = rest[:n1], rest[n1 : n1 + n2], rest[n1 + n2 :]

    @pl.when(pl.program_id(0) == 0)
    def _():
        place(info[0], refs1, slots1, w1)
        place(info[0], refs2, slots2, w2, 2 * HD, 6 * HD)

    pairs = jnp.concatenate([d01a[...], d01b[...]], axis=1)
    singles = jnp.concatenate([d2a[...], d2b[...]], axis=1)
    back[...] = (nt(pairs, w1[...]) + nt(singles, w2[...])).astype(BF16)


def input_back(info, grads, gathered1, gathered2, width, after=()):
    seq = grads[0].shape[0]
    arrays = gathered1[0] + gathered2[0]
    return run(
        functools.partial(input_back_kernel, gathered1[1], gathered2[1]),
        "input_back",
        (info,) + grads + arrays,
        [smem()] + [rows(g.shape[1]) for g in grads] + [whole(a.shape) for a in arrays],
        (array((seq, width), BF16),),
        [rows(width)],
        [pltpu.VMEM((width, 12 * HD), BF16), pltpu.VMEM((width, 8 * HD), BF16)],
        32,
        2 * seq * width * 20 * HD,
        7e6,
        (seq // TILE,),
        after,
    )[0]


def center(z):
    mean = jnp.mean(z, axis=1, keepdims=True)
    moved = z - mean
    spread = jnp.mean(moved * moved, axis=1, keepdims=True)
    scale = lax.rsqrt(spread + EPSILON)
    return moved * scale, scale


def norm_back(n, scale, gy, gain):
    dn = gy * gain
    return scale * (
        dn - jnp.mean(dn, axis=1, keepdims=True) - n * jnp.mean(dn * n, axis=1, keepdims=True)
    )


def add_sums(info, gy, n, sums):
    i = pl.program_id(0)

    @pl.when(i == 0)
    def _():
        sums[...] = jnp.zeros_like(sums)

    @pl.when((i & 1) == info[2])
    def _():
        sums[0:1, :] += jnp.sum(gy * n, axis=0, keepdims=True)
        sums[1:2, :] += jnp.sum(gy, axis=0, keepdims=True)


def norm_one_kernel(tok, p0, p1, gain, bias, z, hn):
    value = tok[...].astype(F32) + (p0[...].astype(F32) + p1[...].astype(F32))
    z[...] = value
    n, _ = center(value)
    hn[...] = (n * gain[...] + bias[...]).astype(BF16)


def norm_one(tok, p0, p1, gain, bias, after=()):
    seq, width = tok.shape
    return run(
        norm_one_kernel,
        "norm_one",
        (tok, p0, p1, gain, bias),
        [rows(width)] * 3 + [whole((1, width))] * 2,
        (array((seq, width), F32), array((seq, width), BF16)),
        (rows(width), rows(width)),
        flops=seq * width * 10,
        moved=9e6,
        grid=(seq // TILE,),
        after=after,
    )


def norm_two_kernel(info, hn, m0, m1, cot, gain, bias, out, dz, dzb, sums):
    value = hn[...].astype(F32) + (m0[...].astype(F32) + m1[...].astype(F32))
    n, scale = center(value)
    out[...] = (n * gain[...] + bias[...]).astype(BF16)
    row = lax.broadcasted_iota(jnp.int32, value.shape, 0) + pl.program_id(0) * TILE
    seq = pl.num_programs(0) * TILE
    position = row + info[4]
    position = jnp.where(position >= seq, position - seq, position)
    gy = jnp.where(position < info[3], cot[...].astype(F32), 0.0)
    grad = norm_back(n, scale, gy, gain[...])
    dz[...] = grad
    dzb[...] = grad.astype(BF16)
    add_sums(info, gy, n, sums)


def norm_two(info, hn, m0, m1, cot, gain, bias, after=()):
    seq, width = hn.shape
    return run(
        norm_two_kernel,
        "norm_two",
        (info, hn, m0, m1, cot, gain, bias),
        [smem()] + [rows(width)] * 4 + [whole((1, width))] * 2,
        (
            array((seq, width), BF16),
            array((seq, width), F32),
            array((seq, width), BF16),
            array((2, width), F32),
        ),
        (rows(width), rows(width), rows(width), whole((2, width))),
        flops=seq * width * 30,
        moved=13e6,
        grid=(seq // TILE,),
        after=after,
    )


def norm_one_back_kernel(info, z, dz2, p0, p1, gain, dz, dzb, sums):
    n, scale = center(z[...])
    gy = dz2[...] + (p0[...].astype(F32) + p1[...].astype(F32))
    grad = norm_back(n, scale, gy, gain[...])
    dz[...] = grad
    dzb[...] = grad.astype(BF16)
    add_sums(info, gy, n, sums)


def norm_one_back(info, z, dz2, p0, p1, gain, after=()):
    seq, width = z.shape
    return run(
        norm_one_back_kernel,
        "norm_one_back",
        (info, z, dz2, p0, p1, gain),
        [smem()] + [rows(width)] * 4 + [whole((1, width))],
        (array((seq, width), F32), array((seq, width), BF16), array((2, width), F32)),
        (rows(width), rows(width), whole((2, width))),
        flops=seq * width * 30,
        moved=14e6,
        grid=(seq // TILE,),
        after=after,
    )


def gelu_pair(u):
    z = jnp.abs(u) * 0.7071067811865476
    t = 1.0 / (1.0 + ERFCX_STEP * z)
    poly = jnp.full_like(t, ERFCX[-1])
    for coefficient in ERFCX[-2::-1]:
        poly = poly * t + coefficient
    e = jnp.exp(-z * z)
    tail = 0.5 * (poly * e)
    phi = jnp.where(u >= 0, 1.0 - tail, tail)
    return u * phi, phi + u * (e * 0.3989422804014327)


def feed_up_kernel(slots, info, hn, *rest):
    refs, (active, slope, wfull) = rest[: len(slots)], rest[len(slots) :]

    @pl.when(pl.program_id(0) == 0)
    def _():
        place(info[0], refs, slots, wfull)

    a, g = gelu_pair(nn(hn[...], wfull[...]))
    active[...] = a.astype(BF16)
    slope[...] = g.astype(BF16)


def feed_up(info, hn, gathered, units, after=()):
    arrays, slots = gathered
    seq, width = hn.shape
    return run(
        functools.partial(feed_up_kernel, slots),
        "feed_up",
        (info, hn) + arrays,
        [smem(), rows(width)] + [whole(a.shape) for a in arrays],
        (array((seq, units), BF16), array((seq, units), BF16)),
        (rows(units), rows(units)),
        [pltpu.VMEM((width, units), BF16)],
        flops=2 * seq * width * units,
        moved=6e6,
        grid=(seq // TILE,),
        after=after,
    )


def feed_down_kernel(slots1, slots2, info, act1, act2, *rest):
    n1, n2 = len(slots1), len(slots2)
    refs1, refs2, (part, w1, w2) = rest[:n1], rest[n1 : n1 + n2], rest[n1 + n2 :]

    @pl.when(pl.program_id(0) == 0)
    def _():
        place(info[0], refs1, slots1, w1)
        place(info[0], refs2, slots2, w2)

    part[...] = (nt(act1[...], w1[...]) + nt(act2[...], w2[...])).astype(BF16)


def feed_down(info, act1, act2, gathered1, gathered2, width, after=()):
    seq, units = act1.shape
    arrays = gathered1[0] + gathered2[0]
    return run(
        functools.partial(feed_down_kernel, gathered1[1], gathered2[1]),
        "feed_down",
        (info, act1, act2) + arrays,
        [smem(), rows(units), rows(units)] + [whole(a.shape) for a in arrays],
        (array((seq, width), BF16),),
        [rows(width)],
        [pltpu.VMEM((width, units), BF16)] * 2,
        flops=4 * seq * width * units,
        moved=8e6,
        grid=(seq // TILE,),
        after=after,
    )[0]


def feed_back_kernel(slots, info, dzb, slope1, slope2, *rest):
    total = sum(len(of) for of in slots)
    refs, (du1, du2, part, u1, u2, d1, d2) = rest[:total], rest[total:]

    @pl.when(pl.program_id(0) == 0)
    def _():
        first = 0
        for of, full in zip(slots, (u1, u2, d1, d2)):
            place(info[0], refs[first : first + len(of)], of, full)
            first += len(of)

    out = None
    for slope, du, up, down in ((slope1, du1, u1, d1), (slope2, du2, u2, d2)):
        da = nn(dzb[...], down[...])
        grad = (da * slope[...].astype(F32)).astype(BF16)
        du[...] = grad
        more = nt(grad, up[...])
        out = more if out is None else out + more
    part[...] = out.astype(BF16)


def feed_back(info, dzb, slope1, slope2, ups, downs, after=()):
    seq, width = dzb.shape
    units = slope1.shape[1]
    chunks = ups + downs
    arrays = sum((c[0] for c in chunks), ())
    return run(
        functools.partial(feed_back_kernel, tuple(c[1] for c in chunks)),
        "feed_back",
        (info, dzb, slope1, slope2) + arrays,
        [smem(), rows(width), rows(units), rows(units)] + [whole(a.shape) for a in arrays],
        (array((seq, units), BF16), array((seq, units), BF16), array((seq, width), BF16)),
        (rows(units), rows(units), rows(width)),
        [pltpu.VMEM((width, units), BF16)] * 4,
        48,
        8 * seq * width * units,
        16e6,
        (seq // TILE,),
        after,
    )


def feed_grad_kernel(places, info, a, d1, d2, keep1, send1, keep2, send2, full):
    for right, keep, send, (kept, sent) in (
        (d1, keep1, send1, places[0]),
        (d2, keep2, send2, places[1]),
    ):
        full[...] = tn(a[...], right[...])
        pick(info[0], full, keep, kept, keep.shape[2])
        pick(info[0], full, send, sent, send.shape[2])


def feed_grad(info, a, d1, d2, places, after=()):
    seq, width = a.shape
    units = d1.shape[1]
    count = len(places[0][0])
    half = array((count, 2 * width // (2 * count), units // 2), BF16)
    return run(
        functools.partial(feed_grad_kernel, places),
        "feed_grad",
        (info, a, d1, d2),
        [smem()] + [vmem()] * 3,
        (half,) * 4,
        [vmem()] * 4,
        [pltpu.VMEM((width, units), F32)],
        40,
        4 * seq * width * units,
        9e6,
        after=after,
    )


def pair_grad_kernel(slots, info, tok, d, out, full):
    full[...] = tn(tok[...], d[...])
    pick(info[0], full, out, slots, out.shape[2])


def pair_grad(info, tok, d, slots, after=()):
    seq, width = tok.shape
    cols = d.shape[1]
    return run(
        functools.partial(pair_grad_kernel, slots),
        "pair_grad",
        (info, tok, d),
        [smem()] + [vmem()] * 2,
        (array((len(slots), width // len(slots), cols), BF16),),
        [vmem()],
        [pltpu.VMEM((width, cols), F32)],
        32,
        2 * seq * width * cols,
        4e6,
        after=after,
    )[0]


def single_grad_kernel(slots, info, tok, d, dz, c01, c2, out, full):
    full[:, :LANES] = tn(dz[...], c01[...])
    mine = tn(tok[...], d[...])
    full[:, LANES : 2 * LANES] = tn(dz[...], c2[...]) + mine[:, :LANES]
    full[:, 2 * LANES :] = mine[:, LANES:]
    pick(info[0], full, out, slots, out.shape[2])


def single_grad(info, tok, d, dz, c01, c2, slots, after=()):
    seq, width = tok.shape
    cols = 6 * HD
    return run(
        functools.partial(single_grad_kernel, slots),
        "single_grad",
        (info, tok, d, dz, c01, c2),
        [smem()] + [vmem()] * 5,
        (array((len(slots), width // len(slots), cols), BF16),),
        [vmem()],
        [pltpu.VMEM((width, cols), F32)],
        32,
        4 * seq * width * cols,
        6e6,
        after=after,
    )[0]


def across(values, axis, pairs):
    return lax.ppermute(values, axis, pairs)


def flip_chip(values):
    return across(values, "mp", CHIP_SWAP)


def flip_core(values):
    return across(values, "mp", CORE_SWAP)


def flip_dp(values, distance):
    size = lax.axis_size("dp")
    return across(values, "dp", [(i, i ^ distance) for i in range(size)])


def join_kernel(count, *refs):
    parts, out, sems = refs[:count], refs[count], refs[count + 1]
    copies = []
    first = 0
    for i, part in enumerate(parts):
        to = out.at[pl.ds(first, part.shape[0])]
        copies.append(pltpu.make_async_copy(part, to, sems.at[i]))
        first += part.shape[0]
    for copy in copies:
        copy.start()
    for copy in copies:
        copy.wait()


def join(parts, after=()):
    total = sum(p.shape[0] for p in parts)
    shape = (total,) + parts[0].shape[1:]
    return run(
        functools.partial(join_kernel, len(parts)),
        "join",
        tuple(parts),
        [anywhere()] * len(parts),
        (array(shape, parts[0].dtype),),
        [anywhere()],
        [pltpu.SemaphoreType.DMA((len(parts),))],
        moved=1e5,
        after=after,
    )[0]


def fold_kernel(own, got, *outs):
    each = own.shape[0] // len(outs)
    for i, out in enumerate(outs):
        at = pl.ds(i * each, each)
        out[...] = (own[at].astype(F32) + got[at].astype(F32)).astype(BF16)


def fold(own, got, parts, after=()):
    shape = (own.shape[0] // parts,) + own.shape[1:]
    return run(
        fold_kernel,
        "fold",
        (own, got),
        [vmem()] * 2,
        (array(shape, BF16),) * parts,
        [vmem()] * parts,
        moved=1e5,
        after=after,
    )


Y_MAJOR = (0, 2, 4, 6, 1, 3, 5, 7)
OWN = tuple((0, j) for j in Y_MAJOR)
OTHER = tuple((1, j) for j in Y_MAJOR)
NEAR_Y = tuple((chip, 2 * z) for chip in range(2) for z in range(4))
FAR_Y = tuple((chip, 2 * z + 1) for chip in range(2) for z in range(4))


def z_sends(values):
    return [flip_dp(values, 2 * z) for z in (1, 2, 3)]


def finish(pieces):
    got = [flip_dp(pieces[z], 2 * z) for z in (1, 2, 3)]
    total = pieces[0].astype(F32)
    for g in got:
        total = total + g.astype(F32)
    return total[0]


def by_chip(x, own, other):
    return jnp.where(x == 0, jnp.stack([own, other]), jnp.stack([other, own]))


def local(
    tokens,
    w_query,
    w_key,
    w_value,
    w_out,
    w_up,
    w_down,
    gain_attn,
    bias_attn,
    gain_ffn,
    bias_ffn,
    lengths,
    random_blocks,
    cotangent,
):
    size = lax.axis_size("dp")
    rank = lax.axis_index("mp")
    me = lax.axis_index("dp")
    x, core = rank // 2, rank % 2
    _, quarter, features = tokens.shape
    seq = 4 * quarter
    height = w_query.shape[0]
    span = w_query.shape[1]
    heads = span // HD
    nblocks = seq // BLOCK
    fast = size == 8 and height % 16 == 0

    length = lax.dynamic_index_in_dim(lengths, x, 0, keepdims=False)
    shift = x * (seq // 2)
    info = jnp.stack([me, x, core, length, shift]).astype(jnp.int32)
    units = w_up.shape[1]
    half = units // 2

    wo = w_out.T
    piece_pair = jnp.concatenate(
        [w[:, : 2 * HD] for w in (w_query, w_key, w_value)], axis=1
    )[None]
    piece_single = jnp.concatenate(
        [wo] + [w[:, 2 * HD :] for w in (w_query, w_key, w_value)], axis=1
    )[None]
    wd = w_down.T
    piece_up = (w_up[None, :, :half], w_up[None, :, half:])
    piece_down = (wd[None, :, :half], wd[None, :, half:])

    def slot_pair(values):
        mine = lax.dynamic_index_in_dim(values, x, 0, keepdims=False)
        theirs = lax.dynamic_index_in_dim(values, 1 - x, 0, keepdims=False)
        return jnp.stack([mine, flip_chip(theirs)])

    def slot_rows(pair):
        sent = flip_core(pair)
        full = jnp.where(
            core == 0, jnp.stack([pair, sent], axis=1), jnp.stack([sent, pair], axis=1)
        )
        return full.reshape(seq, features)

    blocks = (jnp.arange(nblocks) + x * (nblocks // 2)) % nblocks
    near_blocks = jnp.abs(blocks[:, None] - blocks[None, :]) <= 1
    edge = (blocks == 0) | (blocks == nblocks - 1)
    fixed = near_blocks | edge[:, None] | edge[None, :]

    def table(shard):
        chosen = lax.dynamic_slice_in_dim(random_blocks, shard * heads, heads, 0)
        chosen = jnp.roll(chosen, -x * (nblocks // 2), axis=1)
        hit = jnp.any(chosen[:, None, :, :] == blocks[None, :, None, None], axis=3)
        bias = jnp.where(fixed.T[None] | hit, 0.0, NEGATIVE)
        return jnp.concatenate(
            [
                jnp.zeros((heads, nblocks, HD), F32),
                bias,
                jnp.full((heads, nblocks, 3), -1.0, F32),
                jnp.zeros((heads, nblocks, HD - 3 - nblocks), F32),
            ],
            axis=2,
        )

    mask_own, mask_other = table(rank), table(rank ^ 2)

    if fast:
        zs_pair = [piece_pair] + z_sends(piece_pair)
        tok = slot_rows(slot_pair(tokens))
        ys_pair = [flip_dp(z, 1) for z in zs_pair]
        zs_single = [piece_single] + z_sends(piece_single)
        ys_single = [flip_dp(z, 1) for z in zs_single]
        got_up, got_down = flip_chip(piece_up[1]), flip_chip(piece_down[1])
        cot = slot_rows(slot_pair(cotangent))

        held_up = join([piece_up[0]], (zs_pair[1],))
        zs_up = z_sends(held_up)
        chip_up = join([piece_up[1], got_up], (held_up,))
        zs_up2 = z_sends(chip_up)
        own_pair = join(zs_pair + ys_pair, (chip_up,))
        other_pair = flip_chip(own_pair)
        held_down = join([piece_down[0]], (own_pair,))
        zs_down = z_sends(held_down)
        chip_down = join([piece_down[1], got_down], (held_down,))
        zs_down2 = z_sends(chip_down)
        own_single = join(zs_single + ys_single, (chip_down,))
        other_single = flip_chip(own_single)
        four_up = join([held_up] + zs_up, (own_single,))
        y_up = flip_dp(four_up, 1)
        flat = (tuple((0, j) for j in Y_MAJOR),)
        own01 = attend(info, tok, ((own_pair,), flat), mask_own[:2], (four_up,))
        own_up = join([four_up, y_up], (own01[0],))
        other_up = flip_chip(own_up)
        four_up2 = join([chip_up] + zs_up2, (own_up,))
        ys_up2 = flip_dp(four_up2, 1)
        own2 = attend(info, tok, ((own_single,), flat), mask_own[2:], (four_up2,))
        four_down = join([held_down] + zs_down, (own2[0],))
        y_down = flip_dp(four_down, 1)
        other01 = attend(
            info, tok, ((other_pair,), flat), mask_other[:2], (four_down,)
        )
        own_down = join([four_down, y_down], (other01[0],))
        other_down = flip_chip(own_down)
        four_down2 = join([chip_down] + zs_down2, (own_down,))
        ys_down2 = flip_dp(four_down2, 1)
        other2 = attend(
            info, tok, ((other_single,), flat), mask_other[2:], (four_down2, cot)
        )
        flat = (tuple((0, j) for j in Y_MAJOR),)
        pair_w = (((own_pair,), flat), ((other_pair,), flat))
        single_w = (((own_single,), flat), ((other_single,), flat))
        near = tuple((chip, 2 * z) for z in range(4) for chip in range(2))
        far = tuple((chip, 2 * z + 1) for z in range(4) for chip in range(2))
        up1 = ((own_up, other_up), (OWN, OTHER))
        up2 = ((four_up2, ys_up2), (near, far))
        down1 = ((own_down, other_down), (OWN, OTHER))
        down2 = ((four_down2, ys_down2), (near, far))
        both_single = ((own_single, other_single), (OWN, OTHER))
        both_pair = ((own_pair, other_pair), (OWN, OTHER))
    else:
        tok, cot = slot_rows(slot_pair(tokens)), slot_rows(slot_pair(cotangent))

        def plain(piece):
            own = lax.all_gather(piece[0], "dp", axis=0, tiled=True)[None]
            return own, flip_chip(own)

        own_pair, other_pair = plain(piece_pair)
        own_single, other_single = plain(piece_single)
        flat = (((0, 0),),)
        pair_w = (((own_pair,), flat), ((other_pair,), flat))
        single_w = (((own_single,), flat), ((other_single,), flat))
        two = (((0, 0),), ((1, 0),))
        up1 = (plain(piece_up[0]), two)
        up2 = (plain(piece_up[1]), two)
        down1 = (plain(piece_down[0]), two)
        down2 = (plain(piece_down[1]), two)
        both_single = ((own_single, other_single), two)
        both_pair = ((own_pair, other_pair), two)


    g_one, b_one = gain_attn[None], bias_attn[None]
    g_two, b_two = gain_ffn[None], bias_ffn[None]

    if not fast:
        own01 = attend(info, tok, pair_w[0], mask_own[:2])
        own2 = attend(info, tok, single_w[0], mask_own[2:])
        other01 = attend(info, tok, pair_w[1], mask_other[:2])
        other2 = attend(info, tok, single_w[1], mask_other[2:])
    attn_part = project(
        info, (own01[3], own2[3], other01[3], other2[3]), both_single, features
    )
    z_one, hn = norm_one(tok, attn_part, flip_core(attn_part), g_one, b_one)

    act1, slope1 = feed_up(info, hn, up1, units)
    act2, slope2 = feed_up(info, hn, up2, units)
    mixed = feed_down(info, act1, act2, down1, down2, features)
    out, dz_two, dzb_two, sums_two = norm_two(
        info, hn, mixed, flip_core(mixed), cot, g_two, b_two
    )
    out = out.reshape(2, 2, quarter, features)

    out = lax.dynamic_index_in_dim(out, core, 1, keepdims=False)
    output = by_chip(x, out[0], flip_chip(out[1]))

    if fast:
        places = ((NEAR_Y, FAR_Y),) * 2
        att_slots = tuple((0, j) for j in Y_MAJOR)
    else:
        places = ((((0, 0),), ((1, 0),)),) * 2
        att_slots = ((0, 0),)

    keep_d1, send_d1, keep_d2, send_d2 = feed_grad(info, dzb_two, act1, act2, places)
    du1, du2, back = feed_back(
        info, dzb_two, slope1, slope2, (up1, up2), (down1, down2), (keep_d1,)
    )
    back_got = flip_core(back)
    if fast:
        got_d1, got_d2 = flip_dp(send_d1, 1), flip_dp(send_d2, 1)
        keep_d1, send_d1 = fold(keep_d1, got_d1, 2, (du1,))
        got_d1 = flip_chip(send_d1)
    keep_u1, send_u1, keep_u2, send_u2 = feed_grad(info, hn, du1, du2, places, (keep_d1,))
    dz_one, dzb_one, sums_one = norm_one_back(
        info, z_one, dz_two, back, back_got, g_one, (keep_u1,)
    )

    sums = jnp.concatenate([sums_one, sums_two], axis=0)
    sums = sums + flip_core(sums)
    sums = sums + flip_chip(sums)
    for bit in range(size.bit_length() - 1):
        sums = sums + flip_dp(sums, 1 << bit)

    order = (dzb_one,)
    if fast:
        got_u1, got_u2 = flip_dp(send_u1, 1), flip_dp(send_u2, 1)
        zs_d1 = fold(keep_d1, got_d1, 4, order)
        grad_d1 = finish(zs_d1)
        keep_d2, send_d2 = fold(keep_d2, got_d2, 2, (zs_d1[0],))
        got_d2 = flip_chip(send_d2)
        order = (keep_d2,)

    d2b = attend_back(info, dzb_one, single_w[1], other2, order)
    grad_b2 = single_grad(info, tok, d2b, dzb_one, other01[3], other2[3], att_slots)
    got_b2 = flip_chip(grad_b2)
    order = (grad_b2,)
    if fast:
        zs_d2 = fold(keep_d2, got_d2, 4, order)
        grad_d2 = finish(zs_d2)
        keep_u1, send_u1 = fold(keep_u1, got_u1, 2, (zs_d2[0],))
        got_u1 = flip_chip(send_u1)
        order = (keep_u1,)
    d01b = attend_back(info, dzb_one, single_w[1], other01, order)
    grad_b01 = pair_grad(info, tok, d01b, att_slots)
    got_b01 = flip_chip(grad_b01)
    order = (grad_b01,)
    if fast:
        zs_u1 = fold(keep_u1, got_u1, 4, order)
        grad_u1 = finish(zs_u1)
        keep_u2, send_u2 = fold(keep_u2, got_u2, 2, (zs_u1[0],))
        got_u2 = flip_chip(send_u2)
        order = (keep_u2,)
    d2a = attend_back(info, dzb_one, single_w[0], own2, order)
    grad_a2 = single_grad(info, tok, d2a, dzb_one, own01[3], own2[3], att_slots)
    order = (grad_a2,)
    if fast:
        keep_a2, send_a2 = fold(grad_a2, got_b2, 2, order)
        got_a2 = flip_dp(send_a2, 1)
        order = (keep_a2,)
    d01a = attend_back(info, dzb_one, single_w[0], own01, order)
    grad_a01 = pair_grad(info, tok, d01a, att_slots)
    order = (grad_a01,)
    if fast:
        keep_a01, send_a01 = fold(grad_a01, got_b01, 2, order)
        got_a01 = flip_dp(send_a01, 1)
        zs_u2 = fold(keep_u2, got_u2, 4, (keep_a01,))
        grad_u2 = finish(zs_u2)
        zs_a2 = fold(keep_a2, got_a2, 4, (zs_u2[0],))
        grad_single = finish(zs_a2)
        order = (zs_a2[0],)
    back = input_back(info, (d01a, d2a, d01b, d2b), both_pair, both_single, features, order)
    if fast:
        grad_pair = finish(fold(keep_a01, got_a01, 4, (back,)))

    if not fast:

        def plain_sum(own, other):
            total = own.astype(F32) + flip_chip(other).astype(F32)
            return lax.psum_scatter(total[0], "dp", scatter_dimension=0, tiled=True)

        grad_d1, grad_d2 = plain_sum(keep_d1, send_d1), plain_sum(keep_d2, send_d2)
        grad_u1, grad_u2 = plain_sum(keep_u1, send_u1), plain_sum(keep_u2, send_u2)
        grad_single, grad_pair = plain_sum(grad_a2, grad_b2), plain_sum(grad_a01, grad_b01)

    back = back.reshape(2, 2, quarter, features)
    mine = lax.dynamic_index_in_dim(back, core, 1, keepdims=False)
    sent = lax.dynamic_index_in_dim(back, 1 - core, 1, keepdims=False)
    kept = lax.dynamic_index_in_dim(
        dz_one.reshape(2, 2, quarter, features), core, 1, keepdims=False
    )
    final = kept + mine.astype(F32) + flip_core(sent).astype(F32)
    grad_tokens = by_chip(x, final[0], flip_chip(final[1].astype(BF16)).astype(F32))

    def both_heads(i):
        pair = grad_pair[:, 2 * i * HD : 2 * (i + 1) * HD]
        single = grad_single[:, (3 + i) * HD : (4 + i) * HD]
        return jnp.concatenate([pair, single], axis=1)

    return (
        output,
        grad_tokens,
        both_heads(0),
        both_heads(1),
        both_heads(2),
        grad_single[:, : 3 * HD].T,
        jnp.concatenate([grad_u1, grad_u2], axis=1),
        jnp.concatenate([grad_d1, grad_d2], axis=1).T,
        sums[0],
        sums[1],
        sums[2],
        sums[3],
    )


def solution(mesh):
    return jax.shard_map(
        local,
        mesh=mesh,
        in_specs=(
            P("dp", "mp", None),
            P("dp", "mp"),
            P("dp", "mp"),
            P("dp", "mp"),
            P("mp", "dp"),
            P("dp", "mp"),
            P("mp", "dp"),
            P(),
            P(),
            P(),
            P(),
            P("dp"),
            P(),
            P("dp", "mp", None),
        ),
        out_specs=(
            P("dp", "mp", None),
            P("dp", "mp", None),
            P("dp", "mp"),
            P("dp", "mp"),
            P("dp", "mp"),
            P("mp", "dp"),
            P("dp", "mp"),
            P("mp", "dp"),
            P(),
            P(),
            P(),
            P(),
        ),
        check_vma=False,
    )
```

```python
import functools

import jax
import jax.numpy as jnp
from jax import lax
from jax.experimental import pallas as pl
from jax.experimental.pallas import tpu as pltpu
from jax.sharding import PartitionSpec as P

HD = 64
BLOCK = 64
LANES = 128
TILE = 256
EPSILON = 1e-12
TAIL = 32
ROOM = {
    "attend": 24,
    "attend_back": 28,
    "project": 16,
    "input_back": 24,
    "norm_one": 16,
    "norm_two": 24,
    "norm_one_back": 24,
    "feed_up": 20,
    "feed_down": 24,
    "feed_back": 40,
    "feed_grad": 28,
    "pair_grad": 16,
    "single_grad": 24,
    "join": 1,
    "join_sides": 1,
    "turn": 2,
    "pack": 2,
    "split": 1,
    "couple": 1,
    "merge": 1,
    "fold": 6,
    "fold_two": 8,
    "fold_four": 6,
    "halves": 1,
    "slots": 1,
    "tokens_add": 8,
    "tokens_out": 8,
    "feed_out": 6,
    "attend_out": 6,
}
FLOPS = {}
SCALE = 0.125
LOG2E = 1.4426950408889634
LN2 = 0.6931471805599453
NEGATIVE = -1e30
F32 = jnp.float32
BF16 = jnp.bfloat16

ERFCX_STEP = 0.45
ERFCX = (
    -8.220994855312894e-06,
    0.2540684902923417,
    0.25234751996246985,
    0.23373082558517694,
    0.1739141918052578,
    0.06370751405215419,
    0.18661300519520473,
    -0.22870513112792096,
    0.06433208636936971,
)

CORE_SWAP = [(0, 1), (1, 0), (2, 3), (3, 2)]
CHIP_SWAP = [(0, 2), (2, 0), (1, 3), (3, 1)]


def nn(a, b):
    return lax.dot_general(a, b, (((1,), (0,)), ((), ())), preferred_element_type=F32)


def nt(a, b):
    return lax.dot_general(a, b, (((1,), (1,)), ((), ())), preferred_element_type=F32)


def tn(a, b):
    return lax.dot_general(a, b, (((0,), (0,)), ((), ())), preferred_element_type=F32)


def vmem():
    return pl.BlockSpec(memory_space=pltpu.VMEM)


def smem():
    return pl.BlockSpec(memory_space=pltpu.SMEM)


def anywhere():
    return pl.BlockSpec(memory_space=pl.ANY)


def rows(width):
    return pl.BlockSpec((TILE, width), lambda i: (i, 0))


def whole(shape):
    return pl.BlockSpec(shape, lambda i: (0,) * len(shape))


def array(shape, dtype):
    return jax.ShapeDtypeStruct(shape, dtype)


def run(kernel, name, args, specs, outs, out_specs, scratch=(), *, grid=(), after=()):
    given, extra = len(args), len(after)

    def body(*refs):
        kernel(*refs[:given], *refs[given + extra :])

    return pl.pallas_call(
        body,
        grid=grid,
        out_shape=tuple(outs),
        in_specs=list(specs) + [anywhere()] * extra,
        out_specs=tuple(out_specs),
        scratch_shapes=list(scratch),
        compiler_params=pltpu.CompilerParams(vmem_limit_bytes=ROOM[name] * 2**20),
        cost_estimate=pl.CostEstimate(
            flops=FLOPS.get(name, 1), bytes_accessed=0, transcendentals=0
        ),
        name=name,
    )(*args, *after)


def put_rows(parts, value):
    for i, part in enumerate(parts):

        @pl.when(pl.program_id(0) == i)
        def _(part=part):
            part[...] = value


def get_sum(parts, more):
    total = None
    for i, (a, b) in enumerate(zip(parts, more)):
        value = a[...].astype(F32) + b[...].astype(F32)
        total = value if i == 0 else jnp.where(pl.program_id(0) == i, value, total)
    return total


def tiles(seq, width):
    return (array((TILE, width), BF16),) * (seq // TILE), [whole((TILE, width))] * (seq // TILE)


def place(me, refs, slots, dst_ref, first=0, last=None, only=None, to=0):
    for ref, of in zip(refs, slots):
        height, width = ref.shape[1], ref.shape[2]
        end = width if last is None else last
        for e, (chip, j) in enumerate(of):
            if only is not None and chip != only:
                continue
            at = 0 if height == dst_ref.shape[0] else pl.multiple_of((me ^ j) * height, height)
            at_column = to + (0 if only is not None else chip * (end - first))
            dst_ref[pl.ds(at, height), pl.ds(at_column, end - first)] = ref[e, :, first:end]


def pick(me, fulls, out_ref, slots, first):
    _, height, width = out_ref.shape
    for e, (chip, j) in enumerate(slots):
        full = fulls[chip]
        at = 0 if height == full.shape[0] else pl.multiple_of((me ^ j) * height, height)
        out_ref[e] = full[pl.ds(at, height), pl.ds(first, width)].astype(BF16)


def attend_kernel(slots, columns, only, places, info, tok, mask, *rest):
    refs, (qa, ka, va, ctx, wfull) = rest[: len(slots)], rest[len(slots) :]
    seq = tok.shape[0]
    place(info[0], refs, slots, wfull, *columns, only)
    lane = lax.broadcasted_iota(jnp.int32, (TILE, LANES), 1)
    row0 = lax.broadcasted_iota(jnp.int32, (TILE, LANES), 0)
    for t in range(seq // TILE):
        at = pl.ds(t * TILE, TILE)
        row = row0 + t * TILE
        made = nn(tok[at, :], wfull[...])
        onehot = jnp.where(lane - HD == row // BLOCK, 1.0, 0.0)[:, HD:]
        position = row + info[4]
        position = jnp.where(position >= seq, position - seq, position)
        dead = (position >= info[3]) & (lane >= HD) & (lane < HD + 16)
        for h, (q_at, k_at, v_at) in enumerate(places):
            q = made[:, q_at : q_at + HD] * (SCALE * LOG2E)
            k = made[:, k_at : k_at + HD]
            v = made[:, v_at : v_at + HD]
            qa[h, at, :] = jnp.concatenate([q, onehot], axis=1).astype(BF16)
            per = TILE // BLOCK
            table = jnp.concatenate(
                [
                    jnp.broadcast_to(mask[h, t * per + b : t * per + b + 1, :], (BLOCK, LANES))
                    for b in range(per)
                ],
                axis=0,
            )
            table = jnp.where(dead, NEGATIVE, table)
            ka[h, at, :] = jnp.concatenate([k, table[:, HD:]], axis=1).astype(BF16)
            va[h, at, :] = jnp.concatenate([v, jnp.full((TILE, HD), -1.0, F32)], axis=1).astype(BF16)
    for t in range(seq // TILE):
        at = pl.ds(t * TILE, TILE)
        pieces = []
        for h in range(len(places)):
            q = qa[h, at, :]
            s = nt(q, ka[h])
            top = jnp.max(s, axis=1, keepdims=True)
            p = jnp.exp2(s - top).astype(BF16)
            got = nn(p, va[h])
            total = -got[:, HD:]
            pieces.append(got[:, :HD] / total)
            log = top + jnp.log2(-got)
            hi = log.astype(BF16).astype(F32)
            mid = (log - hi).astype(BF16).astype(F32)
            low = log - hi - mid
            new = jnp.where(
                lane == HD + 16,
                hi,
                jnp.where(lane == HD + 17, mid, jnp.where(lane == HD + 18, low, q.astype(F32))),
            )
            qa[h, at, :] = new.astype(BF16)
        ctx[at, :] = jnp.concatenate(pieces, axis=1).astype(BF16)


PAIR = ((0, 2 * HD, 4 * HD), (HD, 3 * HD, 5 * HD))
SINGLES = ((HD, 2 * HD, 3 * HD), (5 * HD, 6 * HD, 7 * HD))


def attend(info, tok, gathered, pair, mask, after=()):
    arrays, slots = gathered
    seq, width = tok.shape
    aug = array((2, seq, LANES), BF16)
    columns, only, cols = ((0, 6 * HD), 0, 6 * HD) if pair else ((2 * HD, 6 * HD), None, 8 * HD)
    return run(
        functools.partial(attend_kernel, slots, columns, only, PAIR if pair else SINGLES),
        "attend",
        (info, tok, mask) + arrays,
        [smem()] + [vmem()] * (2 + len(arrays)),
        (aug, aug, aug, array((seq, LANES), BF16)),
        [vmem()] * 4,
        [pltpu.VMEM((width, cols), BF16)],
        after=after,
    )


def place_out(me, refs, slots, pairs, ends):
    place(me, refs, slots, pairs, 0, 2 * HD)
    place(me, refs, slots, ends, 2 * HD, 4 * HD)
    both = ends[...]
    ends[:, :LANES] = jnp.concatenate([both[:, :HD], both[:, LANES : LANES + HD]], axis=1)


def project_kernel(slots, info, own, other, ends, *rest):
    refs, parts, (w1, w2) = rest[: len(slots)], rest[len(slots) : -2], rest[-2:]

    @pl.when(pl.program_id(0) == 0)
    def _():
        place_out(info[0], refs, slots, w1, w2)

    both = jnp.concatenate([own[...], other[...]], axis=1)
    put_rows(parts, (nt(both, w1[...]) + nt(ends[...], w2[:, :LANES])).astype(BF16))


def project(info, contexts, gathered, width, after=()):
    arrays, slots = gathered
    seq = contexts[0].shape[0]
    return run(
        functools.partial(project_kernel, slots),
        "project",
        (info,) + contexts + arrays,
        [smem()] + [rows(LANES)] * 3 + [whole(a.shape) for a in arrays],
        *tiles(seq, width),
        [pltpu.VMEM((width, 2 * LANES), BF16)] * 2,
        grid=(seq // TILE,),
        after=after,
    )


def attend_back_kernel(slots, chip, info, dz, qa, ka, va, ctx, *rest):
    refs, (dqkv, pairs, ends, da, parts) = rest[: len(slots)], rest[len(slots) :]
    seq = dz.shape[0]
    heads = qa.shape[0]
    if chip is None:
        place_out(info[0], refs, slots, pairs, ends)
        wfull = ends.at[:, pl.ds(0, LANES)]
    else:
        place(info[0], refs, slots, pairs, 0, 2 * HD, chip)
        wfull = pairs.at[:, pl.ds(0, LANES)]
    lane = lax.broadcasted_iota(jnp.int32, (TILE, LANES), 1)
    for t in range(seq // TILE):
        at = pl.ds(t * TILE, TILE)
        dctx = nn(dz[at, :], wfull[...]).astype(BF16).astype(F32)
        both = dctx * ctx[at, :].astype(F32)
        for h in range(heads):
            inner = jnp.sum(both[:, h * HD : (h + 1) * HD], axis=1, keepdims=True)
            hi = inner.astype(BF16).astype(F32)
            mid = (inner - hi).astype(BF16).astype(F32)
            low = inner - hi - mid
            one = jnp.concatenate(
                [dctx[:, h * HD : (h + 1) * HD], jnp.zeros((TILE, HD), F32)], axis=1
            )
            one = jnp.where(lane == HD, hi, one)
            one = jnp.where(lane == HD + 1, mid, one)
            one = jnp.where(lane == HD + 2, low, one)
            da[h, at, :] = one.astype(BF16)
    for h in range(heads):
        k_turned = jnp.transpose(ka[h].astype(F32)).astype(BF16)
        dq_turned = None
        for t in range(seq // TILE):
            at = pl.ds(t * TILE, TILE)
            p = jnp.exp2(nt(ka[h, at, :], qa[h]))
            ds = (p * nt(va[h, at, :], da[h])).astype(BF16)
            parts[2 * heads + h, at, :] = nn(p.astype(BF16), da[h])
            parts[heads + h, at, :] = nn(ds, qa[h]) * LN2
            more = nn(k_turned[:, t * TILE : (t + 1) * TILE], ds)
            dq_turned = more if dq_turned is None else dq_turned + more
        parts[h] = jnp.transpose(dq_turned) * SCALE
    for t in range(seq // TILE):
        at = pl.ds(t * TILE, TILE)
        pieces = [parts[i, at, :][:, :HD] for i in range(3 * heads)]
        if chip is None:
            blank = jnp.zeros((TILE, HD), F32)
            pieces = [blank] + pieces[::2] + [blank] + pieces[1::2]
        dqkv[at, :] = jnp.concatenate(pieces, axis=1).astype(BF16)


def attend_back(info, dz, gathered, chip, saved, after=()):
    arrays, slots = gathered
    qa, ka, va, ctx = saved
    seq, width = dz.shape
    cols = 8 * HD if chip is None else 6 * HD
    return run(
        functools.partial(attend_back_kernel, slots, chip),
        "attend_back",
        (info, dz, qa, ka, va, ctx) + arrays,
        [smem()] + [vmem()] * (5 + len(arrays)),
        (array((seq, cols), BF16),),
        [vmem()],
        [
            pltpu.VMEM((width, 2 * LANES), BF16),
            pltpu.VMEM((width, 2 * LANES), BF16),
            pltpu.VMEM((2, seq, LANES), BF16),
            pltpu.VMEM((6, seq, LANES), F32),
        ],
        after=after,
    )[0]


def input_back_kernel(slots1, slots2, info, own, other, ends, dz, *rest):
    n1, n2 = len(slots1), len(slots2)
    refs1, refs2, (mine, sent, w1, w2) = rest[:n1], rest[n1 : n1 + n2], rest[n1 + n2 :]
    i = pl.program_id(0)

    @pl.when(i == 0)
    def _():
        place(info[0], refs1, slots1, w1)
        place(info[0], refs2, slots2, w2, 2 * HD, 6 * HD)

    pairs = jnp.concatenate([own[...], other[...]], axis=1)
    back = nt(pairs, w1[...]) + nt(ends[...], w2[...])

    @pl.when(i % 2 == info[2])
    def _():
        mine[i // 2] = back + dz[...]

    @pl.when(i % 2 != info[2])
    def _():
        sent[i // 2] = back.astype(BF16)


def input_back(info, own, other, ends, dz, gathered1, gathered2, after=()):
    seq, width = dz.shape
    arrays = gathered1[0] + gathered2[0]
    halves = (seq // TILE // 2, TILE, width)
    grads = (own, other, ends, dz)
    return run(
        functools.partial(input_back_kernel, gathered1[1], gathered2[1]),
        "input_back",
        (info,) + grads + arrays,
        [smem()] + [rows(g.shape[1]) for g in grads] + [whole(a.shape) for a in arrays],
        (array(halves, F32), array(halves, BF16)),
        [whole(halves)] * 2,
        [pltpu.VMEM((width, 12 * HD), BF16), pltpu.VMEM((width, 8 * HD), BF16)],
        grid=(seq // TILE,),
        after=after,
    )


def center(z):
    mean = jnp.mean(z, axis=1, keepdims=True)
    moved = z - mean
    spread = jnp.mean(moved * moved, axis=1, keepdims=True)
    scale = lax.rsqrt(spread + EPSILON)
    return moved * scale, scale


def norm_back(n, scale, gy, gain):
    dn = gy * gain
    return scale * (
        dn - jnp.mean(dn, axis=1, keepdims=True) - n * jnp.mean(dn * n, axis=1, keepdims=True)
    )


def add_sums(gy, n, sums):
    i = pl.program_id(0)

    @pl.when(i == 0)
    def _():
        sums[...] = jnp.zeros_like(sums)

    sums[0:1, :] += jnp.sum(gy * n, axis=0, keepdims=True)
    sums[1:2, :] += jnp.sum(gy, axis=0, keepdims=True)


def norm_one_kernel(tok, gain, bias, *rest):
    *parts, z, hn = rest
    count = len(parts) // 2
    value = tok[...].astype(F32) + get_sum(parts[:count], parts[count:])
    z[...] = value
    n, _ = center(value)
    hn[...] = (n * gain[...] + bias[...]).astype(BF16)


def norm_one(tok, p0, p1, gain, bias, after=()):
    seq, width = tok.shape
    return run(
        norm_one_kernel,
        "norm_one",
        (tok, gain, bias, *p0, *p1),
        [rows(width)] + [whole((1, width))] * 2 + [whole(p.shape) for p in (*p0, *p1)],
        (array((seq, width), F32), array((seq, width), BF16)),
        (rows(width), rows(width)),
        grid=(seq // TILE,),
        after=after,
    )


def norm_two_kernel(info, hn, cot, gain, bias, *rest):
    *parts, out, dz, dzb, sums = rest
    count = len(parts) // 2
    value = hn[...].astype(F32) + get_sum(parts[:count], parts[count:])
    n, scale = center(value)
    out[...] = (n * gain[...] + bias[...]).astype(BF16)
    row = lax.broadcasted_iota(jnp.int32, value.shape, 0) + pl.program_id(0) * TILE
    seq = pl.num_programs(0) * TILE
    position = row + info[4]
    position = jnp.where(position >= seq, position - seq, position)
    gy = jnp.where(position < info[3], cot[...].astype(F32), 0.0)
    grad = norm_back(n, scale, gy, gain[...])
    dz[...] = grad
    dzb[...] = grad.astype(BF16)
    add_sums(gy, n, sums)


def norm_two(info, hn, m0, m1, cot, gain, bias, after=()):
    seq, width = hn.shape
    return run(
        norm_two_kernel,
        "norm_two",
        (info, hn, cot, gain, bias, *m0, *m1),
        [smem()]
        + [rows(width)] * 2
        + [whole((1, width))] * 2
        + [whole(p.shape) for p in (*m0, *m1)],
        (
            array((seq, width), BF16),
            array((seq, width), F32),
            array((seq, width), BF16),
            array((2, width), F32),
        ),
        (rows(width), rows(width), rows(width), whole((2, width))),
        grid=(seq // TILE,),
        after=after,
    )


def norm_one_back_kernel(z, dz2, gain, *rest):
    *parts, dz, dzb, sums = rest
    count = len(parts) // 2
    n, scale = center(z[...])
    gy = dz2[...] + get_sum(parts[:count], parts[count:])
    grad = norm_back(n, scale, gy, gain[...])
    dz[...] = grad
    dzb[...] = grad.astype(BF16)
    add_sums(gy, n, sums)


def norm_one_back(z, dz2, p0, p1, gain, after=()):
    seq, width = z.shape
    return run(
        norm_one_back_kernel,
        "norm_one_back",
        (z, dz2, gain, *p0, *p1),
        [rows(width)] * 2 + [whole((1, width))] + [whole(p.shape) for p in (*p0, *p1)],
        (array((seq, width), F32), array((seq, width), BF16), array((2, width), F32)),
        (rows(width), rows(width), whole((2, width))),
        grid=(seq // TILE,),
        after=after,
    )


def gelu_pair(u):
    z = jnp.abs(u) * 0.7071067811865476
    t = 1.0 / (1.0 + ERFCX_STEP * z)
    poly = jnp.full_like(t, ERFCX[-1])
    for coefficient in ERFCX[-2::-1]:
        poly = poly * t + coefficient
    e = jnp.exp(-z * z)
    tail = 0.5 * (poly * e)
    phi = jnp.where(u >= 0, 1.0 - tail, tail)
    return u * phi, phi + u * (e * 0.3989422804014327)


def feed_up_kernel(slots, info, hn, *rest):
    refs, (active, slope, wfull) = rest[: len(slots)], rest[len(slots) :]

    @pl.when(pl.program_id(0) == 0)
    def _():
        place(info[0], refs, slots, wfull)

    a, g = gelu_pair(nn(hn[...], wfull[...]))
    active[...] = a.astype(BF16)
    slope[...] = g.astype(BF16)


def feed_up(info, hn, gathered, units, after=()):
    arrays, slots = gathered
    seq, width = hn.shape
    return run(
        functools.partial(feed_up_kernel, slots),
        "feed_up",
        (info, hn) + arrays,
        [smem(), rows(width)] + [whole(a.shape) for a in arrays],
        (array((seq, units), BF16), array((seq, units), BF16)),
        (rows(units), rows(units)),
        [pltpu.VMEM((width, units), BF16)],
        grid=(seq // TILE,),
        after=after,
    )


def feed_down_kernel(slots, info, act1, act2, *rest):
    refs, parts, wfull = rest[: len(slots)], rest[len(slots) : -1], rest[-1]

    @pl.when(pl.program_id(0) == 0)
    def _():
        place(info[0], refs, slots, wfull)

    both = jnp.concatenate([act1[...], act2[...]], axis=1)
    put_rows(parts, nt(both, wfull[...]).astype(BF16))


def feed_down(info, act1, act2, gathered, width, after=()):
    seq, units = act1.shape
    arrays, slots = gathered
    return run(
        functools.partial(feed_down_kernel, slots),
        "feed_down",
        (info, act1, act2) + arrays,
        [smem(), rows(units), rows(units)] + [whole(a.shape) for a in arrays],
        *tiles(seq, width),
        [pltpu.VMEM((width, 2 * units), BF16)],
        grid=(seq // TILE,),
        after=after,
    )


def feed_back_kernel(slots_up, slots_down, info, dzb, slope1, slope2, *rest):
    n1, n2 = len(slots_up), len(slots_down)
    ups, downs, (du1, du2, *parts, up, down) = rest[:n1], rest[n1 : n1 + n2], rest[n1 + n2 :]

    @pl.when(pl.program_id(0) == 0)
    def _():
        place(info[0], ups, slots_up, up)
        place(info[0], downs, slots_down, down)

    units = du1.shape[1]
    out = None
    for i, (slope, du) in enumerate(((slope1, du1), (slope2, du2))):
        at = pl.ds(i * units, units)
        grad = (nn(dzb[...], down[:, at]) * slope[...].astype(F32)).astype(BF16)
        du[...] = grad
        more = nt(grad, up[:, at])
        out = more if out is None else out + more
    put_rows(parts, out.astype(BF16))


def feed_back(info, dzb, slope1, slope2, up, down, after=()):
    seq, width = dzb.shape
    units = slope1.shape[1]
    arrays = up[0] + down[0]
    parts, part_specs = tiles(seq, width)
    return run(
        functools.partial(feed_back_kernel, up[1], down[1]),
        "feed_back",
        (info, dzb, slope1, slope2) + arrays,
        [smem(), rows(width), rows(units), rows(units)] + [whole(a.shape) for a in arrays],
        (array((seq, units), BF16),) * 2 + parts,
        [rows(units)] * 2 + part_specs,
        [pltpu.VMEM((width, 2 * units), BF16)] * 2,
        grid=(seq // TILE,),
        after=after,
    )


def feed_grad_kernel(places, info, a, d1, d2, *rest):
    outs, fulls = rest[:4], rest[4:]
    half = outs[0].shape[2]
    fulls[0][...] = tn(a[...], d1[...])
    fulls[1][...] = tn(a[...], d2[...])
    for i, out in enumerate(outs):
        pick(info[0], fulls, out, places[i], (i // 2) * half)


def feed_grad(info, a, d1, d2, places, after=()):
    seq, width = a.shape
    units = d1.shape[1]
    count = len(places[0])
    out = array((count, width // count, units // 2), BF16)
    return run(
        functools.partial(feed_grad_kernel, places),
        "feed_grad",
        (info, a, d1, d2),
        [smem()] + [vmem()] * 3,
        (out,) * 4,
        [vmem()] * 4,
        [pltpu.VMEM((width, units), F32)] * 2,
        after=after,
    )


def pair_grad_kernel(slots, info, tok, d, out, full):
    full[...] = tn(tok[...], d[...])
    pick(info[0], (full,), out, slots, 0)


def pair_grad(info, tok, d, slots, after=()):
    seq, width = tok.shape
    cols = d.shape[1]
    return run(
        functools.partial(pair_grad_kernel, slots),
        "pair_grad",
        (info, tok, d),
        [smem()] + [vmem()] * 2,
        (array((len(slots), width // len(slots), cols), BF16),),
        [vmem()],
        [pltpu.VMEM((width, cols), F32)],
        after=after,
    )[0]


def encode(sums):
    hi = sums.astype(BF16).astype(F32)
    mid = (sums - hi).astype(BF16).astype(F32)
    low = sums - hi - mid
    return jnp.concatenate([hi, mid, low, jnp.zeros_like(low)], axis=0).astype(BF16)


def decode(coded):
    values = coded.astype(F32)
    n = values.shape[0] // 4
    return values[:n] + values[n : 2 * n] + values[2 * n : 3 * n]


def single_grad_kernel(order, info, tok, d, dz, own, other, ends, sums_one, sums_two, keep, send, full):
    mine = tn(tok[...], d[...])
    third = tn(dz[...], ends[...])
    blank = jnp.zeros((third.shape[0], HD), F32)
    count = len(order)
    width = full.shape[1]
    height = full.shape[0] // count
    both = jnp.concatenate([sums_one[...], sums_two[...]], axis=0)
    both = encode(jnp.concatenate([both[:, :width], both[:, width:]], axis=0))
    for chip, (ctx, out) in enumerate(((own, keep), (other, send))):
        full[:, :LANES] = tn(dz[...], ctx[...])
        at = chip * 4 * HD
        o_third = jnp.concatenate([third[:, chip * HD : (chip + 1) * HD], blank], axis=1)
        full[:, LANES : 2 * LANES] = o_third + mine[:, at : at + LANES]
        full[:, 2 * LANES :] = mine[:, at + LANES : at + 2 * LANES]
        for e, j in enumerate(order):
            at = 0 if count == 1 else pl.multiple_of((info[0] ^ j) * height, height)
            out[pl.ds(e * height, height), :] = full[pl.ds(at, height), :].astype(BF16)
        out[pl.ds(count * height, TAIL), :] = both


def single_grad(info, tok, d, dz, contexts, sums_one, sums_two, order, after=()):
    seq, width = tok.shape
    cols = 6 * HD
    out = array((width + TAIL, cols), BF16)
    return run(
        functools.partial(single_grad_kernel, order),
        "single_grad",
        (info, tok, d, dz, *contexts, sums_one, sums_two),
        [smem()] + [vmem()] * 8,
        (out, out),
        [vmem()] * 2,
        [pltpu.VMEM((width, cols), F32)],
        after=after,
    )


def across(values, axis, pairs):
    return lax.ppermute(values, axis, pairs)


def flip_chip(values):
    return across(values, "mp", CHIP_SWAP)


def flip_core(values):
    return across(values, "mp", CORE_SWAP)


def flip_cores(parts):
    return [flip_core(p) for p in parts]


def flip_dp(values, distance):
    size = lax.axis_size("dp")
    return across(values, "dp", [(i, i ^ distance) for i in range(size)])


def join_kernel(count, *refs):
    parts, out, sems = refs[:count], refs[count], refs[count + 1]
    copies = []
    first = 0
    for i, part in enumerate(parts):
        to = out.at[pl.ds(first, part.shape[0])]
        copies.append(pltpu.make_async_copy(part, to, sems.at[i]))
        first += part.shape[0]
    for copy in copies:
        copy.start()
    for copy in copies:
        copy.wait()


def join(parts, after=()):
    total = sum(p.shape[0] for p in parts)
    shape = (total,) + parts[0].shape[1:]
    return run(
        functools.partial(join_kernel, len(parts)),
        "join",
        tuple(parts),
        [anywhere()] * len(parts),
        (array(shape, parts[0].dtype),),
        [anywhere()],
        [pltpu.SemaphoreType.DMA((len(parts),))],
        after=after,
    )[0]


def turn_kernel(w, out):
    out[0] = jnp.transpose(w[...].astype(F32)).astype(BF16)


def turn(w, after=()):
    return run(
        turn_kernel,
        "turn",
        (w,),
        [vmem()],
        (array((1,) + w.shape[::-1], BF16),),
        [vmem()],
        after=after,
    )[0]


def pack_kernel(w_query, w_key, w_value, w_out, out):
    for i, w in enumerate((w_query, w_key, w_value)):
        out[0, :, 2 * i * HD : 2 * (i + 1) * HD] = w[:, : 2 * HD]
    parts = [jnp.transpose(w_out[...].astype(F32))]
    parts += [w[:, 2 * HD :].astype(F32) for w in (w_query, w_key, w_value)]
    out[0, :, 6 * HD :] = jnp.concatenate(parts, axis=1).astype(BF16)


def pack(w_query, w_key, w_value, w_out):
    return run(
        pack_kernel,
        "pack",
        (w_query, w_key, w_value, w_out),
        [vmem()] * 4,
        (array((1, w_query.shape[0], 12 * HD), BF16),),
        [vmem()],
    )[0]


def join_sides_kernel(count, *refs):
    parts, outs, sems = refs[:count], refs[count : count + 2], refs[count + 2]
    width = outs[0].shape[2]
    copies = []
    for i, part in enumerate(parts):
        for side, out in enumerate(outs):
            copies.append(
                pltpu.make_async_copy(
                    part.at[:, :, pl.ds(side * width, width)],
                    out.at[pl.ds(i, 1)],
                    sems.at[2 * i + side],
                )
            )
    for copy in copies:
        copy.start()
    for copy in copies:
        copy.wait()


def join_sides(parts, after=()):
    count = len(parts)
    _, height, width = parts[0].shape
    out = array((count, height, width // 2), BF16)
    return run(
        functools.partial(join_sides_kernel, count),
        "join_sides",
        tuple(parts),
        [anywhere()] * count,
        (out, out),
        [anywhere()] * 2,
        [pltpu.SemaphoreType.DMA((2 * count,))],
        after=after,
    )


def fold_kernel(tail, own, got, *outs):
    body = own.shape[0] - tail
    each = body // len(outs)
    for i, out in enumerate(outs):
        at = pl.ds(i * each, each)
        total = (own[at].astype(F32) + got[at].astype(F32)).astype(BF16)
        if tail:
            out[:each] = total
        else:
            out[...] = total
    if tail:
        coded = encode(decode(own[body:]) + decode(got[body:]))
        for out in outs:
            out[each:] = coded


def fold(own, got, parts, tail=0, after=()):
    shape = ((own.shape[0] - tail) // parts + tail,) + own.shape[1:]
    return run(
        functools.partial(fold_kernel, tail),
        "fold",
        (own, got),
        [vmem()] * 2,
        (array(shape, BF16),) * parts,
        [vmem()] * parts,
        after=after,
    )


def fold_two_kernel(own1, got1, own2, got2, *outs):
    sides = outs[0].shape[2] != own1.shape[2]
    width = own1.shape[2]
    each = outs[0].shape[0]
    for side, (own, got) in enumerate(((own1, got1), (own2, got2))):
        count = len(outs) if sides else len(outs) // 2
        for i in range(count):
            at = pl.ds(i * each, each)
            total = (own[at].astype(F32) + got[at].astype(F32)).astype(BF16)
            if sides:
                outs[i][:, :, side * width : (side + 1) * width] = total
            else:
                outs[side * count + i][...] = total


def fold_two(own1, got1, own2, got2, parts, sides, after=()):
    count, height, width = own1.shape
    shape = (count // parts, height, (2 if sides else 1) * width)
    number = parts if sides else 2 * parts
    return run(
        fold_two_kernel,
        "fold_two",
        (own1, got1, own2, got2),
        [vmem()] * 4,
        (array(shape, BF16),) * number,
        [vmem()] * number,
        after=after,
    )


def fold_four_kernel(a, b, c, d, keep, send1, send2):
    width = send1.shape[2]
    total = (a[...].astype(F32) + b[...].astype(F32)) + (c[...].astype(F32) + d[...].astype(F32))
    keep[...] = total[:1]
    send1[...] = total[1:, :, :width].astype(BF16)
    send2[...] = total[1:, :, width:].astype(BF16)


def fold_four(pieces, after=()):
    _, height, width = pieces[0].shape
    half = array((1, height, width // 2), BF16)
    return run(
        fold_four_kernel,
        "fold_four",
        tuple(pieces),
        [vmem()] * 4,
        (array((1, height, width), F32), half, half),
        [vmem()] * 3,
        after=after,
    )


Y_MAJOR = (0, 2, 4, 6, 1, 3, 5, 7)
OWN = tuple((0, j) for j in Y_MAJOR)
OTHER = tuple((1, j) for j in Y_MAJOR)
CHIP_NEAR = tuple((chip, 2 * z) for chip in range(2) for z in range(4))
CHIP_FAR = tuple((chip, 2 * z + 1) for chip in range(2) for z in range(4))
Z_NEAR = tuple((chip, 2 * z) for z in range(4) for chip in range(2))
Z_FAR = tuple((chip, 2 * z + 1) for z in range(4) for chip in range(2))
Z_OWN = tuple((0, j) for j in range(8))
Z_OTHER = tuple((1, j) for j in range(8))


def z_sends(values):
    return [flip_dp(values, 2 * z) for z in (1, 2, 3)]


def z_trade(pieces):
    return [pieces[0]] + [flip_dp(pieces[z], 2 * z) for z in (1, 2, 3)]


def split_kernel(info, first, second, out1, out2, sems):
    copies = [
        pltpu.make_async_copy(ref.at[1 - info[1]], out, sems.at[i])
        for i, (ref, out) in enumerate(((first, out1), (second, out2)))
    ]
    for copy in copies:
        copy.start()
    for copy in copies:
        copy.wait()


def split(info, first, second):
    out = array(first.shape[1:], first.dtype)
    return run(
        split_kernel,
        "split",
        (info, first, second),
        [smem()] + [anywhere()] * 2,
        (out, out),
        [anywhere()] * 2,
        [pltpu.SemaphoreType.DMA((2,))],
    )


def couple_kernel(info, values, got, out, sems):
    copies = [
        pltpu.make_async_copy(values.at[info[1]], out.at[0], sems.at[0]),
        pltpu.make_async_copy(got, out.at[1], sems.at[1]),
    ]
    for copy in copies:
        copy.start()
    for copy in copies:
        copy.wait()


def couple(info, values, got, after=()):
    return run(
        couple_kernel,
        "couple",
        (info, values, got),
        [smem()] + [anywhere()] * 2,
        (array(values.shape, values.dtype),),
        [anywhere()],
        [pltpu.SemaphoreType.DMA((2,))],
        after=after,
    )[0]


def merge_kernel(info, mine, got, out, sems):
    core = info[2]
    copies = []
    for half in range(2):
        copies += [
            pltpu.make_async_copy(mine.at[half], out.at[half, core], sems.at[2 * half]),
            pltpu.make_async_copy(got.at[half], out.at[half, 1 - core], sems.at[2 * half + 1]),
        ]
    for copy in copies:
        copy.start()
    for copy in copies:
        copy.wait()


def merge(info, mine, got, after=()):
    halves, quarter, width = mine.shape
    out = run(
        merge_kernel,
        "merge",
        (info, mine, got),
        [smem()] + [anywhere()] * 2,
        (array((halves, 2, quarter, width), mine.dtype),),
        [anywhere()],
        [pltpu.SemaphoreType.DMA((4,))],
        after=after,
    )[0]
    return out.reshape(halves * 2 * quarter, width)


def halves_kernel(info, rows_ref, own, send, sems):
    quarter = own.shape[0]
    copies = []
    for half, out in enumerate((own, send)):
        at = pl.multiple_of((2 * half + info[2]) * quarter, quarter)
        copies.append(pltpu.make_async_copy(rows_ref.at[pl.ds(at, quarter)], out, sems.at[half]))
    for copy in copies:
        copy.start()
    for copy in copies:
        copy.wait()


def halves(info, values, after=()):
    seq, width = values.shape
    out = array((seq // 4, width), values.dtype)
    return run(
        halves_kernel,
        "halves",
        (info, values),
        [smem(), anywhere()],
        (out, out),
        [anywhere()] * 2,
        [pltpu.SemaphoreType.DMA((2,))],
        after=after,
    )


def slots_kernel(info, own, other, out, sems):
    copies = [
        pltpu.make_async_copy(own, out.at[info[1]], sems.at[0]),
        pltpu.make_async_copy(other, out.at[1 - info[1]], sems.at[1]),
    ]
    for copy in copies:
        copy.start()
    for copy in copies:
        copy.wait()


def slots_of(info, own, other, after=()):
    return run(
        slots_kernel,
        "slots",
        (info, own, other),
        [smem()] + [anywhere()] * 2,
        (array((2,) + own.shape, own.dtype),),
        [anywhere()],
        [pltpu.SemaphoreType.DMA((2,))],
        after=after,
    )[0]


def tokens_add_kernel(mine, got, own, send):
    own[...] = mine[0] + got[0].astype(F32)
    send[...] = (mine[1] + got[1].astype(F32)).astype(BF16)


def tokens_add(mine, got, after=()):
    shape = mine.shape[1:]
    return run(
        tokens_add_kernel,
        "tokens_add",
        (mine, got),
        [vmem()] * 2,
        (array(shape, F32), array(shape, BF16)),
        [vmem()] * 2,
        after=after,
    )


def tokens_out_kernel(info, own, got, out):
    out[info[1]] = own[...]
    out[1 - info[1]] = got[...].astype(F32)


def tokens_out(info, own, got, after=()):
    return run(
        tokens_out_kernel,
        "tokens_out",
        (info, own, got),
        [smem()] + [vmem()] * 2,
        (array((2,) + own.shape, F32),),
        [vmem()],
        after=after,
    )[0]


def feed_out_kernel(d0, d1, d2, d3, keep, near, far, up, down):
    half = near.shape[2]
    up[:, :half] = keep[0, :, :half] + near[0].astype(F32)
    up[:, half:] = keep[0, :, half:] + far[0].astype(F32)
    down[...] = jnp.transpose(
        (d0[0].astype(F32) + d1[0].astype(F32)) + (d2[0].astype(F32) + d3[0].astype(F32))
    )


def feed_out(zs_down, keep, near, far, after=()):
    _, height, width = keep.shape
    return run(
        feed_out_kernel,
        "feed_out",
        (*zs_down, keep, near, far),
        [vmem()] * 7,
        (array((height, width), F32), array((width, height), F32)),
        [vmem()] * 2,
        after=after,
    )


def attend_out_kernel(*refs):
    pair, single = refs[:4], refs[4:8]
    query, key, value, out, gain1, bias1, gain2, bias2 = refs[8:]
    height = query.shape[0]

    def four(values):
        a, b, c, d = values
        return (a + b) + (c + d)

    two = four([p[0].astype(F32) for p in pair])
    one = four([p[:height].astype(F32) for p in single])
    sums = four([decode(p[height:]) for p in single])
    for i, ref in enumerate((query, key, value)):
        ref[...] = jnp.concatenate(
            [two[:, 2 * i * HD : 2 * (i + 1) * HD], one[:, (3 + i) * HD : (4 + i) * HD]], axis=1
        )
    out[...] = jnp.transpose(one[:, : 3 * HD])
    for i, ref in enumerate((gain1, bias1, gain2, bias2)):
        ref[...] = jnp.concatenate([sums[i : i + 1], sums[4 + i : 5 + i]], axis=1)


def attend_out(pair, single, after=()):
    _, height, cols = pair[0].shape
    span = cols // 2
    return run(
        attend_out_kernel,
        "attend_out",
        (*pair, *single),
        [vmem()] * 8,
        (array((height, span), F32),) * 3
        + (array((span, height), F32),)
        + (array((1, 2 * cols), F32),) * 4,
        [vmem()] * 8,
        after=after,
    )


def local(
    tokens,
    w_query,
    w_key,
    w_value,
    w_out,
    w_up,
    w_down,
    gain_attn,
    bias_attn,
    gain_ffn,
    bias_ffn,
    lengths,
    random_blocks,
    cotangent,
):
    size = lax.axis_size("dp")
    rank = lax.axis_index("mp")
    me = lax.axis_index("dp")
    x, core = rank // 2, rank % 2
    _, quarter, features = tokens.shape
    seq = 4 * quarter
    height = w_query.shape[0]
    span = w_query.shape[1]
    heads = span // HD
    nblocks = seq // BLOCK
    fast = size == 8 and height % 16 == 0

    length = lax.dynamic_index_in_dim(lengths, x, 0, keepdims=False)
    shift = x * (seq // 2)
    info = jnp.stack([me, x, core, length, shift]).astype(jnp.int32)
    units = w_up.shape[1]

    blocks = (jnp.arange(nblocks) + x * (nblocks // 2)) % nblocks
    near_blocks = jnp.abs(blocks[:, None] - blocks[None, :]) <= 1
    edge = (blocks == 0) | (blocks == nblocks - 1)
    fixed = near_blocks | edge[:, None] | edge[None, :]

    def table(shard):
        chosen = lax.dynamic_slice_in_dim(random_blocks, shard * heads, heads, 0)
        chosen = jnp.roll(chosen, -x * (nblocks // 2), axis=1)
        hit = jnp.any(chosen[:, None, :, :] == blocks[None, :, None, None], axis=3)
        bias = jnp.where(fixed.T[None] | hit, 0.0, NEGATIVE)
        return jnp.concatenate(
            [
                jnp.zeros((heads, nblocks, HD), F32),
                bias,
                jnp.full((heads, nblocks, 3), -1.0, F32),
                jnp.zeros((heads, nblocks, HD - 3 - nblocks), F32),
            ],
            axis=2,
        )

    mask_own, mask_other = table(rank), table(rank ^ 2)
    mask_ends = jnp.concatenate([mask_own[2:], mask_other[2:]], axis=0)
    g_one, b_one = gain_attn[None], bias_attn[None]
    g_two, b_two = gain_ffn[None], bias_ffn[None]

    their_tok, their_cot = split(info, tokens, cotangent)
    if fast:
        flat = (tuple((0, j) for j in Y_MAJOR),)
        piece = pack(w_query, w_key, w_value, w_out)
        zs_attn = [piece] + z_sends(piece)
        got_tok = flip_chip(their_tok)
        piece_down = turn(w_down, (piece,))
        x_down = flip_chip(piece_down)
        z_pair, z_single = join_sides(zs_attn, (piece_down,))
        y_pair, x_single = flip_dp(z_pair, 1), flip_chip(z_single)
        tok_pair = couple(info, tokens, got_tok, (z_pair,))
        got_tok = flip_core(tok_pair)
        piece_up = join([w_up[None]], (tok_pair,))
        zs_up = [piece_up] + z_sends(piece_up)
        own_pair = join([z_pair, y_pair], (piece_up,))
        other_pair = flip_chip(own_pair)
        near_single = join([z_single, x_single], (own_pair,))
        far_single = flip_dp(near_single, 1)
        chip_down = join([piece_down, x_down], (near_single,))
        zs_down = [chip_down] + z_sends(chip_down)
        cot_pair = couple(info, cotangent, flip_chip(their_cot), (chip_down,))
        got_cot = flip_core(cot_pair)
        tok = merge(info, tok_pair, got_tok, (cot_pair,))
        pair_w = ((own_pair, other_pair), (OWN, OTHER))
        single_w = ((near_single, far_single), (CHIP_NEAR, CHIP_FAR))
        own01 = attend(info, tok, ((own_pair,), flat), True, mask_own[:2])
        four_up = join(zs_up, (own01[0],))
        y_up = flip_dp(four_up, 1)
        other01 = attend(info, tok, ((other_pair,), flat), True, mask_other[:2], (four_up,))
        ends = attend(info, tok, single_w, False, mask_ends, (other01[0],))
        own_up = join([four_up, y_up], (ends[0],))
        other_up = flip_chip(own_up)
        order = (own_up,)
    else:
        flat = (((0, 0),),)
        two = (((0, 0),), ((1, 0),))

        def plain(piece):
            own = lax.all_gather(piece, "dp", axis=0, tiled=True)[None]
            return own, flip_chip(own)

        tok_pair = couple(info, tokens, flip_chip(their_tok))
        tok = merge(info, tok_pair, flip_core(tok_pair))
        cot_pair = couple(info, cotangent, flip_chip(their_cot))
        got_cot = flip_core(cot_pair)
        thirds = [w_out.T] + [w[:, 2 * HD :] for w in (w_query, w_key, w_value)]
        pair_w = (
            plain(jnp.concatenate([w[:, : 2 * HD] for w in (w_query, w_key, w_value)], axis=1)),
            two,
        )
        single_w = (plain(jnp.concatenate(thirds, axis=1)), two)
        own_up, other_up = plain(w_up)
        own01 = attend(info, tok, ((pair_w[0][0],), flat), True, mask_own[:2])
        other01 = attend(info, tok, ((pair_w[0][1],), flat), True, mask_other[:2])
        ends = attend(info, tok, single_w, False, mask_ends)
        order = ()
    contexts = (own01[3], other01[3], ends[3])
    attn_part = project(info, contexts, single_w, features, order)
    if fast:
        four_down = join(zs_down, (attn_part[0],))
        y_down = flip_dp(four_down, 1)
        up = ((own_up, other_up), (OWN, OTHER))
        down = ((four_down, y_down), (Z_NEAR, Z_FAR))
        order = (four_down,)
    else:
        up = ((own_up, other_up), two)
        down = (plain(w_down.T), two)
    z_one, hn = norm_one(tok, attn_part, flip_cores(attn_part), g_one, b_one, order)

    act1, slope1 = feed_up(info, hn, ((own_up,), flat), units)
    cot = merge(info, cot_pair, got_cot, (act1,))
    act2, slope2 = feed_up(info, hn, ((other_up,), flat), units, (cot,))
    mixed = feed_down(info, act1, act2, down, features)
    out, dz_two, dzb_two, sums_two = norm_two(
        info, hn, mixed, flip_cores(mixed), cot, g_two, b_two
    )

    if fast:
        places_down = (OWN, OTHER, CHIP_NEAR, CHIP_FAR)
        places_up = (Z_OWN, Z_OTHER, Z_NEAR, Z_FAR)
        att_order = Y_MAJOR
    else:
        places_down = places_up = (((0, 0),), ((1, 0),)) * 2
        att_order = (0,)
    att_slots = tuple((0, j) for j in att_order)

    keep_d1, send_d1, keep_d2, send_d2 = feed_grad(info, dzb_two, act1, act2, places_down)
    du1, du2, *back = feed_back(info, dzb_two, slope1, slope2, up, down, (keep_d1,))
    back_got = flip_cores(back)
    order = (du1,)
    if fast:
        keep_d1, send_d1, keep_d2, send_d2 = fold_two(
            keep_d1, flip_chip(send_d1), keep_d2, flip_dp(send_d2, 1), 2, False, order
        )
        order = (keep_d1,)
    keep_u1, send_u1, keep_u2, send_u2 = feed_grad(info, hn, du1, du2, places_up, order)
    dz_one, dzb_one, sums_one = norm_one_back(
        z_one, dz_two, back, back_got, g_one, (keep_u1,)
    )
    order = (dzb_one,)
    if fast:
        zs_d = fold_two(
            keep_d1, flip_dp(send_d1, 1), keep_d2, flip_chip(send_d2), 4, True, order
        )
        zs_d = z_trade(zs_d)
        order = (zs_d[0],)
    d_ends = attend_back(info, dzb_one, single_w, None, ends, order)
    keep_s, send_s = single_grad(
        info, tok, d_ends, dzb_one, contexts, sums_one, sums_two, att_order
    )
    got_s = flip_chip(send_s)
    order = (keep_s,)
    if fast:
        zs_u = fold_two(
            keep_u1, flip_chip(send_u1), keep_u2, flip_dp(send_u2, 1), 4, True, order
        )
        zs_u = z_trade(zs_u)
        order = (zs_u[0],)
    d_other = attend_back(info, dzb_one, single_w, 1, other01, order)
    grad_b = pair_grad(info, tok, d_other, att_slots)
    got_b = flip_chip(grad_b)
    order = (grad_b,)
    if fast:
        keep_s, send_s = fold(keep_s, got_s, 2, TAIL, order)
        got_s = flip_dp(send_s, 1)
        order = (keep_s,)
    own_out, send_out = halves(info, out, order)
    got_out = flip_chip(send_out)
    d_own = attend_back(info, dzb_one, single_w, 0, own01, (own_out,))
    grad_a = pair_grad(info, tok, d_own, att_slots)
    order = (grad_a,)
    if fast:
        keep_a, send_a = fold(grad_a, got_b, 2, 0, order)
        got_a = flip_dp(send_a, 1)
        zs_s = z_trade(fold(keep_s, got_s, 4, TAIL, (keep_a,)))
        keep_u, send_u1, send_u2 = fold_four(zs_u, (zs_s[0],))
        got_u1, got_u2 = flip_dp(send_u1, 1), flip_chip(send_u2)
        order = (keep_u,)
    mine, sent = input_back(info, d_own, d_other, d_ends, dz_one, pair_w, single_w, order)
    own_tok, send_tok = tokens_add(mine, flip_core(sent))
    got_tok = flip_chip(send_tok)
    output = slots_of(info, own_out, got_out, (own_tok,))
    if fast:
        zs_a = z_trade(fold(keep_a, got_a, 4, 0, (own_tok,)))
        grad_up, grad_down = feed_out(zs_d, keep_u, got_u1, got_u2, (zs_a[0],))
        grads = attend_out(zs_a, zs_s, (grad_up,))
        sums = grads[4:]
    else:

        def plain_sum(own, other):
            total = own.astype(F32) + flip_chip(other).astype(F32)
            return lax.psum_scatter(total, "dp", scatter_dimension=0, tiled=True)

        def plain_wide(keep1, send1, keep2, send2):
            return jnp.concatenate([plain_sum(keep1[0], send1[0]), plain_sum(keep2[0], send2[0])], axis=1)

        grad_down = plain_wide(keep_d1, send_d1, keep_d2, send_d2).T
        grad_up = plain_wide(keep_u1, send_u1, keep_u2, send_u2)
        grad_single = plain_sum(keep_s[:features], send_s[:features])
        grad_pair = plain_sum(grad_a[0], grad_b[0])
        grads = [
            jnp.concatenate(
                [
                    grad_pair[:, 2 * i * HD : 2 * (i + 1) * HD],
                    grad_single[:, (3 + i) * HD : (4 + i) * HD],
                ],
                axis=1,
            )
            for i in range(3)
        ] + [grad_single[:, : 3 * HD].T]
        sums = decode(keep_s[features:])
        sums = lax.psum(sums + flip_chip(sums), "dp")
        sums = [jnp.concatenate([sums[i], sums[4 + i]])[None] for i in range(4)]
    grad_tokens = tokens_out(info, own_tok, got_tok)

    return (
        output,
        grad_tokens,
        *grads[:4],
        grad_up,
        grad_down,
        *(v[0] for v in sums),
    )


def solution(mesh):
    return jax.shard_map(
        local,
        mesh=mesh,
        in_specs=(
            P("dp", "mp", None),
            P("dp", "mp"),
            P("dp", "mp"),
            P("dp", "mp"),
            P("mp", "dp"),
            P("dp", "mp"),
            P("mp", "dp"),
            P(),
            P(),
            P(),
            P(),
            P("dp"),
            P(),
            P("dp", "mp", None),
        ),
        out_specs=(
            P("dp", "mp", None),
            P("dp", "mp", None),
            P("dp", "mp"),
            P("dp", "mp"),
            P("dp", "mp"),
            P("mp", "dp"),
            P("dp", "mp"),
            P("mp", "dp"),
            P(),
            P(),
            P(),
            P(),
        ),
        check_vma=False,
    )
```

```python
import functools

import jax
import jax.numpy as jnp
from jax import lax
from jax.experimental import pallas as pl
from jax.experimental.pallas import tpu as pltpu
from jax.sharding import PartitionSpec as P

HD = 64
BLOCK = 64
LANES = 128
TILE = 256
SENT = 256
EPSILON = 1e-12
TAIL = 32
ROOM = {
    "attend": 24,
    "attend_back": 28,
    "project": 16,
    "input_back": 24,
    "norm_one": 16,
    "norm_two": 24,
    "norm_one_back": 24,
    "feed_up": 20,
    "feed_down": 24,
    "feed_back": 40,
    "feed_grad": 28,
    "pair_grad": 16,
    "single_grad": 28,
    "join": 1,
    "join_sides": 1,
    "beside": 1,
    "pack": 2,
    "split": 1,
    "merge": 1,
    "fold": 6,
    "fold_add": 8,
    "fold_feed": 10,
    "fold_sides": 8,
    "fold_last": 6,
    "fold_z": 4,
    "halves": 1,
    "slots": 1,
    "tokens_add": 8,
    "tokens_out": 8,
    "feed_out": 6,
    "attend_out": 6,
}
FLOPS = {}
SCALE = 0.125
LOG2E = 1.4426950408889634
LN2 = 0.6931471805599453
NEGATIVE = -1e30
F32 = jnp.float32
BF16 = jnp.bfloat16

ERFCX_STEP = 0.45
ERFCX = (
    -8.220994855312894e-06,
    0.2540684902923417,
    0.25234751996246985,
    0.23373082558517694,
    0.1739141918052578,
    0.06370751405215419,
    0.18661300519520473,
    -0.22870513112792096,
    0.06433208636936971,
)

CORE_SWAP = [(0, 1), (1, 0), (2, 3), (3, 2)]
CHIP_SWAP = [(0, 2), (2, 0), (1, 3), (3, 1)]


def nn(a, b):
    return lax.dot_general(a, b, (((1,), (0,)), ((), ())), preferred_element_type=F32)


def nt(a, b):
    return lax.dot_general(a, b, (((1,), (1,)), ((), ())), preferred_element_type=F32)


def tn(a, b):
    return lax.dot_general(a, b, (((0,), (0,)), ((), ())), preferred_element_type=F32)


def vmem():
    return pl.BlockSpec(memory_space=pltpu.VMEM)


def smem():
    return pl.BlockSpec(memory_space=pltpu.SMEM)


def anywhere():
    return pl.BlockSpec(memory_space=pl.ANY)


def in_hbm(values):
    return tuple(pltpu.with_memory_space_constraint(v, pltpu.HBM) for v in values)


def rows(width):
    return pl.BlockSpec((TILE, width), lambda i: (i, 0))


def whole(shape):
    return pl.BlockSpec(shape, lambda i: (0,) * len(shape))


def array(shape, dtype):
    return jax.ShapeDtypeStruct(shape, dtype)


CALLS = []


def work(name):
    CALLS.append(name)
    return FLOPS.get(name + str(CALLS.count(name)), 1)


def run(kernel, name, args, specs, outs, out_specs, scratch=(), *, grid=(), after=()):
    given, extra = len(args), len(after)

    def body(*refs):
        kernel(*refs[:given], *refs[given + extra :])

    return pl.pallas_call(
        body,
        grid=grid,
        out_shape=tuple(outs),
        in_specs=list(specs) + [anywhere()] * extra,
        out_specs=tuple(out_specs),
        scratch_shapes=list(scratch),
        compiler_params=pltpu.CompilerParams(vmem_limit_bytes=ROOM[name] * 2**20),
        cost_estimate=pl.CostEstimate(
            flops=work(name), bytes_accessed=0, transcendentals=0
        ),
        name=name,
    )(*args, *after)


def put_rows(parts, value):
    height = parts[0].shape[0]
    tile = value.shape[0]
    i = pl.program_id(0)
    for k, part in enumerate(parts):
        if height <= tile:
            per = tile // height

            @pl.when(i == k // per)
            def _(k=k, part=part):
                at = k % per * height
                part[...] = value[at : at + height]

        else:
            per = height // tile

            @pl.when(i // per == k)
            def _(part=part):
                part[pl.ds(pl.multiple_of(i % per * tile, tile), tile), :] = value


def get_sum(parts, more, count):
    height = parts[0].shape[0]
    tile = len(parts) * height // count
    i = pl.program_id(0)
    total = None
    if height <= tile:
        per = tile // height
        for k in range(count):
            pieces = [
                a[...].astype(F32) + b[...].astype(F32)
                for a, b in zip(parts[k * per : (k + 1) * per], more[k * per : (k + 1) * per])
            ]
            value = pieces[0] if per == 1 else jnp.concatenate(pieces, axis=0)
            total = value if k == 0 else jnp.where(i == k, value, total)
    else:
        per = height // tile
        at = pl.ds(pl.multiple_of(i % per * tile, tile), tile)
        for k, (a, b) in enumerate(zip(parts, more)):
            value = a[at, :].astype(F32) + b[at, :].astype(F32)
            total = value if k == 0 else jnp.where(i // per == k, value, total)
    return total


def far(shape, dtype):
    return pltpu.HBM(shape, dtype)


def tiles(seq, width, height):
    parts = (array((height, width), BF16),) * (seq // height)
    return parts, [whole((height, width))] * len(parts)


def place(me, refs, slots, dst_ref, first=0, last=None, only=None, to=0):
    for ref, of in zip(refs, slots):
        height, width = ref.shape[1], ref.shape[2]
        end = width if last is None else last
        for e, (chip, j) in enumerate(of):
            if only is not None and chip != only:
                continue
            at = 0 if height == dst_ref.shape[0] else pl.multiple_of((me ^ j) * height, height)
            at_column = to + (0 if only is not None else chip * (end - first))
            dst_ref[pl.ds(at, height), pl.ds(at_column, end - first)] = ref[e, :, first:end]


def pick(me, fulls, out_ref, slots, first):
    _, height, width = out_ref.shape
    for e, (chip, j) in enumerate(slots):
        full = fulls[chip]
        at = 0 if height == full.shape[0] else pl.multiple_of((me ^ j) * height, height)
        out_ref[e] = full[pl.ds(at, height), pl.ds(first, width)].astype(BF16)


def attend_kernel(slots, columns, only, places, info, tok, mask, *rest):
    refs, (qa, ka, va, ctx, wfull) = rest[: len(slots)], rest[len(slots) :]
    seq = tok.shape[0]
    place(info[0], refs, slots, wfull, *columns, only)
    lane = lax.broadcasted_iota(jnp.int32, (TILE, LANES), 1)
    row0 = lax.broadcasted_iota(jnp.int32, (TILE, LANES), 0)
    for t in range(seq // TILE):
        at = pl.ds(t * TILE, TILE)
        row = row0 + t * TILE
        made = nn(tok[at, :], wfull[...])
        onehot = jnp.where(lane - HD == row // BLOCK, 1.0, 0.0)[:, HD:]
        position = row + info[4]
        position = jnp.where(position >= seq, position - seq, position)
        dead = (position >= info[3]) & (lane >= HD) & (lane < HD + 16)
        for h, (q_at, k_at, v_at) in enumerate(places):
            q = made[:, q_at : q_at + HD] * (SCALE * LOG2E)
            k = made[:, k_at : k_at + HD]
            v = made[:, v_at : v_at + HD]
            qa[h, at, :] = jnp.concatenate([q, onehot], axis=1).astype(BF16)
            per = TILE // BLOCK
            table = jnp.concatenate(
                [
                    jnp.broadcast_to(mask[h, t * per + b : t * per + b + 1, :], (BLOCK, LANES))
                    for b in range(per)
                ],
                axis=0,
            )
            table = jnp.where(dead, NEGATIVE, table)
            ka[h, at, :] = jnp.concatenate([k, table[:, HD:]], axis=1).astype(BF16)
            va[h, at, :] = jnp.concatenate([v, jnp.full((TILE, HD), -1.0, F32)], axis=1).astype(BF16)
    for t in range(seq // TILE):
        at = pl.ds(t * TILE, TILE)
        pieces = []
        for h in range(len(places)):
            q = qa[h, at, :]
            s = nt(q, ka[h])
            top = jnp.max(s, axis=1, keepdims=True)
            p = jnp.exp2(s - top).astype(BF16)
            got = nn(p, va[h])
            total = -got[:, HD:]
            pieces.append(got[:, :HD] / total)
            log = top + jnp.log2(-got)
            hi = log.astype(BF16).astype(F32)
            mid = (log - hi).astype(BF16).astype(F32)
            low = log - hi - mid
            new = jnp.where(
                lane == HD + 16,
                hi,
                jnp.where(lane == HD + 17, mid, jnp.where(lane == HD + 18, low, q.astype(F32))),
            )
            qa[h, at, :] = new.astype(BF16)
        ctx[at, :] = jnp.concatenate(pieces, axis=1).astype(BF16)


PAIR = ((0, 2 * HD, 4 * HD), (HD, 3 * HD, 5 * HD))
SINGLES = ((HD, 2 * HD, 3 * HD), (5 * HD, 6 * HD, 7 * HD))


def attend(info, tok, gathered, pair, mask, after=()):
    arrays, slots = gathered
    seq, width = tok.shape
    aug = far((2, seq, LANES), BF16)
    columns, only, cols = ((0, 6 * HD), 0, 6 * HD) if pair else ((2 * HD, 6 * HD), None, 8 * HD)
    return run(
        functools.partial(attend_kernel, slots, columns, only, PAIR if pair else SINGLES),
        "attend",
        (info, tok, mask) + arrays,
        [smem()] + [vmem()] * (2 + len(arrays)),
        (aug, aug, aug, array((seq, LANES), BF16)),
        [vmem()] * 4,
        [pltpu.VMEM((width, cols), BF16)],
        after=after,
    )


def place_out(me, refs, slots, pairs, ends):
    place(me, refs, slots, pairs, 0, 2 * HD)
    place(me, refs, slots, ends, 2 * HD, 4 * HD)
    both = ends[...]
    ends[:, :LANES] = jnp.concatenate([both[:, :HD], both[:, LANES : LANES + HD]], axis=1)


def project_kernel(slots, info, own, other, ends, *rest):
    refs, parts, (w1, w2) = rest[: len(slots)], rest[len(slots) : -2], rest[-2:]

    @pl.when(pl.program_id(0) == 0)
    def _():
        place_out(info[0], refs, slots, w1, w2)

    both = jnp.concatenate([own[...], other[...]], axis=1)
    put_rows(parts, (nt(both, w1[...]) + nt(ends[...], w2[:, :LANES])).astype(BF16))


def project(info, contexts, gathered, width, after=()):
    arrays, slots = gathered
    seq = contexts[0].shape[0]
    return run(
        functools.partial(project_kernel, slots),
        "project",
        (info,) + contexts + arrays,
        [smem()] + [rows(LANES)] * 3 + [whole(a.shape) for a in arrays],
        *tiles(seq, width, 2 * TILE),
        [pltpu.VMEM((width, 2 * LANES), BF16)] * 2,
        grid=(seq // TILE,),
        after=after,
    )


def attend_back_kernel(slots, chip, info, dz, qa, ka, va, ctx, *rest):
    refs, (dqkv, pairs, ends, da, parts) = rest[: len(slots)], rest[len(slots) :]
    seq = dz.shape[0]
    heads = qa.shape[0]
    if chip is None:
        place_out(info[0], refs, slots, pairs, ends)
        wfull = ends.at[:, pl.ds(0, LANES)]
    else:
        place(info[0], refs, slots, pairs, 0, 2 * HD, chip)
        wfull = pairs.at[:, pl.ds(0, LANES)]
    lane = lax.broadcasted_iota(jnp.int32, (TILE, LANES), 1)
    for t in range(seq // TILE):
        at = pl.ds(t * TILE, TILE)
        dctx = nn(dz[at, :], wfull[...]).astype(BF16).astype(F32)
        both = dctx * ctx[at, :].astype(F32)
        for h in range(heads):
            inner = jnp.sum(both[:, h * HD : (h + 1) * HD], axis=1, keepdims=True)
            hi = inner.astype(BF16).astype(F32)
            mid = (inner - hi).astype(BF16).astype(F32)
            low = inner - hi - mid
            one = jnp.concatenate(
                [dctx[:, h * HD : (h + 1) * HD], jnp.zeros((TILE, HD), F32)], axis=1
            )
            one = jnp.where(lane == HD, hi, one)
            one = jnp.where(lane == HD + 1, mid, one)
            one = jnp.where(lane == HD + 2, low, one)
            da[h, at, :] = one.astype(BF16)
    for h in range(heads):
        k_turned = jnp.transpose(ka[h].astype(F32)).astype(BF16)
        dq_turned = None
        for t in range(seq // TILE):
            at = pl.ds(t * TILE, TILE)
            p = jnp.exp2(nt(ka[h, at, :], qa[h]))
            ds = (p * nt(va[h, at, :], da[h])).astype(BF16)
            parts[2 * heads + h, at, :] = nn(p.astype(BF16), da[h])
            parts[heads + h, at, :] = nn(ds, qa[h]) * LN2
            more = nn(k_turned[:, t * TILE : (t + 1) * TILE], ds)
            dq_turned = more if dq_turned is None else dq_turned + more
        parts[h] = jnp.transpose(dq_turned) * SCALE
    for t in range(seq // TILE):
        at = pl.ds(t * TILE, TILE)
        pieces = [parts[i, at, :][:, :HD] for i in range(3 * heads)]
        if chip is None:
            blank = jnp.zeros((TILE, HD), F32)
            pieces = [blank] + pieces[::2] + [blank] + pieces[1::2]
        dqkv[at, :] = jnp.concatenate(pieces, axis=1).astype(BF16)


def attend_back(info, dz, gathered, chip, saved, after=()):
    arrays, slots = gathered
    qa, ka, va, ctx = saved
    seq, width = dz.shape
    cols = 8 * HD if chip is None else 6 * HD
    return run(
        functools.partial(attend_back_kernel, slots, chip),
        "attend_back",
        (info, dz, qa, ka, va, ctx) + arrays,
        [smem()] + [vmem()] * (5 + len(arrays)),
        (array((seq, cols), BF16),),
        [vmem()],
        [
            pltpu.VMEM((width, 2 * LANES), BF16),
            pltpu.VMEM((width, 2 * LANES), BF16),
            pltpu.VMEM((2, seq, LANES), BF16),
            pltpu.VMEM((6, seq, LANES), F32),
        ],
        after=after,
    )[0]


def input_back_kernel(slots1, slots2, info, own, other, ends, dz, *rest):
    n1, n2 = len(slots1), len(slots2)
    refs1, refs2, (mine, *sent, w1, w2) = rest[:n1], rest[n1 : n1 + n2], rest[n1 + n2 :]
    i = pl.program_id(0)

    @pl.when(i == 0)
    def _():
        place(info[0], refs1, slots1, w1)
        place(info[0], refs2, slots2, w2, 2 * HD, 6 * HD)

    pairs = jnp.concatenate([own[...], other[...]], axis=1)
    back = nt(pairs, w1[...]) + nt(ends[...], w2[...])

    @pl.when(i % 2 == info[2])
    def _():
        mine[i // 2] = back + dz[...]

    per = len(sent) // 2
    height = sent[0].shape[0]
    for k, part in enumerate(sent):

        @pl.when((i % 2 != info[2]) & (i // 2 == k // per))
        def _(k=k, part=part):
            part[...] = back[k % per * height : (k % per + 1) * height].astype(BF16)


def input_back(info, own, other, ends, dz, gathered1, gathered2, after=()):
    seq, width = dz.shape
    arrays = gathered1[0] + gathered2[0]
    halves = (seq // TILE // 2, TILE, width)
    grads = (own, other, ends, dz)
    return run(
        functools.partial(input_back_kernel, gathered1[1], gathered2[1]),
        "input_back",
        (info,) + grads + arrays,
        [smem()] + [rows(g.shape[1]) for g in grads] + [whole(a.shape) for a in arrays],
        (array(halves, F32),) + (array((SENT, width), BF16),) * (seq // 2 // SENT),
        [whole(halves)] + [whole((SENT, width))] * (seq // 2 // SENT),
        [pltpu.VMEM((width, 12 * HD), BF16), pltpu.VMEM((width, 8 * HD), BF16)],
        grid=(seq // TILE,),
        after=after,
    )


def center(z):
    mean = jnp.mean(z, axis=1, keepdims=True)
    moved = z - mean
    spread = jnp.mean(moved * moved, axis=1, keepdims=True)
    scale = lax.rsqrt(spread + EPSILON)
    return moved * scale, scale


def norm_back(n, scale, gy, gain):
    dn = gy * gain
    return scale * (
        dn - jnp.mean(dn, axis=1, keepdims=True) - n * jnp.mean(dn * n, axis=1, keepdims=True)
    )


def add_sums(gy, n, sums):
    i = pl.program_id(0)

    @pl.when(i == 0)
    def _():
        sums[...] = jnp.zeros_like(sums)

    sums[0:1, :] += jnp.sum(gy * n, axis=0, keepdims=True)
    sums[1:2, :] += jnp.sum(gy, axis=0, keepdims=True)


def norm_one_kernel(tok, gain, bias, *rest):
    *parts, z, hn = rest
    count = len(parts) // 2
    value = tok[...].astype(F32) + get_sum(parts[:count], parts[count:], count * parts[0].shape[0] // TILE)
    z[...] = value
    n, _ = center(value)
    hn[...] = (n * gain[...] + bias[...]).astype(BF16)


def norm_one(tok, p0, p1, gain, bias, after=()):
    seq, width = tok.shape
    return run(
        norm_one_kernel,
        "norm_one",
        (tok, gain, bias, *p0, *p1),
        [rows(width)] + [whole((1, width))] * 2 + [whole(p.shape) for p in (*p0, *p1)],
        (far((seq, width), F32), array((seq, width), BF16)),
        (rows(width), rows(width)),
        grid=(seq // TILE,),
        after=after,
    )


def norm_two_kernel(info, hn, own, got, core_own, core_got, gain, bias, *rest):
    *parts, out, dz, dzb, sums = rest
    count = len(parts) // 2
    value = hn[...].astype(F32) + get_sum(parts[:count], parts[count:], count * parts[0].shape[0] // TILE)
    n, scale = center(value)
    out[...] = (n * gain[...] + bias[...]).astype(BF16)
    row = lax.broadcasted_iota(jnp.int32, value.shape, 0) + pl.program_id(0) * TILE
    seq = pl.num_programs(0) * TILE
    position = row + info[4]
    position = jnp.where(position >= seq, position - seq, position)
    i = pl.program_id(0)
    mine = i % 2 == info[2]
    cot = jnp.where(
        i < 2,
        jnp.where(mine, own[0].astype(F32), core_own[0].astype(F32)),
        jnp.where(mine, got[0].astype(F32), core_got[0].astype(F32)),
    )
    gy = jnp.where(position < info[3], cot, 0.0)
    grad = norm_back(n, scale, gy, gain[...])
    dz[...] = grad
    dzb[...] = grad.astype(BF16)
    add_sums(gy, n, sums)


def norm_two(info, hn, m0, m1, cot, gain, bias, after=()):
    seq, width = hn.shape
    return run(
        norm_two_kernel,
        "norm_two",
        (info, hn, *cot, gain, bias, *m0, *m1),
        [smem(), rows(width)]
        + [pl.BlockSpec((1,) + c.shape[1:], lambda i: (1, 0, 0)) for c in cot]
        + [whole((1, width))] * 2
        + [whole(p.shape) for p in (*m0, *m1)],
        (
            array((seq, width), BF16),
            far((seq, width), F32),
            array((seq, width), BF16),
            array((2, width), F32),
        ),
        (rows(width), rows(width), rows(width), whole((2, width))),
        grid=(seq // TILE,),
        after=after,
    )


def norm_one_back_kernel(z, dz2, gain, *rest):
    *parts, dz, dzb, sums = rest
    count = len(parts) // 2
    n, scale = center(z[...])
    gy = dz2[...] + get_sum(parts[:count], parts[count:], count * parts[0].shape[0] // TILE)
    grad = norm_back(n, scale, gy, gain[...])
    dz[...] = grad
    dzb[...] = grad.astype(BF16)
    add_sums(gy, n, sums)


def norm_one_back(z, dz2, p0, p1, gain, after=()):
    seq, width = z.shape
    return run(
        norm_one_back_kernel,
        "norm_one_back",
        (z, dz2, gain, *p0, *p1),
        [rows(width)] * 2 + [whole((1, width))] + [whole(p.shape) for p in (*p0, *p1)],
        (array((seq, width), F32), array((seq, width), BF16), array((2, width), F32)),
        (rows(width), rows(width), whole((2, width))),
        grid=(seq // TILE,),
        after=after,
    )


def gelu_pair(u):
    z = jnp.abs(u) * 0.7071067811865476
    t = 1.0 / (1.0 + ERFCX_STEP * z)
    poly = jnp.full_like(t, ERFCX[-1])
    for coefficient in ERFCX[-2::-1]:
        poly = poly * t + coefficient
    e = jnp.exp(-z * z)
    tail = 0.5 * (poly * e)
    phi = jnp.where(u >= 0, 1.0 - tail, tail)
    return u * phi, phi + u * (e * 0.3989422804014327)


def feed_up_kernel(slots, info, hn, *rest):
    refs, (active, slope, wfull) = rest[: len(slots)], rest[len(slots) :]

    @pl.when(pl.program_id(0) == 0)
    def _():
        place(info[0], refs, slots, wfull)

    a, g = gelu_pair(nn(hn[...], wfull[...]))
    active[...] = a.astype(BF16)
    slope[...] = g.astype(BF16)


def feed_up(info, hn, gathered, units, after=()):
    arrays, slots = gathered
    seq, width = hn.shape
    return run(
        functools.partial(feed_up_kernel, slots),
        "feed_up",
        (info, hn) + arrays,
        [smem(), rows(width)] + [whole(a.shape) for a in arrays],
        (array((seq, units), BF16), array((seq, units), BF16)),
        (rows(units), rows(units)),
        [pltpu.VMEM((width, units), BF16)],
        grid=(seq // TILE,),
        after=after,
    )


def feed_down_kernel(slots, info, act1, act2, *rest):
    refs, parts, wfull = rest[: len(slots)], rest[len(slots) : -1], rest[-1]

    @pl.when(pl.program_id(0) == 0)
    def _():
        place(info[0], refs, slots, wfull)

    both = jnp.concatenate([act1[...], act2[...]], axis=1)
    put_rows(parts, nt(both, wfull[...]).astype(BF16))


def feed_down(info, act1, act2, gathered, width, after=()):
    seq, units = act1.shape
    arrays, slots = gathered
    return run(
        functools.partial(feed_down_kernel, slots),
        "feed_down",
        (info, act1, act2) + arrays,
        [smem(), rows(units), rows(units)] + [whole(a.shape) for a in arrays],
        *tiles(seq, width, 2 * TILE),
        [pltpu.VMEM((width, 2 * units), BF16)],
        grid=(seq // TILE,),
        after=after,
    )


def feed_back_kernel(slots_up, slots_down, info, dzb, slope1, slope2, *rest):
    n1, n2 = len(slots_up), len(slots_down)
    ups, downs, (du1, du2, *parts, up, down) = rest[:n1], rest[n1 : n1 + n2], rest[n1 + n2 :]

    @pl.when(pl.program_id(0) == 0)
    def _():
        place(info[0], ups, slots_up, up)
        place(info[0], downs, slots_down, down)

    units = du1.shape[1]
    out = None
    for i, (slope, du) in enumerate(((slope1, du1), (slope2, du2))):
        at = pl.ds(i * units, units)
        grad = (nn(dzb[...], down[:, at]) * slope[...].astype(F32)).astype(BF16)
        du[...] = grad
        more = nt(grad, up[:, at])
        out = more if out is None else out + more
    put_rows(parts, out.astype(BF16))


def feed_back(info, dzb, slope1, slope2, up, down, after=()):
    seq, width = dzb.shape
    units = slope1.shape[1]
    arrays = up[0] + down[0]
    parts, part_specs = tiles(seq, width, TILE)
    return run(
        functools.partial(feed_back_kernel, up[1], down[1]),
        "feed_back",
        (info, dzb, slope1, slope2) + arrays,
        [smem(), rows(width), rows(units), rows(units)] + [whole(a.shape) for a in arrays],
        (array((seq, units), BF16),) * 2 + parts,
        [rows(units)] * 2 + part_specs,
        [pltpu.VMEM((width, 2 * units), BF16)] * 2,
        grid=(seq // TILE,),
        after=after,
    )


def feed_grad_kernel(places, info, a, d1, d2, *rest):
    outs, fulls = rest[:4], rest[4:]
    half = outs[0].shape[2]
    fulls[0][...] = tn(a[...], d1[...])
    fulls[1][...] = tn(a[...], d2[...])
    for i, out in enumerate(outs):
        pick(info[0], fulls, out, places[i], (i // 2) * half)


def feed_grad(info, a, d1, d2, places, after=()):
    seq, width = a.shape
    units = d1.shape[1]
    count = len(places[0])
    out = array((count, width // count, units // 2), BF16)
    return run(
        functools.partial(feed_grad_kernel, places),
        "feed_grad",
        (info, a, d1, d2),
        [smem()] + [vmem()] * 3,
        (out,) * 4,
        [vmem()] * 4,
        [pltpu.VMEM((width, units), F32)] * 2,
        after=after,
    )


def pair_grad_kernel(slots, info, tok, d, out, full):
    full[...] = tn(tok[...], d[...])
    pick(info[0], (full,), out, slots, 0)


def pair_grad(info, tok, d, slots, after=()):
    seq, width = tok.shape
    cols = d.shape[1]
    return run(
        functools.partial(pair_grad_kernel, slots),
        "pair_grad",
        (info, tok, d),
        [smem()] + [vmem()] * 2,
        (array((len(slots), width // len(slots), cols), BF16),),
        [vmem()],
        [pltpu.VMEM((width, cols), F32)],
        after=after,
    )[0]


def encode(sums):
    hi = sums.astype(BF16).astype(F32)
    mid = (sums - hi).astype(BF16).astype(F32)
    low = sums - hi - mid
    return jnp.concatenate([hi, mid, low, jnp.zeros_like(low)], axis=0).astype(BF16)


def decode(coded):
    values = coded.astype(F32)
    n = values.shape[0] // 4
    return values[:n] + values[n : 2 * n] + values[2 * n : 3 * n]


def single_grad_kernel(places, info, tok, d, dz, own, other, ends, sums_one, sums_two, keep, send, full):
    mine = tn(tok[...], d[...])
    third = tn(dz[...], ends[...])
    blank = jnp.zeros((third.shape[0], HD), F32)
    width = full.shape[2]
    both = jnp.concatenate([sums_one[...], sums_two[...]], axis=0)
    both = encode(jnp.concatenate([both[:, :width], both[:, width:]], axis=0))
    for chip, ctx in enumerate((own, other)):
        full[chip, :, :LANES] = tn(dz[...], ctx[...])
        at = chip * 4 * HD
        o_third = jnp.concatenate([third[:, chip * HD : (chip + 1) * HD], blank], axis=1)
        full[chip, :, LANES : 2 * LANES] = o_third + mine[:, at : at + LANES]
        full[chip, :, 2 * LANES :] = mine[:, at + LANES : at + 2 * LANES]
    for out, slots in zip((keep, send), places):
        count = len(slots)
        height = full.shape[1] // count
        for e, (chip, j) in enumerate(slots):
            at = 0 if count == 1 else pl.multiple_of((info[0] ^ j) * height, height)
            out[pl.ds(e * height, height), :] = full[chip, pl.ds(at, height), :].astype(BF16)
        out[pl.ds(count * height, TAIL), :] = both


def single_grad(info, tok, d, dz, contexts, sums_one, sums_two, places, after=()):
    seq, width = tok.shape
    cols = 6 * HD
    out = array((width + TAIL, cols), BF16)
    return run(
        functools.partial(single_grad_kernel, places),
        "single_grad",
        (info, tok, d, dz, *contexts, sums_one, sums_two),
        [smem()] + [vmem()] * 8,
        (out, out),
        [vmem()] * 2,
        [pltpu.VMEM((2, width, cols), F32)],
        after=after,
    )


def across(values, axis, pairs):
    return lax.ppermute(values, axis, pairs)


def flip_chip(values):
    return across(values, "mp", CHIP_SWAP)


def flip_core(values):
    return across(values, "mp", CORE_SWAP)


def flip_cores(parts):
    return [flip_core(p) for p in parts]


def flip_dp(values, distance):
    size = lax.axis_size("dp")
    return across(values, "dp", [(i, i ^ distance) for i in range(size)])


def join_kernel(groups, *refs):
    count = sum(groups)
    parts, outs, sems = refs[:count], refs[count:-1], refs[-1]
    copies = []
    for out, number in zip(outs, groups):
        first = 0
        for part in parts[len(copies) : len(copies) + number]:
            to = out.at[pl.ds(first, part.shape[0])]
            copies.append(pltpu.make_async_copy(part, to, sems.at[len(copies)]))
            first += part.shape[0]
    for copy in copies:
        copy.start()
    for copy in copies:
        copy.wait()


def join(*groups, after=()):
    parts = sum((tuple(g) for g in groups), ())
    outs = [array((sum(p.shape[0] for p in g),) + g[0].shape[1:], g[0].dtype) for g in groups]
    return run(
        functools.partial(join_kernel, tuple(len(g) for g in groups)),
        "join",
        parts,
        [anywhere()] * len(parts),
        outs,
        [anywhere()] * len(outs),
        [pltpu.SemaphoreType.DMA((len(parts),))],
        after=after,
    )


def pack_kernel(w_query, w_key, w_value, w_out, out, rows_in, out_in, sems):
    copies = [
        pltpu.make_async_copy(w, rows_in.at[i], sems.at[i])
        for i, w in enumerate((w_query, w_key, w_value))
    ]
    copies.append(pltpu.make_async_copy(w_out, out_in, sems.at[3]))
    for copy in copies:
        copy.start()
    for copy in copies:
        copy.wait()
    for i in range(3):
        out[0, :, 2 * i * HD : 2 * (i + 1) * HD] = rows_in[i, :, : 2 * HD]
    parts = [jnp.transpose(out_in[...].astype(F32))]
    parts += [rows_in[i, :, 2 * HD :].astype(F32) for i in range(3)]
    out[0, :, 6 * HD :] = jnp.concatenate(parts, axis=1).astype(BF16)


def pack(w_query, w_key, w_value, w_out):
    height, span = w_query.shape
    return run(
        pack_kernel,
        "pack",
        in_hbm((w_query, w_key, w_value, w_out)),
        [anywhere()] * 4,
        (array((1, height, 4 * span), BF16),),
        [vmem()],
        [
            pltpu.VMEM((3, height, span), BF16),
            pltpu.VMEM(w_out.shape, BF16),
            pltpu.SemaphoreType.DMA((4,)),
        ],
    )[0]


def beside_kernel(first, second, out, sems):
    width = first.shape[1]
    copies = [
        pltpu.make_async_copy(ref, out.at[0, :, pl.ds(i * width, width)], sems.at[i])
        for i, ref in enumerate((first, second))
    ]
    for copy in copies:
        copy.start()
    for copy in copies:
        copy.wait()


def beside(first, second, after=()):
    height, width = first.shape
    return run(
        beside_kernel,
        "beside",
        in_hbm((first, second)),
        [anywhere()] * 2,
        (array((1, height, 2 * width), BF16),),
        [anywhere()],
        [pltpu.SemaphoreType.DMA((2,))],
        after=after,
    )[0]


def join_sides_kernel(count, *refs):
    parts, outs, sems = refs[:count], refs[count : count + 2], refs[count + 2]
    width = outs[0].shape[2]
    copies = []
    each = parts[0].shape[0]
    for i, part in enumerate(parts):
        for side, out in enumerate(outs):
            copies.append(
                pltpu.make_async_copy(
                    part.at[:, :, pl.ds(side * width, width)],
                    out.at[pl.ds(i * each, each)],
                    sems.at[2 * i + side],
                )
            )
    for copy in copies:
        copy.start()
    for copy in copies:
        copy.wait()


def join_sides(parts, after=()):
    count = len(parts)
    each, height, width = parts[0].shape
    out = array((count * each, height, width // 2), BF16)
    return run(
        functools.partial(join_sides_kernel, count),
        "join_sides",
        tuple(parts),
        [anywhere()] * count,
        (out, out),
        [anywhere()] * 2,
        [pltpu.SemaphoreType.DMA((2 * count,))],
        after=after,
    )


def fold_kernel(tail, own, got, *outs):
    body = own.shape[0] - tail
    each = body // len(outs)
    for i, out in enumerate(outs):
        at = pl.ds(i * each, each)
        total = (own[at].astype(F32) + got[at].astype(F32)).astype(BF16)
        if tail:
            out[:each] = total
        else:
            out[...] = total
    if tail:
        coded = encode(decode(own[body:]) + decode(got[body:]))
        for out in outs:
            out[each:] = coded


def fold(own, got, parts, tail=0, after=()):
    shape = ((own.shape[0] - tail) // parts + tail,) + own.shape[1:]
    return run(
        functools.partial(fold_kernel, tail),
        "fold",
        (own, got),
        [vmem()] * 2,
        (array(shape, BF16),) * parts,
        [vmem()] * parts,
        after=after,
    )


def fold_last_kernel(own1, got1, own2, got2, keep1, send1, keep2, send2):
    height = own2.shape[1]
    each = height + TAIL
    body = own1.shape[0] - TAIL
    coded = encode(decode(own1[body:]) + decode(got1[body:]))
    half = own2.shape[0] // 2
    for i in range(2 * half):
        out, first = (keep1, send1)[i // half], i % half * each
        at = pl.ds(i * height, height)
        out[first : first + height] = (own1[at].astype(F32) + got1[at].astype(F32)).astype(BF16)
        out[first + height : first + each] = coded
        total = own2[i].astype(F32) + got2[i].astype(F32)
        (keep2, send2)[i // half][i % half] = total.astype(BF16)


def fold_last(own1, got1, own2, got2, after=()):
    count, height, width = own2.shape
    first = array((count // 2 * (height + TAIL), width), BF16)
    second = array((count // 2, height, width), BF16)
    return run(
        fold_last_kernel,
        "fold_last",
        (own1, got1, own2, got2),
        [vmem()] * 4,
        (first, first, second, second),
        [vmem()] * 4,
        after=after,
    )


def fold_z_kernel(own1, got1, own2, got2, keep, send):
    height = own2.shape[1]
    each = height + TAIL
    for i, out in enumerate((keep, send)):
        at = pl.ds(i * each, height)
        out[:height] = (own1[at].astype(F32) + got1[at].astype(F32)).astype(BF16)
        at = pl.ds(i * each + height, TAIL)
        out[height:each] = encode(decode(own1[at]) + decode(got1[at]))
        out[each:] = (own2[i].astype(F32) + got2[i].astype(F32)).astype(BF16)


def fold_z(own1, got1, own2, got2, after=()):
    _, height, width = own2.shape
    out = array((2 * height + TAIL, width), BF16)
    return run(
        fold_z_kernel,
        "fold_z",
        (own1, got1, own2, got2),
        [vmem()] * 4,
        (out, out),
        [vmem()] * 2,
        after=after,
    )


def fold_add_kernel(own1, got1, own2, got2, out1, out2):
    for own, got, out in ((own1, got1, out1), (own2, got2, out2)):
        out[...] = (own[...].astype(F32) + got[...].astype(F32)).astype(BF16)


def fold_add(own1, got1, own2, got2, after=()):
    out = array(own1.shape, BF16)
    return run(
        fold_add_kernel,
        "fold_add",
        (own1, got1, own2, got2),
        [vmem()] * 4,
        (out, out),
        [vmem()] * 2,
        after=after,
    )


def fold_feed_kernel(first1, own1, got1, first2, own2, got2, keep1, send1, keep2, send2):
    width = own1.shape[2]
    half = keep1.shape[0]
    for first, own, got, outs in (
        (first1, own1, got1, (keep1, send1)),
        (first2, own2, got2, (keep2, send2)),
    ):
        for i, out in enumerate(outs):
            at = pl.ds(i * half, half)
            out[:, :, :width] = first[at]
            out[:, :, width:] = (own[at].astype(F32) + got[at].astype(F32)).astype(BF16)


def fold_feed(first1, own1, got1, first2, own2, got2, after=()):
    count, height, width = own1.shape
    out = array((count // 2, height, 2 * width), BF16)
    return run(
        fold_feed_kernel,
        "fold_feed",
        (first1, own1, got1, first2, own2, got2),
        [vmem()] * 6,
        (out,) * 4,
        [vmem()] * 4,
        after=after,
    )


def fold_sides_kernel(own1, got1, own2, got2, keep, send):
    width = own1.shape[2]
    half = keep.shape[0]
    for side, (own, got) in enumerate(((own1, got1), (own2, got2))):
        for i, out in enumerate((keep, send)):
            at = pl.ds(i * half, half)
            total = own[at].astype(F32) + got[at].astype(F32)
            out[:, :, side * width : (side + 1) * width] = total.astype(BF16)


def fold_sides(own1, got1, own2, got2, after=()):
    count, height, width = own1.shape
    out = array((count // 2, height, 2 * width), BF16)
    return run(
        fold_sides_kernel,
        "fold_sides",
        (own1, got1, own2, got2),
        [vmem()] * 4,
        (out, out),
        [vmem()] * 2,
        after=after,
    )


BY_Z = (0, 4, 2, 6)
Y_MAJOR = BY_Z + tuple(z + 1 for z in BY_Z)
OWN = tuple((0, j) for j in Y_MAJOR)
OTHER = tuple((1, j) for j in Y_MAJOR)
CHIP_NEAR = tuple((chip, z) for chip in range(2) for z in BY_Z)
CHIP_FAR = tuple((chip, z + 1) for chip in range(2) for z in BY_Z)


def split_kernel(info, first, second, mine, theirs, sems):
    copies = []
    for i, values in enumerate((first, second)):
        copies += [
            pltpu.make_async_copy(values.at[info[1]], mine.at[i], sems.at[2 * i]),
            pltpu.make_async_copy(values.at[1 - info[1]], theirs.at[i], sems.at[2 * i + 1]),
        ]
    for copy in copies:
        copy.start()
    for copy in copies:
        copy.wait()


def split(info, first, second, after=()):
    out = array((2,) + first.shape[1:], first.dtype)
    return run(
        split_kernel,
        "split",
        (info, *in_hbm((first, second))),
        [smem()] + [anywhere()] * 2,
        (out, out),
        [anywhere()] * 2,
        [pltpu.SemaphoreType.DMA((4,))],
        after=after,
    )


def merge_kernel(info, own, got, core_own, core_got, out, sems):
    core = info[2]
    copies = []
    for half, (mine, other) in enumerate(((own, core_own), (got, core_got))):
        copies += [
            pltpu.make_async_copy(mine.at[0], out.at[half, core], sems.at[2 * half]),
            pltpu.make_async_copy(other.at[0], out.at[half, 1 - core], sems.at[2 * half + 1]),
        ]
    for copy in copies:
        copy.start()
    for copy in copies:
        copy.wait()


def merge(info, quarters, after=()):
    _, quarter, width = quarters[0].shape
    out = run(
        merge_kernel,
        "merge",
        (info, *quarters),
        [smem()] + [anywhere()] * 4,
        (array((2, 2, quarter, width), quarters[0].dtype),),
        [anywhere()],
        [pltpu.SemaphoreType.DMA((4,))],
        after=after,
    )[0]
    return out.reshape(4 * quarter, width)


def halves_kernel(info, rows_ref, own, send, sems):
    quarter = own.shape[0]
    copies = []
    for half, out in enumerate((own, send)):
        at = pl.multiple_of((2 * half + info[2]) * quarter, quarter)
        copies.append(pltpu.make_async_copy(rows_ref.at[pl.ds(at, quarter)], out, sems.at[half]))
    for copy in copies:
        copy.start()
    for copy in copies:
        copy.wait()


def halves(info, values, after=()):
    seq, width = values.shape
    out = array((seq // 4, width), values.dtype)
    return run(
        halves_kernel,
        "halves",
        (info, values),
        [smem(), anywhere()],
        (out, out),
        [anywhere()] * 2,
        [pltpu.SemaphoreType.DMA((2,))],
        after=after,
    )


def slots_kernel(info, own, other, out, sems):
    copies = [
        pltpu.make_async_copy(own, out.at[info[1]], sems.at[0]),
        pltpu.make_async_copy(other, out.at[1 - info[1]], sems.at[1]),
    ]
    for copy in copies:
        copy.start()
    for copy in copies:
        copy.wait()


def slots_of(info, own, other, after=()):
    return run(
        slots_kernel,
        "slots",
        (info, own, other),
        [smem()] + [anywhere()] * 2,
        (array((2,) + own.shape, own.dtype),),
        [anywhere()],
        [pltpu.SemaphoreType.DMA((2,))],
        after=after,
    )[0]


def tokens_add_kernel(count, mine, *rest):
    got, own, sends = rest[:count], rest[count], rest[count + 1 :]
    per = count // 2
    height = got[0].shape[0]
    for k, part in enumerate(got):
        at = k % per * height
        total = mine[k // per, pl.ds(at, height)] + part[...].astype(F32)
        if k < per:
            own[pl.ds(at, height)] = total
        else:
            each = sends[0].shape[0]
            for first in range(0, height, each):
                sends[(at + first) // each][...] = total[first : first + each].astype(BF16)


def tokens_add(mine, got, after=()):
    _, quarter, width = mine.shape
    send = array((quarter // 2, width), BF16)
    return run(
        functools.partial(tokens_add_kernel, len(got)),
        "tokens_add",
        (mine, *got),
        [vmem()] * (1 + len(got)),
        (array((quarter, width), F32), send, send),
        [vmem()] * 3,
        after=after,
    )


def tokens_out_kernel(info, own, *rest):
    *got, out = rest
    out[info[1]] = own[...]
    height = got[0].shape[0]
    for k, part in enumerate(got):
        out[1 - info[1], pl.ds(k * height, height), :] = part[...].astype(F32)


def tokens_out(info, own, got, after=()):
    return run(
        tokens_out_kernel,
        "tokens_out",
        (info, own, *got),
        [smem()] + [vmem()] * (1 + len(got)),
        (array((2,) + own.shape, F32),),
        [vmem()],
        after=after,
    )[0]


def feed_out_kernel(own, got, up, down):
    half = up.shape[1] // 2
    for i in range(4):
        at = pl.ds(i * half, half)
        total = own[0, :, at].astype(F32) + got[0, :, at].astype(F32)
        out = (down, up)[i % 2]
        out[:, pl.ds(i // 2 * half, half)] = total


def feed_out(own, got, after=()):
    _, height, width = own.shape
    out = array((height, width // 2), F32)
    return run(
        feed_out_kernel,
        "feed_out",
        (own, got),
        [vmem()] * 2,
        (out, out),
        [vmem()] * 2,
        after=after,
    )


def attend_out_kernel(a, b, query, key, value, out, gain1, bias1, gain2, bias2):
    height = query.shape[0]

    def both(first, last):
        return a[first:last].astype(F32) + b[first:last].astype(F32)

    one = both(0, height)
    two = both(height + TAIL, 2 * height + TAIL)
    at = pl.ds(height, TAIL)
    sums = decode(a[at]) + decode(b[at])
    for i, ref in enumerate((query, key, value)):
        ref[...] = jnp.concatenate(
            [two[:, 2 * i * HD : 2 * (i + 1) * HD], one[:, (3 + i) * HD : (4 + i) * HD]], axis=1
        )
    out[...] = jnp.transpose(one[:, : 3 * HD])
    for i, ref in enumerate((gain1, bias1, gain2, bias2)):
        ref[...] = jnp.concatenate([sums[i], sums[4 + i]], axis=0)


def attend_out(pieces, height, after=()):
    cols = pieces[0].shape[1]
    span = cols // 2
    return run(
        attend_out_kernel,
        "attend_out",
        tuple(pieces),
        [vmem()] * 2,
        (array((height, span), F32),) * 3
        + (array((span, height), F32),)
        + (array((2 * cols,), F32),) * 4,
        [vmem()] * 8,
        after=after,
    )


def local(
    tokens,
    w_query,
    w_key,
    w_value,
    w_out,
    w_up,
    w_down,
    gain_attn,
    bias_attn,
    gain_ffn,
    bias_ffn,
    lengths,
    random_blocks,
    cotangent,
):
    CALLS.clear()
    size = lax.axis_size("dp")
    rank = lax.axis_index("mp")
    me = lax.axis_index("dp")
    x, core = rank // 2, rank % 2
    _, quarter, features = tokens.shape
    seq = 4 * quarter
    height = w_query.shape[0]
    span = w_query.shape[1]
    heads = span // HD
    nblocks = seq // BLOCK
    fast = size == 8 and height % 16 == 0

    length = lax.dynamic_index_in_dim(lengths, x, 0, keepdims=False)
    shift = x * (seq // 2)
    info = jnp.stack([me, x, core, length, shift]).astype(jnp.int32)
    units = w_up.shape[1]

    blocks = (jnp.arange(nblocks) + x * (nblocks // 2)) % nblocks
    near_blocks = jnp.abs(blocks[:, None] - blocks[None, :]) <= 1
    edge = (blocks == 0) | (blocks == nblocks - 1)
    fixed = near_blocks | edge[:, None] | edge[None, :]

    def table(shard):
        chosen = lax.dynamic_slice_in_dim(random_blocks, shard * heads, heads, 0)
        chosen = jnp.roll(chosen, -x * (nblocks // 2), axis=1)
        hit = jnp.any(chosen[:, None, :, :] == blocks[None, :, None, None], axis=3)
        bias = jnp.where(fixed.T[None] | hit, 0.0, NEGATIVE)
        return jnp.concatenate(
            [
                jnp.zeros((heads, nblocks, HD), F32),
                bias,
                jnp.full((heads, nblocks, 3), -1.0, F32),
                jnp.zeros((heads, nblocks, HD - 3 - nblocks), F32),
            ],
            axis=2,
        )

    mask_own, mask_other = table(rank), table(rank ^ 2)
    mask_ends = jnp.concatenate([mask_own[2:], mask_other[2:]], axis=0)
    g_one, b_one = gain_attn[None], bias_attn[None]
    g_two, b_two = gain_ffn[None], bias_ffn[None]

    if fast:
        flat = (tuple((0, j) for j in Y_MAJOR),)
        piece = pack(w_query, w_key, w_value, w_out)
        got = flip_dp(piece, 4)
        own_rows, their_rows = split(info, tokens, cotangent, (piece,))
        got_rows = flip_chip(their_rows)
        feed_piece = beside(w_up, w_down.T, (their_rows,))
        feed_got = flip_dp(feed_piece, 4)
        (two_attn,) = join([piece, got], after=(feed_piece,))
        got = flip_dp(two_attn, 2)
        z_pair, z_single = join_sides([two_attn, got])
        y_pair, x_single = flip_dp(z_pair, 1), flip_chip(z_single)
        two_up, two_down = join_sides([feed_piece, feed_got], (z_pair,))
        got_up, got_down = flip_dp(two_up, 2), flip_dp(two_down, 2)
        own_pair, near_single = join([z_pair, y_pair], [z_single, x_single], after=(two_up,))
        other_pair, far_single = flip_chip(own_pair), flip_dp(near_single, 1)
        quarters = (own_rows, got_rows, flip_core(own_rows), flip_core(got_rows))
        tok = merge(info, quarters, (near_single,))
        pair_w = ((own_pair, other_pair), (OWN, OTHER))
        single_w = ((near_single, far_single), (CHIP_NEAR, CHIP_FAR))
        own01 = attend(info, tok, ((own_pair,), flat), True, mask_own[:2])
        z_up, z_down = join([two_up, got_up], [two_down, got_down], after=(own01[0],))
        y_up, x_down = flip_dp(z_up, 1), flip_chip(z_down)
        other01 = attend(info, tok, ((other_pair,), flat), True, mask_other[:2], (z_up,))
        ends = attend(info, tok, single_w, False, mask_ends, (other01[0],))
        own_up, near_down = join([z_up, y_up], [z_down, x_down], after=(ends[0],))
        other_up, far_down = flip_chip(own_up), flip_dp(near_down, 1)
        up = ((own_up, other_up), (OWN, OTHER))
        down = ((near_down, far_down), (CHIP_NEAR, CHIP_FAR))
        order = (near_down,)
    else:
        flat = (((0, 0),),)
        two = (((0, 0),), ((1, 0),))

        def plain(piece):
            own = lax.all_gather(piece, "dp", axis=0, tiled=True)[None]
            return own, flip_chip(own)

        own_rows, their_rows = split(info, tokens, cotangent)
        got_rows = flip_chip(their_rows)
        quarters = (own_rows, got_rows, flip_core(own_rows), flip_core(got_rows))
        tok = merge(info, quarters)
        thirds = [w_out.T] + [w[:, 2 * HD :] for w in (w_query, w_key, w_value)]
        pair_w = (
            plain(jnp.concatenate([w[:, : 2 * HD] for w in (w_query, w_key, w_value)], axis=1)),
            two,
        )
        single_w = (plain(jnp.concatenate(thirds, axis=1)), two)
        own_up, other_up = plain(w_up)
        own01 = attend(info, tok, ((pair_w[0][0],), flat), True, mask_own[:2])
        other01 = attend(info, tok, ((pair_w[0][1],), flat), True, mask_other[:2])
        ends = attend(info, tok, single_w, False, mask_ends)
        order = ()
    contexts = (own01[3], other01[3], ends[3])
    attn_part = project(info, contexts, single_w, features, order)
    if not fast:
        up = ((own_up, other_up), two)
        down = (plain(w_down.T), two)
    z_one, hn = norm_one(tok, attn_part, flip_cores(attn_part), g_one, b_one)

    act1, slope1 = feed_up(info, hn, ((own_up,), flat), units)
    act2, slope2 = feed_up(info, hn, ((other_up,), flat), units, (act1,))
    mixed = feed_down(info, act1, act2, down, features)
    out, dz_two, dzb_two, sums_two = norm_two(
        info, hn, mixed, flip_cores(mixed), quarters, g_two, b_two
    )

    if fast:
        places = (OWN, OTHER, CHIP_NEAR, CHIP_FAR)
        att_slots = tuple((0, j) for j in Y_MAJOR)
    else:
        places = (((0, 0),), ((1, 0),)) * 2
        att_slots = ((0, 0),)

    keep_d1, send_d1, keep_d2, send_d2 = feed_grad(info, dzb_two, act1, act2, places)
    du1, du2, *back = feed_back(info, dzb_two, slope1, slope2, up, down, (keep_d1,))
    back_got = flip_cores(back)
    keep_u1, send_u1, keep_u2, send_u2 = feed_grad(info, hn, du1, du2, places)
    order = (keep_u1,)
    if fast:
        sum_d1, sum_d2 = fold_add(
            keep_d1, flip_chip(send_d1), keep_d2, flip_dp(send_d2, 1), order
        )
        order = (sum_d1,)
    dz_one, dzb_one, sums_one = norm_one_back(z_one, dz_two, back, back_got, g_one, order)
    d_ends = attend_back(info, dzb_one, single_w, None, ends)
    order = (d_ends,)
    if fast:
        keep_f1, send_f1, keep_f2, send_f2 = fold_feed(
            sum_d1, keep_u1, flip_chip(send_u1), sum_d2, keep_u2, flip_dp(send_u2, 1), order
        )
        got_f1, got_f2 = flip_dp(send_f1, 1), flip_chip(send_f2)
        order = (keep_f1,)
    keep_s, send_s = single_grad(
        info, tok, d_ends, dzb_one, contexts, sums_one, sums_two, places[2:], order
    )
    d_other = attend_back(info, dzb_one, single_w, 1, other01, (keep_s,))
    grad_b = pair_grad(info, tok, d_other, att_slots)
    order = (grad_b,)
    if fast:
        got_s = flip_dp(send_s, 1)
        got_b = flip_chip(grad_b)
        keep_f, send_f = fold_sides(keep_f1, got_f1, keep_f2, got_f2, order)
        got_f = flip_dp(send_f, 2)
        order = (keep_f,)
    own_out, send_out = halves(info, out, order)
    got_out = flip_chip(send_out)
    d_own = attend_back(info, dzb_one, single_w, 0, own01, (own_out,))
    mine, *sent = input_back(info, d_own, d_other, d_ends, dz_one, pair_w, single_w)
    order = (mine,)
    if fast:
        keep_s, send_s = fold(keep_s, got_s, 2, TAIL, order)
        got_s = flip_chip(send_s)
        order = (keep_s,)
    grad_a = pair_grad(info, tok, d_own, att_slots, order)
    order = (grad_a,)
    if fast:
        keep_a, send_a = fold(grad_a, got_b, 2, 0, order)
        got_a = flip_dp(send_a, 1)
        keep_f, send_f = fold(keep_f, got_f, 2, 0, (keep_a,))
        got_f = flip_dp(send_f, 4)
        order = (keep_f,)
    own_tok, *send_tok = tokens_add(mine, flip_cores(sent), order)
    got_tok = [flip_chip(v) for v in send_tok]
    output = slots_of(info, own_out, got_out, (own_tok,))
    if fast:
        keep_s, send_s, keep_a, send_a = fold_last(keep_s, got_s, keep_a, got_a, (own_tok,))
        got_s, got_a = flip_dp(send_s, 2), flip_dp(send_a, 2)
        grad_up, grad_down = feed_out(keep_f, got_f, (output,))
        keep_a, send_a = fold_z(keep_s, got_s, keep_a, got_a)
        grads = attend_out((keep_a, flip_dp(send_a, 4)), height, (grad_up,))
        sums = grads[4:]
    else:

        def plain_sum(own, other):
            total = own.astype(F32) + flip_chip(other).astype(F32)
            return lax.psum_scatter(total, "dp", scatter_dimension=0, tiled=True)

        def plain_wide(keep1, send1, keep2, send2):
            return jnp.concatenate([plain_sum(keep1[0], send1[0]), plain_sum(keep2[0], send2[0])], axis=1)

        grad_down = plain_wide(keep_d1, send_d1, keep_d2, send_d2)
        grad_up = plain_wide(keep_u1, send_u1, keep_u2, send_u2)
        grad_single = plain_sum(keep_s[:features], send_s[:features])
        grad_pair = plain_sum(grad_a[0], grad_b[0])
        grads = [
            jnp.concatenate(
                [
                    grad_pair[:, 2 * i * HD : 2 * (i + 1) * HD],
                    grad_single[:, (3 + i) * HD : (4 + i) * HD],
                ],
                axis=1,
            )
            for i in range(3)
        ] + [grad_single[:, : 3 * HD].T]
        sums = decode(keep_s[features:])
        sums = lax.psum(sums + flip_chip(sums), "dp")
        sums = [jnp.concatenate([sums[i], sums[4 + i]]) for i in range(4)]
    grad_tokens = tokens_out(info, own_tok, got_tok)

    return (
        output,
        grad_tokens,
        *grads[:4],
        grad_up,
        grad_down.T,
        *sums,
    )


def solution(mesh):
    return jax.shard_map(
        local,
        mesh=mesh,
        in_specs=(
            P("dp", "mp", None),
            P("dp", "mp"),
            P("dp", "mp"),
            P("dp", "mp"),
            P("mp", "dp"),
            P("dp", "mp"),
            P("mp", "dp"),
            P(),
            P(),
            P(),
            P(),
            P("dp"),
            P(),
            P("dp", "mp", None),
        ),
        out_specs=(
            P("dp", "mp", None),
            P("dp", "mp", None),
            P("dp", "mp"),
            P("dp", "mp"),
            P("dp", "mp"),
            P("mp", "dp"),
            P("dp", "mp"),
            P("mp", "dp"),
            P(),
            P(),
            P(),
            P(),
        ),
        check_vma=False,
    )
```

```python
import functools

import jax
import jax.numpy as jnp
from jax import lax
from jax.experimental import pallas as pl
from jax.experimental.pallas import tpu as pltpu
from jax.sharding import PartitionSpec as P

HD = 64
BLOCK = 64
LANES = 128
TILE = 256
SENT = 256
EPSILON = 1e-12
TAIL = 32
TOKEN = (8, 128)
ROOM = {
    "attend": 24,
    "attend_back": 28,
    "project": 16,
    "input_back": 24,
    "norm_one": 16,
    "norm_two": 24,
    "norm_one_back": 24,
    "feed_up": 20,
    "feed_down": 24,
    "feed_back": 40,
    "feed_grad": 28,
    "pair_grad": 16,
    "single_grad": 28,
    "join": 1,
    "join_sides": 1,
    "beside": 1,
    "pack": 2,
    "split": 4,
    "merge": 1,
    "fold": 6,
    "fold_add": 8,
    "fold_feed": 10,
    "fold_sides": 8,
    "fold_last": 6,
    "fold_z": 4,
    "halves": 1,
    "slots": 1,
    "tokens_add": 8,
    "tokens_out": 8,
    "feed_out": 6,
    "attend_out": 6,
}
SCALE = 0.125
LOG2E = 1.4426950408889634
LN2 = 0.6931471805599453
NEGATIVE = -1e30
F32 = jnp.float32
BF16 = jnp.bfloat16

CORE_SWAP = [(0, 1), (1, 0), (2, 3), (3, 2)]
CHIP_SWAP = [(0, 2), (2, 0), (1, 3), (3, 1)]


def nn(a, b):
    return lax.dot_general(a, b, (((1,), (0,)), ((), ())), preferred_element_type=F32)


def nt(a, b):
    return lax.dot_general(a, b, (((1,), (1,)), ((), ())), preferred_element_type=F32)


def tn(a, b):
    return lax.dot_general(a, b, (((0,), (0,)), ((), ())), preferred_element_type=F32)


def vmem():
    return pl.BlockSpec(memory_space=pltpu.VMEM)


def smem():
    return pl.BlockSpec(memory_space=pltpu.SMEM)


def anywhere():
    return pl.BlockSpec(memory_space=pl.ANY)


def in_hbm(values):
    return tuple(pltpu.with_memory_space_constraint(v, pltpu.HBM) for v in values)


def rows(width):
    return pl.BlockSpec((TILE, width), lambda i: (i, 0))


def whole(shape):
    return pl.BlockSpec(shape, lambda i: (0,) * len(shape))


def array(shape, dtype):
    return jax.ShapeDtypeStruct(shape, dtype)


ORDER = []


def run(kernel, name, args, specs, outs, out_specs, scratch=(), *, grid=()):
    given, made = len(args), len(outs)
    extra = tuple(ORDER)

    def body(*refs):
        ins, rest = refs[:given], refs[given + len(extra) :]
        rest[made][...] = jnp.zeros(TOKEN, F32)
        kernel(*ins, *rest[:made], *rest[made + 1 :])

    token_spec = whole(TOKEN) if grid else vmem()
    results = pl.pallas_call(
        body,
        grid=grid,
        out_shape=tuple(outs) + (array(TOKEN, F32),),
        in_specs=list(specs) + [anywhere()] * len(extra),
        out_specs=tuple(out_specs) + (token_spec,),
        scratch_shapes=list(scratch),
        compiler_params=pltpu.CompilerParams(vmem_limit_bytes=ROOM[name] * 2**20),
        cost_estimate=pl.CostEstimate(flops=1, bytes_accessed=0, transcendentals=0),
        name=name,
    )(*args, *extra)
    ORDER[:] = [results[-1]]
    return results[:-1]


def put_rows(parts, value):
    height = parts[0].shape[0]
    tile = value.shape[0]
    i = pl.program_id(0)
    for k, part in enumerate(parts):
        if height <= tile:
            per = tile // height

            @pl.when(i == k // per)
            def _(k=k, part=part):
                at = k % per * height
                part[...] = value[at : at + height]

        else:
            per = height // tile

            @pl.when(i // per == k)
            def _(part=part):
                part[pl.ds(pl.multiple_of(i % per * tile, tile), tile), :] = value


def get_sum(parts, more, count):
    height = parts[0].shape[0]
    tile = len(parts) * height // count
    i = pl.program_id(0)
    total = None
    if height <= tile:
        per = tile // height
        for k in range(count):
            pieces = [
                a[...].astype(F32) + b[...].astype(F32)
                for a, b in zip(parts[k * per : (k + 1) * per], more[k * per : (k + 1) * per])
            ]
            value = pieces[0] if per == 1 else jnp.concatenate(pieces, axis=0)
            total = value if k == 0 else jnp.where(i == k, value, total)
    else:
        per = height // tile
        at = pl.ds(pl.multiple_of(i % per * tile, tile), tile)
        for k, (a, b) in enumerate(zip(parts, more)):
            value = a[at, :].astype(F32) + b[at, :].astype(F32)
            total = value if k == 0 else jnp.where(i // per == k, value, total)
    return total


def far(shape, dtype):
    return pltpu.HBM(shape, dtype)


def tiles(seq, width, height):
    parts = (array((height, width), BF16),) * (seq // height)
    return parts, [whole((height, width))] * len(parts)


def place(me, refs, slots, dst_ref, first=0, last=None, only=None, to=0):
    for ref, of in zip(refs, slots):
        height, width = ref.shape[1], ref.shape[2]
        end = width if last is None else last
        for e, (chip, j) in enumerate(of):
            if only is not None and chip != only:
                continue
            at = 0 if height == dst_ref.shape[0] else pl.multiple_of((me ^ j) * height, height)
            at_column = to + (0 if only is not None else chip * (end - first))
            dst_ref[pl.ds(at, height), pl.ds(at_column, end - first)] = ref[e, :, first:end]


def pick(me, fulls, out_ref, slots, first):
    _, height, width = out_ref.shape
    for e, (chip, j) in enumerate(slots):
        full = fulls[chip]
        at = 0 if height == full.shape[0] else pl.multiple_of((me ^ j) * height, height)
        out_ref[e] = full[pl.ds(at, height), pl.ds(first, width)].astype(BF16)


def attend_kernel(slots, columns, only, places, info, tok, mask, *rest):
    refs, (qa, ka, va, ctx, wfull) = rest[: len(slots)], rest[len(slots) :]
    seq = tok.shape[0]
    place(info[0], refs, slots, wfull, *columns, only)
    lane = lax.broadcasted_iota(jnp.int32, (TILE, LANES), 1)
    row0 = lax.broadcasted_iota(jnp.int32, (TILE, LANES), 0)
    for t in range(seq // TILE):
        at = pl.ds(t * TILE, TILE)
        row = row0 + t * TILE
        made = nn(tok[at, :], wfull[...])
        onehot = jnp.where(lane - HD == row // BLOCK, 1.0, 0.0)[:, HD:]
        position = row + info[4]
        position = jnp.where(position >= seq, position - seq, position)
        dead = (position >= info[3]) & (lane >= HD) & (lane < HD + 16)
        for h, (q_at, k_at, v_at) in enumerate(places):
            q = made[:, q_at : q_at + HD] * (SCALE * LOG2E)
            k = made[:, k_at : k_at + HD]
            v = made[:, v_at : v_at + HD]
            qa[h, at, :] = jnp.concatenate([q, onehot], axis=1).astype(BF16)
            per = TILE // BLOCK
            table = jnp.concatenate(
                [
                    jnp.broadcast_to(mask[h, t * per + b : t * per + b + 1, :], (BLOCK, LANES))
                    for b in range(per)
                ],
                axis=0,
            )
            table = jnp.where(dead, NEGATIVE, table)
            ka[h, at, :] = jnp.concatenate([k, table[:, HD:]], axis=1).astype(BF16)
            va[h, at, :] = jnp.concatenate([v, jnp.full((TILE, HD), -1.0, F32)], axis=1).astype(BF16)
    for t in range(seq // TILE):
        at = pl.ds(t * TILE, TILE)
        pieces = []
        for h in range(len(places)):
            q = qa[h, at, :]
            s = nt(q, ka[h])
            top = jnp.max(s, axis=1, keepdims=True)
            p = jnp.exp2(s - top).astype(BF16)
            got = nn(p, va[h])
            total = -got[:, HD:]
            pieces.append(got[:, :HD] / total)
            log = top + jnp.log2(-got)
            hi = log.astype(BF16).astype(F32)
            mid = (log - hi).astype(BF16).astype(F32)
            low = log - hi - mid
            new = jnp.where(
                lane == HD + 16,
                hi,
                jnp.where(lane == HD + 17, mid, jnp.where(lane == HD + 18, low, q.astype(F32))),
            )
            qa[h, at, :] = new.astype(BF16)
        ctx[at, :] = jnp.concatenate(pieces, axis=1).astype(BF16)


PAIR = ((0, 2 * HD, 4 * HD), (HD, 3 * HD, 5 * HD))
SINGLES = ((HD, 2 * HD, 3 * HD), (5 * HD, 6 * HD, 7 * HD))


def attend(info, tok, gathered, pair, mask):
    arrays, slots = gathered
    seq, width = tok.shape
    aug = far((2, seq, LANES), BF16)
    columns, only, cols = ((0, 6 * HD), 0, 6 * HD) if pair else ((2 * HD, 6 * HD), None, 8 * HD)
    return run(
        functools.partial(attend_kernel, slots, columns, only, PAIR if pair else SINGLES),
        "attend",
        (info, tok, mask) + arrays,
        [smem()] + [vmem()] * (2 + len(arrays)),
        (aug, aug, aug, array((seq, LANES), BF16)),
        [vmem()] * 4,
        [pltpu.VMEM((width, cols), BF16)],
    )


def place_out(me, refs, slots, pairs, ends):
    place(me, refs, slots, pairs, 0, 2 * HD)
    place(me, refs, slots, ends, 2 * HD, 4 * HD)
    both = ends[...]
    ends[:, :LANES] = jnp.concatenate([both[:, :HD], both[:, LANES : LANES + HD]], axis=1)


def project_kernel(slots, info, own, other, ends, *rest):
    refs, parts, (w1, w2) = rest[: len(slots)], rest[len(slots) : -2], rest[-2:]

    @pl.when(pl.program_id(0) == 0)
    def _():
        place_out(info[0], refs, slots, w1, w2)

    both = jnp.concatenate([own[...], other[...]], axis=1)
    put_rows(parts, (nt(both, w1[...]) + nt(ends[...], w2[:, :LANES])).astype(BF16))


def project(info, contexts, gathered, width):
    arrays, slots = gathered
    seq = contexts[0].shape[0]
    return run(
        functools.partial(project_kernel, slots),
        "project",
        (info,) + contexts + arrays,
        [smem()] + [rows(LANES)] * 3 + [whole(a.shape) for a in arrays],
        *tiles(seq, width, 2 * TILE),
        [pltpu.VMEM((width, 2 * LANES), BF16)] * 2,
        grid=(seq // TILE,),
    )


def attend_back_kernel(slots, chip, info, dz, qa_in, ka_in, va_in, ctx, *rest):
    refs, (dqkv, pairs, ends, da, parts, qa, ka, va, sems) = rest[: len(slots)], rest[len(slots) :]
    fetches = [
        [
            pltpu.make_async_copy(a.at[h], b.at[h], sems.at[3 * h + i])
            for i, (a, b) in enumerate(((ka_in, ka), (qa_in, qa), (va_in, va)))
        ]
        for h in range(2)
    ]
    for fetch in fetches:
        for copy in fetch:
            copy.start()
    seq = dz.shape[0]
    heads = qa.shape[0]
    if chip is None:
        place_out(info[0], refs, slots, pairs, ends)
        wfull = ends.at[:, pl.ds(0, LANES)]
    else:
        place(info[0], refs, slots, pairs, 0, 2 * HD, chip)
        wfull = pairs.at[:, pl.ds(0, LANES)]
    lane = lax.broadcasted_iota(jnp.int32, (TILE, LANES), 1)
    for t in range(seq // TILE):
        at = pl.ds(t * TILE, TILE)
        dctx = nn(dz[at, :], wfull[...]).astype(BF16).astype(F32)
        both = dctx * ctx[at, :].astype(F32)
        for h in range(heads):
            inner = jnp.sum(both[:, h * HD : (h + 1) * HD], axis=1, keepdims=True)
            hi = inner.astype(BF16).astype(F32)
            mid = (inner - hi).astype(BF16).astype(F32)
            low = inner - hi - mid
            one = jnp.concatenate(
                [dctx[:, h * HD : (h + 1) * HD], jnp.zeros((TILE, HD), F32)], axis=1
            )
            one = jnp.where(lane == HD, hi, one)
            one = jnp.where(lane == HD + 1, mid, one)
            one = jnp.where(lane == HD + 2, low, one)
            da[h, at, :] = one.astype(BF16)
    for h in range(heads):
        for copy in fetches[h]:
            copy.wait()
        k_turned = jnp.transpose(ka[h].astype(F32)).astype(BF16)
        dq_turned = None
        for t in range(seq // TILE):
            at = pl.ds(t * TILE, TILE)
            p = jnp.exp2(nt(ka[h, at, :], qa[h]))
            ds = (p * nt(va[h, at, :], da[h])).astype(BF16)
            parts[2 * heads + h, at, :] = nn(p.astype(BF16), da[h])
            parts[heads + h, at, :] = nn(ds, qa[h]) * LN2
            more = nn(k_turned[:, t * TILE : (t + 1) * TILE], ds)
            dq_turned = more if dq_turned is None else dq_turned + more
        parts[h] = jnp.transpose(dq_turned) * SCALE
    for t in range(seq // TILE):
        at = pl.ds(t * TILE, TILE)
        pieces = [parts[i, at, :][:, :HD] for i in range(3 * heads)]
        if chip is None:
            blank = jnp.zeros((TILE, HD), F32)
            pieces = [blank] + pieces[::2] + [blank] + pieces[1::2]
        dqkv[at, :] = jnp.concatenate(pieces, axis=1).astype(BF16)


def attend_back(info, dz, gathered, chip, saved):
    arrays, slots = gathered
    qa, ka, va, ctx = saved
    seq, width = dz.shape
    cols = 8 * HD if chip is None else 6 * HD
    return run(
        functools.partial(attend_back_kernel, slots, chip),
        "attend_back",
        (info, dz, *in_hbm((qa, ka, va)), ctx) + arrays,
        [smem(), vmem()] + [anywhere()] * 3 + [vmem()] * (1 + len(arrays)),
        (array((seq, cols), BF16),),
        [vmem()],
        [
            pltpu.VMEM((width, 2 * LANES), BF16),
            pltpu.VMEM((width, 2 * LANES), BF16),
            pltpu.VMEM((2, seq, LANES), BF16),
            pltpu.VMEM((6, seq, LANES), F32),
            *[pltpu.VMEM((2, seq, LANES), BF16)] * 3,
            pltpu.SemaphoreType.DMA((6,)),
        ],
    )[0]


def input_back_kernel(slots1, slots2, info, own, other, ends, dz, *rest):
    n1, n2 = len(slots1), len(slots2)
    refs1, refs2, (mine, *sent, w1, w2) = rest[:n1], rest[n1 : n1 + n2], rest[n1 + n2 :]
    i = pl.program_id(0)

    @pl.when(i == 0)
    def _():
        place(info[0], refs1, slots1, w1)
        place(info[0], refs2, slots2, w2, 2 * HD, 6 * HD)

    pairs = jnp.concatenate([own[...], other[...]], axis=1)
    back = nt(pairs, w1[...]) + nt(ends[...], w2[...])

    @pl.when(i % 2 == info[2])
    def _():
        mine[i // 2] = back + dz[...]

    per = len(sent) // 2
    height = sent[0].shape[0]
    for k, part in enumerate(sent):

        @pl.when((i % 2 != info[2]) & (i // 2 == k // per))
        def _(k=k, part=part):
            part[...] = back[k % per * height : (k % per + 1) * height].astype(BF16)


def input_back(info, own, other, ends, dz, gathered1, gathered2):
    seq, width = dz.shape
    arrays = gathered1[0] + gathered2[0]
    halves = (seq // TILE // 2, TILE, width)
    grads = (own, other, ends, dz)
    return run(
        functools.partial(input_back_kernel, gathered1[1], gathered2[1]),
        "input_back",
        (info,) + grads + arrays,
        [smem()] + [rows(g.shape[1]) for g in grads] + [whole(a.shape) for a in arrays],
        (array(halves, F32),) + (array((SENT, width), BF16),) * (seq // 2 // SENT),
        [whole(halves)] + [whole((SENT, width))] * (seq // 2 // SENT),
        [pltpu.VMEM((width, 12 * HD), BF16), pltpu.VMEM((width, 8 * HD), BF16)],
        grid=(seq // TILE,),
    )


def center(z):
    mean = jnp.mean(z, axis=1, keepdims=True)
    moved = z - mean
    spread = jnp.mean(moved * moved, axis=1, keepdims=True)
    scale = lax.rsqrt(spread + EPSILON)
    return moved * scale, scale


def norm_back(n, scale, gy, gain):
    dn = gy * gain
    return scale * (
        dn - jnp.mean(dn, axis=1, keepdims=True) - n * jnp.mean(dn * n, axis=1, keepdims=True)
    )


def add_sums(gy, n, sums):
    i = pl.program_id(0)

    @pl.when(i == 0)
    def _():
        sums[...] = jnp.zeros_like(sums)

    sums[0:1, :] += jnp.sum(gy * n, axis=0, keepdims=True)
    sums[1:2, :] += jnp.sum(gy, axis=0, keepdims=True)


def norm_one_kernel(tok, gain, bias, *rest):
    *parts, z, hn = rest
    count = len(parts) // 2
    value = tok[...].astype(F32) + get_sum(parts[:count], parts[count:], count * parts[0].shape[0] // TILE)
    z[...] = value
    n, _ = center(value)
    hn[...] = (n * gain[...] + bias[...]).astype(BF16)


def norm_one(tok, p0, p1, gain, bias):
    seq, width = tok.shape
    return run(
        norm_one_kernel,
        "norm_one",
        (tok, gain, bias, *p0, *p1),
        [rows(width)] + [whole((1, width))] * 2 + [whole(p.shape) for p in (*p0, *p1)],
        (far((seq, width), F32), array((seq, width), BF16)),
        (rows(width), rows(width)),
        grid=(seq // TILE,),
    )


def norm_two_kernel(info, hn, own, got, core_own, core_got, gain, bias, *rest):
    *parts, out, dz, dzb, sums = rest
    count = len(parts) // 2
    value = hn[...].astype(F32) + get_sum(parts[:count], parts[count:], count * parts[0].shape[0] // TILE)
    n, scale = center(value)
    out[...] = (n * gain[...] + bias[...]).astype(BF16)
    row = lax.broadcasted_iota(jnp.int32, value.shape, 0) + pl.program_id(0) * TILE
    seq = pl.num_programs(0) * TILE
    position = row + info[4]
    position = jnp.where(position >= seq, position - seq, position)
    i = pl.program_id(0)
    mine = i % 2 == info[2]
    cot = jnp.where(
        i < 2,
        jnp.where(mine, own[0].astype(F32), core_own[0].astype(F32)),
        jnp.where(mine, got[0].astype(F32), core_got[0].astype(F32)),
    )
    gy = jnp.where(position < info[3], cot, 0.0)
    grad = norm_back(n, scale, gy, gain[...])
    dz[...] = grad
    dzb[...] = grad.astype(BF16)
    add_sums(gy, n, sums)


def norm_two(info, hn, m0, m1, cot, gain, bias):
    seq, width = hn.shape
    return run(
        norm_two_kernel,
        "norm_two",
        (info, hn, *cot, gain, bias, *m0, *m1),
        [smem(), rows(width)]
        + [pl.BlockSpec((1,) + c.shape[1:], lambda i: (1, 0, 0)) for c in cot]
        + [whole((1, width))] * 2
        + [whole(p.shape) for p in (*m0, *m1)],
        (
            array((seq, width), BF16),
            far((seq, width), F32),
            array((seq, width), BF16),
            array((2, width), F32),
        ),
        (rows(width), rows(width), rows(width), whole((2, width))),
        grid=(seq // TILE,),
    )


def norm_one_back_kernel(z, dz2, gain, *rest):
    *parts, dz, dzb, sums = rest
    count = len(parts) // 2
    n, scale = center(z[...])
    gy = dz2[...] + get_sum(parts[:count], parts[count:], count * parts[0].shape[0] // TILE)
    grad = norm_back(n, scale, gy, gain[...])
    dz[...] = grad
    dzb[...] = grad.astype(BF16)
    add_sums(gy, n, sums)


def norm_one_back(z, dz2, p0, p1, gain):
    seq, width = z.shape
    return run(
        norm_one_back_kernel,
        "norm_one_back",
        (z, dz2, gain, *p0, *p1),
        [rows(width)] * 2 + [whole((1, width))] + [whole(p.shape) for p in (*p0, *p1)],
        (array((seq, width), F32), array((seq, width), BF16), array((2, width), F32)),
        (rows(width), rows(width), whole((2, width))),
        grid=(seq // TILE,),
    )


def gelu_pair(u):
    phi = 0.5 + 0.5 * lax.erf(u * 0.7071067811865476)
    return u * phi, phi + u * (jnp.exp(-0.5 * u * u) * 0.3989422804014327)


def feed_up_kernel(slots, info, hn, *rest):
    refs, (active, slope, wfull) = rest[: len(slots)], rest[len(slots) :]

    @pl.when(pl.program_id(0) == 0)
    def _():
        place(info[0], refs, slots, wfull)

    a, g = gelu_pair(nn(hn[...], wfull[...]))
    active[...] = a.astype(BF16)
    slope[...] = g.astype(BF16)


def feed_up(info, hn, gathered, units):
    arrays, slots = gathered
    seq, width = hn.shape
    return run(
        functools.partial(feed_up_kernel, slots),
        "feed_up",
        (info, hn) + arrays,
        [smem(), rows(width)] + [whole(a.shape) for a in arrays],
        (array((seq, units), BF16), array((seq, units), BF16)),
        (rows(units), rows(units)),
        [pltpu.VMEM((width, units), BF16)],
        grid=(seq // TILE,),
    )


def feed_down_kernel(slots, info, act1, act2, *rest):
    refs, parts, wfull = rest[: len(slots)], rest[len(slots) : -1], rest[-1]

    @pl.when(pl.program_id(0) == 0)
    def _():
        place(info[0], refs, slots, wfull)

    both = jnp.concatenate([act1[...], act2[...]], axis=1)
    put_rows(parts, nt(both, wfull[...]).astype(BF16))


def feed_down(info, act1, act2, gathered, width):
    seq, units = act1.shape
    arrays, slots = gathered
    return run(
        functools.partial(feed_down_kernel, slots),
        "feed_down",
        (info, act1, act2) + arrays,
        [smem(), rows(units), rows(units)] + [whole(a.shape) for a in arrays],
        *tiles(seq, width, seq),
        [pltpu.VMEM((width, 2 * units), BF16)],
        grid=(seq // TILE,),
    )


def feed_back_kernel(slots_up, slots_down, info, dzb, slope1, slope2, *rest):
    n1, n2 = len(slots_up), len(slots_down)
    ups, downs, (du1, du2, *parts, up, down) = rest[:n1], rest[n1 : n1 + n2], rest[n1 + n2 :]

    @pl.when(pl.program_id(0) == 0)
    def _():
        place(info[0], ups, slots_up, up)
        place(info[0], downs, slots_down, down)

    units = du1.shape[1]
    out = None
    for i, (slope, du) in enumerate(((slope1, du1), (slope2, du2))):
        at = pl.ds(i * units, units)
        grad = (nn(dzb[...], down[:, at]) * slope[...].astype(F32)).astype(BF16)
        du[...] = grad
        more = nt(grad, up[:, at])
        out = more if out is None else out + more
    put_rows(parts, out.astype(BF16))


def feed_back(info, dzb, slope1, slope2, up, down):
    seq, width = dzb.shape
    units = slope1.shape[1]
    arrays = up[0] + down[0]
    parts, part_specs = tiles(seq, width, TILE)
    return run(
        functools.partial(feed_back_kernel, up[1], down[1]),
        "feed_back",
        (info, dzb, slope1, slope2) + arrays,
        [smem(), rows(width), rows(units), rows(units)] + [whole(a.shape) for a in arrays],
        (array((seq, units), BF16),) * 2 + parts,
        [rows(units)] * 2 + part_specs,
        [pltpu.VMEM((width, 2 * units), BF16)] * 2,
        grid=(seq // TILE,),
    )


def feed_grad_kernel(places, info, a, d1, d2, *rest):
    outs, fulls = rest[:4], rest[4:]
    half = outs[0].shape[2]
    fulls[0][...] = tn(a[...], d1[...])
    fulls[1][...] = tn(a[...], d2[...])
    for i, out in enumerate(outs):
        pick(info[0], fulls, out, places[i], (i // 2) * half)


def feed_grad(info, a, d1, d2, places):
    seq, width = a.shape
    units = d1.shape[1]
    count = len(places[0])
    out = array((count, width // count, units // 2), BF16)
    return run(
        functools.partial(feed_grad_kernel, places),
        "feed_grad",
        (info, a, d1, d2),
        [smem()] + [vmem()] * 3,
        (out,) * 4,
        [vmem()] * 4,
        [pltpu.VMEM((width, units), F32)] * 2,
    )


def pair_grad_kernel(slots, info, tok, d, out, full):
    full[...] = tn(tok[...], d[...])
    pick(info[0], (full,), out, slots, 0)


def pair_grad(info, tok, d, slots):
    seq, width = tok.shape
    cols = d.shape[1]
    return run(
        functools.partial(pair_grad_kernel, slots),
        "pair_grad",
        (info, tok, d),
        [smem()] + [vmem()] * 2,
        (array((len(slots), width // len(slots), cols), BF16),),
        [vmem()],
        [pltpu.VMEM((width, cols), F32)],
    )[0]


def encode(sums):
    hi = sums.astype(BF16).astype(F32)
    mid = (sums - hi).astype(BF16).astype(F32)
    low = sums - hi - mid
    return jnp.concatenate([hi, mid, low, jnp.zeros_like(low)], axis=0).astype(BF16)


def decode(coded):
    values = coded.astype(F32)
    n = values.shape[0] // 4
    return values[:n] + values[n : 2 * n] + values[2 * n : 3 * n]


def single_grad_kernel(places, info, tok, d, dz, own, other, ends, sums_one, sums_two, keep, send, full):
    mine = tn(tok[...], d[...])
    third = tn(dz[...], ends[...])
    blank = jnp.zeros((third.shape[0], HD), F32)
    width = full.shape[2]
    both = jnp.concatenate([sums_one[...], sums_two[...]], axis=0)
    both = encode(jnp.concatenate([both[:, :width], both[:, width:]], axis=0))
    for chip, ctx in enumerate((own, other)):
        full[chip, :, :LANES] = tn(dz[...], ctx[...])
        at = chip * 4 * HD
        o_third = jnp.concatenate([third[:, chip * HD : (chip + 1) * HD], blank], axis=1)
        full[chip, :, LANES : 2 * LANES] = o_third + mine[:, at : at + LANES]
        full[chip, :, 2 * LANES :] = mine[:, at + LANES : at + 2 * LANES]
    for out, slots in zip((keep, send), places):
        count = len(slots)
        height = full.shape[1] // count
        for e, (chip, j) in enumerate(slots):
            at = 0 if count == 1 else pl.multiple_of((info[0] ^ j) * height, height)
            out[pl.ds(e * height, height), :] = full[chip, pl.ds(at, height), :].astype(BF16)
        out[pl.ds(count * height, TAIL), :] = both


def single_grad(info, tok, d, dz, contexts, sums_one, sums_two, places):
    seq, width = tok.shape
    cols = 6 * HD
    out = array((width + TAIL, cols), BF16)
    return run(
        functools.partial(single_grad_kernel, places),
        "single_grad",
        (info, tok, d, dz, *contexts, sums_one, sums_two),
        [smem()] + [vmem()] * 8,
        (out, out),
        [vmem()] * 2,
        [pltpu.VMEM((2, width, cols), F32)],
    )


def across(values, axis, pairs):
    return lax.ppermute(values, axis, pairs)


def flip_chip(values):
    return across(values, "mp", CHIP_SWAP)


def flip_core(values):
    return across(values, "mp", CORE_SWAP)


def flip_cores(parts):
    return [flip_core(p) for p in parts]


def flip_dp(values, distance):
    size = lax.axis_size("dp")
    return across(values, "dp", [(i, i ^ distance) for i in range(size)])


def join_kernel(groups, *refs):
    count = sum(groups)
    parts, outs, sems = refs[:count], refs[count:-1], refs[-1]
    copies = []
    for out, number in zip(outs, groups):
        first = 0
        for part in parts[len(copies) : len(copies) + number]:
            to = out.at[pl.ds(first, part.shape[0])]
            copies.append(pltpu.make_async_copy(part, to, sems.at[len(copies)]))
            first += part.shape[0]
    for copy in copies:
        copy.start()
    for copy in copies:
        copy.wait()


def join(*groups):
    parts = sum((tuple(g) for g in groups), ())
    outs = [array((sum(p.shape[0] for p in g),) + g[0].shape[1:], g[0].dtype) for g in groups]
    return run(
        functools.partial(join_kernel, tuple(len(g) for g in groups)),
        "join",
        parts,
        [anywhere()] * len(parts),
        outs,
        [anywhere()] * len(outs),
        [pltpu.SemaphoreType.DMA((len(parts),))],
    )


def pack_kernel(w_query, w_key, w_value, w_out, out, rows_in, out_in, sems):
    copies = [
        pltpu.make_async_copy(w, rows_in.at[i], sems.at[i])
        for i, w in enumerate((w_query, w_key, w_value))
    ]
    copies.append(pltpu.make_async_copy(w_out, out_in, sems.at[3]))
    for copy in copies:
        copy.start()
    for copy in copies:
        copy.wait()
    for i in range(3):
        out[0, :, 2 * i * HD : 2 * (i + 1) * HD] = rows_in[i, :, : 2 * HD]
    parts = [jnp.transpose(out_in[...].astype(F32))]
    parts += [rows_in[i, :, 2 * HD :].astype(F32) for i in range(3)]
    out[0, :, 6 * HD :] = jnp.concatenate(parts, axis=1).astype(BF16)


def pack(w_query, w_key, w_value, w_out):
    height, span = w_query.shape
    return run(
        pack_kernel,
        "pack",
        in_hbm((w_query, w_key, w_value, w_out)),
        [anywhere()] * 4,
        (array((1, height, 4 * span), BF16),),
        [vmem()],
        [
            pltpu.VMEM((3, height, span), BF16),
            pltpu.VMEM(w_out.shape, BF16),
            pltpu.SemaphoreType.DMA((4,)),
        ],
    )[0]


def beside_kernel(first, second, out, sems):
    width = first.shape[1]
    copies = [
        pltpu.make_async_copy(ref, out.at[0, :, pl.ds(i * width, width)], sems.at[i])
        for i, ref in enumerate((first, second))
    ]
    for copy in copies:
        copy.start()
    for copy in copies:
        copy.wait()


def beside(first, second):
    height, width = first.shape
    return run(
        beside_kernel,
        "beside",
        in_hbm((first, second)),
        [anywhere()] * 2,
        (array((1, height, 2 * width), BF16),),
        [anywhere()],
        [pltpu.SemaphoreType.DMA((2,))],
    )[0]


def join_sides_kernel(count, *refs):
    parts, outs, sems = refs[:count], refs[count : count + 2], refs[count + 2]
    width = outs[0].shape[2]
    copies = []
    each = parts[0].shape[0]
    for i, part in enumerate(parts):
        for side, out in enumerate(outs):
            copies.append(
                pltpu.make_async_copy(
                    part.at[:, :, pl.ds(side * width, width)],
                    out.at[pl.ds(i * each, each)],
                    sems.at[2 * i + side],
                )
            )
    for copy in copies:
        copy.start()
    for copy in copies:
        copy.wait()


def join_sides(parts):
    count = len(parts)
    each, height, width = parts[0].shape
    out = array((count * each, height, width // 2), BF16)
    return run(
        functools.partial(join_sides_kernel, count),
        "join_sides",
        tuple(parts),
        [anywhere()] * count,
        (out, out),
        [anywhere()] * 2,
        [pltpu.SemaphoreType.DMA((2 * count,))],
    )


def fold_kernel(tail, own, got, *outs):
    body = own.shape[0] - tail
    each = body // len(outs)
    for i, out in enumerate(outs):
        at = pl.ds(i * each, each)
        total = (own[at].astype(F32) + got[at].astype(F32)).astype(BF16)
        if tail:
            out[:each] = total
        else:
            out[...] = total
    if tail:
        coded = encode(decode(own[body:]) + decode(got[body:]))
        for out in outs:
            out[each:] = coded


def fold(own, got, parts, tail=0):
    shape = ((own.shape[0] - tail) // parts + tail,) + own.shape[1:]
    return run(
        functools.partial(fold_kernel, tail),
        "fold",
        (own, got),
        [vmem()] * 2,
        (array(shape, BF16),) * parts,
        [vmem()] * parts,
    )


def fold_last_kernel(own1, got1, own2, got2, keep1, send1, keep2, send2):
    height = own2.shape[1]
    each = height + TAIL
    body = own1.shape[0] - TAIL
    coded = encode(decode(own1[body:]) + decode(got1[body:]))
    half = own2.shape[0] // 2
    for i in range(2 * half):
        out, first = (keep1, send1)[i // half], i % half * each
        at = pl.ds(i * height, height)
        out[first : first + height] = (own1[at].astype(F32) + got1[at].astype(F32)).astype(BF16)
        out[first + height : first + each] = coded
        total = own2[i].astype(F32) + got2[i].astype(F32)
        (keep2, send2)[i // half][i % half] = total.astype(BF16)


def fold_last(own1, got1, own2, got2):
    count, height, width = own2.shape
    first = array((count // 2 * (height + TAIL), width), BF16)
    second = array((count // 2, height, width), BF16)
    return run(
        fold_last_kernel,
        "fold_last",
        (own1, got1, own2, got2),
        [vmem()] * 4,
        (first, first, second, second),
        [vmem()] * 4,
    )


def fold_z_kernel(own1, got1, own2, got2, keep, send):
    height = own2.shape[1]
    each = height + TAIL
    for i, out in enumerate((keep, send)):
        at = pl.ds(i * each, height)
        out[:height] = (own1[at].astype(F32) + got1[at].astype(F32)).astype(BF16)
        at = pl.ds(i * each + height, TAIL)
        out[height:each] = encode(decode(own1[at]) + decode(got1[at]))
        out[each:] = (own2[i].astype(F32) + got2[i].astype(F32)).astype(BF16)


def fold_z(own1, got1, own2, got2):
    _, height, width = own2.shape
    out = array((2 * height + TAIL, width), BF16)
    return run(
        fold_z_kernel,
        "fold_z",
        (own1, got1, own2, got2),
        [vmem()] * 4,
        (out, out),
        [vmem()] * 2,
    )


def fold_add_kernel(own1, got1, own2, got2, out1, out2):
    for own, got, out in ((own1, got1, out1), (own2, got2, out2)):
        out[...] = (own[...].astype(F32) + got[...].astype(F32)).astype(BF16)


def fold_add(own1, got1, own2, got2):
    out = array(own1.shape, BF16)
    return run(
        fold_add_kernel,
        "fold_add",
        (own1, got1, own2, got2),
        [vmem()] * 4,
        (out, out),
        [vmem()] * 2,
    )


def fold_feed_kernel(first1, own1, got1, first2, own2, got2, keep1, send1, keep2, send2):
    width = own1.shape[2]
    half = keep1.shape[0]
    for first, own, got, outs in (
        (first1, own1, got1, (keep1, send1)),
        (first2, own2, got2, (keep2, send2)),
    ):
        for i, out in enumerate(outs):
            at = pl.ds(i * half, half)
            out[:, :, :width] = first[at]
            out[:, :, width:] = (own[at].astype(F32) + got[at].astype(F32)).astype(BF16)


def fold_feed(first1, own1, got1, first2, own2, got2):
    count, height, width = own1.shape
    out = array((count // 2, height, 2 * width), BF16)
    return run(
        fold_feed_kernel,
        "fold_feed",
        (first1, own1, got1, first2, own2, got2),
        [vmem()] * 6,
        (out,) * 4,
        [vmem()] * 4,
    )


def fold_sides_kernel(own1, got1, own2, got2, keep, send):
    width = own1.shape[2]
    half = keep.shape[0]
    for side, (own, got) in enumerate(((own1, got1), (own2, got2))):
        for i, out in enumerate((keep, send)):
            at = pl.ds(i * half, half)
            total = own[at].astype(F32) + got[at].astype(F32)
            out[:, :, side * width : (side + 1) * width] = total.astype(BF16)


def fold_sides(own1, got1, own2, got2):
    count, height, width = own1.shape
    out = array((count // 2, height, 2 * width), BF16)
    return run(
        fold_sides_kernel,
        "fold_sides",
        (own1, got1, own2, got2),
        [vmem()] * 4,
        (out, out),
        [vmem()] * 2,
    )


BY_Z = (0, 4, 2, 6)
Y_MAJOR = BY_Z + tuple(z + 1 for z in BY_Z)
OWN = tuple((0, j) for j in Y_MAJOR)
OTHER = tuple((1, j) for j in Y_MAJOR)
CHIP_NEAR = tuple((chip, z) for chip in range(2) for z in BY_Z)
CHIP_FAR = tuple((chip, z + 1) for chip in range(2) for z in BY_Z)


def split_kernel(info, first, second, mine, theirs, sems):
    copies = []
    for i, values in enumerate((first, second)):
        copies += [
            pltpu.make_async_copy(values.at[info[1]], mine.at[i], sems.at[2 * i]),
            pltpu.make_async_copy(values.at[1 - info[1]], theirs.at[i], sems.at[2 * i + 1]),
        ]
    for copy in copies:
        copy.start()
    for copy in copies:
        copy.wait()


def split(info, first, second):
    out = array((2,) + first.shape[1:], first.dtype)
    return run(
        split_kernel,
        "split",
        (info, *in_hbm((first, second))),
        [smem()] + [anywhere()] * 2,
        (out, out),
        [vmem()] * 2,
        [pltpu.SemaphoreType.DMA((4,))],
    )


def merge_kernel(info, own, got, core_own, core_got, out, sems):
    core = info[2]
    copies = []
    for half, (mine, other) in enumerate(((own, core_own), (got, core_got))):
        copies += [
            pltpu.make_async_copy(mine.at[0], out.at[half, core], sems.at[2 * half]),
            pltpu.make_async_copy(other.at[0], out.at[half, 1 - core], sems.at[2 * half + 1]),
        ]
    for copy in copies:
        copy.start()
    for copy in copies:
        copy.wait()


def merge(info, quarters):
    _, quarter, width = quarters[0].shape
    out = run(
        merge_kernel,
        "merge",
        (info, *quarters),
        [smem()] + [anywhere()] * 4,
        (array((2, 2, quarter, width), quarters[0].dtype),),
        [anywhere()],
        [pltpu.SemaphoreType.DMA((4,))],
    )[0]
    return out.reshape(4 * quarter, width)


def halves_kernel(info, rows_ref, own, send, sems):
    quarter = own.shape[0]
    copies = []
    for half, out in enumerate((own, send)):
        at = pl.multiple_of((2 * half + info[2]) * quarter, quarter)
        copies.append(pltpu.make_async_copy(rows_ref.at[pl.ds(at, quarter)], out, sems.at[half]))
    for copy in copies:
        copy.start()
    for copy in copies:
        copy.wait()


def halves(info, values):
    seq, width = values.shape
    out = array((seq // 4, width), values.dtype)
    return run(
        halves_kernel,
        "halves",
        (info, values),
        [smem(), anywhere()],
        (out, out),
        [anywhere()] * 2,
        [pltpu.SemaphoreType.DMA((2,))],
    )


def slots_kernel(info, own, other, out, sems):
    copies = [
        pltpu.make_async_copy(own, out.at[info[1]], sems.at[0]),
        pltpu.make_async_copy(other, out.at[1 - info[1]], sems.at[1]),
    ]
    for copy in copies:
        copy.start()
    for copy in copies:
        copy.wait()


def slots_of(info, own, other):
    return run(
        slots_kernel,
        "slots",
        (info, own, other),
        [smem()] + [anywhere()] * 2,
        (array((2,) + own.shape, own.dtype),),
        [anywhere()],
        [pltpu.SemaphoreType.DMA((2,))],
    )[0]


def tokens_add_kernel(count, mine, *rest):
    got, own, sends = rest[:count], rest[count], rest[count + 1 :]
    per = count // 2
    height = got[0].shape[0]
    for k, part in enumerate(got):
        at = k % per * height
        total = mine[k // per, pl.ds(at, height)] + part[...].astype(F32)
        if k < per:
            own[pl.ds(at, height)] = total
        else:
            each = sends[0].shape[0]
            for first in range(0, height, each):
                sends[(at + first) // each][...] = total[first : first + each].astype(BF16)


def tokens_add(mine, got):
    _, quarter, width = mine.shape
    send = array((quarter // 2, width), BF16)
    return run(
        functools.partial(tokens_add_kernel, len(got)),
        "tokens_add",
        (mine, *got),
        [vmem()] * (1 + len(got)),
        (array((quarter, width), F32), send, send),
        [vmem()] * 3,
    )


def tokens_out_kernel(info, own, *rest):
    *got, out = rest
    out[info[1]] = own[...]
    height = got[0].shape[0]
    for k, part in enumerate(got):
        out[1 - info[1], pl.ds(k * height, height), :] = part[...].astype(F32)


def tokens_out(info, own, got):
    return run(
        tokens_out_kernel,
        "tokens_out",
        (info, own, *got),
        [smem()] + [vmem()] * (1 + len(got)),
        (array((2,) + own.shape, F32),),
        [vmem()],
    )[0]


def feed_out_kernel(own, got, up, down):
    half = up.shape[1] // 2
    for i in range(4):
        at = pl.ds(i * half, half)
        total = own[0, :, at].astype(F32) + got[0, :, at].astype(F32)
        out = (down, up)[i % 2]
        out[:, pl.ds(i // 2 * half, half)] = total


def feed_out(own, got):
    _, height, width = own.shape
    out = array((height, width // 2), F32)
    return run(
        feed_out_kernel,
        "feed_out",
        (own, got),
        [vmem()] * 2,
        (out, out),
        [vmem()] * 2,
    )


def attend_out_kernel(a, b, query, key, value, out, gain1, bias1, gain2, bias2):
    height = query.shape[0]

    def both(first, last):
        return a[first:last].astype(F32) + b[first:last].astype(F32)

    one = both(0, height)
    two = both(height + TAIL, 2 * height + TAIL)
    at = pl.ds(height, TAIL)
    sums = decode(a[at]) + decode(b[at])
    for i, ref in enumerate((query, key, value)):
        ref[...] = jnp.concatenate(
            [two[:, 2 * i * HD : 2 * (i + 1) * HD], one[:, (3 + i) * HD : (4 + i) * HD]], axis=1
        )
    out[...] = jnp.transpose(one[:, : 3 * HD])
    for i, ref in enumerate((gain1, bias1, gain2, bias2)):
        ref[...] = jnp.concatenate([sums[i], sums[4 + i]], axis=0)


def attend_out(pieces, height):
    cols = pieces[0].shape[1]
    span = cols // 2
    return run(
        attend_out_kernel,
        "attend_out",
        tuple(pieces),
        [vmem()] * 2,
        (array((height, span), F32),) * 3
        + (array((span, height), F32),)
        + (array((2 * cols,), F32),) * 4,
        [vmem()] * 8,
    )


def local(
    tokens,
    w_query,
    w_key,
    w_value,
    w_out,
    w_up,
    w_down,
    gain_attn,
    bias_attn,
    gain_ffn,
    bias_ffn,
    lengths,
    random_blocks,
    cotangent,
):
    ORDER.clear()
    size = lax.axis_size("dp")
    rank = lax.axis_index("mp")
    me = lax.axis_index("dp")
    x, core = rank // 2, rank % 2
    _, quarter, features = tokens.shape
    seq = 4 * quarter
    height = w_query.shape[0]
    span = w_query.shape[1]
    heads = span // HD
    nblocks = seq // BLOCK
    fast = size == 8 and height % 16 == 0

    length = lax.dynamic_index_in_dim(lengths, x, 0, keepdims=False)
    shift = x * (seq // 2)
    info = jnp.stack([me, x, core, length, shift]).astype(jnp.int32)
    units = w_up.shape[1]

    blocks = (jnp.arange(nblocks) + x * (nblocks // 2)) % nblocks
    near_blocks = jnp.abs(blocks[:, None] - blocks[None, :]) <= 1
    edge = (blocks == 0) | (blocks == nblocks - 1)
    fixed = near_blocks | edge[:, None] | edge[None, :]

    def table(shard):
        chosen = lax.dynamic_slice_in_dim(random_blocks, shard * heads, heads, 0)
        chosen = jnp.roll(chosen, -x * (nblocks // 2), axis=1)
        hit = jnp.any(chosen[:, None, :, :] == blocks[None, :, None, None], axis=3)
        bias = jnp.where(fixed.T[None] | hit, 0.0, NEGATIVE)
        return jnp.concatenate(
            [
                jnp.zeros((heads, nblocks, HD), F32),
                bias,
                jnp.full((heads, nblocks, 3), -1.0, F32),
                jnp.zeros((heads, nblocks, HD - 3 - nblocks), F32),
            ],
            axis=2,
        )

    mask_own, mask_other = table(rank), table(rank ^ 2)
    mask_ends = jnp.concatenate([mask_own[2:], mask_other[2:]], axis=0)
    g_one, b_one = gain_attn[None], bias_attn[None]
    g_two, b_two = gain_ffn[None], bias_ffn[None]

    if fast:
        flat = (tuple((0, j) for j in Y_MAJOR),)
        piece = pack(w_query, w_key, w_value, w_out)
        got = flip_dp(piece, 4)
        own_rows, their_rows = split(info, tokens, cotangent)
        got_rows = flip_chip(their_rows)
        feed_piece = beside(w_up, w_down.T)
        feed_got = flip_dp(feed_piece, 4)
        (two_attn,) = join([piece, got])
        got = flip_dp(two_attn, 2)
        z_pair, z_single = join_sides([two_attn, got])
        y_pair, x_single = flip_dp(z_pair, 1), flip_chip(z_single)
        two_up, two_down = join_sides([feed_piece, feed_got])
        got_up, got_down = flip_dp(two_up, 2), flip_dp(two_down, 2)
        own_pair, near_single = join([z_pair, y_pair], [z_single, x_single])
        other_pair, far_single = flip_chip(own_pair), flip_dp(near_single, 1)
        quarters = (own_rows, got_rows, flip_core(own_rows), flip_core(got_rows))
        tok = merge(info, quarters)
        pair_w = ((own_pair, other_pair), (OWN, OTHER))
        single_w = ((near_single, far_single), (CHIP_NEAR, CHIP_FAR))
        own01 = attend(info, tok, ((own_pair,), flat), True, mask_own[:2])
        z_up, z_down = join([two_up, got_up], [two_down, got_down])
        y_up, x_down = flip_dp(z_up, 1), flip_chip(z_down)
        other01 = attend(info, tok, ((other_pair,), flat), True, mask_other[:2])
        ends = attend(info, tok, single_w, False, mask_ends)
        own_up, near_down = join([z_up, y_up], [z_down, x_down])
        other_up, far_down = flip_chip(own_up), flip_dp(near_down, 1)
        up = ((own_up, other_up), (OWN, OTHER))
        down = ((near_down, far_down), (CHIP_NEAR, CHIP_FAR))
    else:
        flat = (((0, 0),),)
        two = (((0, 0),), ((1, 0),))

        def plain(piece):
            own = lax.all_gather(piece, "dp", axis=0, tiled=True)[None]
            return own, flip_chip(own)

        own_rows, their_rows = split(info, tokens, cotangent)
        got_rows = flip_chip(their_rows)
        quarters = (own_rows, got_rows, flip_core(own_rows), flip_core(got_rows))
        tok = merge(info, quarters)
        thirds = [w_out.T] + [w[:, 2 * HD :] for w in (w_query, w_key, w_value)]
        pair_w = (
            plain(jnp.concatenate([w[:, : 2 * HD] for w in (w_query, w_key, w_value)], axis=1)),
            two,
        )
        single_w = (plain(jnp.concatenate(thirds, axis=1)), two)
        own_up, other_up = plain(w_up)
        own01 = attend(info, tok, ((pair_w[0][0],), flat), True, mask_own[:2])
        other01 = attend(info, tok, ((pair_w[0][1],), flat), True, mask_other[:2])
        ends = attend(info, tok, single_w, False, mask_ends)
    contexts = (own01[3], other01[3], ends[3])
    attn_part = project(info, contexts, single_w, features)
    if not fast:
        up = ((own_up, other_up), two)
        down = (plain(w_down.T), two)
    z_one, hn = norm_one(tok, attn_part, flip_cores(attn_part), g_one, b_one)

    act1, slope1 = feed_up(info, hn, ((own_up,), flat), units)
    act2, slope2 = feed_up(info, hn, ((other_up,), flat), units)
    mixed = feed_down(info, act1, act2, down, features)
    out, dz_two, dzb_two, sums_two = norm_two(
        info, hn, mixed, flip_cores(mixed), quarters, g_two, b_two
    )

    if fast:
        places = (OWN, OTHER, CHIP_NEAR, CHIP_FAR)
        att_slots = tuple((0, j) for j in Y_MAJOR)
    else:
        places = (((0, 0),), ((1, 0),)) * 2
        att_slots = ((0, 0),)

    keep_d1, send_d1, keep_d2, send_d2 = feed_grad(info, dzb_two, act1, act2, places)
    du1, du2, *back = feed_back(info, dzb_two, slope1, slope2, up, down)
    back_got = flip_cores(back)
    keep_u1, send_u1, keep_u2, send_u2 = feed_grad(info, hn, du1, du2, places)
    if fast:
        sum_d1, sum_d2 = fold_add(
            keep_d1, flip_chip(send_d1), keep_d2, flip_dp(send_d2, 1)
        )
    dz_one, dzb_one, sums_one = norm_one_back(z_one, dz_two, back, back_got, g_one)
    d_ends = attend_back(info, dzb_one, single_w, None, ends)
    if fast:
        keep_f1, send_f1, keep_f2, send_f2 = fold_feed(
            sum_d1, keep_u1, flip_chip(send_u1), sum_d2, keep_u2, flip_dp(send_u2, 1)
        )
        got_f1, got_f2 = flip_dp(send_f1, 1), flip_chip(send_f2)
    keep_s, send_s = single_grad(
        info, tok, d_ends, dzb_one, contexts, sums_one, sums_two, places[2:]
    )
    d_other = attend_back(info, dzb_one, single_w, 1, other01)
    grad_b = pair_grad(info, tok, d_other, att_slots)
    if fast:
        got_s = flip_dp(send_s, 1)
        got_b = flip_chip(grad_b)
        keep_f, send_f = fold_sides(keep_f1, got_f1, keep_f2, got_f2)
        got_f = flip_dp(send_f, 2)
    own_out, send_out = halves(info, out)
    got_out = flip_chip(send_out)
    d_own = attend_back(info, dzb_one, single_w, 0, own01)
    mine, *sent = input_back(info, d_own, d_other, d_ends, dz_one, pair_w, single_w)
    grad_a = pair_grad(info, tok, d_own, att_slots)
    if fast:
        keep_a, send_a = fold(grad_a, got_b, 2, 0)
        got_a = flip_dp(send_a, 1)
    if fast:
        keep_s, send_s = fold(keep_s, got_s, 2, TAIL)
        got_s = flip_chip(send_s)
    if fast:
        keep_f, send_f = fold(keep_f, got_f, 2, 0)
        got_f = flip_dp(send_f, 4)
    own_tok, *send_tok = tokens_add(mine, flip_cores(sent))
    got_tok = [flip_chip(v) for v in send_tok]
    if fast:
        keep_s, send_s, keep_a, send_a = fold_last(keep_s, got_s, keep_a, got_a)
        got_s, got_a = flip_dp(send_s, 2), flip_dp(send_a, 2)
    if fast:
        grad_up, grad_down = feed_out(keep_f, got_f)
    if fast:
        keep_a, send_a = fold_z(keep_s, got_s, keep_a, got_a)
        got_a = flip_dp(send_a, 4)
    grad_tokens = tokens_out(info, own_tok, got_tok)
    output = slots_of(info, own_out, got_out)
    if fast:
        grads = attend_out((keep_a, got_a), height)
        sums = grads[4:]
    else:

        def plain_sum(own, other):
            total = own.astype(F32) + flip_chip(other).astype(F32)
            return lax.psum_scatter(total, "dp", scatter_dimension=0, tiled=True)

        def plain_wide(keep1, send1, keep2, send2):
            return jnp.concatenate([plain_sum(keep1[0], send1[0]), plain_sum(keep2[0], send2[0])], axis=1)

        grad_down = plain_wide(keep_d1, send_d1, keep_d2, send_d2)
        grad_up = plain_wide(keep_u1, send_u1, keep_u2, send_u2)
        grad_single = plain_sum(keep_s[:features], send_s[:features])
        grad_pair = plain_sum(grad_a[0], grad_b[0])
        grads = [
            jnp.concatenate(
                [
                    grad_pair[:, 2 * i * HD : 2 * (i + 1) * HD],
                    grad_single[:, (3 + i) * HD : (4 + i) * HD],
                ],
                axis=1,
            )
            for i in range(3)
        ] + [grad_single[:, : 3 * HD].T]
        sums = decode(keep_s[features:])
        sums = lax.psum(sums + flip_chip(sums), "dp")
        sums = [jnp.concatenate([sums[i], sums[4 + i]]) for i in range(4)]

    return (
        output,
        grad_tokens,
        *grads[:4],
        grad_up,
        grad_down.T,
        *sums,
    )


def solution(mesh):
    return jax.shard_map(
        local,
        mesh=mesh,
        in_specs=(
            P("dp", "mp", None),
            P("dp", "mp"),
            P("dp", "mp"),
            P("dp", "mp"),
            P("mp", "dp"),
            P("dp", "mp"),
            P("mp", "dp"),
            P(),
            P(),
            P(),
            P(),
            P("dp"),
            P(),
            P("dp", "mp", None),
        ),
        out_specs=(
            P("dp", "mp", None),
            P("dp", "mp", None),
            P("dp", "mp"),
            P("dp", "mp"),
            P("dp", "mp"),
            P("mp", "dp"),
            P("dp", "mp"),
            P("mp", "dp"),
            P(),
            P(),
            P(),
            P(),
        ),
        check_vma=False,
    )
```

```python
import functools

import jax
import jax.numpy as jnp
from jax import lax
from jax.experimental import pallas as pl
from jax.experimental.pallas import tpu as pltpu
from jax.sharding import PartitionSpec as P

HD = 64
BLOCK = 64
LANES = 128
TILE = 256
SENT = 256
EPSILON = 1e-12
TAIL = 32
TOKEN = (8, 128)
ROOM = {
    "attend": 24,
    "attend_back": 28,
    "project": 16,
    "input_back": 24,
    "norm_one": 16,
    "norm_two": 24,
    "norm_one_back": 24,
    "feed_up": 20,
    "feed_down": 24,
    "feed_back": 40,
    "feed_grad": 28,
    "pair_grad": 16,
    "single_grad": 28,
    "join": 1,
    "join_sides": 1,
    "beside": 1,
    "pack": 2,
    "split": 4,
    "merge": 1,
    "fold": 6,
    "fold_add": 8,
    "fold_feed": 10,
    "fold_sides": 8,
    "fold_last": 6,
    "fold_z": 4,
    "halves": 1,
    "slots": 1,
    "tokens_add": 8,
    "tokens_out": 8,
    "feed_out": 6,
    "attend_out": 6,
}
SCALE = 0.125
LOG2E = 1.4426950408889634
LN2 = 0.6931471805599453
NEGATIVE = -1e30
F32 = jnp.float32
BF16 = jnp.bfloat16

CORE_SWAP = [(0, 1), (1, 0), (2, 3), (3, 2)]
CHIP_SWAP = [(0, 2), (2, 0), (1, 3), (3, 1)]


def nn(a, b):
    return lax.dot_general(a, b, (((1,), (0,)), ((), ())), preferred_element_type=F32)


def nt(a, b):
    return lax.dot_general(a, b, (((1,), (1,)), ((), ())), preferred_element_type=F32)


def tn(a, b):
    return lax.dot_general(a, b, (((0,), (0,)), ((), ())), preferred_element_type=F32)


def vmem():
    return pl.BlockSpec(memory_space=pltpu.VMEM)


def smem():
    return pl.BlockSpec(memory_space=pltpu.SMEM)


def anywhere():
    return pl.BlockSpec(memory_space=pl.ANY)


def in_hbm(values):
    return tuple(pltpu.with_memory_space_constraint(v, pltpu.HBM) for v in values)


def rows(width):
    return pl.BlockSpec((TILE, width), lambda i: (i, 0))


def whole(shape):
    return pl.BlockSpec(shape, lambda i: (0,) * len(shape))


def array(shape, dtype):
    return jax.ShapeDtypeStruct(shape, dtype)


ORDER = []


def run(kernel, name, args, specs, outs, out_specs, scratch=(), *, grid=()):
    given, made = len(args), len(outs)
    extra = tuple(ORDER)

    def body(*refs):
        ins, rest = refs[:given], refs[given + len(extra) :]
        rest[made][...] = jnp.zeros(TOKEN, F32)
        kernel(*ins, *rest[:made], *rest[made + 1 :])

    token_spec = whole(TOKEN) if grid else vmem()
    results = pl.pallas_call(
        body,
        grid=grid,
        out_shape=tuple(outs) + (array(TOKEN, F32),),
        in_specs=list(specs) + [anywhere()] * len(extra),
        out_specs=tuple(out_specs) + (token_spec,),
        scratch_shapes=list(scratch),
        compiler_params=pltpu.CompilerParams(vmem_limit_bytes=ROOM[name] * 2**20),
        cost_estimate=pl.CostEstimate(flops=1, bytes_accessed=0, transcendentals=0),
        name=name,
    )(*args, *extra)
    ORDER[:] = [results[-1]]
    return results[:-1]


def put_rows(parts, value):
    height = parts[0].shape[0]
    tile = value.shape[0]
    i = pl.program_id(0)
    for k, part in enumerate(parts):
        if height <= tile:
            per = tile // height

            @pl.when(i == k // per)
            def _(k=k, part=part):
                at = k % per * height
                part[...] = value[at : at + height]

        else:
            per = height // tile

            @pl.when(i // per == k)
            def _(part=part):
                part[pl.ds(pl.multiple_of(i % per * tile, tile), tile), :] = value


def get_sum(parts, more, count):
    height = parts[0].shape[0]
    tile = len(parts) * height // count
    i = pl.program_id(0)
    total = None
    if height <= tile:
        per = tile // height
        for k in range(count):
            pieces = [
                a[...].astype(F32) + b[...].astype(F32)
                for a, b in zip(parts[k * per : (k + 1) * per], more[k * per : (k + 1) * per])
            ]
            value = pieces[0] if per == 1 else jnp.concatenate(pieces, axis=0)
            total = value if k == 0 else jnp.where(i == k, value, total)
    else:
        per = height // tile
        at = pl.ds(pl.multiple_of(i % per * tile, tile), tile)
        for k, (a, b) in enumerate(zip(parts, more)):
            value = a[at, :].astype(F32) + b[at, :].astype(F32)
            total = value if k == 0 else jnp.where(i // per == k, value, total)
    return total


def far(shape, dtype):
    return pltpu.HBM(shape, dtype)


def tiles(seq, width, height):
    parts = (array((height, width), BF16),) * (seq // height)
    return parts, [whole((height, width))] * len(parts)


def place(me, refs, slots, dst_ref, first=0, last=None, only=None, to=0):
    for ref, of in zip(refs, slots):
        height, width = ref.shape[1], ref.shape[2]
        end = width if last is None else last
        for e, (chip, j) in enumerate(of):
            if only is not None and chip != only:
                continue
            at = 0 if height == dst_ref.shape[0] else pl.multiple_of((me ^ j) * height, height)
            at_column = to + (0 if only is not None else chip * (end - first))
            dst_ref[pl.ds(at, height), pl.ds(at_column, end - first)] = ref[e, :, first:end]


def pick(me, fulls, out_ref, slots, first):
    _, height, width = out_ref.shape
    for e, (chip, j) in enumerate(slots):
        full = fulls[chip]
        at = 0 if height == full.shape[0] else pl.multiple_of((me ^ j) * height, height)
        out_ref[e] = full[pl.ds(at, height), pl.ds(first, width)].astype(BF16)


def attend_kernel(slots, columns, only, places, info, tok, mask, *rest):
    refs, (qa, ka, va, ctx, wfull) = rest[: len(slots)], rest[len(slots) :]
    seq = tok.shape[0]
    place(info[0], refs, slots, wfull, *columns, only)
    lane = lax.broadcasted_iota(jnp.int32, (TILE, LANES), 1)
    row0 = lax.broadcasted_iota(jnp.int32, (TILE, LANES), 0)
    for t in range(seq // TILE):
        at = pl.ds(t * TILE, TILE)
        row = row0 + t * TILE
        made = nn(tok[at, :], wfull[...])
        onehot = jnp.where(lane - HD == row // BLOCK, 1.0, 0.0)[:, HD:]
        position = row + info[4]
        position = jnp.where(position >= seq, position - seq, position)
        dead = (position >= info[3]) & (lane >= HD) & (lane < HD + 16)
        for h, (q_at, k_at, v_at) in enumerate(places):
            q = made[:, q_at : q_at + HD] * (SCALE * LOG2E)
            k = made[:, k_at : k_at + HD]
            v = made[:, v_at : v_at + HD]
            qa[h, at, :] = jnp.concatenate([q, onehot], axis=1).astype(BF16)
            per = TILE // BLOCK
            table = jnp.concatenate(
                [
                    jnp.broadcast_to(mask[h, t * per + b : t * per + b + 1, :], (BLOCK, LANES))
                    for b in range(per)
                ],
                axis=0,
            )
            table = jnp.where(dead, NEGATIVE, table)
            ka[h, at, :] = jnp.concatenate([k, table[:, HD:]], axis=1).astype(BF16)
            va[h, at, :] = jnp.concatenate([v, jnp.full((TILE, HD), -1.0, F32)], axis=1).astype(BF16)
    for t in range(seq // TILE):
        at = pl.ds(t * TILE, TILE)
        pieces = []
        for h in range(len(places)):
            q = qa[h, at, :]
            s = nt(q, ka[h])
            top = jnp.max(s, axis=1, keepdims=True)
            p = jnp.exp2(s - top).astype(BF16)
            got = nn(p, va[h])
            total = -got[:, HD:]
            pieces.append(got[:, :HD] / total)
            log = top + jnp.log2(-got)
            hi = log.astype(BF16).astype(F32)
            mid = (log - hi).astype(BF16).astype(F32)
            low = log - hi - mid
            new = jnp.where(
                lane == HD + 16,
                hi,
                jnp.where(lane == HD + 17, mid, jnp.where(lane == HD + 18, low, q.astype(F32))),
            )
            qa[h, at, :] = new.astype(BF16)
        ctx[at, :] = jnp.concatenate(pieces, axis=1).astype(BF16)


PAIR = ((0, 2 * HD, 4 * HD), (HD, 3 * HD, 5 * HD))
SINGLES = ((HD, 2 * HD, 3 * HD), (5 * HD, 6 * HD, 7 * HD))


def attend(info, tok, gathered, pair, mask):
    arrays, slots = gathered
    seq, width = tok.shape
    aug = far((2, seq, LANES), BF16)
    columns, only, cols = ((0, 6 * HD), 0, 6 * HD) if pair else ((2 * HD, 6 * HD), None, 8 * HD)
    return run(
        functools.partial(attend_kernel, slots, columns, only, PAIR if pair else SINGLES),
        "attend",
        (info, tok, mask) + arrays,
        [smem()] + [vmem()] * (2 + len(arrays)),
        (aug, aug, aug, array((seq, LANES), BF16)),
        [vmem()] * 4,
        [pltpu.VMEM((width, cols), BF16)],
    )


def place_out(me, refs, slots, pairs, ends):
    place(me, refs, slots, pairs, 0, 2 * HD)
    place(me, refs, slots, ends, 2 * HD, 4 * HD)
    both = ends[...]
    ends[:, :LANES] = jnp.concatenate([both[:, :HD], both[:, LANES : LANES + HD]], axis=1)


def project_kernel(slots, info, own, other, ends, *rest):
    refs, parts, (w1, w2) = rest[: len(slots)], rest[len(slots) : -2], rest[-2:]

    @pl.when(pl.program_id(0) == 0)
    def _():
        place_out(info[0], refs, slots, w1, w2)

    both = jnp.concatenate([own[...], other[...]], axis=1)
    put_rows(parts, (nt(both, w1[...]) + nt(ends[...], w2[:, :LANES])).astype(BF16))


def project(info, contexts, gathered, width):
    arrays, slots = gathered
    seq = contexts[0].shape[0]
    return run(
        functools.partial(project_kernel, slots),
        "project",
        (info,) + contexts + arrays,
        [smem()] + [rows(LANES)] * 3 + [whole(a.shape) for a in arrays],
        *tiles(seq, width, 2 * TILE),
        [pltpu.VMEM((width, 2 * LANES), BF16)] * 2,
        grid=(seq // TILE,),
    )


def attend_back_kernel(slots, chip, info, dz, qa, ka, va, ctx, *rest):
    refs, (dqkv, pairs, ends, da, parts) = rest[: len(slots)], rest[len(slots) :]
    seq = dz.shape[0]
    heads = qa.shape[0]
    if chip is None:
        place_out(info[0], refs, slots, pairs, ends)
        wfull = ends.at[:, pl.ds(0, LANES)]
    else:
        place(info[0], refs, slots, pairs, 0, 2 * HD, chip)
        wfull = pairs.at[:, pl.ds(0, LANES)]
    lane = lax.broadcasted_iota(jnp.int32, (TILE, LANES), 1)
    for t in range(seq // TILE):
        at = pl.ds(t * TILE, TILE)
        dctx = nn(dz[at, :], wfull[...]).astype(BF16).astype(F32)
        both = dctx * ctx[at, :].astype(F32)
        for h in range(heads):
            inner = jnp.sum(both[:, h * HD : (h + 1) * HD], axis=1, keepdims=True)
            hi = inner.astype(BF16).astype(F32)
            mid = (inner - hi).astype(BF16).astype(F32)
            low = inner - hi - mid
            one = jnp.concatenate(
                [dctx[:, h * HD : (h + 1) * HD], jnp.zeros((TILE, HD), F32)], axis=1
            )
            one = jnp.where(lane == HD, hi, one)
            one = jnp.where(lane == HD + 1, mid, one)
            one = jnp.where(lane == HD + 2, low, one)
            da[h, at, :] = one.astype(BF16)
    for h in range(heads):
        k_turned = jnp.transpose(ka[h].astype(F32)).astype(BF16)
        dq_turned = None
        for t in range(seq // TILE):
            at = pl.ds(t * TILE, TILE)
            p = jnp.exp2(nt(ka[h, at, :], qa[h]))
            ds = (p * nt(va[h, at, :], da[h])).astype(BF16)
            parts[2 * heads + h, at, :] = nn(p.astype(BF16), da[h])
            parts[heads + h, at, :] = nn(ds, qa[h]) * LN2
            more = nn(k_turned[:, t * TILE : (t + 1) * TILE], ds)
            dq_turned = more if dq_turned is None else dq_turned + more
        parts[h] = jnp.transpose(dq_turned) * SCALE
    for t in range(seq // TILE):
        at = pl.ds(t * TILE, TILE)
        pieces = [parts[i, at, :][:, :HD] for i in range(3 * heads)]
        if chip is None:
            blank = jnp.zeros((TILE, HD), F32)
            pieces = [blank] + pieces[::2] + [blank] + pieces[1::2]
        dqkv[at, :] = jnp.concatenate(pieces, axis=1).astype(BF16)


def attend_back(info, dz, gathered, chip, saved):
    arrays, slots = gathered
    qa, ka, va, ctx = saved
    seq, width = dz.shape
    cols = 8 * HD if chip is None else 6 * HD
    return run(
        functools.partial(attend_back_kernel, slots, chip),
        "attend_back",
        (info, dz, qa, ka, va, ctx) + arrays,
        [smem()] + [vmem()] * (5 + len(arrays)),
        (array((seq, cols), BF16),),
        [vmem()],
        [
            pltpu.VMEM((width, 2 * LANES), BF16),
            pltpu.VMEM((width, 2 * LANES), BF16),
            pltpu.VMEM((2, seq, LANES), BF16),
            pltpu.VMEM((6, seq, LANES), F32),
        ],
    )[0]


def input_back_kernel(slots1, slots2, info, own, other, ends, dz, *rest):
    n1, n2 = len(slots1), len(slots2)
    refs1, refs2, (mine, *sent, w1, w2) = rest[:n1], rest[n1 : n1 + n2], rest[n1 + n2 :]
    i = pl.program_id(0)

    @pl.when(i == 0)
    def _():
        place(info[0], refs1, slots1, w1)
        place(info[0], refs2, slots2, w2, 2 * HD, 6 * HD)

    pairs = jnp.concatenate([own[...], other[...]], axis=1)
    back = nt(pairs, w1[...]) + nt(ends[...], w2[...])

    @pl.when(i % 2 == info[2])
    def _():
        mine[i // 2] = back + dz[...]

    per = len(sent) // 2
    height = sent[0].shape[0]
    for k, part in enumerate(sent):

        @pl.when((i % 2 != info[2]) & (i // 2 == k // per))
        def _(k=k, part=part):
            part[...] = back[k % per * height : (k % per + 1) * height].astype(BF16)


def input_back(info, own, other, ends, dz, gathered1, gathered2):
    seq, width = dz.shape
    arrays = gathered1[0] + gathered2[0]
    halves = (seq // TILE // 2, TILE, width)
    grads = (own, other, ends, dz)
    return run(
        functools.partial(input_back_kernel, gathered1[1], gathered2[1]),
        "input_back",
        (info,) + grads + arrays,
        [smem()] + [rows(g.shape[1]) for g in grads] + [whole(a.shape) for a in arrays],
        (array(halves, F32),) + (array((SENT, width), BF16),) * (seq // 2 // SENT),
        [whole(halves)] + [whole((SENT, width))] * (seq // 2 // SENT),
        [pltpu.VMEM((width, 12 * HD), BF16), pltpu.VMEM((width, 8 * HD), BF16)],
        grid=(seq // TILE,),
    )


def center(z):
    mean = jnp.mean(z, axis=1, keepdims=True)
    moved = z - mean
    spread = jnp.mean(moved * moved, axis=1, keepdims=True)
    scale = lax.rsqrt(spread + EPSILON)
    return moved * scale, scale


def norm_back(n, scale, gy, gain):
    dn = gy * gain
    return scale * (
        dn - jnp.mean(dn, axis=1, keepdims=True) - n * jnp.mean(dn * n, axis=1, keepdims=True)
    )


def add_sums(gy, n, sums):
    i = pl.program_id(0)

    @pl.when(i == 0)
    def _():
        sums[...] = jnp.zeros_like(sums)

    sums[0:1, :] += jnp.sum(gy * n, axis=0, keepdims=True)
    sums[1:2, :] += jnp.sum(gy, axis=0, keepdims=True)


def norm_one_kernel(tok, gain, bias, *rest):
    *parts, z, hn = rest
    count = len(parts) // 2
    value = tok[...].astype(F32) + get_sum(parts[:count], parts[count:], count * parts[0].shape[0] // TILE)
    z[...] = value
    n, _ = center(value)
    hn[...] = (n * gain[...] + bias[...]).astype(BF16)


def norm_one(tok, p0, p1, gain, bias):
    seq, width = tok.shape
    return run(
        norm_one_kernel,
        "norm_one",
        (tok, gain, bias, *p0, *p1),
        [rows(width)] + [whole((1, width))] * 2 + [whole(p.shape) for p in (*p0, *p1)],
        (far((seq, width), F32), array((seq, width), BF16)),
        (rows(width), rows(width)),
        grid=(seq // TILE,),
    )


def norm_two_kernel(info, hn, own, got, core_own, core_got, gain, bias, *rest):
    *parts, out, dz, dzb, sums = rest
    count = len(parts) // 2
    value = hn[...].astype(F32) + get_sum(parts[:count], parts[count:], count * parts[0].shape[0] // TILE)
    n, scale = center(value)
    out[...] = (n * gain[...] + bias[...]).astype(BF16)
    row = lax.broadcasted_iota(jnp.int32, value.shape, 0) + pl.program_id(0) * TILE
    seq = pl.num_programs(0) * TILE
    position = row + info[4]
    position = jnp.where(position >= seq, position - seq, position)
    i = pl.program_id(0)
    mine = i % 2 == info[2]
    cot = jnp.where(
        i < 2,
        jnp.where(mine, own[0].astype(F32), core_own[0].astype(F32)),
        jnp.where(mine, got[0].astype(F32), core_got[0].astype(F32)),
    )
    gy = jnp.where(position < info[3], cot, 0.0)
    grad = norm_back(n, scale, gy, gain[...])
    dz[...] = grad
    dzb[...] = grad.astype(BF16)
    add_sums(gy, n, sums)


def norm_two(info, hn, m0, m1, cot, gain, bias):
    seq, width = hn.shape
    return run(
        norm_two_kernel,
        "norm_two",
        (info, hn, *cot, gain, bias, *m0, *m1),
        [smem(), rows(width)]
        + [pl.BlockSpec((1,) + c.shape[1:], lambda i: (1, 0, 0)) for c in cot]
        + [whole((1, width))] * 2
        + [whole(p.shape) for p in (*m0, *m1)],
        (
            array((seq, width), BF16),
            far((seq, width), F32),
            array((seq, width), BF16),
            array((2, width), F32),
        ),
        (rows(width), rows(width), rows(width), whole((2, width))),
        grid=(seq // TILE,),
    )


def norm_one_back_kernel(z, dz2, gain, *rest):
    *parts, dz, dzb, sums = rest
    count = len(parts) // 2
    n, scale = center(z[...])
    gy = dz2[...] + get_sum(parts[:count], parts[count:], count * parts[0].shape[0] // TILE)
    grad = norm_back(n, scale, gy, gain[...])
    dz[...] = grad
    dzb[...] = grad.astype(BF16)
    add_sums(gy, n, sums)


def norm_one_back(z, dz2, p0, p1, gain):
    seq, width = z.shape
    return run(
        norm_one_back_kernel,
        "norm_one_back",
        (z, dz2, gain, *p0, *p1),
        [rows(width)] * 2 + [whole((1, width))] + [whole(p.shape) for p in (*p0, *p1)],
        (array((seq, width), F32), array((seq, width), BF16), array((2, width), F32)),
        (rows(width), rows(width), whole((2, width))),
        grid=(seq // TILE,),
    )


def gelu_pair(u):
    phi = 0.5 + 0.5 * lax.erf(u * 0.7071067811865476)
    return u * phi, phi + u * (jnp.exp(-0.5 * u * u) * 0.3989422804014327)


def feed_up_kernel(slots, info, hn, *rest):
    refs, (active, slope, wfull) = rest[: len(slots)], rest[len(slots) :]

    @pl.when(pl.program_id(0) == 0)
    def _():
        place(info[0], refs, slots, wfull)

    a, g = gelu_pair(nn(hn[...], wfull[...]))
    active[...] = a.astype(BF16)
    slope[...] = g.astype(BF16)


def feed_up(info, hn, gathered, units):
    arrays, slots = gathered
    seq, width = hn.shape
    return run(
        functools.partial(feed_up_kernel, slots),
        "feed_up",
        (info, hn) + arrays,
        [smem(), rows(width)] + [whole(a.shape) for a in arrays],
        (array((seq, units), BF16), array((seq, units), BF16)),
        (rows(units), rows(units)),
        [pltpu.VMEM((width, units), BF16)],
        grid=(seq // TILE,),
    )


def feed_down_kernel(slots, info, act1, act2, *rest):
    refs, parts, wfull = rest[: len(slots)], rest[len(slots) : -1], rest[-1]

    @pl.when(pl.program_id(0) == 0)
    def _():
        place(info[0], refs, slots, wfull)

    both = jnp.concatenate([act1[...], act2[...]], axis=1)
    put_rows(parts, nt(both, wfull[...]).astype(BF16))


def feed_down(info, act1, act2, gathered, width):
    seq, units = act1.shape
    arrays, slots = gathered
    return run(
        functools.partial(feed_down_kernel, slots),
        "feed_down",
        (info, act1, act2) + arrays,
        [smem(), rows(units), rows(units)] + [whole(a.shape) for a in arrays],
        *tiles(seq, width, seq),
        [pltpu.VMEM((width, 2 * units), BF16)],
        grid=(seq // TILE,),
    )


def feed_back_kernel(slots_up, slots_down, info, dzb, slope1, slope2, *rest):
    n1, n2 = len(slots_up), len(slots_down)
    ups, downs, (du1, du2, *parts, up, down) = rest[:n1], rest[n1 : n1 + n2], rest[n1 + n2 :]

    @pl.when(pl.program_id(0) == 0)
    def _():
        place(info[0], ups, slots_up, up)
        place(info[0], downs, slots_down, down)

    units = du1.shape[1]
    out = None
    for i, (slope, du) in enumerate(((slope1, du1), (slope2, du2))):
        at = pl.ds(i * units, units)
        grad = (nn(dzb[...], down[:, at]) * slope[...].astype(F32)).astype(BF16)
        du[...] = grad
        more = nt(grad, up[:, at])
        out = more if out is None else out + more
    put_rows(parts, out.astype(BF16))


def feed_back(info, dzb, slope1, slope2, up, down):
    seq, width = dzb.shape
    units = slope1.shape[1]
    arrays = up[0] + down[0]
    parts, part_specs = tiles(seq, width, TILE)
    return run(
        functools.partial(feed_back_kernel, up[1], down[1]),
        "feed_back",
        (info, dzb, slope1, slope2) + arrays,
        [smem(), rows(width), rows(units), rows(units)] + [whole(a.shape) for a in arrays],
        (array((seq, units), BF16),) * 2 + parts,
        [rows(units)] * 2 + part_specs,
        [pltpu.VMEM((width, 2 * units), BF16)] * 2,
        grid=(seq // TILE,),
    )


def feed_grad_kernel(places, info, a, d1, d2, *rest):
    outs, fulls = rest[:4], rest[4:]
    half = outs[0].shape[2]
    fulls[0][...] = tn(a[...], d1[...])
    fulls[1][...] = tn(a[...], d2[...])
    for i, out in enumerate(outs):
        pick(info[0], fulls, out, places[i], (i // 2) * half)


def feed_grad(info, a, d1, d2, places):
    seq, width = a.shape
    units = d1.shape[1]
    count = len(places[0])
    out = array((count, width // count, units // 2), BF16)
    return run(
        functools.partial(feed_grad_kernel, places),
        "feed_grad",
        (info, a, d1, d2),
        [smem()] + [vmem()] * 3,
        (out,) * 4,
        [vmem()] * 4,
        [pltpu.VMEM((width, units), F32)] * 2,
    )


def pair_grad_kernel(slots, info, tok, d, out, full):
    full[...] = tn(tok[...], d[...])
    pick(info[0], (full,), out, slots, 0)


def pair_grad(info, tok, d, slots):
    seq, width = tok.shape
    cols = d.shape[1]
    return run(
        functools.partial(pair_grad_kernel, slots),
        "pair_grad",
        (info, tok, d),
        [smem()] + [vmem()] * 2,
        (array((len(slots), width // len(slots), cols), BF16),),
        [vmem()],
        [pltpu.VMEM((width, cols), F32)],
    )[0]


def encode(sums):
    hi = sums.astype(BF16).astype(F32)
    mid = (sums - hi).astype(BF16).astype(F32)
    low = sums - hi - mid
    return jnp.concatenate([hi, mid, low, jnp.zeros_like(low)], axis=0).astype(BF16)


def decode(coded):
    values = coded.astype(F32)
    n = values.shape[0] // 4
    return values[:n] + values[n : 2 * n] + values[2 * n : 3 * n]


def single_grad_kernel(places, info, tok, d, dz, own, other, ends, sums_one, sums_two, keep, send, full):
    mine = tn(tok[...], d[...])
    third = tn(dz[...], ends[...])
    blank = jnp.zeros((third.shape[0], HD), F32)
    width = full.shape[2]
    both = jnp.concatenate([sums_one[...], sums_two[...]], axis=0)
    both = encode(jnp.concatenate([both[:, :width], both[:, width:]], axis=0))
    for chip, ctx in enumerate((own, other)):
        full[chip, :, :LANES] = tn(dz[...], ctx[...])
        at = chip * 4 * HD
        o_third = jnp.concatenate([third[:, chip * HD : (chip + 1) * HD], blank], axis=1)
        full[chip, :, LANES : 2 * LANES] = o_third + mine[:, at : at + LANES]
        full[chip, :, 2 * LANES :] = mine[:, at + LANES : at + 2 * LANES]
    for out, slots in zip((keep, send), places):
        count = len(slots)
        height = full.shape[1] // count
        for e, (chip, j) in enumerate(slots):
            at = 0 if count == 1 else pl.multiple_of((info[0] ^ j) * height, height)
            out[pl.ds(e * height, height), :] = full[chip, pl.ds(at, height), :].astype(BF16)
        out[pl.ds(count * height, TAIL), :] = both


def single_grad(info, tok, d, dz, contexts, sums_one, sums_two, places):
    seq, width = tok.shape
    cols = 6 * HD
    out = array((width + TAIL, cols), BF16)
    return run(
        functools.partial(single_grad_kernel, places),
        "single_grad",
        (info, tok, d, dz, *contexts, sums_one, sums_two),
        [smem()] + [vmem()] * 8,
        (out, out),
        [vmem()] * 2,
        [pltpu.VMEM((2, width, cols), F32)],
    )


def across(values, axis, pairs):
    return lax.ppermute(values, axis, pairs)


def flip_chip(values):
    return across(values, "mp", CHIP_SWAP)


def flip_core(values):
    return across(values, "mp", CORE_SWAP)


def flip_cores(parts):
    return [flip_core(p) for p in parts]


def flip_dp(values, distance):
    size = lax.axis_size("dp")
    return across(values, "dp", [(i, i ^ distance) for i in range(size)])


def join_kernel(groups, *refs):
    count = sum(groups)
    parts, outs, sems = refs[:count], refs[count:-1], refs[-1]
    copies = []
    for out, number in zip(outs, groups):
        first = 0
        for part in parts[len(copies) : len(copies) + number]:
            to = out.at[pl.ds(first, part.shape[0])]
            copies.append(pltpu.make_async_copy(part, to, sems.at[len(copies)]))
            first += part.shape[0]
    for copy in copies:
        copy.start()
    for copy in copies:
        copy.wait()


def join(*groups):
    parts = sum((tuple(g) for g in groups), ())
    outs = [array((sum(p.shape[0] for p in g),) + g[0].shape[1:], g[0].dtype) for g in groups]
    return run(
        functools.partial(join_kernel, tuple(len(g) for g in groups)),
        "join",
        parts,
        [anywhere()] * len(parts),
        outs,
        [anywhere()] * len(outs),
        [pltpu.SemaphoreType.DMA((len(parts),))],
    )


def pack_kernel(w_query, w_key, w_value, w_out, out, rows_in, out_in, sems):
    copies = [
        pltpu.make_async_copy(w, rows_in.at[i], sems.at[i])
        for i, w in enumerate((w_query, w_key, w_value))
    ]
    copies.append(pltpu.make_async_copy(w_out, out_in, sems.at[3]))
    for copy in copies:
        copy.start()
    for copy in copies:
        copy.wait()
    for i in range(3):
        out[0, :, 2 * i * HD : 2 * (i + 1) * HD] = rows_in[i, :, : 2 * HD]
    parts = [jnp.transpose(out_in[...].astype(F32))]
    parts += [rows_in[i, :, 2 * HD :].astype(F32) for i in range(3)]
    out[0, :, 6 * HD :] = jnp.concatenate(parts, axis=1).astype(BF16)


def pack(w_query, w_key, w_value, w_out):
    height, span = w_query.shape
    return run(
        pack_kernel,
        "pack",
        in_hbm((w_query, w_key, w_value, w_out)),
        [anywhere()] * 4,
        (array((1, height, 4 * span), BF16),),
        [vmem()],
        [
            pltpu.VMEM((3, height, span), BF16),
            pltpu.VMEM(w_out.shape, BF16),
            pltpu.SemaphoreType.DMA((4,)),
        ],
    )[0]


def beside_kernel(first, second, out, sems):
    width = first.shape[1]
    copies = [
        pltpu.make_async_copy(ref, out.at[0, :, pl.ds(i * width, width)], sems.at[i])
        for i, ref in enumerate((first, second))
    ]
    for copy in copies:
        copy.start()
    for copy in copies:
        copy.wait()


def beside(first, second):
    height, width = first.shape
    return run(
        beside_kernel,
        "beside",
        in_hbm((first, second)),
        [anywhere()] * 2,
        (array((1, height, 2 * width), BF16),),
        [anywhere()],
        [pltpu.SemaphoreType.DMA((2,))],
    )[0]


def join_sides_kernel(count, *refs):
    parts, outs, sems = refs[:count], refs[count : count + 2], refs[count + 2]
    width = outs[0].shape[2]
    copies = []
    each = parts[0].shape[0]
    for i, part in enumerate(parts):
        for side, out in enumerate(outs):
            copies.append(
                pltpu.make_async_copy(
                    part.at[:, :, pl.ds(side * width, width)],
                    out.at[pl.ds(i * each, each)],
                    sems.at[2 * i + side],
                )
            )
    for copy in copies:
        copy.start()
    for copy in copies:
        copy.wait()


def join_sides(parts):
    count = len(parts)
    each, height, width = parts[0].shape
    out = array((count * each, height, width // 2), BF16)
    return run(
        functools.partial(join_sides_kernel, count),
        "join_sides",
        tuple(parts),
        [anywhere()] * count,
        (out, out),
        [anywhere()] * 2,
        [pltpu.SemaphoreType.DMA((2 * count,))],
    )


def fold_kernel(tail, own, got, *outs):
    body = own.shape[0] - tail
    each = body // len(outs)
    for i, out in enumerate(outs):
        at = pl.ds(i * each, each)
        total = (own[at].astype(F32) + got[at].astype(F32)).astype(BF16)
        if tail:
            out[:each] = total
        else:
            out[...] = total
    if tail:
        coded = encode(decode(own[body:]) + decode(got[body:]))
        for out in outs:
            out[each:] = coded


def fold(own, got, parts, tail=0):
    shape = ((own.shape[0] - tail) // parts + tail,) + own.shape[1:]
    return run(
        functools.partial(fold_kernel, tail),
        "fold",
        (own, got),
        [vmem()] * 2,
        (array(shape, BF16),) * parts,
        [vmem()] * parts,
    )


def fold_last_kernel(own1, got1, own2, got2, keep1, send1, keep2, send2):
    height = own2.shape[1]
    each = height + TAIL
    body = own1.shape[0] - TAIL
    coded = encode(decode(own1[body:]) + decode(got1[body:]))
    half = own2.shape[0] // 2
    for i in range(2 * half):
        out, first = (keep1, send1)[i // half], i % half * each
        at = pl.ds(i * height, height)
        out[first : first + height] = (own1[at].astype(F32) + got1[at].astype(F32)).astype(BF16)
        out[first + height : first + each] = coded
        total = own2[i].astype(F32) + got2[i].astype(F32)
        (keep2, send2)[i // half][i % half] = total.astype(BF16)


def fold_last(own1, got1, own2, got2):
    count, height, width = own2.shape
    first = array((count // 2 * (height + TAIL), width), BF16)
    second = array((count // 2, height, width), BF16)
    return run(
        fold_last_kernel,
        "fold_last",
        (own1, got1, own2, got2),
        [vmem()] * 4,
        (first, first, second, second),
        [vmem()] * 4,
    )


def fold_z_kernel(own1, got1, own2, got2, keep, send):
    height = own2.shape[1]
    each = height + TAIL
    for i, out in enumerate((keep, send)):
        at = pl.ds(i * each, height)
        out[:height] = (own1[at].astype(F32) + got1[at].astype(F32)).astype(BF16)
        at = pl.ds(i * each + height, TAIL)
        out[height:each] = encode(decode(own1[at]) + decode(got1[at]))
        out[each:] = (own2[i].astype(F32) + got2[i].astype(F32)).astype(BF16)


def fold_z(own1, got1, own2, got2):
    _, height, width = own2.shape
    out = array((2 * height + TAIL, width), BF16)
    return run(
        fold_z_kernel,
        "fold_z",
        (own1, got1, own2, got2),
        [vmem()] * 4,
        (out, out),
        [vmem()] * 2,
    )


def fold_add_kernel(own1, got1, own2, got2, out1, out2):
    for own, got, out in ((own1, got1, out1), (own2, got2, out2)):
        out[...] = (own[...].astype(F32) + got[...].astype(F32)).astype(BF16)


def fold_add(own1, got1, own2, got2):
    out = array(own1.shape, BF16)
    return run(
        fold_add_kernel,
        "fold_add",
        (own1, got1, own2, got2),
        [vmem()] * 4,
        (out, out),
        [vmem()] * 2,
    )


def fold_feed_kernel(first1, own1, got1, first2, own2, got2, keep1, send1, keep2, send2):
    width = own1.shape[2]
    half = keep1.shape[0]
    for first, own, got, outs in (
        (first1, own1, got1, (keep1, send1)),
        (first2, own2, got2, (keep2, send2)),
    ):
        for i, out in enumerate(outs):
            at = pl.ds(i * half, half)
            out[:, :, :width] = first[at]
            out[:, :, width:] = (own[at].astype(F32) + got[at].astype(F32)).astype(BF16)


def fold_feed(first1, own1, got1, first2, own2, got2):
    count, height, width = own1.shape
    out = array((count // 2, height, 2 * width), BF16)
    return run(
        fold_feed_kernel,
        "fold_feed",
        (first1, own1, got1, first2, own2, got2),
        [vmem()] * 6,
        (out,) * 4,
        [vmem()] * 4,
    )


def fold_sides_kernel(own1, got1, own2, got2, keep, send):
    width = own1.shape[2]
    half = keep.shape[0]
    for side, (own, got) in enumerate(((own1, got1), (own2, got2))):
        for i, out in enumerate((keep, send)):
            at = pl.ds(i * half, half)
            total = own[at].astype(F32) + got[at].astype(F32)
            out[:, :, side * width : (side + 1) * width] = total.astype(BF16)


def fold_sides(own1, got1, own2, got2):
    count, height, width = own1.shape
    out = array((count // 2, height, 2 * width), BF16)
    return run(
        fold_sides_kernel,
        "fold_sides",
        (own1, got1, own2, got2),
        [vmem()] * 4,
        (out, out),
        [vmem()] * 2,
    )


BY_Z = (0, 4, 2, 6)
Y_MAJOR = BY_Z + tuple(z + 1 for z in BY_Z)
OWN = tuple((0, j) for j in Y_MAJOR)
OTHER = tuple((1, j) for j in Y_MAJOR)
CHIP_NEAR = tuple((chip, z) for chip in range(2) for z in BY_Z)
CHIP_FAR = tuple((chip, z + 1) for chip in range(2) for z in BY_Z)


def split_kernel(info, first, second, mine, theirs, sems):
    copies = []
    for i, values in enumerate((first, second)):
        copies += [
            pltpu.make_async_copy(values.at[info[1]], mine.at[i], sems.at[2 * i]),
            pltpu.make_async_copy(values.at[1 - info[1]], theirs.at[i], sems.at[2 * i + 1]),
        ]
    for copy in copies:
        copy.start()
    for copy in copies:
        copy.wait()


def split(info, first, second):
    out = array((2,) + first.shape[1:], first.dtype)
    return run(
        split_kernel,
        "split",
        (info, *in_hbm((first, second))),
        [smem()] + [anywhere()] * 2,
        (out, out),
        [vmem()] * 2,
        [pltpu.SemaphoreType.DMA((4,))],
    )


def merge_kernel(info, own, got, core_own, core_got, out, sems):
    core = info[2]
    copies = []
    for half, (mine, other) in enumerate(((own, core_own), (got, core_got))):
        copies += [
            pltpu.make_async_copy(mine.at[0], out.at[half, core], sems.at[2 * half]),
            pltpu.make_async_copy(other.at[0], out.at[half, 1 - core], sems.at[2 * half + 1]),
        ]
    for copy in copies:
        copy.start()
    for copy in copies:
        copy.wait()


def merge(info, quarters):
    _, quarter, width = quarters[0].shape
    out = run(
        merge_kernel,
        "merge",
        (info, *quarters),
        [smem()] + [anywhere()] * 4,
        (array((2, 2, quarter, width), quarters[0].dtype),),
        [anywhere()],
        [pltpu.SemaphoreType.DMA((4,))],
    )[0]
    return out.reshape(4 * quarter, width)


def halves_kernel(info, rows_ref, own, send, sems):
    quarter = own.shape[0]
    copies = []
    for half, out in enumerate((own, send)):
        at = pl.multiple_of((2 * half + info[2]) * quarter, quarter)
        copies.append(pltpu.make_async_copy(rows_ref.at[pl.ds(at, quarter)], out, sems.at[half]))
    for copy in copies:
        copy.start()
    for copy in copies:
        copy.wait()


def halves(info, values):
    seq, width = values.shape
    out = array((seq // 4, width), values.dtype)
    return run(
        halves_kernel,
        "halves",
        (info, values),
        [smem(), anywhere()],
        (out, out),
        [anywhere()] * 2,
        [pltpu.SemaphoreType.DMA((2,))],
    )


def slots_kernel(info, own, other, out, sems):
    copies = [
        pltpu.make_async_copy(own, out.at[info[1]], sems.at[0]),
        pltpu.make_async_copy(other, out.at[1 - info[1]], sems.at[1]),
    ]
    for copy in copies:
        copy.start()
    for copy in copies:
        copy.wait()


def slots_of(info, own, other):
    return run(
        slots_kernel,
        "slots",
        (info, own, other),
        [smem()] + [anywhere()] * 2,
        (array((2,) + own.shape, own.dtype),),
        [anywhere()],
        [pltpu.SemaphoreType.DMA((2,))],
    )[0]


def tokens_add_kernel(count, mine, *rest):
    got, own, sends = rest[:count], rest[count], rest[count + 1 :]
    per = count // 2
    height = got[0].shape[0]
    for k, part in enumerate(got):
        at = k % per * height
        total = mine[k // per, pl.ds(at, height)] + part[...].astype(F32)
        if k < per:
            own[pl.ds(at, height)] = total
        else:
            each = sends[0].shape[0]
            for first in range(0, height, each):
                sends[(at + first) // each][...] = total[first : first + each].astype(BF16)


def tokens_add(mine, got):
    _, quarter, width = mine.shape
    send = array((quarter // 2, width), BF16)
    return run(
        functools.partial(tokens_add_kernel, len(got)),
        "tokens_add",
        (mine, *got),
        [vmem()] * (1 + len(got)),
        (array((quarter, width), F32), send, send),
        [vmem()] * 3,
    )


def tokens_out_kernel(info, own, *rest):
    *got, out = rest
    out[info[1]] = own[...]
    height = got[0].shape[0]
    for k, part in enumerate(got):
        out[1 - info[1], pl.ds(k * height, height), :] = part[...].astype(F32)


def tokens_out(info, own, got):
    return run(
        tokens_out_kernel,
        "tokens_out",
        (info, own, *got),
        [smem()] + [vmem()] * (1 + len(got)),
        (array((2,) + own.shape, F32),),
        [vmem()],
    )[0]


def feed_out_kernel(own, got, up, down):
    half = up.shape[1] // 2
    for i in range(4):
        at = pl.ds(i * half, half)
        total = own[0, :, at].astype(F32) + got[0, :, at].astype(F32)
        out = (down, up)[i % 2]
        out[:, pl.ds(i // 2 * half, half)] = total


def feed_out(own, got):
    _, height, width = own.shape
    out = array((height, width // 2), F32)
    return run(
        feed_out_kernel,
        "feed_out",
        (own, got),
        [vmem()] * 2,
        (out, out),
        [vmem()] * 2,
    )


def attend_out_kernel(a, b, query, key, value, out, gain1, bias1, gain2, bias2):
    height = query.shape[0]

    def both(first, last):
        return a[first:last].astype(F32) + b[first:last].astype(F32)

    one = both(0, height)
    two = both(height + TAIL, 2 * height + TAIL)
    at = pl.ds(height, TAIL)
    sums = decode(a[at]) + decode(b[at])
    for i, ref in enumerate((query, key, value)):
        ref[...] = jnp.concatenate(
            [two[:, 2 * i * HD : 2 * (i + 1) * HD], one[:, (3 + i) * HD : (4 + i) * HD]], axis=1
        )
    out[...] = jnp.transpose(one[:, : 3 * HD])
    for i, ref in enumerate((gain1, bias1, gain2, bias2)):
        ref[...] = jnp.concatenate([sums[i], sums[4 + i]], axis=0)


def attend_out(pieces, height):
    cols = pieces[0].shape[1]
    span = cols // 2
    return run(
        attend_out_kernel,
        "attend_out",
        tuple(pieces),
        [vmem()] * 2,
        (array((height, span), F32),) * 3
        + (array((span, height), F32),)
        + (array((2 * cols,), F32),) * 4,
        [vmem()] * 8,
    )


def local(
    tokens,
    w_query,
    w_key,
    w_value,
    w_out,
    w_up,
    w_down,
    gain_attn,
    bias_attn,
    gain_ffn,
    bias_ffn,
    lengths,
    random_blocks,
    cotangent,
):
    ORDER.clear()
    size = lax.axis_size("dp")
    rank = lax.axis_index("mp")
    me = lax.axis_index("dp")
    x, core = rank // 2, rank % 2
    _, quarter, features = tokens.shape
    seq = 4 * quarter
    height = w_query.shape[0]
    span = w_query.shape[1]
    heads = span // HD
    nblocks = seq // BLOCK
    fast = size == 8 and height % 16 == 0

    length = lax.dynamic_index_in_dim(lengths, x, 0, keepdims=False)
    shift = x * (seq // 2)
    info = jnp.stack([me, x, core, length, shift]).astype(jnp.int32)
    units = w_up.shape[1]

    blocks = (jnp.arange(nblocks) + x * (nblocks // 2)) % nblocks
    near_blocks = jnp.abs(blocks[:, None] - blocks[None, :]) <= 1
    edge = (blocks == 0) | (blocks == nblocks - 1)
    fixed = near_blocks | edge[:, None] | edge[None, :]

    def table(shard):
        chosen = lax.dynamic_slice_in_dim(random_blocks, shard * heads, heads, 0)
        chosen = jnp.roll(chosen, -x * (nblocks // 2), axis=1)
        hit = jnp.any(chosen[:, None, :, :] == blocks[None, :, None, None], axis=3)
        bias = jnp.where(fixed.T[None] | hit, 0.0, NEGATIVE)
        return jnp.concatenate(
            [
                jnp.zeros((heads, nblocks, HD), F32),
                bias,
                jnp.full((heads, nblocks, 3), -1.0, F32),
                jnp.zeros((heads, nblocks, HD - 3 - nblocks), F32),
            ],
            axis=2,
        )

    mask_own, mask_other = table(rank), table(rank ^ 2)
    mask_ends = jnp.concatenate([mask_own[2:], mask_other[2:]], axis=0)
    g_one, b_one = gain_attn[None], bias_attn[None]
    g_two, b_two = gain_ffn[None], bias_ffn[None]

    if fast:
        flat = (tuple((0, j) for j in Y_MAJOR),)
        piece = pack(w_query, w_key, w_value, w_out)
        got = flip_dp(piece, 4)
        own_rows, their_rows = split(info, tokens, cotangent)
        got_rows = flip_chip(their_rows)
        (two_attn,) = join([piece, got])
        feed_piece = beside(w_up, w_down.T)
        feed_got = flip_dp(feed_piece, 4)
        got = flip_dp(two_attn, 2)
        z_pair, z_single = join_sides([two_attn, got])
        y_pair, x_single = flip_dp(z_pair, 1), flip_chip(z_single)
        own_pair, near_single = join([z_pair, y_pair], [z_single, x_single])
        other_pair, far_single = flip_chip(own_pair), flip_dp(near_single, 1)
        two_up, two_down = join_sides([feed_piece, feed_got])
        got_up, got_down = flip_dp(two_up, 2), flip_dp(two_down, 2)
        quarters = (own_rows, got_rows, flip_core(own_rows), flip_core(got_rows))
        tok = merge(info, quarters)
        pair_w = ((own_pair, other_pair), (OWN, OTHER))
        single_w = ((near_single, far_single), (CHIP_NEAR, CHIP_FAR))
        own01 = attend(info, tok, ((own_pair,), flat), True, mask_own[:2])
        z_up, z_down = join([two_up, got_up], [two_down, got_down])
        y_up, x_down = flip_dp(z_up, 1), flip_chip(z_down)
        other01 = attend(info, tok, ((other_pair,), flat), True, mask_other[:2])
        ends = attend(info, tok, single_w, False, mask_ends)
        own_up, near_down = join([z_up, y_up], [z_down, x_down])
        other_up, far_down = flip_chip(own_up), flip_dp(near_down, 1)
        up = ((own_up, other_up), (OWN, OTHER))
        down = ((near_down, far_down), (CHIP_NEAR, CHIP_FAR))
    else:
        flat = (((0, 0),),)
        two = (((0, 0),), ((1, 0),))

        def plain(piece):
            own = lax.all_gather(piece, "dp", axis=0, tiled=True)[None]
            return own, flip_chip(own)

        own_rows, their_rows = split(info, tokens, cotangent)
        got_rows = flip_chip(their_rows)
        quarters = (own_rows, got_rows, flip_core(own_rows), flip_core(got_rows))
        tok = merge(info, quarters)
        thirds = [w_out.T] + [w[:, 2 * HD :] for w in (w_query, w_key, w_value)]
        pair_w = (
            plain(jnp.concatenate([w[:, : 2 * HD] for w in (w_query, w_key, w_value)], axis=1)),
            two,
        )
        single_w = (plain(jnp.concatenate(thirds, axis=1)), two)
        own_up, other_up = plain(w_up)
        own01 = attend(info, tok, ((pair_w[0][0],), flat), True, mask_own[:2])
        other01 = attend(info, tok, ((pair_w[0][1],), flat), True, mask_other[:2])
        ends = attend(info, tok, single_w, False, mask_ends)
    contexts = (own01[3], other01[3], ends[3])
    attn_part = project(info, contexts, single_w, features)
    if not fast:
        up = ((own_up, other_up), two)
        down = (plain(w_down.T), two)
    z_one, hn = norm_one(tok, attn_part, flip_cores(attn_part), g_one, b_one)

    act1, slope1 = feed_up(info, hn, ((own_up,), flat), units)
    act2, slope2 = feed_up(info, hn, ((other_up,), flat), units)
    mixed = feed_down(info, act1, act2, down, features)
    out, dz_two, dzb_two, sums_two = norm_two(
        info, hn, mixed, flip_cores(mixed), quarters, g_two, b_two
    )

    if fast:
        places = (OWN, OTHER, CHIP_NEAR, CHIP_FAR)
        att_slots = tuple((0, j) for j in Y_MAJOR)
    else:
        places = (((0, 0),), ((1, 0),)) * 2
        att_slots = ((0, 0),)

    keep_d1, send_d1, keep_d2, send_d2 = feed_grad(info, dzb_two, act1, act2, places)
    du1, du2, *back = feed_back(info, dzb_two, slope1, slope2, up, down)
    back_got = flip_cores(back)
    keep_u1, send_u1, keep_u2, send_u2 = feed_grad(info, hn, du1, du2, places)
    if fast:
        sum_d1, sum_d2 = fold_add(
            keep_d1, flip_chip(send_d1), keep_d2, flip_dp(send_d2, 1)
        )
    dz_one, dzb_one, sums_one = norm_one_back(z_one, dz_two, back, back_got, g_one)
    d_ends = attend_back(info, dzb_one, single_w, None, ends)
    if fast:
        keep_f1, send_f1, keep_f2, send_f2 = fold_feed(
            sum_d1, keep_u1, flip_chip(send_u1), sum_d2, keep_u2, flip_dp(send_u2, 1)
        )
        got_f1, got_f2 = flip_dp(send_f1, 1), flip_chip(send_f2)
    keep_s, send_s = single_grad(
        info, tok, d_ends, dzb_one, contexts, sums_one, sums_two, places[2:]
    )
    d_other = attend_back(info, dzb_one, single_w, 1, other01)
    grad_b = pair_grad(info, tok, d_other, att_slots)
    if fast:
        got_s = flip_dp(send_s, 1)
        got_b = flip_chip(grad_b)
        keep_f, send_f = fold_sides(keep_f1, got_f1, keep_f2, got_f2)
        got_f = flip_dp(send_f, 2)
    d_own = attend_back(info, dzb_one, single_w, 0, own01)
    grad_a = pair_grad(info, tok, d_own, att_slots)
    if fast:
        keep_a, send_a = fold(grad_a, got_b, 2, 0)
        got_a = flip_dp(send_a, 1)
    mine, *sent = input_back(info, d_own, d_other, d_ends, dz_one, pair_w, single_w)
    if fast:
        keep_s, send_s = fold(keep_s, got_s, 2, TAIL)
        got_s = flip_chip(send_s)
    if fast:
        keep_f, send_f = fold(keep_f, got_f, 2, 0)
        got_f = flip_dp(send_f, 4)
    own_tok, *send_tok = tokens_add(mine, flip_cores(sent))
    got_tok = [flip_chip(v) for v in send_tok]
    if fast:
        keep_s, send_s, keep_a, send_a = fold_last(keep_s, got_s, keep_a, got_a)
        got_s, got_a = flip_dp(send_s, 2), flip_dp(send_a, 2)
    own_out, send_out = halves(info, out)
    got_out = flip_chip(send_out)
    if fast:
        grad_up, grad_down = feed_out(keep_f, got_f)
    if fast:
        keep_a, send_a = fold_z(keep_s, got_s, keep_a, got_a)
        got_a = flip_dp(send_a, 4)
    grad_tokens = tokens_out(info, own_tok, got_tok)
    output = slots_of(info, own_out, got_out)
    if fast:
        grads = attend_out((keep_a, got_a), height)
        sums = grads[4:]
    else:

        def plain_sum(own, other):
            total = own.astype(F32) + flip_chip(other).astype(F32)
            return lax.psum_scatter(total, "dp", scatter_dimension=0, tiled=True)

        def plain_wide(keep1, send1, keep2, send2):
            return jnp.concatenate([plain_sum(keep1[0], send1[0]), plain_sum(keep2[0], send2[0])], axis=1)

        grad_down = plain_wide(keep_d1, send_d1, keep_d2, send_d2)
        grad_up = plain_wide(keep_u1, send_u1, keep_u2, send_u2)
        grad_single = plain_sum(keep_s[:features], send_s[:features])
        grad_pair = plain_sum(grad_a[0], grad_b[0])
        grads = [
            jnp.concatenate(
                [
                    grad_pair[:, 2 * i * HD : 2 * (i + 1) * HD],
                    grad_single[:, (3 + i) * HD : (4 + i) * HD],
                ],
                axis=1,
            )
            for i in range(3)
        ] + [grad_single[:, : 3 * HD].T]
        sums = decode(keep_s[features:])
        sums = lax.psum(sums + flip_chip(sums), "dp")
        sums = [jnp.concatenate([sums[i], sums[4 + i]]) for i in range(4)]

    return (
        output,
        grad_tokens,
        *grads[:4],
        grad_up,
        grad_down.T,
        *sums,
    )


def solution(mesh):
    return jax.shard_map(
        local,
        mesh=mesh,
        in_specs=(
            P("dp", "mp", None),
            P("dp", "mp"),
            P("dp", "mp"),
            P("dp", "mp"),
            P("mp", "dp"),
            P("dp", "mp"),
            P("mp", "dp"),
            P(),
            P(),
            P(),
            P(),
            P("dp"),
            P(),
            P("dp", "mp", None),
        ),
        out_specs=(
            P("dp", "mp", None),
            P("dp", "mp", None),
            P("dp", "mp"),
            P("dp", "mp"),
            P("dp", "mp"),
            P("mp", "dp"),
            P("dp", "mp"),
            P("mp", "dp"),
            P(),
            P(),
            P(),
            P(),
        ),
        check_vma=False,
    )
```

```python
import functools

import jax
import jax.numpy as jnp
from jax import lax
from jax.experimental import pallas as pl
from jax.experimental.pallas import tpu as pltpu
from jax.sharding import PartitionSpec as P

HD = 64
BLOCK = 64
LANES = 128
TILE = 256
SENT = 256
EPSILON = 1e-12
TAIL = 32
TOKEN = (8, 128)
ROOM = {
    "attend": 24,
    "attend_back": 28,
    "project": 16,
    "input_back": 24,
    "norm_one": 16,
    "norm_two": 24,
    "norm_one_back": 24,
    "feed_up": 20,
    "feed_down": 24,
    "feed_back": 40,
    "feed_grad": 28,
    "pair_grad": 16,
    "single_grad": 28,
    "join": 1,
    "join_sides": 1,
    "beside": 1,
    "pack": 2,
    "split": 4,
    "merge": 1,
    "fold": 6,
    "fold_add": 8,
    "fold_feed": 10,
    "fold_sides": 8,
    "fold_last": 6,
    "fold_z": 4,
    "halves": 1,
    "slots": 1,
    "tokens_add": 8,
    "tokens_out": 8,
    "feed_out": 6,
    "attend_out": 6,
}
SCALE = 0.125
LOG2E = 1.4426950408889634
LN2 = 0.6931471805599453
NEGATIVE = -1e30
F32 = jnp.float32
BF16 = jnp.bfloat16

CORE_SWAP = [(0, 1), (1, 0), (2, 3), (3, 2)]
CHIP_SWAP = [(0, 2), (2, 0), (1, 3), (3, 1)]


def nn(a, b):
    return lax.dot_general(a, b, (((1,), (0,)), ((), ())), preferred_element_type=F32)


def nt(a, b):
    return lax.dot_general(a, b, (((1,), (1,)), ((), ())), preferred_element_type=F32)


def tn(a, b):
    return lax.dot_general(a, b, (((0,), (0,)), ((), ())), preferred_element_type=F32)


def vmem():
    return pl.BlockSpec(memory_space=pltpu.VMEM)


def smem():
    return pl.BlockSpec(memory_space=pltpu.SMEM)


def anywhere():
    return pl.BlockSpec(memory_space=pl.ANY)


def in_hbm(values):
    return tuple(pltpu.with_memory_space_constraint(v, pltpu.HBM) for v in values)


def rows(width):
    return pl.BlockSpec((TILE, width), lambda i: (i, 0))


def whole(shape):
    return pl.BlockSpec(shape, lambda i: (0,) * len(shape))


def array(shape, dtype):
    return jax.ShapeDtypeStruct(shape, dtype)


ORDER = []


def run(kernel, name, args, specs, outs, out_specs, scratch=(), *, grid=()):
    given, made = len(args), len(outs)
    extra = tuple(ORDER)

    def body(*refs):
        ins, rest = refs[:given], refs[given + len(extra) :]
        rest[made][...] = jnp.zeros(TOKEN, F32)
        kernel(*ins, *rest[:made], *rest[made + 1 :])

    token_spec = whole(TOKEN) if grid else vmem()
    results = pl.pallas_call(
        body,
        grid=grid,
        out_shape=tuple(outs) + (array(TOKEN, F32),),
        in_specs=list(specs) + [anywhere()] * len(extra),
        out_specs=tuple(out_specs) + (token_spec,),
        scratch_shapes=list(scratch),
        compiler_params=pltpu.CompilerParams(vmem_limit_bytes=ROOM[name] * 2**20),
        cost_estimate=pl.CostEstimate(flops=1, bytes_accessed=0, transcendentals=0),
        name=name,
    )(*args, *extra)
    ORDER[:] = [results[-1]]
    return results[:-1]


def put_rows(parts, value):
    height = parts[0].shape[0]
    tile = value.shape[0]
    i = pl.program_id(0)
    for k, part in enumerate(parts):
        if height <= tile:
            per = tile // height

            @pl.when(i == k // per)
            def _(k=k, part=part):
                at = k % per * height
                part[...] = value[at : at + height]

        else:
            per = height // tile

            @pl.when(i // per == k)
            def _(part=part):
                part[pl.ds(pl.multiple_of(i % per * tile, tile), tile), :] = value


def get_sum(parts, more, count):
    height = parts[0].shape[0]
    tile = len(parts) * height // count
    i = pl.program_id(0)
    total = None
    if height <= tile:
        per = tile // height
        for k in range(count):
            pieces = [
                a[...].astype(F32) + b[...].astype(F32)
                for a, b in zip(parts[k * per : (k + 1) * per], more[k * per : (k + 1) * per])
            ]
            value = pieces[0] if per == 1 else jnp.concatenate(pieces, axis=0)
            total = value if k == 0 else jnp.where(i == k, value, total)
    else:
        per = height // tile
        at = pl.ds(pl.multiple_of(i % per * tile, tile), tile)
        for k, (a, b) in enumerate(zip(parts, more)):
            value = a[at, :].astype(F32) + b[at, :].astype(F32)
            total = value if k == 0 else jnp.where(i // per == k, value, total)
    return total


def far(shape, dtype):
    return pltpu.HBM(shape, dtype)


def tiles(seq, width, height):
    parts = (array((height, width), BF16),) * (seq // height)
    return parts, [whole((height, width))] * len(parts)


def place(me, refs, slots, dst_ref, first=0, last=None, only=None, to=0):
    for ref, of in zip(refs, slots):
        height, width = ref.shape[1], ref.shape[2]
        end = width if last is None else last
        for e, (chip, j) in enumerate(of):
            if only is not None and chip != only:
                continue
            at = 0 if height == dst_ref.shape[0] else pl.multiple_of((me ^ j) * height, height)
            at_column = to + (0 if only is not None else chip * (end - first))
            dst_ref[pl.ds(at, height), pl.ds(at_column, end - first)] = ref[e, :, first:end]


def pick(me, fulls, out_ref, slots, first):
    _, height, width = out_ref.shape
    for e, (chip, j) in enumerate(slots):
        full = fulls[chip]
        at = 0 if height == full.shape[0] else pl.multiple_of((me ^ j) * height, height)
        out_ref[e] = full[pl.ds(at, height), pl.ds(first, width)].astype(BF16)


def attend_kernel(slots, columns, only, places, info, lengths, tok, mask, *rest):
    refs, (qa, ka, va, ctx, wfull) = rest[: len(slots)], rest[len(slots) :]
    seq = tok.shape[0]
    place(info[0], refs, slots, wfull, *columns, only)
    lane = lax.broadcasted_iota(jnp.int32, (TILE, LANES), 1)
    row0 = lax.broadcasted_iota(jnp.int32, (TILE, LANES), 0)
    for t in range(seq // TILE):
        at = pl.ds(t * TILE, TILE)
        row = row0 + t * TILE
        made = nn(tok[at, :], wfull[...])
        onehot = jnp.where(lane - HD == row // BLOCK, 1.0, 0.0)[:, HD:]
        position = row + info[3]
        position = jnp.where(position >= seq, position - seq, position)
        dead = (position >= lengths[info[1]]) & (lane >= HD) & (lane < HD + 16)
        for h, (q_at, k_at, v_at) in enumerate(places):
            q = made[:, q_at : q_at + HD] * (SCALE * LOG2E)
            k = made[:, k_at : k_at + HD]
            v = made[:, v_at : v_at + HD]
            qa[h, at, :] = jnp.concatenate([q, onehot], axis=1).astype(BF16)
            per = TILE // BLOCK
            table = jnp.concatenate(
                [
                    jnp.broadcast_to(mask[h, t * per + b : t * per + b + 1, :], (BLOCK, LANES))
                    for b in range(per)
                ],
                axis=0,
            )
            table = jnp.where(dead, NEGATIVE, table)
            ka[h, at, :] = jnp.concatenate([k, table[:, HD:]], axis=1).astype(BF16)
            va[h, at, :] = jnp.concatenate([v, jnp.full((TILE, HD), -1.0, F32)], axis=1).astype(BF16)
    for t in range(seq // TILE):
        at = pl.ds(t * TILE, TILE)
        pieces = []
        for h in range(len(places)):
            q = qa[h, at, :]
            s = nt(q, ka[h])
            top = jnp.max(s, axis=1, keepdims=True)
            p = jnp.exp2(s - top).astype(BF16)
            got = nn(p, va[h])
            total = -got[:, HD:]
            pieces.append(got[:, :HD] / total)
            log = top + jnp.log2(-got)
            hi = log.astype(BF16).astype(F32)
            mid = (log - hi).astype(BF16).astype(F32)
            low = log - hi - mid
            new = jnp.where(
                lane == HD + 16,
                hi,
                jnp.where(lane == HD + 17, mid, jnp.where(lane == HD + 18, low, q.astype(F32))),
            )
            qa[h, at, :] = new.astype(BF16)
        ctx[at, :] = jnp.concatenate(pieces, axis=1).astype(BF16)


PAIR = ((0, 2 * HD, 4 * HD), (HD, 3 * HD, 5 * HD))
SINGLES = ((HD, 2 * HD, 3 * HD), (5 * HD, 6 * HD, 7 * HD))


def attend(info, lengths, tok, gathered, pair, mask):
    arrays, slots = gathered
    seq, width = tok.shape
    aug = far((2, seq, LANES), BF16)
    columns, only, cols = ((0, 6 * HD), 0, 6 * HD) if pair else ((2 * HD, 6 * HD), None, 8 * HD)
    return run(
        functools.partial(attend_kernel, slots, columns, only, PAIR if pair else SINGLES),
        "attend",
        (info, lengths, tok, mask) + arrays,
        [smem()] * 2 + [vmem()] * (2 + len(arrays)),
        (aug, aug, aug, array((seq, LANES), BF16)),
        [vmem()] * 4,
        [pltpu.VMEM((width, cols), BF16)],
    )


def place_out(me, refs, slots, pairs, ends):
    place(me, refs, slots, pairs, 0, 2 * HD)
    place(me, refs, slots, ends, 2 * HD, 4 * HD)
    both = ends[...]
    ends[:, :LANES] = jnp.concatenate([both[:, :HD], both[:, LANES : LANES + HD]], axis=1)


def project_kernel(slots, info, own, other, ends, *rest):
    refs, parts, (w1, w2) = rest[: len(slots)], rest[len(slots) : -2], rest[-2:]

    @pl.when(pl.program_id(0) == 0)
    def _():
        place_out(info[0], refs, slots, w1, w2)

    both = jnp.concatenate([own[...], other[...]], axis=1)
    put_rows(parts, (nt(both, w1[...]) + nt(ends[...], w2[:, :LANES])).astype(BF16))


def project(info, contexts, gathered, width):
    arrays, slots = gathered
    seq = contexts[0].shape[0]
    return run(
        functools.partial(project_kernel, slots),
        "project",
        (info,) + contexts + arrays,
        [smem()] + [rows(LANES)] * 3 + [whole(a.shape) for a in arrays],
        *tiles(seq, width, 2 * TILE),
        [pltpu.VMEM((width, 2 * LANES), BF16)] * 2,
        grid=(seq // TILE,),
    )


def attend_back_kernel(slots, chip, info, dz, qa, ka, va, ctx, *rest):
    refs, (dqkv, pairs, ends, da, parts) = rest[: len(slots)], rest[len(slots) :]
    seq = dz.shape[0]
    heads = qa.shape[0]
    if chip is None:
        place_out(info[0], refs, slots, pairs, ends)
        wfull = ends.at[:, pl.ds(0, LANES)]
    else:
        place(info[0], refs, slots, pairs, 0, 2 * HD, chip)
        wfull = pairs.at[:, pl.ds(0, LANES)]
    lane = lax.broadcasted_iota(jnp.int32, (TILE, LANES), 1)
    for t in range(seq // TILE):
        at = pl.ds(t * TILE, TILE)
        dctx = nn(dz[at, :], wfull[...]).astype(BF16).astype(F32)
        both = dctx * ctx[at, :].astype(F32)
        for h in range(heads):
            inner = jnp.sum(both[:, h * HD : (h + 1) * HD], axis=1, keepdims=True)
            hi = inner.astype(BF16).astype(F32)
            mid = (inner - hi).astype(BF16).astype(F32)
            low = inner - hi - mid
            one = jnp.concatenate(
                [dctx[:, h * HD : (h + 1) * HD], jnp.zeros((TILE, HD), F32)], axis=1
            )
            one = jnp.where(lane == HD, hi, one)
            one = jnp.where(lane == HD + 1, mid, one)
            one = jnp.where(lane == HD + 2, low, one)
            da[h, at, :] = one.astype(BF16)
    for h in range(heads):
        k_turned = jnp.transpose(ka[h].astype(F32)).astype(BF16)
        dq_turned = None
        for t in range(seq // TILE):
            at = pl.ds(t * TILE, TILE)
            p = jnp.exp2(nt(ka[h, at, :], qa[h]))
            ds = (p * nt(va[h, at, :], da[h])).astype(BF16)
            parts[2 * heads + h, at, :] = nn(p.astype(BF16), da[h])
            parts[heads + h, at, :] = nn(ds, qa[h]) * LN2
            more = nn(k_turned[:, t * TILE : (t + 1) * TILE], ds)
            dq_turned = more if dq_turned is None else dq_turned + more
        parts[h] = jnp.transpose(dq_turned) * SCALE
    for t in range(seq // TILE):
        at = pl.ds(t * TILE, TILE)
        pieces = [parts[i, at, :][:, :HD] for i in range(3 * heads)]
        if chip is None:
            blank = jnp.zeros((TILE, HD), F32)
            pieces = [blank] + pieces[::2] + [blank] + pieces[1::2]
        dqkv[at, :] = jnp.concatenate(pieces, axis=1).astype(BF16)


def attend_back(info, dz, gathered, chip, saved):
    arrays, slots = gathered
    qa, ka, va, ctx = saved
    seq, width = dz.shape
    cols = 8 * HD if chip is None else 6 * HD
    return run(
        functools.partial(attend_back_kernel, slots, chip),
        "attend_back",
        (info, dz, qa, ka, va, ctx) + arrays,
        [smem()] + [vmem()] * (5 + len(arrays)),
        (array((seq, cols), BF16),),
        [vmem()],
        [
            pltpu.VMEM((width, 2 * LANES), BF16),
            pltpu.VMEM((width, 2 * LANES), BF16),
            pltpu.VMEM((2, seq, LANES), BF16),
            pltpu.VMEM((6, seq, LANES), F32),
        ],
    )[0]


def input_back_kernel(slots1, slots2, info, own, other, ends, dz, *rest):
    n1, n2 = len(slots1), len(slots2)
    refs1, refs2, (mine, *sent, w1, w2) = rest[:n1], rest[n1 : n1 + n2], rest[n1 + n2 :]
    i = pl.program_id(0)

    @pl.when(i == 0)
    def _():
        place(info[0], refs1, slots1, w1)
        place(info[0], refs2, slots2, w2, 2 * HD, 6 * HD)

    pairs = jnp.concatenate([own[...], other[...]], axis=1)
    back = nt(pairs, w1[...]) + nt(ends[...], w2[...])

    @pl.when(i % 2 == info[2])
    def _():
        mine[i // 2] = back + dz[...].astype(F32)

    per = len(sent) // 2
    height = sent[0].shape[0]
    for k, part in enumerate(sent):

        @pl.when((i % 2 != info[2]) & (i // 2 == k // per))
        def _(k=k, part=part):
            part[...] = back[k % per * height : (k % per + 1) * height].astype(BF16)


def input_back(info, own, other, ends, dz, gathered1, gathered2):
    seq, width = dz.shape
    arrays = gathered1[0] + gathered2[0]
    halves = (seq // TILE // 2, TILE, width)
    grads = (own, other, ends, dz)
    return run(
        functools.partial(input_back_kernel, gathered1[1], gathered2[1]),
        "input_back",
        (info,) + grads + arrays,
        [smem()] + [rows(g.shape[1]) for g in grads] + [whole(a.shape) for a in arrays],
        (array(halves, F32),) + (array((SENT, width), BF16),) * (seq // 2 // SENT),
        [whole(halves)] + [whole((SENT, width))] * (seq // 2 // SENT),
        [pltpu.VMEM((width, 12 * HD), BF16), pltpu.VMEM((width, 8 * HD), BF16)],
        grid=(seq // TILE,),
    )


def center(z):
    mean = jnp.mean(z, axis=1, keepdims=True)
    moved = z - mean
    spread = jnp.mean(moved * moved, axis=1, keepdims=True)
    scale = lax.rsqrt(spread + EPSILON)
    return moved * scale, scale


def norm_back(n, scale, gy, gain):
    dn = gy * gain
    return scale * (
        dn - jnp.mean(dn, axis=1, keepdims=True) - n * jnp.mean(dn * n, axis=1, keepdims=True)
    )


def add_sums(gy, n, sums):
    i = pl.program_id(0)

    @pl.when(i == 0)
    def _():
        sums[...] = jnp.zeros_like(sums)

    sums[0:1, :] += jnp.sum(gy * n, axis=0, keepdims=True)
    sums[1:2, :] += jnp.sum(gy, axis=0, keepdims=True)


def norm_one_kernel(tok, gain, bias, *rest):
    *parts, normal, scale, hn = rest
    count = len(parts) // 2
    value = tok[...].astype(F32) + get_sum(parts[:count], parts[count:], count * parts[0].shape[0] // TILE)
    n, r = center(value)
    normal[...] = n.astype(BF16)
    scale[...] = r
    hn[...] = (n * gain[...] + bias[...]).astype(BF16)


def norm_one(tok, p0, p1, gain, bias):
    seq, width = tok.shape
    return run(
        norm_one_kernel,
        "norm_one",
        (tok, gain, bias, *p0, *p1),
        [rows(width)] + [whole((1, width))] * 2 + [whole(p.shape) for p in (*p0, *p1)],
        (array((seq, width), BF16), array((seq, 1), F32), array((seq, width), BF16)),
        (rows(width), rows(1), rows(width)),
        grid=(seq // TILE,),
    )


def norm_two_kernel(info, lengths, hn, own, got, core_own, core_got, gain, bias, *rest):
    *parts, out, dzb, sums = rest
    count = len(parts) // 2
    value = hn[...].astype(F32) + get_sum(parts[:count], parts[count:], count * parts[0].shape[0] // TILE)
    n, scale = center(value)
    out[...] = (n * gain[...] + bias[...]).astype(BF16)
    row = lax.broadcasted_iota(jnp.int32, value.shape, 0) + pl.program_id(0) * TILE
    seq = pl.num_programs(0) * TILE
    position = row + info[3]
    position = jnp.where(position >= seq, position - seq, position)
    i = pl.program_id(0)
    mine = i % 2 == info[2]
    cot = jnp.where(
        i < 2,
        jnp.where(mine, own[0].astype(F32), core_own[0].astype(F32)),
        jnp.where(mine, got[0].astype(F32), core_got[0].astype(F32)),
    )
    gy = jnp.where(position < lengths[info[1]], cot, 0.0)
    dzb[...] = norm_back(n, scale, gy, gain[...]).astype(BF16)
    add_sums(gy, n, sums)


def norm_two(info, lengths, hn, m0, m1, cot, gain, bias):
    seq, width = hn.shape
    return run(
        norm_two_kernel,
        "norm_two",
        (info, lengths, hn, *cot, gain, bias, *m0, *m1),
        [smem(), smem(), rows(width)]
        + [pl.BlockSpec((1,) + c.shape[1:], lambda i: (1, 0, 0)) for c in cot]
        + [whole((1, width))] * 2
        + [whole(p.shape) for p in (*m0, *m1)],
        (
            array((seq, width), BF16),
            array((seq, width), BF16),
            array((2, width), F32),
        ),
        (rows(width), rows(width), whole((2, width))),
        grid=(seq // TILE,),
    )


def norm_one_back_kernel(normal, scale, dz2, gain, *rest):
    *parts, dzb, sums = rest
    count = len(parts) // 2
    n = normal[...].astype(F32)
    gy = dz2[...].astype(F32)
    gy = gy + get_sum(parts[:count], parts[count:], count * parts[0].shape[0] // TILE)
    dzb[...] = norm_back(n, scale[...], gy, gain[...]).astype(BF16)
    add_sums(gy, n, sums)


def norm_one_back(normal, scale, dz2, p0, p1, gain):
    seq, width = normal.shape
    return run(
        norm_one_back_kernel,
        "norm_one_back",
        (normal, scale, dz2, gain, *p0, *p1),
        [rows(width), rows(1), rows(width)]
        + [whole((1, width))]
        + [whole(p.shape) for p in (*p0, *p1)],
        (array((seq, width), BF16), array((2, width), F32)),
        (rows(width), whole((2, width))),
        grid=(seq // TILE,),
    )


def gelu_pair(u):
    phi = 0.5 + 0.5 * lax.erf(u * 0.7071067811865476)
    return u * phi, phi + u * (jnp.exp(-0.5 * u * u) * 0.3989422804014327)


def feed_up_kernel(slots, info, hn, *rest):
    refs, (active, slope, wfull) = rest[: len(slots)], rest[len(slots) :]

    @pl.when(pl.program_id(0) == 0)
    def _():
        place(info[0], refs, slots, wfull)

    a, g = gelu_pair(nn(hn[...], wfull[...]))
    active[...] = a.astype(BF16)
    slope[...] = g.astype(BF16)


def feed_up(info, hn, gathered, units):
    arrays, slots = gathered
    seq, width = hn.shape
    return run(
        functools.partial(feed_up_kernel, slots),
        "feed_up",
        (info, hn) + arrays,
        [smem(), rows(width)] + [whole(a.shape) for a in arrays],
        (array((seq, units), BF16), array((seq, units), BF16)),
        (rows(units), rows(units)),
        [pltpu.VMEM((width, units), BF16)],
        grid=(seq // TILE,),
    )


def feed_down_kernel(slots, info, act1, act2, *rest):
    refs, parts, wfull = rest[: len(slots)], rest[len(slots) : -1], rest[-1]

    @pl.when(pl.program_id(0) == 0)
    def _():
        place(info[0], refs, slots, wfull)

    both = jnp.concatenate([act1[...], act2[...]], axis=1)
    put_rows(parts, nt(both, wfull[...]).astype(BF16))


def feed_down(info, act1, act2, gathered, width):
    seq, units = act1.shape
    arrays, slots = gathered
    return run(
        functools.partial(feed_down_kernel, slots),
        "feed_down",
        (info, act1, act2) + arrays,
        [smem(), rows(units), rows(units)] + [whole(a.shape) for a in arrays],
        *tiles(seq, width, seq),
        [pltpu.VMEM((width, 2 * units), BF16)],
        grid=(seq // TILE,),
    )


def feed_back_kernel(slots_up, slots_down, info, dzb, slope1, slope2, *rest):
    n1, n2 = len(slots_up), len(slots_down)
    ups, downs, (du1, du2, *parts, up, down) = rest[:n1], rest[n1 : n1 + n2], rest[n1 + n2 :]

    @pl.when(pl.program_id(0) == 0)
    def _():
        place(info[0], ups, slots_up, up)
        place(info[0], downs, slots_down, down)

    units = du1.shape[1]
    out = None
    for i, (slope, du) in enumerate(((slope1, du1), (slope2, du2))):
        at = pl.ds(i * units, units)
        grad = (nn(dzb[...], down[:, at]) * slope[...].astype(F32)).astype(BF16)
        du[...] = grad
        more = nt(grad, up[:, at])
        out = more if out is None else out + more
    put_rows(parts, out.astype(BF16))


def feed_back(info, dzb, slope1, slope2, up, down):
    seq, width = dzb.shape
    units = slope1.shape[1]
    arrays = up[0] + down[0]
    parts, part_specs = tiles(seq, width, TILE)
    return run(
        functools.partial(feed_back_kernel, up[1], down[1]),
        "feed_back",
        (info, dzb, slope1, slope2) + arrays,
        [smem(), rows(width), rows(units), rows(units)] + [whole(a.shape) for a in arrays],
        (array((seq, units), BF16),) * 2 + parts,
        [rows(units)] * 2 + part_specs,
        [pltpu.VMEM((width, 2 * units), BF16)] * 2,
        grid=(seq // TILE,),
    )


def feed_grad_kernel(places, info, a, d1, d2, *rest):
    outs, fulls = rest[:4], rest[4:]
    half = outs[0].shape[2]
    fulls[0][...] = tn(a[...], d1[...])
    fulls[1][...] = tn(a[...], d2[...])
    for i, out in enumerate(outs):
        pick(info[0], fulls, out, places[i], (i // 2) * half)


def feed_grad(info, a, d1, d2, places):
    seq, width = a.shape
    units = d1.shape[1]
    count = len(places[0])
    out = array((count, width // count, units // 2), BF16)
    return run(
        functools.partial(feed_grad_kernel, places),
        "feed_grad",
        (info, a, d1, d2),
        [smem()] + [vmem()] * 3,
        (out,) * 4,
        [vmem()] * 4,
        [pltpu.VMEM((width, units), F32)] * 2,
    )


def pair_grad_kernel(slots, info, tok, d, out, full):
    full[...] = tn(tok[...], d[...])
    pick(info[0], (full,), out, slots, 0)


def pair_grad(info, tok, d, slots):
    seq, width = tok.shape
    cols = d.shape[1]
    return run(
        functools.partial(pair_grad_kernel, slots),
        "pair_grad",
        (info, tok, d),
        [smem()] + [vmem()] * 2,
        (array((len(slots), width // len(slots), cols), BF16),),
        [vmem()],
        [pltpu.VMEM((width, cols), F32)],
    )[0]


def encode(sums):
    hi = sums.astype(BF16).astype(F32)
    mid = (sums - hi).astype(BF16).astype(F32)
    low = sums - hi - mid
    return jnp.concatenate([hi, mid, low, jnp.zeros_like(low)], axis=0).astype(BF16)


def decode(coded):
    values = coded.astype(F32)
    n = values.shape[0] // 4
    return values[:n] + values[n : 2 * n] + values[2 * n : 3 * n]


def single_grad_kernel(places, info, tok, d, dz, own, other, ends, sums_one, sums_two, keep, send, full):
    mine = tn(tok[...], d[...])
    third = tn(dz[...], ends[...])
    blank = jnp.zeros((third.shape[0], HD), F32)
    width = full.shape[2]
    both = jnp.concatenate([sums_one[...], sums_two[...]], axis=0)
    both = encode(jnp.concatenate([both[:, :width], both[:, width:]], axis=0))
    for chip, ctx in enumerate((own, other)):
        full[chip, :, :LANES] = tn(dz[...], ctx[...])
        at = chip * 4 * HD
        o_third = jnp.concatenate([third[:, chip * HD : (chip + 1) * HD], blank], axis=1)
        full[chip, :, LANES : 2 * LANES] = o_third + mine[:, at : at + LANES]
        full[chip, :, 2 * LANES :] = mine[:, at + LANES : at + 2 * LANES]
    for out, slots in zip((keep, send), places):
        count = len(slots)
        height = full.shape[1] // count
        for e, (chip, j) in enumerate(slots):
            at = 0 if count == 1 else pl.multiple_of((info[0] ^ j) * height, height)
            out[pl.ds(e * height, height), :] = full[chip, pl.ds(at, height), :].astype(BF16)
        out[pl.ds(count * height, TAIL), :] = both


def single_grad(info, tok, d, dz, contexts, sums_one, sums_two, places):
    seq, width = tok.shape
    cols = 6 * HD
    out = array((width + TAIL, cols), BF16)
    return run(
        functools.partial(single_grad_kernel, places),
        "single_grad",
        (info, tok, d, dz, *contexts, sums_one, sums_two),
        [smem()] + [vmem()] * 8,
        (out, out),
        [vmem()] * 2,
        [pltpu.VMEM((2, width, cols), F32)],
    )


def across(values, axis, pairs):
    return lax.ppermute(values, axis, pairs)


def flip_chip(values):
    return across(values, "mp", CHIP_SWAP)


def flip_core(values):
    return across(values, "mp", CORE_SWAP)


def flip_cores(parts):
    return [flip_core(p) for p in parts]


def flip_dp(values, distance):
    size = lax.axis_size("dp")
    return across(values, "dp", [(i, i ^ distance) for i in range(size)])


def join_kernel(groups, *refs):
    count = sum(groups)
    parts, outs, sems = refs[:count], refs[count:-1], refs[-1]
    copies = []
    for out, number in zip(outs, groups):
        first = 0
        for part in parts[len(copies) : len(copies) + number]:
            to = out.at[pl.ds(first, part.shape[0])]
            copies.append(pltpu.make_async_copy(part, to, sems.at[len(copies)]))
            first += part.shape[0]
    for copy in copies:
        copy.start()
    for copy in copies:
        copy.wait()


def join(*groups):
    parts = sum((tuple(g) for g in groups), ())
    outs = [array((sum(p.shape[0] for p in g),) + g[0].shape[1:], g[0].dtype) for g in groups]
    return run(
        functools.partial(join_kernel, tuple(len(g) for g in groups)),
        "join",
        parts,
        [anywhere()] * len(parts),
        outs,
        [anywhere()] * len(outs),
        [pltpu.SemaphoreType.DMA((len(parts),))],
    )


def pack_kernel(w_query, w_key, w_value, w_out, out, rows_in, out_in, sems):
    copies = [
        pltpu.make_async_copy(w, rows_in.at[i], sems.at[i])
        for i, w in enumerate((w_query, w_key, w_value))
    ]
    copies.append(pltpu.make_async_copy(w_out, out_in, sems.at[3]))
    for copy in copies:
        copy.start()
    for copy in copies:
        copy.wait()
    for i in range(3):
        out[0, :, 2 * i * HD : 2 * (i + 1) * HD] = rows_in[i, :, : 2 * HD]
    parts = [jnp.transpose(out_in[...].astype(F32))]
    parts += [rows_in[i, :, 2 * HD :].astype(F32) for i in range(3)]
    out[0, :, 6 * HD :] = jnp.concatenate(parts, axis=1).astype(BF16)


def pack(w_query, w_key, w_value, w_out):
    height, span = w_query.shape
    return run(
        pack_kernel,
        "pack",
        in_hbm((w_query, w_key, w_value, w_out)),
        [anywhere()] * 4,
        (array((1, height, 4 * span), BF16),),
        [vmem()],
        [
            pltpu.VMEM((3, height, span), BF16),
            pltpu.VMEM(w_out.shape, BF16),
            pltpu.SemaphoreType.DMA((4,)),
        ],
    )[0]


def beside_kernel(first, second, out, sems):
    width = first.shape[1]
    copies = [
        pltpu.make_async_copy(ref, out.at[0, :, pl.ds(i * width, width)], sems.at[i])
        for i, ref in enumerate((first, second))
    ]
    for copy in copies:
        copy.start()
    for copy in copies:
        copy.wait()


def beside(first, second):
    height, width = first.shape
    return run(
        beside_kernel,
        "beside",
        in_hbm((first, second)),
        [anywhere()] * 2,
        (array((1, height, 2 * width), BF16),),
        [anywhere()],
        [pltpu.SemaphoreType.DMA((2,))],
    )[0]


def join_sides_kernel(count, *refs):
    parts, outs, sems = refs[:count], refs[count : count + 2], refs[count + 2]
    width = outs[0].shape[2]
    copies = []
    each = parts[0].shape[0]
    for i, part in enumerate(parts):
        for side, out in enumerate(outs):
            copies.append(
                pltpu.make_async_copy(
                    part.at[:, :, pl.ds(side * width, width)],
                    out.at[pl.ds(i * each, each)],
                    sems.at[2 * i + side],
                )
            )
    for copy in copies:
        copy.start()
    for copy in copies:
        copy.wait()


def join_sides(parts):
    count = len(parts)
    each, height, width = parts[0].shape
    out = array((count * each, height, width // 2), BF16)
    return run(
        functools.partial(join_sides_kernel, count),
        "join_sides",
        tuple(parts),
        [anywhere()] * count,
        (out, out),
        [anywhere()] * 2,
        [pltpu.SemaphoreType.DMA((2 * count,))],
    )


def fold_kernel(tail, own, got, *outs):
    body = own.shape[0] - tail
    each = body // len(outs)
    for i, out in enumerate(outs):
        at = pl.ds(i * each, each)
        total = (own[at].astype(F32) + got[at].astype(F32)).astype(BF16)
        if tail:
            out[:each] = total
        else:
            out[...] = total
    if tail:
        coded = encode(decode(own[body:]) + decode(got[body:]))
        for out in outs:
            out[each:] = coded


def fold(own, got, parts, tail=0):
    shape = ((own.shape[0] - tail) // parts + tail,) + own.shape[1:]
    return run(
        functools.partial(fold_kernel, tail),
        "fold",
        (own, got),
        [vmem()] * 2,
        (array(shape, BF16),) * parts,
        [vmem()] * parts,
    )


def fold_last_kernel(own1, got1, own2, got2, keep1, send1, keep2, send2):
    height = own2.shape[1]
    each = height + TAIL
    body = own1.shape[0] - TAIL
    coded = encode(decode(own1[body:]) + decode(got1[body:]))
    half = own2.shape[0] // 2
    for i in range(2 * half):
        out, first = (keep1, send1)[i // half], i % half * each
        at = pl.ds(i * height, height)
        out[first : first + height] = (own1[at].astype(F32) + got1[at].astype(F32)).astype(BF16)
        out[first + height : first + each] = coded
        total = own2[i].astype(F32) + got2[i].astype(F32)
        (keep2, send2)[i // half][i % half] = total.astype(BF16)


def fold_last(own1, got1, own2, got2):
    count, height, width = own2.shape
    first = array((count // 2 * (height + TAIL), width), BF16)
    second = array((count // 2, height, width), BF16)
    return run(
        fold_last_kernel,
        "fold_last",
        (own1, got1, own2, got2),
        [vmem()] * 4,
        (first, first, second, second),
        [vmem()] * 4,
    )


def fold_z_kernel(own1, got1, own2, got2, keep, send):
    height = own2.shape[1]
    each = height + TAIL
    for i, out in enumerate((keep, send)):
        at = pl.ds(i * each, height)
        out[:height] = (own1[at].astype(F32) + got1[at].astype(F32)).astype(BF16)
        at = pl.ds(i * each + height, TAIL)
        out[height:each] = encode(decode(own1[at]) + decode(got1[at]))
        out[each:] = (own2[i].astype(F32) + got2[i].astype(F32)).astype(BF16)


def fold_z(own1, got1, own2, got2):
    _, height, width = own2.shape
    out = array((2 * height + TAIL, width), BF16)
    return run(
        fold_z_kernel,
        "fold_z",
        (own1, got1, own2, got2),
        [vmem()] * 4,
        (out, out),
        [vmem()] * 2,
    )


def fold_add_kernel(own1, got1, own2, got2, out1, out2):
    for own, got, out in ((own1, got1, out1), (own2, got2, out2)):
        out[...] = (own[...].astype(F32) + got[...].astype(F32)).astype(BF16)


def fold_add(own1, got1, own2, got2):
    out = array(own1.shape, BF16)
    return run(
        fold_add_kernel,
        "fold_add",
        (own1, got1, own2, got2),
        [vmem()] * 4,
        (out, out),
        [vmem()] * 2,
    )


def fold_feed_kernel(first1, own1, got1, first2, own2, got2, keep1, send1, keep2, send2):
    width = own1.shape[2]
    half = keep1.shape[0]
    for first, own, got, outs in (
        (first1, own1, got1, (keep1, send1)),
        (first2, own2, got2, (keep2, send2)),
    ):
        for i, out in enumerate(outs):
            at = pl.ds(i * half, half)
            out[:, :, :width] = first[at]
            out[:, :, width:] = (own[at].astype(F32) + got[at].astype(F32)).astype(BF16)


def fold_feed(first1, own1, got1, first2, own2, got2):
    count, height, width = own1.shape
    out = array((count // 2, height, 2 * width), BF16)
    return run(
        fold_feed_kernel,
        "fold_feed",
        (first1, own1, got1, first2, own2, got2),
        [vmem()] * 6,
        (out,) * 4,
        [vmem()] * 4,
    )


def fold_sides_kernel(own1, got1, own2, got2, keep, send):
    width = own1.shape[2]
    half = keep.shape[0]
    for side, (own, got) in enumerate(((own1, got1), (own2, got2))):
        for i, out in enumerate((keep, send)):
            at = pl.ds(i * half, half)
            total = own[at].astype(F32) + got[at].astype(F32)
            out[:, :, side * width : (side + 1) * width] = total.astype(BF16)


def fold_sides(own1, got1, own2, got2):
    count, height, width = own1.shape
    out = array((count // 2, height, 2 * width), BF16)
    return run(
        fold_sides_kernel,
        "fold_sides",
        (own1, got1, own2, got2),
        [vmem()] * 4,
        (out, out),
        [vmem()] * 2,
    )


BY_Z = (0, 4, 2, 6)
Y_MAJOR = BY_Z + tuple(z + 1 for z in BY_Z)
OWN = tuple((0, j) for j in Y_MAJOR)
OTHER = tuple((1, j) for j in Y_MAJOR)
CHIP_NEAR = tuple((chip, z) for chip in range(2) for z in BY_Z)
CHIP_FAR = tuple((chip, z + 1) for chip in range(2) for z in BY_Z)


def split_kernel(other, info, first, second, out, sems):
    slot = 1 - info[1] if other else info[1]
    half = first.shape[1] // 2
    copies = []
    for i, values in enumerate((first, second)):
        for j in range(2):
            at = pl.ds(j * half, half)
            copies.append(
                pltpu.make_async_copy(values.at[slot, at], out.at[i, at], sems.at[2 * i + j])
            )
    for copy in copies:
        copy.start()
    for copy in copies:
        copy.wait()


def split(info, first, second, other):
    return run(
        functools.partial(split_kernel, other),
        "split",
        (info, *in_hbm((first, second))),
        [smem()] + [anywhere()] * 2,
        (array((2,) + first.shape[1:], first.dtype),),
        [vmem()],
        [pltpu.SemaphoreType.DMA((4,))],
    )[0]


def merge_kernel(info, own, got, core_own, core_got, out, sems):
    core = info[2]
    copies = []
    for half, (mine, other) in enumerate(((own, core_own), (got, core_got))):
        copies += [
            pltpu.make_async_copy(mine.at[0], out.at[half, core], sems.at[2 * half]),
            pltpu.make_async_copy(other.at[0], out.at[half, 1 - core], sems.at[2 * half + 1]),
        ]
    for copy in copies:
        copy.start()
    for copy in copies:
        copy.wait()


def merge(info, quarters):
    _, quarter, width = quarters[0].shape
    out = run(
        merge_kernel,
        "merge",
        (info, *quarters),
        [smem()] + [anywhere()] * 4,
        (array((2, 2, quarter, width), quarters[0].dtype),),
        [anywhere()],
        [pltpu.SemaphoreType.DMA((4,))],
    )[0]
    return out.reshape(4 * quarter, width)


def halves_kernel(info, rows_ref, own, send, sems):
    quarter = own.shape[0]
    copies = []
    for half, out in enumerate((own, send)):
        at = pl.multiple_of((2 * half + info[2]) * quarter, quarter)
        copies.append(pltpu.make_async_copy(rows_ref.at[pl.ds(at, quarter)], out, sems.at[half]))
    for copy in copies:
        copy.start()
    for copy in copies:
        copy.wait()


def halves(info, values):
    seq, width = values.shape
    out = array((seq // 4, width), values.dtype)
    return run(
        halves_kernel,
        "halves",
        (info, values),
        [smem(), anywhere()],
        (out, out),
        [anywhere()] * 2,
        [pltpu.SemaphoreType.DMA((2,))],
    )


def slots_kernel(info, own, other, out, sems):
    copies = [
        pltpu.make_async_copy(own, out.at[info[1]], sems.at[0]),
        pltpu.make_async_copy(other, out.at[1 - info[1]], sems.at[1]),
    ]
    for copy in copies:
        copy.start()
    for copy in copies:
        copy.wait()


def slots_of(info, own, other):
    return run(
        slots_kernel,
        "slots",
        (info, own, other),
        [smem()] + [anywhere()] * 2,
        (array((2,) + own.shape, own.dtype),),
        [anywhere()],
        [pltpu.SemaphoreType.DMA((2,))],
    )[0]


def tokens_add_kernel(count, mine, *rest):
    got, own, sends = rest[:count], rest[count], rest[count + 1 :]
    per = count // 2
    height = got[0].shape[0]
    for k, part in enumerate(got):
        at = k % per * height
        total = mine[k // per, pl.ds(at, height)] + part[...].astype(F32)
        if k < per:
            own[pl.ds(at, height)] = total
        else:
            each = sends[0].shape[0]
            for first in range(0, height, each):
                sends[(at + first) // each][...] = total[first : first + each].astype(BF16)


def tokens_add(mine, got):
    _, quarter, width = mine.shape
    send = array((quarter // 2, width), BF16)
    return run(
        functools.partial(tokens_add_kernel, len(got)),
        "tokens_add",
        (mine, *got),
        [vmem()] * (1 + len(got)),
        (array((quarter, width), F32), send, send),
        [vmem()] * 3,
    )


def tokens_out_kernel(info, own, *rest):
    *got, out = rest
    out[info[1]] = own[...]
    height = got[0].shape[0]
    for k, part in enumerate(got):
        out[1 - info[1], pl.ds(k * height, height), :] = part[...].astype(F32)


def tokens_out(info, own, got):
    return run(
        tokens_out_kernel,
        "tokens_out",
        (info, own, *got),
        [smem()] + [vmem()] * (1 + len(got)),
        (array((2,) + own.shape, F32),),
        [vmem()],
    )[0]


def feed_out_kernel(own, got, up, down):
    half = up.shape[1] // 2
    for i in range(4):
        at = pl.ds(i * half, half)
        total = own[0, :, at].astype(F32) + got[0, :, at].astype(F32)
        out = (down, up)[i % 2]
        out[:, pl.ds(i // 2 * half, half)] = total


def feed_out(own, got):
    _, height, width = own.shape
    out = array((height, width // 2), F32)
    return run(
        feed_out_kernel,
        "feed_out",
        (own, got),
        [vmem()] * 2,
        (out, out),
        [vmem()] * 2,
    )


def attend_out_kernel(a, b, query, key, value, out, gain1, bias1, gain2, bias2):
    height = query.shape[0]

    def both(first, last):
        return a[first:last].astype(F32) + b[first:last].astype(F32)

    one = both(0, height)
    two = both(height + TAIL, 2 * height + TAIL)
    at = pl.ds(height, TAIL)
    sums = decode(a[at]) + decode(b[at])
    for i, ref in enumerate((query, key, value)):
        ref[...] = jnp.concatenate(
            [two[:, 2 * i * HD : 2 * (i + 1) * HD], one[:, (3 + i) * HD : (4 + i) * HD]], axis=1
        )
    out[...] = jnp.transpose(one[:, : 3 * HD])
    for i, ref in enumerate((gain1, bias1, gain2, bias2)):
        ref[...] = jnp.concatenate([sums[i], sums[4 + i]], axis=0)


def attend_out(pieces, height):
    cols = pieces[0].shape[1]
    span = cols // 2
    return run(
        attend_out_kernel,
        "attend_out",
        tuple(pieces),
        [vmem()] * 2,
        (array((height, span), F32),) * 3
        + (array((span, height), F32),)
        + (array((2 * cols,), F32),) * 4,
        [vmem()] * 8,
    )


def local(
    tokens,
    w_query,
    w_key,
    w_value,
    w_out,
    w_up,
    w_down,
    gain_attn,
    bias_attn,
    gain_ffn,
    bias_ffn,
    lengths,
    random_blocks,
    cotangent,
):
    ORDER.clear()
    size = lax.axis_size("dp")
    rank = lax.axis_index("mp")
    me = lax.axis_index("dp")
    x, core = rank // 2, rank % 2
    _, quarter, features = tokens.shape
    seq = 4 * quarter
    height = w_query.shape[0]
    span = w_query.shape[1]
    heads = span // HD
    nblocks = seq // BLOCK
    fast = size == 8 and height % 16 == 0

    shift = x * (seq // 2)
    info = jnp.stack([me, x, core, shift]).astype(jnp.int32)
    units = w_up.shape[1]

    blocks = (jnp.arange(nblocks) + x * (nblocks // 2)) % nblocks
    near_blocks = jnp.abs(blocks[:, None] - blocks[None, :]) <= 1
    edge = (blocks == 0) | (blocks == nblocks - 1)
    fixed = near_blocks | edge[:, None] | edge[None, :]

    def table(shard):
        chosen = lax.dynamic_slice_in_dim(random_blocks, shard * heads, heads, 0)
        chosen = jnp.roll(chosen, -x * (nblocks // 2), axis=1)
        hit = jnp.any(chosen[:, None, :, :] == blocks[None, :, None, None], axis=3)
        bias = jnp.where(fixed.T[None] | hit, 0.0, NEGATIVE)
        return jnp.concatenate(
            [
                jnp.zeros((heads, nblocks, HD), F32),
                bias,
                jnp.full((heads, nblocks, 3), -1.0, F32),
                jnp.zeros((heads, nblocks, HD - 3 - nblocks), F32),
            ],
            axis=2,
        )

    mask_own, mask_other = table(rank), table(rank ^ 2)
    mask_ends = jnp.concatenate([mask_own[2:], mask_other[2:]], axis=0)
    g_one, b_one = gain_attn[None], bias_attn[None]
    g_two, b_two = gain_ffn[None], bias_ffn[None]

    if fast:
        flat = (tuple((0, j) for j in Y_MAJOR),)
        got_rows = flip_chip(split(info, tokens, cotangent, True))
        piece = pack(w_query, w_key, w_value, w_out)
        got = flip_dp(piece, 4)
        own_rows = split(info, tokens, cotangent, False)
        (two_attn,) = join([piece, got])
        feed_piece = beside(w_up, w_down.T)
        feed_got = flip_dp(feed_piece, 4)
        got = flip_dp(two_attn, 2)
        z_pair, z_single = join_sides([two_attn, got])
        y_pair, x_single = flip_dp(z_pair, 1), flip_chip(z_single)
        own_pair, near_single = join([z_pair, y_pair], [z_single, x_single])
        other_pair, far_single = flip_chip(own_pair), flip_dp(near_single, 1)
        two_up, two_down = join_sides([feed_piece, feed_got])
        got_up, got_down = flip_dp(two_up, 2), flip_dp(two_down, 2)
        quarters = (own_rows, got_rows, flip_core(own_rows), flip_core(got_rows))
        tok = merge(info, quarters)
        pair_w = ((own_pair, other_pair), (OWN, OTHER))
        single_w = ((near_single, far_single), (CHIP_NEAR, CHIP_FAR))
        own01 = attend(info, lengths, tok, ((own_pair,), flat), True, mask_own[:2])
        z_up, z_down = join([two_up, got_up], [two_down, got_down])
        y_up, x_down = flip_dp(z_up, 1), flip_chip(z_down)
        other01 = attend(info, lengths, tok, ((other_pair,), flat), True, mask_other[:2])
        ends = attend(info, lengths, tok, single_w, False, mask_ends)
        own_up, near_down = join([z_up, y_up], [z_down, x_down])
        other_up, far_down = flip_chip(own_up), flip_dp(near_down, 1)
        up = ((own_up, other_up), (OWN, OTHER))
        down = ((near_down, far_down), (CHIP_NEAR, CHIP_FAR))
    else:
        flat = (((0, 0),),)
        two = (((0, 0),), ((1, 0),))

        def plain(piece):
            own = lax.all_gather(piece, "dp", axis=0, tiled=True)[None]
            return own, flip_chip(own)

        got_rows = flip_chip(split(info, tokens, cotangent, True))
        own_rows = split(info, tokens, cotangent, False)
        quarters = (own_rows, got_rows, flip_core(own_rows), flip_core(got_rows))
        tok = merge(info, quarters)
        thirds = [w_out.T] + [w[:, 2 * HD :] for w in (w_query, w_key, w_value)]
        pair_w = (
            plain(jnp.concatenate([w[:, : 2 * HD] for w in (w_query, w_key, w_value)], axis=1)),
            two,
        )
        single_w = (plain(jnp.concatenate(thirds, axis=1)), two)
        own_up, other_up = plain(w_up)
        own01 = attend(info, lengths, tok, ((pair_w[0][0],), flat), True, mask_own[:2])
        other01 = attend(info, lengths, tok, ((pair_w[0][1],), flat), True, mask_other[:2])
        ends = attend(info, lengths, tok, single_w, False, mask_ends)
    contexts = (own01[3], other01[3], ends[3])
    attn_part = project(info, contexts, single_w, features)
    if not fast:
        up = ((own_up, other_up), two)
        down = (plain(w_down.T), two)
    normal, scale_one, hn = norm_one(tok, attn_part, flip_cores(attn_part), g_one, b_one)

    act1, slope1 = feed_up(info, hn, ((own_up,), flat), units)
    act2, slope2 = feed_up(info, hn, ((other_up,), flat), units)
    mixed = feed_down(info, act1, act2, down, features)
    out, dzb_two, sums_two = norm_two(
        info, lengths, hn, mixed, flip_cores(mixed), quarters, g_two, b_two
    )

    if fast:
        places = (OWN, OTHER, CHIP_NEAR, CHIP_FAR)
        att_slots = tuple((0, j) for j in Y_MAJOR)
    else:
        places = (((0, 0),), ((1, 0),)) * 2
        att_slots = ((0, 0),)

    keep_d1, send_d1, keep_d2, send_d2 = feed_grad(info, dzb_two, act1, act2, places)
    du1, du2, *back = feed_back(info, dzb_two, slope1, slope2, up, down)
    back_got = flip_cores(back)
    keep_u1, send_u1, keep_u2, send_u2 = feed_grad(info, hn, du1, du2, places)
    if fast:
        sum_d1, sum_d2 = fold_add(
            keep_d1, flip_chip(send_d1), keep_d2, flip_dp(send_d2, 1)
        )
    dzb_one, sums_one = norm_one_back(normal, scale_one, dzb_two, back, back_got, g_one)
    d_ends = attend_back(info, dzb_one, single_w, None, ends)
    if fast:
        keep_f1, send_f1, keep_f2, send_f2 = fold_feed(
            sum_d1, keep_u1, flip_chip(send_u1), sum_d2, keep_u2, flip_dp(send_u2, 1)
        )
        got_f1, got_f2 = flip_dp(send_f1, 1), flip_chip(send_f2)
    keep_s, send_s = single_grad(
        info, tok, d_ends, dzb_one, contexts, sums_one, sums_two, places[2:]
    )
    d_other = attend_back(info, dzb_one, single_w, 1, other01)
    grad_b = pair_grad(info, tok, d_other, att_slots)
    if fast:
        got_s = flip_dp(send_s, 1)
        got_b = flip_chip(grad_b)
        keep_f, send_f = fold_sides(keep_f1, got_f1, keep_f2, got_f2)
        got_f = flip_dp(send_f, 2)
    d_own = attend_back(info, dzb_one, single_w, 0, own01)
    grad_a = pair_grad(info, tok, d_own, att_slots)
    if fast:
        keep_a, send_a = fold(grad_a, got_b, 2, 0)
        got_a = flip_dp(send_a, 1)
    mine, *sent = input_back(info, d_own, d_other, d_ends, dzb_one, pair_w, single_w)
    if fast:
        keep_s, send_s = fold(keep_s, got_s, 2, TAIL)
        got_s = flip_chip(send_s)
    if fast:
        keep_f, send_f = fold(keep_f, got_f, 2, 0)
        got_f = flip_dp(send_f, 4)
    own_tok, *send_tok = tokens_add(mine, flip_cores(sent))
    got_tok = [flip_chip(v) for v in send_tok]
    if fast:
        keep_s, send_s, keep_a, send_a = fold_last(keep_s, got_s, keep_a, got_a)
        got_s, got_a = flip_dp(send_s, 2), flip_dp(send_a, 2)
    own_out, send_out = halves(info, out)
    got_out = flip_chip(send_out)
    if fast:
        grad_up, grad_down = feed_out(keep_f, got_f)
    if fast:
        keep_a, send_a = fold_z(keep_s, got_s, keep_a, got_a)
        got_a = flip_dp(send_a, 4)
    grad_tokens = tokens_out(info, own_tok, got_tok)
    output = slots_of(info, own_out, got_out)
    if fast:
        grads = attend_out((keep_a, got_a), height)
        sums = grads[4:]
    else:

        def plain_sum(own, other):
            total = own.astype(F32) + flip_chip(other).astype(F32)
            return lax.psum_scatter(total, "dp", scatter_dimension=0, tiled=True)

        def plain_wide(keep1, send1, keep2, send2):
            return jnp.concatenate([plain_sum(keep1[0], send1[0]), plain_sum(keep2[0], send2[0])], axis=1)

        grad_down = plain_wide(keep_d1, send_d1, keep_d2, send_d2)
        grad_up = plain_wide(keep_u1, send_u1, keep_u2, send_u2)
        grad_single = plain_sum(keep_s[:features], send_s[:features])
        grad_pair = plain_sum(grad_a[0], grad_b[0])
        grads = [
            jnp.concatenate(
                [
                    grad_pair[:, 2 * i * HD : 2 * (i + 1) * HD],
                    grad_single[:, (3 + i) * HD : (4 + i) * HD],
                ],
                axis=1,
            )
            for i in range(3)
        ] + [grad_single[:, : 3 * HD].T]
        sums = decode(keep_s[features:])
        sums = lax.psum(sums + flip_chip(sums), "dp")
        sums = [jnp.concatenate([sums[i], sums[4 + i]]) for i in range(4)]

    return (
        output,
        grad_tokens,
        *grads[:4],
        grad_up,
        grad_down.T,
        *sums,
    )


def solution(mesh):
    return jax.shard_map(
        local,
        mesh=mesh,
        in_specs=(
            P("dp", "mp", None),
            P("dp", "mp"),
            P("dp", "mp"),
            P("dp", "mp"),
            P("mp", "dp"),
            P("dp", "mp"),
            P("mp", "dp"),
            P(),
            P(),
            P(),
            P(),
            P("dp"),
            P(),
            P("dp", "mp", None),
        ),
        out_specs=(
            P("dp", "mp", None),
            P("dp", "mp", None),
            P("dp", "mp"),
            P("dp", "mp"),
            P("dp", "mp"),
            P("mp", "dp"),
            P("dp", "mp"),
            P("mp", "dp"),
            P(),
            P(),
            P(),
            P(),
        ),
        check_vma=False,
    )
```

```python
import functools

import jax
import jax.numpy as jnp
from jax import lax
from jax.experimental import pallas as pl
from jax.experimental.pallas import tpu as pltpu
from jax.sharding import PartitionSpec as P

HD = 64
BLOCK = 64
LANES = 128
TILE = 256
SENT = 256
EPSILON = 1e-12
TAIL = 32
TOKEN = (8, 128)
ROOM = {
    "attend": 24,
    "attend_back": 28,
    "project": 16,
    "input_back": 24,
    "norm_one": 16,
    "norm_two": 24,
    "norm_one_back": 24,
    "feed_up": 20,
    "feed_down": 24,
    "feed_back": 40,
    "feed_grad": 28,
    "pair_grad": 16,
    "single_grad": 28,
    "join": 1,
    "join_sides": 1,
    "beside": 1,
    "pack": 2,
    "split": 4,
    "merge": 1,
    "fold": 6,
    "fold_add": 8,
    "fold_feed": 10,
    "fold_sides": 8,
    "fold_last": 6,
    "fold_z": 4,
    "halves": 1,
    "slots": 1,
    "tokens_add": 8,
    "tokens_out": 8,
    "feed_out": 6,
    "attend_out": 6,
}
SCALE = 0.125
LOG2E = 1.4426950408889634
LN2 = 0.6931471805599453
NEGATIVE = -1e30
F32 = jnp.float32
BF16 = jnp.bfloat16

CORE_SWAP = [(0, 1), (1, 0), (2, 3), (3, 2)]
CHIP_SWAP = [(0, 2), (2, 0), (1, 3), (3, 1)]


def nn(a, b):
    return lax.dot_general(a, b, (((1,), (0,)), ((), ())), preferred_element_type=F32)


def nt(a, b):
    return lax.dot_general(a, b, (((1,), (1,)), ((), ())), preferred_element_type=F32)


def tn(a, b):
    return lax.dot_general(a, b, (((0,), (0,)), ((), ())), preferred_element_type=F32)


def vmem():
    return pl.BlockSpec(memory_space=pltpu.VMEM)


def smem():
    return pl.BlockSpec(memory_space=pltpu.SMEM)


def anywhere():
    return pl.BlockSpec(memory_space=pl.ANY)


def in_hbm(values):
    return tuple(pltpu.with_memory_space_constraint(v, pltpu.HBM) for v in values)


def rows(width):
    return pl.BlockSpec((TILE, width), lambda i: (i, 0))


def whole(shape):
    return pl.BlockSpec(shape, lambda i: (0,) * len(shape))


def array(shape, dtype):
    return jax.ShapeDtypeStruct(shape, dtype)


ORDER = []


def run(kernel, name, args, specs, outs, out_specs, scratch=(), *, grid=()):
    given, made = len(args), len(outs)
    extra = tuple(ORDER)

    def body(*refs):
        ins, rest = refs[:given], refs[given + len(extra) :]
        rest[made][...] = jnp.zeros(TOKEN, F32)
        kernel(*ins, *rest[:made], *rest[made + 1 :])

    token_spec = whole(TOKEN) if grid else vmem()
    results = pl.pallas_call(
        body,
        grid=grid,
        out_shape=tuple(outs) + (array(TOKEN, F32),),
        in_specs=list(specs) + [anywhere()] * len(extra),
        out_specs=tuple(out_specs) + (token_spec,),
        scratch_shapes=list(scratch),
        compiler_params=pltpu.CompilerParams(vmem_limit_bytes=ROOM[name] * 2**20),
        cost_estimate=pl.CostEstimate(flops=1, bytes_accessed=0, transcendentals=0),
        name=name,
    )(*args, *extra)
    ORDER[:] = [results[-1]]
    return results[:-1]


def put_rows(parts, value):
    height = parts[0].shape[0]
    tile = value.shape[0]
    i = pl.program_id(0)
    for k, part in enumerate(parts):
        if height <= tile:
            per = tile // height

            @pl.when(i == k // per)
            def _(k=k, part=part):
                at = k % per * height
                part[...] = value[at : at + height]

        else:
            per = height // tile

            @pl.when(i // per == k)
            def _(part=part):
                part[pl.ds(pl.multiple_of(i % per * tile, tile), tile), :] = value


def get_sum(parts, more, count):
    height = parts[0].shape[0]
    tile = len(parts) * height // count
    i = pl.program_id(0)
    total = None
    if height <= tile:
        per = tile // height
        for k in range(count):
            pieces = [
                a[...].astype(F32) + b[...].astype(F32)
                for a, b in zip(parts[k * per : (k + 1) * per], more[k * per : (k + 1) * per])
            ]
            value = pieces[0] if per == 1 else jnp.concatenate(pieces, axis=0)
            total = value if k == 0 else jnp.where(i == k, value, total)
    else:
        per = height // tile
        at = pl.ds(pl.multiple_of(i % per * tile, tile), tile)
        for k, (a, b) in enumerate(zip(parts, more)):
            value = a[at, :].astype(F32) + b[at, :].astype(F32)
            total = value if k == 0 else jnp.where(i // per == k, value, total)
    return total


def far(shape, dtype):
    return pltpu.HBM(shape, dtype)


def tiles(seq, width, height):
    parts = (array((height, width), BF16),) * (seq // height)
    return parts, [whole((height, width))] * len(parts)


def place(me, refs, slots, dst_ref, first=0, last=None, only=None, to=0):
    for ref, of in zip(refs, slots):
        height, width = ref.shape[1], ref.shape[2]
        end = width if last is None else last
        for e, (chip, j) in enumerate(of):
            if only is not None and chip != only:
                continue
            at = 0 if height == dst_ref.shape[0] else pl.multiple_of((me ^ j) * height, height)
            at_column = to + (0 if only is not None else chip * (end - first))
            dst_ref[pl.ds(at, height), pl.ds(at_column, end - first)] = ref[e, :, first:end]


def pick(me, fulls, out_ref, slots, first):
    _, height, width = out_ref.shape
    for e, (chip, j) in enumerate(slots):
        full = fulls[chip]
        at = 0 if height == full.shape[0] else pl.multiple_of((me ^ j) * height, height)
        out_ref[e] = full[pl.ds(at, height), pl.ds(first, width)].astype(BF16)


def attend_kernel(slots, columns, only, places, info, lengths, tok, mask, *rest):
    refs, (qa, ka, va, ctx, wfull) = rest[: len(slots)], rest[len(slots) :]
    seq = tok.shape[0]
    place(info[0], refs, slots, wfull, *columns, only)
    lane = lax.broadcasted_iota(jnp.int32, (TILE, LANES), 1)
    row0 = lax.broadcasted_iota(jnp.int32, (TILE, LANES), 0)
    for t in range(seq // TILE):
        at = pl.ds(t * TILE, TILE)
        row = row0 + t * TILE
        made = nn(tok[at, :], wfull[...])
        onehot = jnp.where(lane - HD == row // BLOCK, 1.0, 0.0)[:, HD:]
        position = row + info[3]
        position = jnp.where(position >= seq, position - seq, position)
        dead = (position >= lengths[info[1]]) & (lane >= HD) & (lane < HD + 16)
        for h, (q_at, k_at, v_at) in enumerate(places):
            q = made[:, q_at : q_at + HD] * (SCALE * LOG2E)
            k = made[:, k_at : k_at + HD]
            v = made[:, v_at : v_at + HD]
            qa[h, at, :] = jnp.concatenate([q, onehot], axis=1).astype(BF16)
            per = TILE // BLOCK
            table = jnp.concatenate(
                [
                    jnp.broadcast_to(mask[h, t * per + b : t * per + b + 1, :], (BLOCK, LANES))
                    for b in range(per)
                ],
                axis=0,
            )
            table = jnp.where(dead, NEGATIVE, table)
            ka[h, at, :] = jnp.concatenate([k, table[:, HD:]], axis=1).astype(BF16)
            va[h, at, :] = jnp.concatenate([v, jnp.full((TILE, HD), -1.0, F32)], axis=1).astype(BF16)
    for t in range(seq // TILE):
        at = pl.ds(t * TILE, TILE)
        pieces = []
        for h in range(len(places)):
            q = qa[h, at, :]
            s = nt(q, ka[h])
            top = jnp.max(s, axis=1, keepdims=True)
            p = jnp.exp2(s - top).astype(BF16)
            got = nn(p, va[h])
            total = -got[:, HD:]
            pieces.append(got[:, :HD] / total)
            log = top + jnp.log2(-got)
            hi = log.astype(BF16).astype(F32)
            mid = (log - hi).astype(BF16).astype(F32)
            low = log - hi - mid
            new = jnp.where(
                lane == HD + 16,
                hi,
                jnp.where(lane == HD + 17, mid, jnp.where(lane == HD + 18, low, q.astype(F32))),
            )
            qa[h, at, :] = new.astype(BF16)
        ctx[at, :] = jnp.concatenate(pieces, axis=1).astype(BF16)


PAIR = ((0, 2 * HD, 4 * HD), (HD, 3 * HD, 5 * HD))
SINGLES = ((HD, 2 * HD, 3 * HD), (5 * HD, 6 * HD, 7 * HD))


def attend(info, lengths, tok, gathered, pair, mask):
    arrays, slots = gathered
    seq, width = tok.shape
    aug = far((2, seq, LANES), BF16)
    columns, only, cols = ((0, 6 * HD), 0, 6 * HD) if pair else ((2 * HD, 6 * HD), None, 8 * HD)
    return run(
        functools.partial(attend_kernel, slots, columns, only, PAIR if pair else SINGLES),
        "attend",
        (info, lengths, tok, mask) + arrays,
        [smem()] * 2 + [vmem()] * (2 + len(arrays)),
        (aug, aug, aug, array((seq, LANES), BF16)),
        [vmem()] * 4,
        [pltpu.VMEM((width, cols), BF16)],
    )


def place_out(me, refs, slots, pairs, ends):
    place(me, refs, slots, pairs, 0, 2 * HD)
    place(me, refs, slots, ends, 2 * HD, 4 * HD)
    both = ends[...]
    ends[:, :LANES] = jnp.concatenate([both[:, :HD], both[:, LANES : LANES + HD]], axis=1)


def project_kernel(slots, info, own, other, ends, *rest):
    refs, parts, (w1, w2) = rest[: len(slots)], rest[len(slots) : -2], rest[-2:]

    @pl.when(pl.program_id(0) == 0)
    def _():
        place_out(info[0], refs, slots, w1, w2)

    both = jnp.concatenate([own[...], other[...]], axis=1)
    put_rows(parts, (nt(both, w1[...]) + nt(ends[...], w2[:, :LANES])).astype(BF16))


def project(info, contexts, gathered, width):
    arrays, slots = gathered
    seq = contexts[0].shape[0]
    return run(
        functools.partial(project_kernel, slots),
        "project",
        (info,) + contexts + arrays,
        [smem()] + [rows(LANES)] * 3 + [whole(a.shape) for a in arrays],
        *tiles(seq, width, 2 * TILE),
        [pltpu.VMEM((width, 2 * LANES), BF16)] * 2,
        grid=(seq // TILE,),
    )


def attend_back_kernel(slots, chip, info, dz, qa, ka, va, ctx, *rest):
    refs, (dqkv, pairs, ends, da) = rest[: len(slots)], rest[len(slots) :]
    seq = dz.shape[0]
    heads = qa.shape[0]
    if chip is None:
        place_out(info[0], refs, slots, pairs, ends)
        wfull = ends.at[:, pl.ds(0, LANES)]
    else:
        place(info[0], refs, slots, pairs, 0, 2 * HD, chip)
        wfull = pairs.at[:, pl.ds(0, LANES)]
    lane = lax.broadcasted_iota(jnp.int32, (TILE, LANES), 1)
    for t in range(seq // TILE):
        at = pl.ds(t * TILE, TILE)
        dctx = nn(dz[at, :], wfull[...]).astype(BF16).astype(F32)
        both = dctx * ctx[at, :].astype(F32)
        for h in range(heads):
            inner = jnp.sum(both[:, h * HD : (h + 1) * HD], axis=1, keepdims=True)
            hi = inner.astype(BF16).astype(F32)
            mid = (inner - hi).astype(BF16).astype(F32)
            low = inner - hi - mid
            one = jnp.concatenate(
                [dctx[:, h * HD : (h + 1) * HD], jnp.zeros((TILE, HD), F32)], axis=1
            )
            one = jnp.where(lane == HD, hi, one)
            one = jnp.where(lane == HD + 1, mid, one)
            one = jnp.where(lane == HD + 2, low, one)
            da[h, at, :] = one.astype(BF16)

    def turned(values):
        return jnp.transpose(values.astype(F32))[:HD].astype(BF16)

    grads = []
    for h in range(heads):
        k_turned, q_turned, d_turned = turned(ka[h]), turned(qa[h]), turned(da[h])
        dq, dk, dv = None, [], []
        for t in range(seq // TILE):
            at = pl.ds(t * TILE, TILE)
            p = jnp.exp2(nt(ka[h, at, :], qa[h]))
            ds = (p * nt(va[h, at, :], da[h])).astype(BF16)
            dv.append(nt(d_turned, p.astype(BF16)))
            dk.append(nt(q_turned, ds))
            more = nn(k_turned[:, t * TILE : (t + 1) * TILE], ds)
            dq = more if dq is None else dq + more
        dk = jnp.concatenate(dk, axis=1) * LN2
        grads.append((dq * SCALE, dk, jnp.concatenate(dv, axis=1)))
    (dq0, dk0, dv0), (dq1, dk1, dv1) = grads
    if chip is None:
        blank = jnp.zeros_like(dq0)
        stacks = ((blank, dq0), (dk0, dv0), (blank, dq1), (dk1, dv1))
    else:
        stacks = ((dq0, dq1), (dk0, dk1), (dv0, dv1))
    for i, stack in enumerate(stacks):
        both = jnp.transpose(jnp.concatenate(stack, axis=0))
        dqkv[:, i * LANES : (i + 1) * LANES] = both.astype(BF16)


def attend_back(info, dz, gathered, chip, saved):
    arrays, slots = gathered
    qa, ka, va, ctx = saved
    seq, width = dz.shape
    cols = 8 * HD if chip is None else 6 * HD
    return run(
        functools.partial(attend_back_kernel, slots, chip),
        "attend_back",
        (info, dz, qa, ka, va, ctx) + arrays,
        [smem()] + [vmem()] * (5 + len(arrays)),
        (array((seq, cols), BF16),),
        [vmem()],
        [
            pltpu.VMEM((width, 2 * LANES), BF16),
            pltpu.VMEM((width, 2 * LANES), BF16),
            pltpu.VMEM((2, seq, LANES), BF16),
        ],
    )[0]


def input_back_kernel(slots1, slots2, info, own, other, ends, dz, *rest):
    n1, n2 = len(slots1), len(slots2)
    refs1, refs2, (mine, *sent, w1, w2) = rest[:n1], rest[n1 : n1 + n2], rest[n1 + n2 :]
    i = pl.program_id(0)

    @pl.when(i == 0)
    def _():
        place(info[0], refs1, slots1, w1)
        place(info[0], refs2, slots2, w2, 2 * HD, 6 * HD)

    pairs = jnp.concatenate([own[...], other[...]], axis=1)
    back = nt(pairs, w1[...]) + nt(ends[...], w2[...])

    @pl.when(i % 2 == info[2])
    def _():
        mine[i // 2] = back + dz[...].astype(F32)

    per = len(sent) // 2
    height = sent[0].shape[0]
    for k, part in enumerate(sent):

        @pl.when((i % 2 != info[2]) & (i // 2 == k // per))
        def _(k=k, part=part):
            part[...] = back[k % per * height : (k % per + 1) * height].astype(BF16)


def input_back(info, own, other, ends, dz, gathered1, gathered2):
    seq, width = dz.shape
    arrays = gathered1[0] + gathered2[0]
    halves = (seq // TILE // 2, TILE, width)
    grads = (own, other, ends, dz)
    return run(
        functools.partial(input_back_kernel, gathered1[1], gathered2[1]),
        "input_back",
        (info,) + grads + arrays,
        [smem()] + [rows(g.shape[1]) for g in grads] + [whole(a.shape) for a in arrays],
        (array(halves, F32),) + (array((SENT, width), BF16),) * (seq // 2 // SENT),
        [whole(halves)] + [whole((SENT, width))] * (seq // 2 // SENT),
        [pltpu.VMEM((width, 12 * HD), BF16), pltpu.VMEM((width, 8 * HD), BF16)],
        grid=(seq // TILE,),
    )


def center(z):
    mean = jnp.mean(z, axis=1, keepdims=True)
    moved = z - mean
    spread = jnp.mean(moved * moved, axis=1, keepdims=True)
    scale = lax.rsqrt(spread + EPSILON)
    return moved * scale, scale


def norm_back(n, scale, gy, gain):
    dn = gy * gain
    return scale * (
        dn - jnp.mean(dn, axis=1, keepdims=True) - n * jnp.mean(dn * n, axis=1, keepdims=True)
    )


def add_sums(gy, n, sums):
    i = pl.program_id(0)

    @pl.when(i == 0)
    def _():
        sums[...] = jnp.zeros_like(sums)

    sums[0:1, :] += jnp.sum(gy * n, axis=0, keepdims=True)
    sums[1:2, :] += jnp.sum(gy, axis=0, keepdims=True)


def norm_one_kernel(tok, gain, bias, *rest):
    *parts, normal, scale, hn = rest
    count = len(parts) // 2
    value = tok[...].astype(F32) + get_sum(parts[:count], parts[count:], count * parts[0].shape[0] // TILE)
    n, r = center(value)
    normal[...] = n.astype(BF16)
    scale[...] = r
    hn[...] = (n * gain[...] + bias[...]).astype(BF16)


def norm_one(tok, p0, p1, gain, bias):
    seq, width = tok.shape
    return run(
        norm_one_kernel,
        "norm_one",
        (tok, gain, bias, *p0, *p1),
        [rows(width)] + [whole((1, width))] * 2 + [whole(p.shape) for p in (*p0, *p1)],
        (array((seq, width), BF16), array((seq, 1), F32), array((seq, width), BF16)),
        (rows(width), rows(1), rows(width)),
        grid=(seq // TILE,),
    )


def norm_two_kernel(info, lengths, hn, own, got, core_own, core_got, gain, bias, *rest):
    *parts, out, dzb, sums = rest
    count = len(parts) // 2
    value = hn[...].astype(F32) + get_sum(parts[:count], parts[count:], count * parts[0].shape[0] // TILE)
    n, scale = center(value)
    out[...] = (n * gain[...] + bias[...]).astype(BF16)
    row = lax.broadcasted_iota(jnp.int32, value.shape, 0) + pl.program_id(0) * TILE
    seq = pl.num_programs(0) * TILE
    position = row + info[3]
    position = jnp.where(position >= seq, position - seq, position)
    i = pl.program_id(0)
    mine = i % 2 == info[2]
    cot = jnp.where(
        i < 2,
        jnp.where(mine, own[0].astype(F32), core_own[0].astype(F32)),
        jnp.where(mine, got[0].astype(F32), core_got[0].astype(F32)),
    )
    gy = jnp.where(position < lengths[info[1]], cot, 0.0)
    dzb[...] = norm_back(n, scale, gy, gain[...]).astype(BF16)
    add_sums(gy, n, sums)


def norm_two(info, lengths, hn, m0, m1, cot, gain, bias):
    seq, width = hn.shape
    return run(
        norm_two_kernel,
        "norm_two",
        (info, lengths, hn, *cot, gain, bias, *m0, *m1),
        [smem(), smem(), rows(width)]
        + [pl.BlockSpec((1,) + c.shape[1:], lambda i: (1, 0, 0)) for c in cot]
        + [whole((1, width))] * 2
        + [whole(p.shape) for p in (*m0, *m1)],
        (
            array((seq, width), BF16),
            array((seq, width), BF16),
            array((2, width), F32),
        ),
        (rows(width), rows(width), whole((2, width))),
        grid=(seq // TILE,),
    )


def norm_one_back_kernel(normal, scale, dz2, gain, *rest):
    *parts, dzb, sums = rest
    count = len(parts) // 2
    n = normal[...].astype(F32)
    gy = dz2[...].astype(F32)
    gy = gy + get_sum(parts[:count], parts[count:], count * parts[0].shape[0] // TILE)
    dzb[...] = norm_back(n, scale[...], gy, gain[...]).astype(BF16)
    add_sums(gy, n, sums)


def norm_one_back(normal, scale, dz2, p0, p1, gain):
    seq, width = normal.shape
    return run(
        norm_one_back_kernel,
        "norm_one_back",
        (normal, scale, dz2, gain, *p0, *p1),
        [rows(width), rows(1), rows(width)]
        + [whole((1, width))]
        + [whole(p.shape) for p in (*p0, *p1)],
        (array((seq, width), BF16), array((2, width), F32)),
        (rows(width), whole((2, width))),
        grid=(seq // TILE,),
    )


def gelu_pair(u):
    phi = 0.5 + 0.5 * lax.erf(u * 0.7071067811865476)
    return u * phi, phi + u * (jnp.exp(-0.5 * u * u) * 0.3989422804014327)


def feed_up_kernel(slots, info, hn, *rest):
    refs, (active, slope, wfull) = rest[: len(slots)], rest[len(slots) :]

    @pl.when(pl.program_id(0) == 0)
    def _():
        place(info[0], refs, slots, wfull)

    a, g = gelu_pair(nn(hn[...], wfull[...]))
    active[...] = a.astype(BF16)
    slope[...] = g.astype(BF16)


def feed_up(info, hn, gathered, units):
    arrays, slots = gathered
    seq, width = hn.shape
    return run(
        functools.partial(feed_up_kernel, slots),
        "feed_up",
        (info, hn) + arrays,
        [smem(), rows(width)] + [whole(a.shape) for a in arrays],
        (array((seq, units), BF16), array((seq, units), BF16)),
        (rows(units), rows(units)),
        [pltpu.VMEM((width, units), BF16)],
        grid=(seq // TILE,),
    )


def feed_down_kernel(slots, info, act1, act2, *rest):
    refs, parts, wfull = rest[: len(slots)], rest[len(slots) : -1], rest[-1]

    @pl.when(pl.program_id(0) == 0)
    def _():
        place(info[0], refs, slots, wfull)

    both = jnp.concatenate([act1[...], act2[...]], axis=1)
    put_rows(parts, nt(both, wfull[...]).astype(BF16))


def feed_down(info, act1, act2, gathered, width):
    seq, units = act1.shape
    arrays, slots = gathered
    return run(
        functools.partial(feed_down_kernel, slots),
        "feed_down",
        (info, act1, act2) + arrays,
        [smem(), rows(units), rows(units)] + [whole(a.shape) for a in arrays],
        *tiles(seq, width, seq),
        [pltpu.VMEM((width, 2 * units), BF16)],
        grid=(seq // TILE,),
    )


def feed_back_kernel(slots_up, slots_down, info, dzb, slope1, slope2, *rest):
    n1, n2 = len(slots_up), len(slots_down)
    ups, downs, (du1, du2, *parts, up, down) = rest[:n1], rest[n1 : n1 + n2], rest[n1 + n2 :]

    @pl.when(pl.program_id(0) == 0)
    def _():
        place(info[0], ups, slots_up, up)
        place(info[0], downs, slots_down, down)

    units = du1.shape[1]
    out = None
    for i, (slope, du) in enumerate(((slope1, du1), (slope2, du2))):
        at = pl.ds(i * units, units)
        grad = (nn(dzb[...], down[:, at]) * slope[...].astype(F32)).astype(BF16)
        du[...] = grad
        more = nt(grad, up[:, at])
        out = more if out is None else out + more
    put_rows(parts, out.astype(BF16))


def feed_back(info, dzb, slope1, slope2, up, down):
    seq, width = dzb.shape
    units = slope1.shape[1]
    arrays = up[0] + down[0]
    parts, part_specs = tiles(seq, width, TILE)
    return run(
        functools.partial(feed_back_kernel, up[1], down[1]),
        "feed_back",
        (info, dzb, slope1, slope2) + arrays,
        [smem(), rows(width), rows(units), rows(units)] + [whole(a.shape) for a in arrays],
        (array((seq, units), BF16),) * 2 + parts,
        [rows(units)] * 2 + part_specs,
        [pltpu.VMEM((width, 2 * units), BF16)] * 2,
        grid=(seq // TILE,),
    )


def feed_grad_kernel(places, info, a, d1, d2, *rest):
    outs, fulls = rest[:4], rest[4:]
    half = outs[0].shape[2]
    fulls[0][...] = tn(a[...], d1[...])
    fulls[1][...] = tn(a[...], d2[...])
    for i, out in enumerate(outs):
        pick(info[0], fulls, out, places[i], (i // 2) * half)


def feed_grad(info, a, d1, d2, places):
    seq, width = a.shape
    units = d1.shape[1]
    count = len(places[0])
    out = array((count, width // count, units // 2), BF16)
    return run(
        functools.partial(feed_grad_kernel, places),
        "feed_grad",
        (info, a, d1, d2),
        [smem()] + [vmem()] * 3,
        (out,) * 4,
        [vmem()] * 4,
        [pltpu.VMEM((width, units), F32)] * 2,
    )


def pair_grad_kernel(slots, info, tok, d, out, full):
    full[...] = tn(tok[...], d[...])
    pick(info[0], (full,), out, slots, 0)


def pair_grad(info, tok, d, slots):
    seq, width = tok.shape
    cols = d.shape[1]
    return run(
        functools.partial(pair_grad_kernel, slots),
        "pair_grad",
        (info, tok, d),
        [smem()] + [vmem()] * 2,
        (array((len(slots), width // len(slots), cols), BF16),),
        [vmem()],
        [pltpu.VMEM((width, cols), F32)],
    )[0]


def encode(sums):
    hi = sums.astype(BF16).astype(F32)
    mid = (sums - hi).astype(BF16).astype(F32)
    low = sums - hi - mid
    return jnp.concatenate([hi, mid, low, jnp.zeros_like(low)], axis=0).astype(BF16)


def decode(coded):
    values = coded.astype(F32)
    n = values.shape[0] // 4
    return values[:n] + values[n : 2 * n] + values[2 * n : 3 * n]


def single_grad_kernel(places, info, tok, d, dz, own, other, ends, sums_one, sums_two, keep, send, full):
    mine = tn(tok[...], d[...])
    third = tn(dz[...], ends[...])
    blank = jnp.zeros((third.shape[0], HD), F32)
    width = full.shape[2]
    both = jnp.concatenate([sums_one[...], sums_two[...]], axis=0)
    both = encode(jnp.concatenate([both[:, :width], both[:, width:]], axis=0))
    for chip, ctx in enumerate((own, other)):
        full[chip, :, :LANES] = tn(dz[...], ctx[...])
        at = chip * 4 * HD
        o_third = jnp.concatenate([third[:, chip * HD : (chip + 1) * HD], blank], axis=1)
        full[chip, :, LANES : 2 * LANES] = o_third + mine[:, at : at + LANES]
        full[chip, :, 2 * LANES :] = mine[:, at + LANES : at + 2 * LANES]
    for out, slots in zip((keep, send), places):
        count = len(slots)
        height = full.shape[1] // count
        for e, (chip, j) in enumerate(slots):
            at = 0 if count == 1 else pl.multiple_of((info[0] ^ j) * height, height)
            out[pl.ds(e * height, height), :] = full[chip, pl.ds(at, height), :].astype(BF16)
        out[pl.ds(count * height, TAIL), :] = both


def single_grad(info, tok, d, dz, contexts, sums_one, sums_two, places):
    seq, width = tok.shape
    cols = 6 * HD
    out = array((width + TAIL, cols), BF16)
    return run(
        functools.partial(single_grad_kernel, places),
        "single_grad",
        (info, tok, d, dz, *contexts, sums_one, sums_two),
        [smem()] + [vmem()] * 8,
        (out, out),
        [vmem()] * 2,
        [pltpu.VMEM((2, width, cols), F32)],
    )


def across(values, axis, pairs):
    return lax.ppermute(values, axis, pairs)


def flip_chip(values):
    return across(values, "mp", CHIP_SWAP)


def flip_core(values):
    return across(values, "mp", CORE_SWAP)


def flip_cores(parts):
    return [flip_core(p) for p in parts]


def flip_dp(values, distance):
    size = lax.axis_size("dp")
    return across(values, "dp", [(i, i ^ distance) for i in range(size)])


def join_kernel(groups, *refs):
    count = sum(groups)
    parts, outs, sems = refs[:count], refs[count:-1], refs[-1]
    copies = []
    for out, number in zip(outs, groups):
        first = 0
        for part in parts[len(copies) : len(copies) + number]:
            to = out.at[pl.ds(first, part.shape[0])]
            copies.append(pltpu.make_async_copy(part, to, sems.at[len(copies)]))
            first += part.shape[0]
    for copy in copies:
        copy.start()
    for copy in copies:
        copy.wait()


def join(*groups):
    parts = sum((tuple(g) for g in groups), ())
    outs = [array((sum(p.shape[0] for p in g),) + g[0].shape[1:], g[0].dtype) for g in groups]
    return run(
        functools.partial(join_kernel, tuple(len(g) for g in groups)),
        "join",
        parts,
        [anywhere()] * len(parts),
        outs,
        [anywhere()] * len(outs),
        [pltpu.SemaphoreType.DMA((len(parts),))],
    )


def pack_kernel(w_query, w_key, w_value, w_out, out, rows_in, out_in, sems):
    copies = [
        pltpu.make_async_copy(w, rows_in.at[i], sems.at[i])
        for i, w in enumerate((w_query, w_key, w_value))
    ]
    copies.append(pltpu.make_async_copy(w_out, out_in, sems.at[3]))
    for copy in copies:
        copy.start()
    for copy in copies:
        copy.wait()
    for i in range(3):
        out[0, :, 2 * i * HD : 2 * (i + 1) * HD] = rows_in[i, :, : 2 * HD]
    parts = [jnp.transpose(out_in[...].astype(F32))]
    parts += [rows_in[i, :, 2 * HD :].astype(F32) for i in range(3)]
    out[0, :, 6 * HD :] = jnp.concatenate(parts, axis=1).astype(BF16)


def pack(w_query, w_key, w_value, w_out):
    height, span = w_query.shape
    return run(
        pack_kernel,
        "pack",
        in_hbm((w_query, w_key, w_value, w_out)),
        [anywhere()] * 4,
        (array((1, height, 4 * span), BF16),),
        [vmem()],
        [
            pltpu.VMEM((3, height, span), BF16),
            pltpu.VMEM(w_out.shape, BF16),
            pltpu.SemaphoreType.DMA((4,)),
        ],
    )[0]


def beside_kernel(first, second, out, sems):
    width = first.shape[1]
    copies = [
        pltpu.make_async_copy(ref, out.at[0, :, pl.ds(i * width, width)], sems.at[i])
        for i, ref in enumerate((first, second))
    ]
    for copy in copies:
        copy.start()
    for copy in copies:
        copy.wait()


def beside(first, second):
    height, width = first.shape
    return run(
        beside_kernel,
        "beside",
        in_hbm((first, second)),
        [anywhere()] * 2,
        (array((1, height, 2 * width), BF16),),
        [anywhere()],
        [pltpu.SemaphoreType.DMA((2,))],
    )[0]


def join_sides_kernel(count, *refs):
    parts, outs, sems = refs[:count], refs[count : count + 2], refs[count + 2]
    width = outs[0].shape[2]
    copies = []
    each = parts[0].shape[0]
    for i, part in enumerate(parts):
        for side, out in enumerate(outs):
            copies.append(
                pltpu.make_async_copy(
                    part.at[:, :, pl.ds(side * width, width)],
                    out.at[pl.ds(i * each, each)],
                    sems.at[2 * i + side],
                )
            )
    for copy in copies:
        copy.start()
    for copy in copies:
        copy.wait()


def join_sides(parts):
    count = len(parts)
    each, height, width = parts[0].shape
    out = array((count * each, height, width // 2), BF16)
    return run(
        functools.partial(join_sides_kernel, count),
        "join_sides",
        tuple(parts),
        [anywhere()] * count,
        (out, out),
        [anywhere()] * 2,
        [pltpu.SemaphoreType.DMA((2 * count,))],
    )


def fold_kernel(tail, own, got, *outs):
    body = own.shape[0] - tail
    each = body // len(outs)
    for i, out in enumerate(outs):
        at = pl.ds(i * each, each)
        total = (own[at].astype(F32) + got[at].astype(F32)).astype(BF16)
        if tail:
            out[:each] = total
        else:
            out[...] = total
    if tail:
        coded = encode(decode(own[body:]) + decode(got[body:]))
        for out in outs:
            out[each:] = coded


def fold(own, got, parts, tail=0):
    shape = ((own.shape[0] - tail) // parts + tail,) + own.shape[1:]
    return run(
        functools.partial(fold_kernel, tail),
        "fold",
        (own, got),
        [vmem()] * 2,
        (array(shape, BF16),) * parts,
        [vmem()] * parts,
    )


def fold_last_kernel(own1, got1, own2, got2, keep1, send1, keep2, send2):
    height = own2.shape[1]
    each = height + TAIL
    body = own1.shape[0] - TAIL
    coded = encode(decode(own1[body:]) + decode(got1[body:]))
    half = own2.shape[0] // 2
    for i in range(2 * half):
        out, first = (keep1, send1)[i // half], i % half * each
        at = pl.ds(i * height, height)
        out[first : first + height] = (own1[at].astype(F32) + got1[at].astype(F32)).astype(BF16)
        out[first + height : first + each] = coded
        total = own2[i].astype(F32) + got2[i].astype(F32)
        (keep2, send2)[i // half][i % half] = total.astype(BF16)


def fold_last(own1, got1, own2, got2):
    count, height, width = own2.shape
    first = array((count // 2 * (height + TAIL), width), BF16)
    second = array((count // 2, height, width), BF16)
    return run(
        fold_last_kernel,
        "fold_last",
        (own1, got1, own2, got2),
        [vmem()] * 4,
        (first, first, second, second),
        [vmem()] * 4,
    )


def fold_z_kernel(own1, got1, own2, got2, keep, send):
    height = own2.shape[1]
    each = height + TAIL
    for i, out in enumerate((keep, send)):
        at = pl.ds(i * each, height)
        out[:height] = (own1[at].astype(F32) + got1[at].astype(F32)).astype(BF16)
        at = pl.ds(i * each + height, TAIL)
        out[height:each] = encode(decode(own1[at]) + decode(got1[at]))
        out[each:] = (own2[i].astype(F32) + got2[i].astype(F32)).astype(BF16)


def fold_z(own1, got1, own2, got2):
    _, height, width = own2.shape
    out = array((2 * height + TAIL, width), BF16)
    return run(
        fold_z_kernel,
        "fold_z",
        (own1, got1, own2, got2),
        [vmem()] * 4,
        (out, out),
        [vmem()] * 2,
    )


def fold_add_kernel(own1, got1, own2, got2, out1, out2):
    for own, got, out in ((own1, got1, out1), (own2, got2, out2)):
        out[...] = (own[...].astype(F32) + got[...].astype(F32)).astype(BF16)


def fold_add(own1, got1, own2, got2):
    out = array(own1.shape, BF16)
    return run(
        fold_add_kernel,
        "fold_add",
        (own1, got1, own2, got2),
        [vmem()] * 4,
        (out, out),
        [vmem()] * 2,
    )


def fold_feed_kernel(first1, own1, got1, first2, own2, got2, keep1, send1, keep2, send2):
    width = own1.shape[2]
    half = keep1.shape[0]
    for first, own, got, outs in (
        (first1, own1, got1, (keep1, send1)),
        (first2, own2, got2, (keep2, send2)),
    ):
        for i, out in enumerate(outs):
            at = pl.ds(i * half, half)
            out[:, :, :width] = first[at]
            out[:, :, width:] = (own[at].astype(F32) + got[at].astype(F32)).astype(BF16)


def fold_feed(first1, own1, got1, first2, own2, got2):
    count, height, width = own1.shape
    out = array((count // 2, height, 2 * width), BF16)
    return run(
        fold_feed_kernel,
        "fold_feed",
        (first1, own1, got1, first2, own2, got2),
        [vmem()] * 6,
        (out,) * 4,
        [vmem()] * 4,
    )


def fold_sides_kernel(own1, got1, own2, got2, keep, send):
    width = own1.shape[2]
    half = keep.shape[0]
    for side, (own, got) in enumerate(((own1, got1), (own2, got2))):
        for i, out in enumerate((keep, send)):
            at = pl.ds(i * half, half)
            total = own[at].astype(F32) + got[at].astype(F32)
            out[:, :, side * width : (side + 1) * width] = total.astype(BF16)


def fold_sides(own1, got1, own2, got2):
    count, height, width = own1.shape
    out = array((count // 2, height, 2 * width), BF16)
    return run(
        fold_sides_kernel,
        "fold_sides",
        (own1, got1, own2, got2),
        [vmem()] * 4,
        (out, out),
        [vmem()] * 2,
    )


BY_Z = (0, 4, 2, 6)
Y_MAJOR = BY_Z + tuple(z + 1 for z in BY_Z)
OWN = tuple((0, j) for j in Y_MAJOR)
OTHER = tuple((1, j) for j in Y_MAJOR)
CHIP_NEAR = tuple((chip, z) for chip in range(2) for z in BY_Z)
CHIP_FAR = tuple((chip, z + 1) for chip in range(2) for z in BY_Z)


def split_kernel(other, info, first, second, out, sems):
    slot = 1 - info[1] if other else info[1]
    half = first.shape[1] // 2
    copies = []
    for i, values in enumerate((first, second)):
        for j in range(2):
            at = pl.ds(j * half, half)
            copies.append(
                pltpu.make_async_copy(values.at[slot, at], out.at[i, at], sems.at[2 * i + j])
            )
    for copy in copies:
        copy.start()
    for copy in copies:
        copy.wait()


def split(info, first, second, other):
    return run(
        functools.partial(split_kernel, other),
        "split",
        (info, *in_hbm((first, second))),
        [smem()] + [anywhere()] * 2,
        (array((2,) + first.shape[1:], first.dtype),),
        [vmem()],
        [pltpu.SemaphoreType.DMA((4,))],
    )[0]


def merge_kernel(info, own, got, core_own, core_got, out, sems):
    core = info[2]
    copies = []
    for half, (mine, other) in enumerate(((own, core_own), (got, core_got))):
        copies += [
            pltpu.make_async_copy(mine.at[0], out.at[half, core], sems.at[2 * half]),
            pltpu.make_async_copy(other.at[0], out.at[half, 1 - core], sems.at[2 * half + 1]),
        ]
    for copy in copies:
        copy.start()
    for copy in copies:
        copy.wait()


def merge(info, quarters):
    _, quarter, width = quarters[0].shape
    out = run(
        merge_kernel,
        "merge",
        (info, *quarters),
        [smem()] + [anywhere()] * 4,
        (array((2, 2, quarter, width), quarters[0].dtype),),
        [anywhere()],
        [pltpu.SemaphoreType.DMA((4,))],
    )[0]
    return out.reshape(4 * quarter, width)


def halves_kernel(info, rows_ref, own, send, sems):
    quarter = own.shape[0]
    copies = []
    for half, out in enumerate((own, send)):
        at = pl.multiple_of((2 * half + info[2]) * quarter, quarter)
        copies.append(pltpu.make_async_copy(rows_ref.at[pl.ds(at, quarter)], out, sems.at[half]))
    for copy in copies:
        copy.start()
    for copy in copies:
        copy.wait()


def halves(info, values):
    seq, width = values.shape
    out = array((seq // 4, width), values.dtype)
    return run(
        halves_kernel,
        "halves",
        (info, values),
        [smem(), anywhere()],
        (out, out),
        [anywhere()] * 2,
        [pltpu.SemaphoreType.DMA((2,))],
    )


def slots_kernel(info, own, other, out, sems):
    copies = [
        pltpu.make_async_copy(own, out.at[info[1]], sems.at[0]),
        pltpu.make_async_copy(other, out.at[1 - info[1]], sems.at[1]),
    ]
    for copy in copies:
        copy.start()
    for copy in copies:
        copy.wait()


def slots_of(info, own, other):
    return run(
        slots_kernel,
        "slots",
        (info, own, other),
        [smem()] + [anywhere()] * 2,
        (array((2,) + own.shape, own.dtype),),
        [anywhere()],
        [pltpu.SemaphoreType.DMA((2,))],
    )[0]


def tokens_add_kernel(count, mine, *rest):
    got, own, sends = rest[:count], rest[count], rest[count + 1 :]
    per = count // 2
    height = got[0].shape[0]
    for k, part in enumerate(got):
        at = k % per * height
        total = mine[k // per, pl.ds(at, height)] + part[...].astype(F32)
        if k < per:
            own[pl.ds(at, height)] = total
        else:
            each = sends[0].shape[0]
            for first in range(0, height, each):
                sends[(at + first) // each][...] = total[first : first + each].astype(BF16)


def tokens_add(mine, got):
    _, quarter, width = mine.shape
    send = array((quarter // 2, width), BF16)
    return run(
        functools.partial(tokens_add_kernel, len(got)),
        "tokens_add",
        (mine, *got),
        [vmem()] * (1 + len(got)),
        (array((quarter, width), F32), send, send),
        [vmem()] * 3,
    )


def tokens_out_kernel(info, own, *rest):
    *got, out = rest
    out[info[1]] = own[...]
    height = got[0].shape[0]
    for k, part in enumerate(got):
        out[1 - info[1], pl.ds(k * height, height), :] = part[...].astype(F32)


def tokens_out(info, own, got):
    return run(
        tokens_out_kernel,
        "tokens_out",
        (info, own, *got),
        [smem()] + [vmem()] * (1 + len(got)),
        (array((2,) + own.shape, F32),),
        [vmem()],
    )[0]


def feed_out_kernel(own, got, up, down):
    half = up.shape[1] // 2
    for i in range(4):
        at = pl.ds(i * half, half)
        total = own[0, :, at].astype(F32) + got[0, :, at].astype(F32)
        out = (down, up)[i % 2]
        out[:, pl.ds(i // 2 * half, half)] = total


def feed_out(own, got):
    _, height, width = own.shape
    out = array((height, width // 2), F32)
    return run(
        feed_out_kernel,
        "feed_out",
        (own, got),
        [vmem()] * 2,
        (out, out),
        [vmem()] * 2,
    )


def attend_out_kernel(a, b, query, key, value, out, gain1, bias1, gain2, bias2):
    height = query.shape[0]

    def both(first, last):
        return a[first:last].astype(F32) + b[first:last].astype(F32)

    one = both(0, height)
    two = both(height + TAIL, 2 * height + TAIL)
    at = pl.ds(height, TAIL)
    sums = decode(a[at]) + decode(b[at])
    for i, ref in enumerate((query, key, value)):
        ref[...] = jnp.concatenate(
            [two[:, 2 * i * HD : 2 * (i + 1) * HD], one[:, (3 + i) * HD : (4 + i) * HD]], axis=1
        )
    out[...] = jnp.transpose(one[:, : 3 * HD])
    for i, ref in enumerate((gain1, bias1, gain2, bias2)):
        ref[...] = jnp.concatenate([sums[i], sums[4 + i]], axis=0)


def attend_out(pieces, height):
    cols = pieces[0].shape[1]
    span = cols // 2
    return run(
        attend_out_kernel,
        "attend_out",
        tuple(pieces),
        [vmem()] * 2,
        (array((height, span), F32),) * 3
        + (array((span, height), F32),)
        + (array((2 * cols,), F32),) * 4,
        [vmem()] * 8,
    )


def fast_path(info, tokens, cotangent, weights, lengths, masks, norms):
    w_query, w_key, w_value, w_out, w_up, w_down = weights
    mask_own, mask_other, mask_ends = masks
    g_one, b_one, g_two, b_two = norms
    height, features, units = w_query.shape[0], tokens.shape[2], w_up.shape[1]
    flat = (tuple((0, j) for j in Y_MAJOR),)
    got_rows = flip_chip(split(info, tokens, cotangent, True))
    piece = pack(w_query, w_key, w_value, w_out)
    got_piece = flip_dp(piece, 4)
    own_rows = split(info, tokens, cotangent, False)
    (two_attn,) = join([piece, got_piece])
    got_attn = flip_dp(two_attn, 2)
    feed_piece = beside(w_up, w_down.T)
    got_feed = flip_dp(feed_piece, 4)
    z_pair, z_single = join_sides([two_attn, got_attn])
    y_pair, x_single = flip_dp(z_pair, 1), flip_chip(z_single)
    own_pair, near_single = join([z_pair, y_pair], [z_single, x_single])
    other_pair, far_single = flip_chip(own_pair), flip_dp(near_single, 1)
    single_w = ((near_single, far_single), (CHIP_NEAR, CHIP_FAR))
    two_up, two_down = join_sides([feed_piece, got_feed])
    got_up, got_down = flip_dp(two_up, 2), flip_dp(two_down, 2)
    quarters = (own_rows, got_rows, flip_core(own_rows), flip_core(got_rows))
    tok = merge(info, quarters)
    own01 = attend(info, lengths, tok, ((own_pair,), flat), True, mask_own[:2])
    z_up, z_down = join([two_up, got_up], [two_down, got_down])
    y_up, x_down = flip_dp(z_up, 1), flip_chip(z_down)
    other01 = attend(info, lengths, tok, ((other_pair,), flat), True, mask_other[:2])
    ends = attend(info, lengths, tok, single_w, False, mask_ends)
    own_up, near_down = join([z_up, y_up], [z_down, x_down])
    other_up, far_down = flip_chip(own_up), flip_dp(near_down, 1)
    up = ((own_up, other_up), (OWN, OTHER))
    down = ((near_down, far_down), (CHIP_NEAR, CHIP_FAR))
    contexts = (own01[3], other01[3], ends[3])
    attn_part = project(info, contexts, single_w, features)
    attn_got = flip_cores(attn_part)
    normal, scale_one, hn = norm_one(tok, attn_part, attn_got, g_one, b_one)
    act1, slope1 = feed_up(info, hn, ((own_up,), flat), units)
    act2, slope2 = feed_up(info, hn, ((other_up,), flat), units)
    mixed = feed_down(info, act1, act2, down, features)
    mixed_got = flip_cores(mixed)
    out, dzb_two, sums_two = norm_two(
        info, lengths, hn, mixed, mixed_got, quarters, g_two, b_two
    )
    keep_d1, send_d1, keep_d2, send_d2 = feed_grad(info, dzb_two, act1, act2, (OWN, OTHER, CHIP_NEAR, CHIP_FAR))
    got_d1, got_d2 = flip_chip(send_d1), flip_dp(send_d2, 1)
    du1, du2, *back = feed_back(info, dzb_two, slope1, slope2, up, down)
    back_got = flip_cores(back)
    keep_u1, send_u1, keep_u2, send_u2 = feed_grad(info, hn, du1, du2, (OWN, OTHER, CHIP_NEAR, CHIP_FAR))
    got_u1, got_u2 = flip_chip(send_u1), flip_dp(send_u2, 1)
    sum_d1, sum_d2 = fold_add(keep_d1, got_d1, keep_d2, got_d2)
    dzb_one, sums_one = norm_one_back(normal, scale_one, dzb_two, back, back_got, g_one)
    d_ends = attend_back(info, dzb_one, single_w, None, ends)
    keep_f1, send_f1, keep_f2, send_f2 = fold_feed(
        sum_d1, keep_u1, got_u1, sum_d2, keep_u2, got_u2
    )
    got_f1, got_f2 = flip_dp(send_f1, 1), flip_chip(send_f2)
    keep_s, send_s = single_grad(
        info, tok, d_ends, dzb_one, contexts, sums_one, sums_two, (CHIP_NEAR, CHIP_FAR)
    )
    got_s = flip_dp(send_s, 1)
    d_other = attend_back(info, dzb_one, single_w, 1, other01)
    grad_b = pair_grad(info, tok, d_other, OWN)
    got_b = flip_chip(grad_b)
    keep_f, send_f = fold_sides(keep_f1, got_f1, keep_f2, got_f2)
    got_f = flip_dp(send_f, 2)
    d_own = attend_back(info, dzb_one, single_w, 0, own01)
    grad_a = pair_grad(info, tok, d_own, OWN)
    keep_a, send_a = fold(grad_a, got_b, 2, 0)
    got_a = flip_dp(send_a, 1)
    mine, *sent = input_back(
        info, d_own, d_other, d_ends, dzb_one, ((own_pair, other_pair), (OWN, OTHER)), single_w
    )
    sent_got = flip_cores(sent)
    keep_s2, send_s2 = fold(keep_s, got_s, 2, TAIL)
    got_s2 = flip_chip(send_s2)
    keep_f3, send_f3 = fold(keep_f, got_f, 2, 0)
    got_f3 = flip_dp(send_f3, 4)
    own_tok, *send_tok = tokens_add(mine, sent_got)
    got_tok = [flip_chip(v) for v in send_tok]
    keep_s3, send_s3, keep_a3, send_a3 = fold_last(keep_s2, got_s2, keep_a, got_a)
    got_s3, got_a3 = flip_dp(send_s3, 2), flip_dp(send_a3, 2)
    own_out, send_out = halves(info, out)
    got_out = flip_chip(send_out)
    grad_up, grad_down = feed_out(keep_f3, got_f3)
    keep_z, send_z = fold_z(keep_s3, got_s3, keep_a3, got_a3)
    got_z = flip_dp(send_z, 4)
    grad_tokens = tokens_out(info, own_tok, got_tok)
    output = slots_of(info, own_out, got_out)
    grads = attend_out((keep_z, got_z), height)
    return (output, grad_tokens, *grads[:4], grad_up, grad_down.T, *grads[4:])


def plain_path(info, tokens, cotangent, weights, lengths, masks, norms):
    w_query, w_key, w_value, w_out, w_up, w_down = weights
    mask_own, mask_other, mask_ends = masks
    g_one, b_one, g_two, b_two = norms
    features, units = tokens.shape[2], w_up.shape[1]
    flat = (((0, 0),),)
    two = (((0, 0),), ((1, 0),))

    def gathered(piece):
        own = lax.all_gather(piece, "dp", axis=0, tiled=True)[None]
        return own, flip_chip(own)

    got_rows = flip_chip(split(info, tokens, cotangent, True))
    own_rows = split(info, tokens, cotangent, False)
    quarters = (own_rows, got_rows, flip_core(own_rows), flip_core(got_rows))
    tok = merge(info, quarters)
    firsts = [w[:, : 2 * HD] for w in (w_query, w_key, w_value)]
    thirds = [w_out.T] + [w[:, 2 * HD :] for w in (w_query, w_key, w_value)]
    pair_w = (gathered(jnp.concatenate(firsts, axis=1)), two)
    single_w = (gathered(jnp.concatenate(thirds, axis=1)), two)
    up, down = (gathered(w_up), two), (gathered(w_down.T), two)
    own01 = attend(info, lengths, tok, ((pair_w[0][0],), flat), True, mask_own[:2])
    other01 = attend(info, lengths, tok, ((pair_w[0][1],), flat), True, mask_other[:2])
    ends = attend(info, lengths, tok, single_w, False, mask_ends)
    contexts = (own01[3], other01[3], ends[3])
    part = project(info, contexts, single_w, features)
    normal, scale_one, hn = norm_one(tok, part, flip_cores(part), g_one, b_one)
    act1, slope1 = feed_up(info, hn, ((up[0][0],), flat), units)
    act2, slope2 = feed_up(info, hn, ((up[0][1],), flat), units)
    part = feed_down(info, act1, act2, down, features)
    out, dzb_two, sums_two = norm_two(
        info, lengths, hn, part, flip_cores(part), quarters, g_two, b_two
    )
    places = (((0, 0),), ((1, 0),)) * 2
    grad_d = feed_grad(info, dzb_two, act1, act2, places)
    du1, du2, *part = feed_back(info, dzb_two, slope1, slope2, up, down)
    grad_u = feed_grad(info, hn, du1, du2, places)
    dzb_one, sums_one = norm_one_back(
        normal, scale_one, dzb_two, part, flip_cores(part), g_one
    )
    d_ends = attend_back(info, dzb_one, single_w, None, ends)
    keep_s, send_s = single_grad(
        info, tok, d_ends, dzb_one, contexts, sums_one, sums_two, places[2:]
    )
    d_other = attend_back(info, dzb_one, single_w, 1, other01)
    grad_b = pair_grad(info, tok, d_other, places[0])
    d_own = attend_back(info, dzb_one, single_w, 0, own01)
    grad_a = pair_grad(info, tok, d_own, places[0])
    mine, *sent = input_back(info, d_own, d_other, d_ends, dzb_one, pair_w, single_w)
    own_tok, *send_tok = tokens_add(mine, flip_cores(sent))
    own_out, send_out = halves(info, out)
    output = slots_of(info, own_out, flip_chip(send_out))
    grad_tokens = tokens_out(info, own_tok, [flip_chip(v) for v in send_tok])

    def summed(own, other):
        total = own.astype(F32) + flip_chip(other).astype(F32)
        return lax.psum_scatter(total, "dp", scatter_dimension=0, tiled=True)

    def wide(keep1, send1, keep2, send2):
        return jnp.concatenate([summed(keep1[0], send1[0]), summed(keep2[0], send2[0])], axis=1)

    single = summed(keep_s[:features], send_s[:features])
    pair = summed(grad_a[0], grad_b[0])
    grads = [
        jnp.concatenate(
            [pair[:, 2 * i * HD : 2 * (i + 1) * HD], single[:, (3 + i) * HD : (4 + i) * HD]],
            axis=1,
        )
        for i in range(3)
    ] + [single[:, : 3 * HD].T]
    sums = decode(keep_s[features:])
    sums = lax.psum(sums + flip_chip(sums), "dp")
    sums = [jnp.concatenate([sums[i], sums[4 + i]]) for i in range(4)]
    return (output, grad_tokens, *grads, wide(*grad_u), wide(*grad_d).T, *sums)


def local(
    tokens,
    w_query,
    w_key,
    w_value,
    w_out,
    w_up,
    w_down,
    gain_attn,
    bias_attn,
    gain_ffn,
    bias_ffn,
    lengths,
    random_blocks,
    cotangent,
):
    ORDER.clear()
    size = lax.axis_size("dp")
    rank = lax.axis_index("mp")
    me = lax.axis_index("dp")
    x, core = rank // 2, rank % 2
    quarter = tokens.shape[1]
    seq = 4 * quarter
    height = w_query.shape[0]
    span = w_query.shape[1]
    heads = span // HD
    nblocks = seq // BLOCK
    fast = size == 8 and height % 16 == 0

    shift = x * (seq // 2)
    info = jnp.stack([me, x, core, shift]).astype(jnp.int32)

    blocks = (jnp.arange(nblocks) + x * (nblocks // 2)) % nblocks
    near_blocks = jnp.abs(blocks[:, None] - blocks[None, :]) <= 1
    edge = (blocks == 0) | (blocks == nblocks - 1)
    fixed = near_blocks | edge[:, None] | edge[None, :]

    def table(shard):
        chosen = lax.dynamic_slice_in_dim(random_blocks, shard * heads, heads, 0)
        chosen = jnp.roll(chosen, -x * (nblocks // 2), axis=1)
        hit = jnp.any(chosen[:, None, :, :] == blocks[None, :, None, None], axis=3)
        bias = jnp.where(fixed.T[None] | hit, 0.0, NEGATIVE)
        return jnp.concatenate(
            [
                jnp.zeros((heads, nblocks, HD), F32),
                bias,
                jnp.full((heads, nblocks, 3), -1.0, F32),
                jnp.zeros((heads, nblocks, HD - 3 - nblocks), F32),
            ],
            axis=2,
        )

    mask_own, mask_other = table(rank), table(rank ^ 2)
    mask_ends = jnp.concatenate([mask_own[2:], mask_other[2:]], axis=0)
    g_one, b_one = gain_attn[None], bias_attn[None]
    g_two, b_two = gain_ffn[None], bias_ffn[None]

    path = fast_path if fast else plain_path
    return path(
        info,
        tokens,
        cotangent,
        (w_query, w_key, w_value, w_out, w_up, w_down),
        lengths,
        (mask_own, mask_other, mask_ends),
        (g_one, b_one, g_two, b_two),
    )


def solution(mesh):
    return jax.shard_map(
        local,
        mesh=mesh,
        in_specs=(
            P("dp", "mp", None),
            P("dp", "mp"),
            P("dp", "mp"),
            P("dp", "mp"),
            P("mp", "dp"),
            P("dp", "mp"),
            P("mp", "dp"),
            P(),
            P(),
            P(),
            P(),
            P("dp"),
            P(),
            P("dp", "mp", None),
        ),
        out_specs=(
            P("dp", "mp", None),
            P("dp", "mp", None),
            P("dp", "mp"),
            P("dp", "mp"),
            P("dp", "mp"),
            P("mp", "dp"),
            P("dp", "mp"),
            P("mp", "dp"),
            P(),
            P(),
            P(),
            P(),
        ),
        check_vma=False,
    )
```

```python
import functools

import jax
import jax.numpy as jnp
from jax import lax
from jax.experimental import pallas as pl
from jax.experimental.pallas import tpu as pltpu
from jax.sharding import PartitionSpec as P

HD = 64
BLOCK = 64
LANES = 128
TILE = 256
SENT = 256
EPSILON = 1e-12
TAIL = 32
TOKEN = (8, 128)
ROOM = {
    "attend": 20,
    "attend_back": 20,
    "project": 12,
    "input_back": 24,
    "norm_one": 12,
    "norm_two": 16,
    "norm_one_back": 14,
    "feed_up": 16,
    "feed_down": 18,
    "feed_back": 32,
    "feed_grad": 24,
    "pair_grad": 16,
    "single_grad": 20,
    "join": 1,
    "join_sides": 1,
    "beside": 1,
    "pack": 2,
    "split": 4,
    "merge": 1,
    "fold": 6,
    "fold_add": 8,
    "fold_feed": 10,
    "fold_sides": 8,
    "fold_last": 6,
    "fold_z": 4,
    "halves": 1,
    "slots": 1,
    "tokens_add": 8,
    "tokens_out": 8,
    "feed_out": 6,
    "attend_out": 6,
}
SCALE = 0.125
LOG2E = 1.4426950408889634
LN2 = 0.6931471805599453
NEGATIVE = -1e30
F32 = jnp.float32
BF16 = jnp.bfloat16

CORE_SWAP = [(0, 1), (1, 0), (2, 3), (3, 2)]
CHIP_SWAP = [(0, 2), (2, 0), (1, 3), (3, 1)]


def nn(a, b):
    return lax.dot_general(a, b, (((1,), (0,)), ((), ())), preferred_element_type=F32)


def nt(a, b):
    return lax.dot_general(a, b, (((1,), (1,)), ((), ())), preferred_element_type=F32)


def tn(a, b):
    return lax.dot_general(a, b, (((0,), (0,)), ((), ())), preferred_element_type=F32)


def vmem():
    return pl.BlockSpec(memory_space=pltpu.VMEM)


def smem():
    return pl.BlockSpec(memory_space=pltpu.SMEM)


def anywhere():
    return pl.BlockSpec(memory_space=pl.ANY)


def in_hbm(values):
    return tuple(pltpu.with_memory_space_constraint(v, pltpu.HBM) for v in values)


def array(shape, dtype):
    return jax.ShapeDtypeStruct(shape, dtype)


ORDER = []


def run(kernel, name, args, specs, outs, out_specs, scratch=()):
    given, made = len(args), len(outs)
    extra = tuple(ORDER)

    def body(*refs):
        ins, rest = refs[:given], refs[given + len(extra) :]
        rest[made][...] = jnp.zeros(TOKEN, F32)
        kernel(*ins, *rest[:made], *rest[made + 1 :])

    results = pl.pallas_call(
        body,
        out_shape=tuple(outs) + (array(TOKEN, F32),),
        in_specs=list(specs) + [anywhere()] * len(extra),
        out_specs=tuple(out_specs) + (vmem(),),
        scratch_shapes=list(scratch),
        compiler_params=pltpu.CompilerParams(vmem_limit_bytes=ROOM[name] * 2**20),
        cost_estimate=pl.CostEstimate(flops=1, bytes_accessed=0, transcendentals=0),
        name=name,
    )(*args, *extra)
    ORDER[:] = [results[-1]]
    return results[:-1]


def put_rows(parts, t, value):
    height, tile = parts[0].shape[0], value.shape[0]
    if height <= tile:
        per = tile // height
        for k in range(per):
            parts[t * per + k][...] = value[k * height : (k + 1) * height]
    else:
        per = height // tile
        parts[t // per][pl.ds(t % per * tile, tile), :] = value


def get_sum(parts, more, t):
    height = parts[0].shape[0]
    if height <= TILE:
        per = TILE // height
        at = range(t * per, (t + 1) * per)
        pieces = [parts[k][...].astype(F32) + more[k][...].astype(F32) for k in at]
        return pieces[0] if per == 1 else jnp.concatenate(pieces, axis=0)
    per = height // TILE
    at = pl.ds(t % per * TILE, TILE)
    return parts[t // per][at, :].astype(F32) + more[t // per][at, :].astype(F32)


def tile_rows(ref):
    return [(t, pl.ds(t * TILE, TILE)) for t in range(ref.shape[0] // TILE)]


def far(shape, dtype):
    return pltpu.HBM(shape, dtype)


def tiles(seq, width, height):
    parts = (array((height, width), BF16),) * (seq // height)
    return parts, [vmem()] * len(parts)


def place(me, refs, slots, dst_ref, first=0, last=None, only=None, to=0):
    for ref, of in zip(refs, slots):
        height, width = ref.shape[1], ref.shape[2]
        end = width if last is None else last
        for e, (chip, j) in enumerate(of):
            if only is not None and chip != only:
                continue
            at = 0 if height == dst_ref.shape[0] else pl.multiple_of((me ^ j) * height, height)
            at_column = to + (0 if only is not None else chip * (end - first))
            dst_ref[pl.ds(at, height), pl.ds(at_column, end - first)] = ref[e, :, first:end]


def pick(me, fulls, out_ref, slots, first):
    _, height, width = out_ref.shape
    for e, (chip, j) in enumerate(slots):
        full = fulls[chip]
        at = 0 if height == full.shape[0] else pl.multiple_of((me ^ j) * height, height)
        out_ref[e] = full[pl.ds(at, height), pl.ds(first, width)].astype(BF16)


def attend_kernel(slots, columns, only, places, info, lengths, tok, mask, *rest):
    refs, (qa, ka, va, ctx, wfull) = rest[: len(slots)], rest[len(slots) :]
    seq = tok.shape[0]
    place(info[0], refs, slots, wfull, *columns, only)
    lane = lax.broadcasted_iota(jnp.int32, (TILE, LANES), 1)
    row0 = lax.broadcasted_iota(jnp.int32, (TILE, LANES), 0)
    for t in range(seq // TILE):
        at = pl.ds(t * TILE, TILE)
        row = row0 + t * TILE
        made = nn(tok[at, :], wfull[...])
        onehot = jnp.where(lane - HD == row // BLOCK, 1.0, 0.0)[:, HD:]
        position = row + info[3]
        position = jnp.where(position >= seq, position - seq, position)
        dead = (position >= lengths[info[1]]) & (lane >= HD) & (lane < HD + 16)
        for h, (q_at, k_at, v_at) in enumerate(places):
            q = made[:, q_at : q_at + HD] * (SCALE * LOG2E)
            k = made[:, k_at : k_at + HD]
            v = made[:, v_at : v_at + HD]
            qa[h, at, :] = jnp.concatenate([q, onehot], axis=1).astype(BF16)
            per = TILE // BLOCK
            table = jnp.concatenate(
                [
                    jnp.broadcast_to(mask[h, t * per + b : t * per + b + 1, :], (BLOCK, LANES))
                    for b in range(per)
                ],
                axis=0,
            )
            table = jnp.where(dead, NEGATIVE, table)
            ka[h, at, :] = jnp.concatenate([k, table[:, HD:]], axis=1).astype(BF16)
            va[h, at, :] = jnp.concatenate([v, jnp.full((TILE, HD), -1.0, F32)], axis=1).astype(BF16)
    for t in range(seq // TILE):
        at = pl.ds(t * TILE, TILE)
        pieces = []
        for h in range(len(places)):
            q = qa[h, at, :]
            s = nt(q, ka[h])
            top = jnp.max(s, axis=1, keepdims=True)
            p = jnp.exp2(s - top).astype(BF16)
            got = nn(p, va[h])
            total = -got[:, HD:]
            pieces.append(got[:, :HD] / total)
            log = top + jnp.log2(-got)
            hi = log.astype(BF16).astype(F32)
            mid = (log - hi).astype(BF16).astype(F32)
            low = log - hi - mid
            new = jnp.where(
                lane == HD + 16,
                hi,
                jnp.where(lane == HD + 17, mid, jnp.where(lane == HD + 18, low, q.astype(F32))),
            )
            qa[h, at, :] = new.astype(BF16)
        ctx[at, :] = jnp.concatenate(pieces, axis=1).astype(BF16)


PAIR = ((0, 2 * HD, 4 * HD), (HD, 3 * HD, 5 * HD))
SINGLES = ((HD, 2 * HD, 3 * HD), (5 * HD, 6 * HD, 7 * HD))


def attend(info, lengths, tok, gathered, pair, mask):
    arrays, slots = gathered
    seq, width = tok.shape
    aug = far((2, seq, LANES), BF16)
    columns, only, cols = ((0, 6 * HD), 0, 6 * HD) if pair else ((2 * HD, 6 * HD), None, 8 * HD)
    return run(
        functools.partial(attend_kernel, slots, columns, only, PAIR if pair else SINGLES),
        "attend",
        (info, lengths, tok, mask) + arrays,
        [smem()] * 2 + [vmem()] * (2 + len(arrays)),
        (aug, aug, aug, array((seq, LANES), BF16)),
        [vmem()] * 4,
        [pltpu.VMEM((width, cols), BF16)],
    )


def place_out(me, refs, slots, pairs, ends):
    place(me, refs, slots, pairs, 0, 2 * HD)
    place(me, refs, slots, ends, 2 * HD, 4 * HD)
    both = ends[...]
    ends[:, :LANES] = jnp.concatenate([both[:, :HD], both[:, LANES : LANES + HD]], axis=1)


def project_kernel(slots, info, own, other, ends, *rest):
    refs, parts, (w1, w2) = rest[: len(slots)], rest[len(slots) : -2], rest[-2:]
    place_out(info[0], refs, slots, w1, w2)
    for t, at in tile_rows(own):
        both = jnp.concatenate([own[at, :], other[at, :]], axis=1)
        out = nt(both, w1[...]) + nt(ends[at, :], w2[:, :LANES])
        put_rows(parts, t, out.astype(BF16))


def project(info, contexts, gathered, width):
    arrays, slots = gathered
    seq = contexts[0].shape[0]
    return run(
        functools.partial(project_kernel, slots),
        "project",
        (info,) + contexts + arrays,
        [smem()] + [vmem()] * (3 + len(arrays)),
        *tiles(seq, width, 2 * TILE),
        [pltpu.VMEM((width, 2 * LANES), BF16)] * 2,
    )


def attend_back_kernel(slots, chip, info, dz, qa, ka, va, ctx, *rest):
    refs, (dqkv, pairs, ends, da) = rest[: len(slots)], rest[len(slots) :]
    seq = dz.shape[0]
    heads = qa.shape[0]
    if chip is None:
        place_out(info[0], refs, slots, pairs, ends)
        wfull = ends.at[:, pl.ds(0, LANES)]
    else:
        place(info[0], refs, slots, pairs, 0, 2 * HD, chip)
        wfull = pairs.at[:, pl.ds(0, LANES)]
    lane = lax.broadcasted_iota(jnp.int32, (TILE, LANES), 1)
    for t in range(seq // TILE):
        at = pl.ds(t * TILE, TILE)
        dctx = nn(dz[at, :], wfull[...]).astype(BF16).astype(F32)
        both = dctx * ctx[at, :].astype(F32)
        for h in range(heads):
            inner = jnp.sum(both[:, h * HD : (h + 1) * HD], axis=1, keepdims=True)
            hi = inner.astype(BF16).astype(F32)
            mid = (inner - hi).astype(BF16).astype(F32)
            low = inner - hi - mid
            one = jnp.concatenate(
                [dctx[:, h * HD : (h + 1) * HD], jnp.zeros((TILE, HD), F32)], axis=1
            )
            one = jnp.where(lane == HD, hi, one)
            one = jnp.where(lane == HD + 1, mid, one)
            one = jnp.where(lane == HD + 2, low, one)
            da[h, at, :] = one.astype(BF16)

    unit = jnp.where(
        lax.broadcasted_iota(jnp.int32, (HD, LANES), 0)
        == lax.broadcasted_iota(jnp.int32, (HD, LANES), 1),
        1.0,
        0.0,
    ).astype(BF16)

    def turned(values):
        return nt(unit, values).astype(BF16)

    grads = []
    for h in range(heads):
        k_turned, q_turned, d_turned = turned(ka[h]), turned(qa[h]), turned(da[h])
        dq, dk, dv = None, [], []
        for t in range(seq // TILE):
            at = pl.ds(t * TILE, TILE)
            p = jnp.exp2(nt(ka[h, at, :], qa[h]))
            ds = (p * nt(va[h, at, :], da[h])).astype(BF16)
            dv.append(nt(d_turned, p.astype(BF16)))
            dk.append(nt(q_turned, ds))
            more = nn(k_turned[:, t * TILE : (t + 1) * TILE], ds)
            dq = more if dq is None else dq + more
        dk = jnp.concatenate(dk, axis=1) * LN2
        grads.append((dq * SCALE, dk, jnp.concatenate(dv, axis=1)))
    (dq0, dk0, dv0), (dq1, dk1, dv1) = grads
    if chip is None:
        blank = jnp.zeros_like(dq0)
        stacks = ((blank, dq0), (dk0, dv0), (blank, dq1), (dk1, dv1))
    else:
        stacks = ((dq0, dq1), (dk0, dk1), (dv0, dv1))
    for i, stack in enumerate(stacks):
        both = jnp.concatenate(stack, axis=0).astype(BF16)
        dqkv[:, i * LANES : (i + 1) * LANES] = jnp.transpose(both)


def attend_back(info, dz, gathered, chip, saved):
    arrays, slots = gathered
    qa, ka, va, ctx = saved
    seq, width = dz.shape
    cols = 8 * HD if chip is None else 6 * HD
    return run(
        functools.partial(attend_back_kernel, slots, chip),
        "attend_back",
        (info, dz, qa, ka, va, ctx) + arrays,
        [smem()] + [vmem()] * (5 + len(arrays)),
        (array((seq, cols), BF16),),
        [vmem()],
        [
            pltpu.VMEM((width, 2 * LANES), BF16),
            pltpu.VMEM((width, 2 * LANES), BF16),
            pltpu.VMEM((2, seq, LANES), BF16),
        ],
    )[0]


def input_back_kernel(slots1, slots2, info, own, other, ends, dz, *rest):
    n1, n2 = len(slots1), len(slots2)
    refs1, refs2, (mine, *sent, w1, w2) = rest[:n1], rest[n1 : n1 + n2], rest[n1 + n2 :]
    place(info[0], refs1, slots1, w1)
    place(info[0], refs2, slots2, w2, 2 * HD, 6 * HD)
    per = len(sent) // 2
    height = sent[0].shape[0]
    for t, at in tile_rows(dz):
        pairs = jnp.concatenate([own[at, :], other[at, :]], axis=1)
        back = nt(pairs, w1[...]) + nt(ends[at, :], w2[...])

        @pl.when(info[2] == t % 2)
        def _(t=t, at=at, back=back):
            mine[t // 2] = back + dz[at, :].astype(F32)

        @pl.when(info[2] != t % 2)
        def _(t=t, back=back):
            for k in range(per):
                part = back[k * height : (k + 1) * height]
                sent[t // 2 * per + k][...] = part.astype(BF16)


def input_back(info, own, other, ends, dz, gathered1, gathered2):
    seq, width = dz.shape
    arrays = gathered1[0] + gathered2[0]
    halves = (seq // TILE // 2, TILE, width)
    grads = (own, other, ends, dz)
    return run(
        functools.partial(input_back_kernel, gathered1[1], gathered2[1]),
        "input_back",
        (info,) + grads + arrays,
        [smem()] + [vmem()] * (len(grads) + len(arrays)),
        (array(halves, F32),) + (array((SENT, width), BF16),) * (seq // 2 // SENT),
        [vmem()] * (1 + seq // 2 // SENT),
        [pltpu.VMEM((width, 12 * HD), BF16), pltpu.VMEM((width, 8 * HD), BF16)],
    )


def center(z):
    mean = jnp.mean(z, axis=1, keepdims=True)
    moved = z - mean
    spread = jnp.mean(moved * moved, axis=1, keepdims=True)
    scale = lax.rsqrt(spread + EPSILON)
    return moved * scale, scale


def norm_back(n, scale, gy, gain):
    dn = gy * gain
    return scale * (
        dn - jnp.mean(dn, axis=1, keepdims=True) - n * jnp.mean(dn * n, axis=1, keepdims=True)
    )


def add_sums(gy, n, sums):
    more = [jnp.sum(v, axis=0, keepdims=True) for v in (gy * n, gy)]
    return more if sums is None else [a + b for a, b in zip(sums, more)]


def norm_one_kernel(tok, gain, bias, *rest):
    *parts, normal, scale, hn = rest
    count = len(parts) // 2
    for t, at in tile_rows(tok):
        value = tok[at, :].astype(F32) + get_sum(parts[:count], parts[count:], t)
        n, r = center(value)
        normal[at, :] = n.astype(BF16)
        scale[at, :] = r
        hn[at, :] = (n * gain[...] + bias[...]).astype(BF16)


def norm_one(tok, p0, p1, gain, bias):
    seq, width = tok.shape
    return run(
        norm_one_kernel,
        "norm_one",
        (tok, gain, bias, *p0, *p1),
        [vmem()] * (3 + len(p0) + len(p1)),
        (array((seq, width), BF16), array((seq, 1), F32), array((seq, width), BF16)),
        [vmem()] * 3,
    )


def norm_two_kernel(info, lengths, hn, own, got, core_own, core_got, gain, bias, *rest):
    *parts, out, dzb, sums = rest
    count = len(parts) // 2
    seq = hn.shape[0]
    total = None
    for t, at in tile_rows(hn):
        value = hn[at, :].astype(F32) + get_sum(parts[:count], parts[count:], t)
        n, scale = center(value)
        out[at, :] = (n * gain[...] + bias[...]).astype(BF16)
        position = lax.broadcasted_iota(jnp.int32, value.shape, 0) + t * TILE + info[3]
        position = jnp.where(position >= seq, position - seq, position)
        mine, others = ((own, core_own), (got, core_got))[t // 2]
        cot = jnp.where(info[2] == t % 2, mine[1].astype(F32), others[1].astype(F32))
        gy = jnp.where(position < lengths[info[1]], cot, 0.0)
        dzb[at, :] = norm_back(n, scale, gy, gain[...]).astype(BF16)
        total = add_sums(gy, n, total)
    sums[...] = jnp.concatenate(total, axis=0)


def norm_two(info, lengths, hn, m0, m1, cot, gain, bias):
    seq, width = hn.shape
    return run(
        norm_two_kernel,
        "norm_two",
        (info, lengths, hn, *cot, gain, bias, *m0, *m1),
        [smem()] * 2 + [vmem()] * (3 + len(cot) + len(m0) + len(m1)),
        (
            array((seq, width), BF16),
            array((seq, width), BF16),
            array((2, width), F32),
        ),
        [vmem()] * 3,
    )


def norm_one_back_kernel(normal, scale, dz2, gain, *rest):
    *parts, dzb, sums = rest
    count = len(parts) // 2
    total = None
    for t, at in tile_rows(dz2):
        n = normal[at, :].astype(F32)
        gy = dz2[at, :].astype(F32) + get_sum(parts[:count], parts[count:], t)
        dzb[at, :] = norm_back(n, scale[at, :], gy, gain[...]).astype(BF16)
        total = add_sums(gy, n, total)
    sums[...] = jnp.concatenate(total, axis=0)


def norm_one_back(normal, scale, dz2, p0, p1, gain):
    seq, width = normal.shape
    return run(
        norm_one_back_kernel,
        "norm_one_back",
        (normal, scale, dz2, gain, *p0, *p1),
        [vmem()] * (4 + len(p0) + len(p1)),
        (array((seq, width), BF16), array((2, width), F32)),
        [vmem()] * 2,
    )


def gelu_pair(u):
    phi = 0.5 + 0.5 * lax.erf(u * 0.7071067811865476)
    return u * phi, phi + u * (jnp.exp(-0.5 * u * u) * 0.3989422804014327)


def feed_up_kernel(slots, info, hn, *rest):
    refs, (active, slope, wfull) = rest[: len(slots)], rest[len(slots) :]
    place(info[0], refs, slots, wfull)
    for _, at in tile_rows(hn):
        a, g = gelu_pair(nn(hn[at, :], wfull[...]))
        active[at, :] = a.astype(BF16)
        slope[at, :] = g.astype(BF16)


def feed_up(info, hn, gathered, units):
    arrays, slots = gathered
    seq, width = hn.shape
    return run(
        functools.partial(feed_up_kernel, slots),
        "feed_up",
        (info, hn) + arrays,
        [smem()] + [vmem()] * (1 + len(arrays)),
        (array((seq, units), BF16), array((seq, units), BF16)),
        [vmem()] * 2,
        [pltpu.VMEM((width, units), BF16)],
    )


def feed_down_kernel(slots, info, act1, act2, *rest):
    refs, parts, wfull = rest[: len(slots)], rest[len(slots) : -1], rest[-1]
    place(info[0], refs, slots, wfull)
    for t, at in tile_rows(act1):
        both = jnp.concatenate([act1[at, :], act2[at, :]], axis=1)
        put_rows(parts, t, nt(both, wfull[...]).astype(BF16))


def feed_down(info, act1, act2, gathered, width):
    seq, units = act1.shape
    arrays, slots = gathered
    return run(
        functools.partial(feed_down_kernel, slots),
        "feed_down",
        (info, act1, act2) + arrays,
        [smem()] + [vmem()] * (2 + len(arrays)),
        *tiles(seq, width, seq),
        [pltpu.VMEM((width, 2 * units), BF16)],
    )


def feed_back_kernel(slots_up, slots_down, info, dzb, slope1, slope2, *rest):
    n1, n2 = len(slots_up), len(slots_down)
    ups, downs, (du1, du2, *parts, up, down) = rest[:n1], rest[n1 : n1 + n2], rest[n1 + n2 :]
    place(info[0], ups, slots_up, up)
    place(info[0], downs, slots_down, down)
    units = du1.shape[1]
    for t, at in tile_rows(dzb):
        out = None
        for i, (slope, du) in enumerate(((slope1, du1), (slope2, du2))):
            cols = pl.ds(i * units, units)
            grad = (nn(dzb[at, :], down[:, cols]) * slope[at, :].astype(F32)).astype(BF16)
            du[at, :] = grad
            more = nt(grad, up[:, cols])
            out = more if out is None else out + more
        put_rows(parts, t, out.astype(BF16))


def feed_back(info, dzb, slope1, slope2, up, down):
    seq, width = dzb.shape
    units = slope1.shape[1]
    arrays = up[0] + down[0]
    parts, part_specs = tiles(seq, width, TILE)
    return run(
        functools.partial(feed_back_kernel, up[1], down[1]),
        "feed_back",
        (info, dzb, slope1, slope2) + arrays,
        [smem()] + [vmem()] * (3 + len(arrays)),
        (array((seq, units), BF16),) * 2 + parts,
        [vmem()] * 2 + part_specs,
        [pltpu.VMEM((width, 2 * units), BF16)] * 2,
    )


def feed_grad_kernel(places, info, a, d1, d2, *rest):
    outs, fulls = rest[:4], rest[4:]
    half = outs[0].shape[2]
    fulls[0][...] = tn(a[...], d1[...])
    fulls[1][...] = tn(a[...], d2[...])
    for i, out in enumerate(outs):
        pick(info[0], fulls, out, places[i], (i // 2) * half)


def feed_grad(info, a, d1, d2, places):
    seq, width = a.shape
    units = d1.shape[1]
    count = len(places[0])
    out = array((count, width // count, units // 2), BF16)
    return run(
        functools.partial(feed_grad_kernel, places),
        "feed_grad",
        (info, a, d1, d2),
        [smem()] + [vmem()] * 3,
        (out,) * 4,
        [vmem()] * 4,
        [pltpu.VMEM((width, units), F32)] * 2,
    )


def pair_grad_kernel(slots, info, tok, d, out, full):
    full[...] = tn(tok[...], d[...])
    pick(info[0], (full,), out, slots, 0)


def pair_grad(info, tok, d, slots):
    seq, width = tok.shape
    cols = d.shape[1]
    return run(
        functools.partial(pair_grad_kernel, slots),
        "pair_grad",
        (info, tok, d),
        [smem()] + [vmem()] * 2,
        (array((len(slots), width // len(slots), cols), BF16),),
        [vmem()],
        [pltpu.VMEM((width, cols), F32)],
    )[0]


def encode(sums):
    hi = sums.astype(BF16).astype(F32)
    mid = (sums - hi).astype(BF16).astype(F32)
    low = sums - hi - mid
    return jnp.concatenate([hi, mid, low, jnp.zeros_like(low)], axis=0).astype(BF16)


def decode(coded):
    values = coded.astype(F32)
    n = values.shape[0] // 4
    return values[:n] + values[n : 2 * n] + values[2 * n : 3 * n]


def single_grad_kernel(places, info, tok, d, dz, own, other, ends, sums_one, sums_two, keep, send, full):
    mine = tn(tok[...], d[...])
    third = tn(dz[...], ends[...])
    blank = jnp.zeros((third.shape[0], HD), F32)
    width = full.shape[2]
    both = jnp.concatenate([sums_one[...], sums_two[...]], axis=0)
    both = encode(jnp.concatenate([both[:, :width], both[:, width:]], axis=0))
    for chip, ctx in enumerate((own, other)):
        full[chip, :, :LANES] = tn(dz[...], ctx[...])
        at = chip * 4 * HD
        o_third = jnp.concatenate([third[:, chip * HD : (chip + 1) * HD], blank], axis=1)
        full[chip, :, LANES : 2 * LANES] = o_third + mine[:, at : at + LANES]
        full[chip, :, 2 * LANES :] = mine[:, at + LANES : at + 2 * LANES]
    for out, slots in zip((keep, send), places):
        count = len(slots)
        height = full.shape[1] // count
        for e, (chip, j) in enumerate(slots):
            at = 0 if count == 1 else pl.multiple_of((info[0] ^ j) * height, height)
            out[pl.ds(e * height, height), :] = full[chip, pl.ds(at, height), :].astype(BF16)
        out[pl.ds(count * height, TAIL), :] = both


def single_grad(info, tok, d, dz, contexts, sums_one, sums_two, places):
    seq, width = tok.shape
    cols = 6 * HD
    out = array((width + TAIL, cols), BF16)
    return run(
        functools.partial(single_grad_kernel, places),
        "single_grad",
        (info, tok, d, dz, *contexts, sums_one, sums_two),
        [smem()] + [vmem()] * 8,
        (out, out),
        [vmem()] * 2,
        [pltpu.VMEM((2, width, cols), F32)],
    )


def across(values, axis, pairs):
    return lax.ppermute(values, axis, pairs)


def flip_chip(values):
    return across(values, "mp", CHIP_SWAP)


def flip_core(values):
    return across(values, "mp", CORE_SWAP)


def flip_cores(parts):
    return [flip_core(p) for p in parts]


def flip_dp(values, distance):
    size = lax.axis_size("dp")
    return across(values, "dp", [(i, i ^ distance) for i in range(size)])


def join_kernel(groups, *refs):
    count = sum(groups)
    parts, outs, sems = refs[:count], refs[count:-1], refs[-1]
    copies = []
    for out, number in zip(outs, groups):
        first = 0
        for part in parts[len(copies) : len(copies) + number]:
            to = out.at[pl.ds(first, part.shape[0])]
            copies.append(pltpu.make_async_copy(part, to, sems.at[len(copies)]))
            first += part.shape[0]
    for copy in copies:
        copy.start()
    for copy in copies:
        copy.wait()


def join(*groups):
    parts = sum((tuple(g) for g in groups), ())
    outs = [array((sum(p.shape[0] for p in g),) + g[0].shape[1:], g[0].dtype) for g in groups]
    return run(
        functools.partial(join_kernel, tuple(len(g) for g in groups)),
        "join",
        parts,
        [anywhere()] * len(parts),
        outs,
        [anywhere()] * len(outs),
        [pltpu.SemaphoreType.DMA((len(parts),))],
    )


def pack_kernel(w_query, w_key, w_value, w_out, out, rows_in, out_in, sems):
    copies = [
        pltpu.make_async_copy(w, rows_in.at[i], sems.at[i])
        for i, w in enumerate((w_query, w_key, w_value))
    ]
    copies.append(pltpu.make_async_copy(w_out, out_in, sems.at[3]))
    for copy in copies:
        copy.start()
    for copy in copies:
        copy.wait()
    for i in range(3):
        out[0, :, 2 * i * HD : 2 * (i + 1) * HD] = rows_in[i, :, : 2 * HD]
    parts = [jnp.transpose(out_in[...].astype(F32))]
    parts += [rows_in[i, :, 2 * HD :].astype(F32) for i in range(3)]
    out[0, :, 6 * HD :] = jnp.concatenate(parts, axis=1).astype(BF16)


def pack(w_query, w_key, w_value, w_out):
    height, span = w_query.shape
    return run(
        pack_kernel,
        "pack",
        in_hbm((w_query, w_key, w_value, w_out)),
        [anywhere()] * 4,
        (array((1, height, 4 * span), BF16),),
        [vmem()],
        [
            pltpu.VMEM((3, height, span), BF16),
            pltpu.VMEM(w_out.shape, BF16),
            pltpu.SemaphoreType.DMA((4,)),
        ],
    )[0]


def beside_kernel(first, second, out, sems):
    width = first.shape[1]
    copies = [
        pltpu.make_async_copy(ref, out.at[0, :, pl.ds(i * width, width)], sems.at[i])
        for i, ref in enumerate((first, second))
    ]
    for copy in copies:
        copy.start()
    for copy in copies:
        copy.wait()


def beside(first, second):
    height, width = first.shape
    return run(
        beside_kernel,
        "beside",
        in_hbm((first, second)),
        [anywhere()] * 2,
        (array((1, height, 2 * width), BF16),),
        [anywhere()],
        [pltpu.SemaphoreType.DMA((2,))],
    )[0]


def join_sides_kernel(count, *refs):
    parts, outs, sems = refs[:count], refs[count : count + 2], refs[count + 2]
    width = outs[0].shape[2]
    copies = []
    each = parts[0].shape[0]
    for i, part in enumerate(parts):
        for side, out in enumerate(outs):
            copies.append(
                pltpu.make_async_copy(
                    part.at[:, :, pl.ds(side * width, width)],
                    out.at[pl.ds(i * each, each)],
                    sems.at[2 * i + side],
                )
            )
    for copy in copies:
        copy.start()
    for copy in copies:
        copy.wait()


def join_sides(parts):
    count = len(parts)
    each, height, width = parts[0].shape
    out = array((count * each, height, width // 2), BF16)
    return run(
        functools.partial(join_sides_kernel, count),
        "join_sides",
        tuple(parts),
        [anywhere()] * count,
        (out, out),
        [anywhere()] * 2,
        [pltpu.SemaphoreType.DMA((2 * count,))],
    )


def fold_kernel(tail, own, got, *outs):
    body = own.shape[0] - tail
    each = body // len(outs)
    for i, out in enumerate(outs):
        at = pl.ds(i * each, each)
        total = (own[at].astype(F32) + got[at].astype(F32)).astype(BF16)
        if tail:
            out[:each] = total
        else:
            out[...] = total
    if tail:
        coded = encode(decode(own[body:]) + decode(got[body:]))
        for out in outs:
            out[each:] = coded


def fold(own, got, parts, tail=0):
    shape = ((own.shape[0] - tail) // parts + tail,) + own.shape[1:]
    return run(
        functools.partial(fold_kernel, tail),
        "fold",
        (own, got),
        [vmem()] * 2,
        (array(shape, BF16),) * parts,
        [vmem()] * parts,
    )


def fold_last_kernel(own1, got1, own2, got2, keep1, send1, keep2, send2):
    height = own2.shape[1]
    each = height + TAIL
    body = own1.shape[0] - TAIL
    coded = encode(decode(own1[body:]) + decode(got1[body:]))
    half = own2.shape[0] // 2
    for i in range(2 * half):
        out, first = (keep1, send1)[i // half], i % half * each
        at = pl.ds(i * height, height)
        out[first : first + height] = (own1[at].astype(F32) + got1[at].astype(F32)).astype(BF16)
        out[first + height : first + each] = coded
        total = own2[i].astype(F32) + got2[i].astype(F32)
        (keep2, send2)[i // half][i % half] = total.astype(BF16)


def fold_last(own1, got1, own2, got2):
    count, height, width = own2.shape
    first = array((count // 2 * (height + TAIL), width), BF16)
    second = array((count // 2, height, width), BF16)
    return run(
        fold_last_kernel,
        "fold_last",
        (own1, got1, own2, got2),
        [vmem()] * 4,
        (first, first, second, second),
        [vmem()] * 4,
    )


def fold_z_kernel(own1, got1, own2, got2, keep, send):
    height = own2.shape[1]
    each = height + TAIL
    for i, out in enumerate((keep, send)):
        at = pl.ds(i * each, height)
        out[:height] = (own1[at].astype(F32) + got1[at].astype(F32)).astype(BF16)
        at = pl.ds(i * each + height, TAIL)
        out[height:each] = encode(decode(own1[at]) + decode(got1[at]))
        out[each:] = (own2[i].astype(F32) + got2[i].astype(F32)).astype(BF16)


def fold_z(own1, got1, own2, got2):
    _, height, width = own2.shape
    out = array((2 * height + TAIL, width), BF16)
    return run(
        fold_z_kernel,
        "fold_z",
        (own1, got1, own2, got2),
        [vmem()] * 4,
        (out, out),
        [vmem()] * 2,
    )


def fold_add_kernel(own1, got1, own2, got2, out1, out2):
    for own, got, out in ((own1, got1, out1), (own2, got2, out2)):
        out[...] = (own[...].astype(F32) + got[...].astype(F32)).astype(BF16)


def fold_add(own1, got1, own2, got2):
    out = array(own1.shape, BF16)
    return run(
        fold_add_kernel,
        "fold_add",
        (own1, got1, own2, got2),
        [vmem()] * 4,
        (out, out),
        [vmem()] * 2,
    )


def fold_feed_kernel(first1, own1, got1, first2, own2, got2, keep1, send1, keep2, send2):
    width = own1.shape[2]
    half = keep1.shape[0]
    for first, own, got, outs in (
        (first1, own1, got1, (keep1, send1)),
        (first2, own2, got2, (keep2, send2)),
    ):
        for i, out in enumerate(outs):
            at = pl.ds(i * half, half)
            out[:, :, :width] = first[at]
            out[:, :, width:] = (own[at].astype(F32) + got[at].astype(F32)).astype(BF16)


def fold_feed(first1, own1, got1, first2, own2, got2):
    count, height, width = own1.shape
    out = array((count // 2, height, 2 * width), BF16)
    return run(
        fold_feed_kernel,
        "fold_feed",
        (first1, own1, got1, first2, own2, got2),
        [vmem()] * 6,
        (out,) * 4,
        [vmem()] * 4,
    )


def fold_sides_kernel(own1, got1, own2, got2, keep, send):
    width = own1.shape[2]
    half = keep.shape[0]
    for side, (own, got) in enumerate(((own1, got1), (own2, got2))):
        for i, out in enumerate((keep, send)):
            at = pl.ds(i * half, half)
            total = own[at].astype(F32) + got[at].astype(F32)
            out[:, :, side * width : (side + 1) * width] = total.astype(BF16)


def fold_sides(own1, got1, own2, got2):
    count, height, width = own1.shape
    out = array((count // 2, height, 2 * width), BF16)
    return run(
        fold_sides_kernel,
        "fold_sides",
        (own1, got1, own2, got2),
        [vmem()] * 4,
        (out, out),
        [vmem()] * 2,
    )


BY_Z = (0, 4, 2, 6)
Y_MAJOR = BY_Z + tuple(z + 1 for z in BY_Z)
OWN = tuple((0, j) for j in Y_MAJOR)
OTHER = tuple((1, j) for j in Y_MAJOR)
CHIP_NEAR = tuple((chip, z) for chip in range(2) for z in BY_Z)
CHIP_FAR = tuple((chip, z + 1) for chip in range(2) for z in BY_Z)


def split_kernel(other, info, first, second, out, sems):
    slot = 1 - info[1] if other else info[1]
    half = first.shape[1] // 2
    copies = []
    for i, values in enumerate((first, second)):
        for j in range(2):
            at = pl.ds(j * half, half)
            copies.append(
                pltpu.make_async_copy(values.at[slot, at], out.at[i, at], sems.at[2 * i + j])
            )
    for copy in copies:
        copy.start()
    for copy in copies:
        copy.wait()


def split(info, first, second, other):
    return run(
        functools.partial(split_kernel, other),
        "split",
        (info, *in_hbm((first, second))),
        [smem()] + [anywhere()] * 2,
        (array((2,) + first.shape[1:], first.dtype),),
        [vmem()],
        [pltpu.SemaphoreType.DMA((4,))],
    )[0]


def merge_kernel(info, own, got, core_own, core_got, out, sems):
    core = info[2]
    copies = []
    for half, (mine, other) in enumerate(((own, core_own), (got, core_got))):
        copies += [
            pltpu.make_async_copy(mine.at[0], out.at[half, core], sems.at[2 * half]),
            pltpu.make_async_copy(other.at[0], out.at[half, 1 - core], sems.at[2 * half + 1]),
        ]
    for copy in copies:
        copy.start()
    for copy in copies:
        copy.wait()


def merge(info, quarters):
    _, quarter, width = quarters[0].shape
    out = run(
        merge_kernel,
        "merge",
        (info, *quarters),
        [smem()] + [anywhere()] * 4,
        (array((2, 2, quarter, width), quarters[0].dtype),),
        [anywhere()],
        [pltpu.SemaphoreType.DMA((4,))],
    )[0]
    return out.reshape(4 * quarter, width)


def halves_kernel(info, rows_ref, own, send, sems):
    quarter = own.shape[0]
    copies = []
    for half, out in enumerate((own, send)):
        at = pl.multiple_of((2 * half + info[2]) * quarter, quarter)
        copies.append(pltpu.make_async_copy(rows_ref.at[pl.ds(at, quarter)], out, sems.at[half]))
    for copy in copies:
        copy.start()
    for copy in copies:
        copy.wait()


def halves(info, values):
    seq, width = values.shape
    out = array((seq // 4, width), values.dtype)
    return run(
        halves_kernel,
        "halves",
        (info, values),
        [smem(), anywhere()],
        (out, out),
        [anywhere()] * 2,
        [pltpu.SemaphoreType.DMA((2,))],
    )


def slots_kernel(info, own, other, out, sems):
    copies = [
        pltpu.make_async_copy(own, out.at[info[1]], sems.at[0]),
        pltpu.make_async_copy(other, out.at[1 - info[1]], sems.at[1]),
    ]
    for copy in copies:
        copy.start()
    for copy in copies:
        copy.wait()


def slots_of(info, own, other):
    return run(
        slots_kernel,
        "slots",
        (info, own, other),
        [smem()] + [anywhere()] * 2,
        (array((2,) + own.shape, own.dtype),),
        [anywhere()],
        [pltpu.SemaphoreType.DMA((2,))],
    )[0]


def tokens_add_kernel(count, mine, *rest):
    got, own, sends = rest[:count], rest[count], rest[count + 1 :]
    per = count // 2
    height = got[0].shape[0]
    for k, part in enumerate(got):
        at = k % per * height
        total = mine[k // per, pl.ds(at, height)] + part[...].astype(F32)
        if k < per:
            own[pl.ds(at, height)] = total
        else:
            each = sends[0].shape[0]
            for first in range(0, height, each):
                sends[(at + first) // each][...] = total[first : first + each].astype(BF16)


def tokens_add(mine, got):
    _, quarter, width = mine.shape
    send = array((quarter // 2, width), BF16)
    return run(
        functools.partial(tokens_add_kernel, len(got)),
        "tokens_add",
        (mine, *got),
        [vmem()] * (1 + len(got)),
        (array((quarter, width), F32), send, send),
        [vmem()] * 3,
    )


def tokens_out_kernel(info, own, *rest):
    *got, out = rest
    out[info[1]] = own[...]
    height = got[0].shape[0]
    for k, part in enumerate(got):
        out[1 - info[1], pl.ds(k * height, height), :] = part[...].astype(F32)


def tokens_out(info, own, got):
    return run(
        tokens_out_kernel,
        "tokens_out",
        (info, own, *got),
        [smem()] + [vmem()] * (1 + len(got)),
        (array((2,) + own.shape, F32),),
        [vmem()],
    )[0]


def feed_out_kernel(own, got, up, down):
    half = up.shape[1] // 2
    for i in range(4):
        at = pl.ds(i * half, half)
        total = own[0, :, at].astype(F32) + got[0, :, at].astype(F32)
        out = (down, up)[i % 2]
        out[:, pl.ds(i // 2 * half, half)] = total


def feed_out(own, got):
    _, height, width = own.shape
    out = array((height, width // 2), F32)
    return run(
        feed_out_kernel,
        "feed_out",
        (own, got),
        [vmem()] * 2,
        (out, out),
        [vmem()] * 2,
    )


def attend_out_kernel(a, b, query, key, value, out, gain1, bias1, gain2, bias2):
    height = query.shape[0]

    def both(first, last):
        return a[first:last].astype(F32) + b[first:last].astype(F32)

    one = both(0, height)
    two = both(height + TAIL, 2 * height + TAIL)
    at = pl.ds(height, TAIL)
    sums = decode(a[at]) + decode(b[at])
    for i, ref in enumerate((query, key, value)):
        ref[...] = jnp.concatenate(
            [two[:, 2 * i * HD : 2 * (i + 1) * HD], one[:, (3 + i) * HD : (4 + i) * HD]], axis=1
        )
    out[...] = jnp.transpose(one[:, : 3 * HD])
    for i, ref in enumerate((gain1, bias1, gain2, bias2)):
        ref[...] = jnp.concatenate([sums[i], sums[4 + i]], axis=0)


def attend_out(pieces, height):
    cols = pieces[0].shape[1]
    span = cols // 2
    return run(
        attend_out_kernel,
        "attend_out",
        tuple(pieces),
        [vmem()] * 2,
        (array((height, span), F32),) * 3
        + (array((span, height), F32),)
        + (array((2 * cols,), F32),) * 4,
        [vmem()] * 8,
    )


def fast_path(info, tokens, cotangent, weights, lengths, masks, norms):
    w_query, w_key, w_value, w_out, w_up, w_down = weights
    mask_own, mask_other, mask_ends = masks
    g_one, b_one, g_two, b_two = norms
    height, features, units = w_query.shape[0], tokens.shape[2], w_up.shape[1]
    flat = (tuple((0, j) for j in Y_MAJOR),)
    got_rows = flip_chip(split(info, tokens, cotangent, True))
    piece = pack(w_query, w_key, w_value, w_out)
    got_piece = flip_dp(piece, 4)
    own_rows = split(info, tokens, cotangent, False)
    (two_attn,) = join([piece, got_piece])
    got_attn = flip_dp(two_attn, 2)
    feed_piece = beside(w_up, w_down.T)
    got_feed = flip_dp(feed_piece, 4)
    z_pair, z_single = join_sides([two_attn, got_attn])
    y_pair, x_single = flip_dp(z_pair, 1), flip_chip(z_single)
    own_pair, near_single = join([z_pair, y_pair], [z_single, x_single])
    other_pair, far_single = flip_chip(own_pair), flip_dp(near_single, 1)
    single_w = ((near_single, far_single), (CHIP_NEAR, CHIP_FAR))
    two_up, two_down = join_sides([feed_piece, got_feed])
    got_up, got_down = flip_dp(two_up, 2), flip_dp(two_down, 2)
    quarters = (own_rows, got_rows, flip_core(own_rows), flip_core(got_rows))
    tok = merge(info, quarters)
    own01 = attend(info, lengths, tok, ((own_pair,), flat), True, mask_own[:2])
    z_up, z_down = join([two_up, got_up], [two_down, got_down])
    y_up, x_down = flip_dp(z_up, 1), flip_chip(z_down)
    other01 = attend(info, lengths, tok, ((other_pair,), flat), True, mask_other[:2])
    ends = attend(info, lengths, tok, single_w, False, mask_ends)
    own_up, near_down = join([z_up, y_up], [z_down, x_down])
    other_up, far_down = flip_chip(own_up), flip_dp(near_down, 1)
    up = ((own_up, other_up), (OWN, OTHER))
    down = ((near_down, far_down), (CHIP_NEAR, CHIP_FAR))
    contexts = (own01[3], other01[3], ends[3])
    attn_part = project(info, contexts, single_w, features)
    attn_got = flip_cores(attn_part)
    normal, scale_one, hn = norm_one(tok, attn_part, attn_got, g_one, b_one)
    act1, slope1 = feed_up(info, hn, ((own_up,), flat), units)
    act2, slope2 = feed_up(info, hn, ((other_up,), flat), units)
    mixed = feed_down(info, act1, act2, down, features)
    mixed_got = flip_cores(mixed)
    out, dzb_two, sums_two = norm_two(
        info, lengths, hn, mixed, mixed_got, quarters, g_two, b_two
    )
    keep_d1, send_d1, keep_d2, send_d2 = feed_grad(info, dzb_two, act1, act2, (OWN, OTHER, CHIP_NEAR, CHIP_FAR))
    got_d1, got_d2 = flip_chip(send_d1), flip_dp(send_d2, 1)
    du1, du2, *back = feed_back(info, dzb_two, slope1, slope2, up, down)
    back_got = flip_cores(back)
    keep_u1, send_u1, keep_u2, send_u2 = feed_grad(info, hn, du1, du2, (OWN, OTHER, CHIP_NEAR, CHIP_FAR))
    got_u1, got_u2 = flip_chip(send_u1), flip_dp(send_u2, 1)
    sum_d1, sum_d2 = fold_add(keep_d1, got_d1, keep_d2, got_d2)
    dzb_one, sums_one = norm_one_back(normal, scale_one, dzb_two, back, back_got, g_one)
    d_ends = attend_back(info, dzb_one, single_w, None, ends)
    keep_f1, send_f1, keep_f2, send_f2 = fold_feed(
        sum_d1, keep_u1, got_u1, sum_d2, keep_u2, got_u2
    )
    got_f1, got_f2 = flip_dp(send_f1, 1), flip_chip(send_f2)
    keep_s, send_s = single_grad(
        info, tok, d_ends, dzb_one, contexts, sums_one, sums_two, (CHIP_NEAR, CHIP_FAR)
    )
    got_s = flip_dp(send_s, 1)
    d_other = attend_back(info, dzb_one, single_w, 1, other01)
    grad_b = pair_grad(info, tok, d_other, OWN)
    got_b = flip_chip(grad_b)
    keep_f, send_f = fold_sides(keep_f1, got_f1, keep_f2, got_f2)
    got_f = flip_dp(send_f, 2)
    d_own = attend_back(info, dzb_one, single_w, 0, own01)
    grad_a = pair_grad(info, tok, d_own, OWN)
    keep_a, send_a = fold(grad_a, got_b, 2, 0)
    got_a = flip_dp(send_a, 1)
    mine, *sent = input_back(
        info, d_own, d_other, d_ends, dzb_one, ((own_pair, other_pair), (OWN, OTHER)), single_w
    )
    sent_got = flip_cores(sent)
    keep_s2, send_s2 = fold(keep_s, got_s, 2, TAIL)
    got_s2 = flip_chip(send_s2)
    keep_f3, send_f3 = fold(keep_f, got_f, 2, 0)
    got_f3 = flip_dp(send_f3, 4)
    own_tok, *send_tok = tokens_add(mine, sent_got)
    got_tok = [flip_chip(v) for v in send_tok]
    keep_s3, send_s3, keep_a3, send_a3 = fold_last(keep_s2, got_s2, keep_a, got_a)
    got_s3, got_a3 = flip_dp(send_s3, 2), flip_dp(send_a3, 2)
    own_out, send_out = halves(info, out)
    got_out = flip_chip(send_out)
    grad_up, grad_down = feed_out(keep_f3, got_f3)
    keep_z, send_z = fold_z(keep_s3, got_s3, keep_a3, got_a3)
    got_z = flip_dp(send_z, 4)
    grad_tokens = tokens_out(info, own_tok, got_tok)
    output = slots_of(info, own_out, got_out)
    grads = attend_out((keep_z, got_z), height)
    return (output, grad_tokens, *grads[:4], grad_up, grad_down.T, *grads[4:])


def plain_path(info, tokens, cotangent, weights, lengths, masks, norms):
    w_query, w_key, w_value, w_out, w_up, w_down = weights
    mask_own, mask_other, mask_ends = masks
    g_one, b_one, g_two, b_two = norms
    features, units = tokens.shape[2], w_up.shape[1]
    flat = (((0, 0),),)
    two = (((0, 0),), ((1, 0),))

    def gathered(piece):
        own = lax.all_gather(piece, "dp", axis=0, tiled=True)[None]
        return own, flip_chip(own)

    got_rows = flip_chip(split(info, tokens, cotangent, True))
    own_rows = split(info, tokens, cotangent, False)
    quarters = (own_rows, got_rows, flip_core(own_rows), flip_core(got_rows))
    tok = merge(info, quarters)
    firsts = [w[:, : 2 * HD] for w in (w_query, w_key, w_value)]
    thirds = [w_out.T] + [w[:, 2 * HD :] for w in (w_query, w_key, w_value)]
    pair_w = (gathered(jnp.concatenate(firsts, axis=1)), two)
    single_w = (gathered(jnp.concatenate(thirds, axis=1)), two)
    up, down = (gathered(w_up), two), (gathered(w_down.T), two)
    own01 = attend(info, lengths, tok, ((pair_w[0][0],), flat), True, mask_own[:2])
    other01 = attend(info, lengths, tok, ((pair_w[0][1],), flat), True, mask_other[:2])
    ends = attend(info, lengths, tok, single_w, False, mask_ends)
    contexts = (own01[3], other01[3], ends[3])
    part = project(info, contexts, single_w, features)
    normal, scale_one, hn = norm_one(tok, part, flip_cores(part), g_one, b_one)
    act1, slope1 = feed_up(info, hn, ((up[0][0],), flat), units)
    act2, slope2 = feed_up(info, hn, ((up[0][1],), flat), units)
    part = feed_down(info, act1, act2, down, features)
    out, dzb_two, sums_two = norm_two(
        info, lengths, hn, part, flip_cores(part), quarters, g_two, b_two
    )
    places = (((0, 0),), ((1, 0),)) * 2
    grad_d = feed_grad(info, dzb_two, act1, act2, places)
    du1, du2, *part = feed_back(info, dzb_two, slope1, slope2, up, down)
    grad_u = feed_grad(info, hn, du1, du2, places)
    dzb_one, sums_one = norm_one_back(
        normal, scale_one, dzb_two, part, flip_cores(part), g_one
    )
    d_ends = attend_back(info, dzb_one, single_w, None, ends)
    keep_s, send_s = single_grad(
        info, tok, d_ends, dzb_one, contexts, sums_one, sums_two, places[2:]
    )
    d_other = attend_back(info, dzb_one, single_w, 1, other01)
    grad_b = pair_grad(info, tok, d_other, places[0])
    d_own = attend_back(info, dzb_one, single_w, 0, own01)
    grad_a = pair_grad(info, tok, d_own, places[0])
    mine, *sent = input_back(info, d_own, d_other, d_ends, dzb_one, pair_w, single_w)
    own_tok, *send_tok = tokens_add(mine, flip_cores(sent))
    own_out, send_out = halves(info, out)
    output = slots_of(info, own_out, flip_chip(send_out))
    grad_tokens = tokens_out(info, own_tok, [flip_chip(v) for v in send_tok])

    def summed(own, other):
        total = own.astype(F32) + flip_chip(other).astype(F32)
        return lax.psum_scatter(total, "dp", scatter_dimension=0, tiled=True)

    def wide(keep1, send1, keep2, send2):
        return jnp.concatenate([summed(keep1[0], send1[0]), summed(keep2[0], send2[0])], axis=1)

    single = summed(keep_s[:features], send_s[:features])
    pair = summed(grad_a[0], grad_b[0])
    grads = [
        jnp.concatenate(
            [pair[:, 2 * i * HD : 2 * (i + 1) * HD], single[:, (3 + i) * HD : (4 + i) * HD]],
            axis=1,
        )
        for i in range(3)
    ] + [single[:, : 3 * HD].T]
    sums = decode(keep_s[features:])
    sums = lax.psum(sums + flip_chip(sums), "dp")
    sums = [jnp.concatenate([sums[i], sums[4 + i]]) for i in range(4)]
    return (output, grad_tokens, *grads, wide(*grad_u), wide(*grad_d).T, *sums)


def local(
    tokens,
    w_query,
    w_key,
    w_value,
    w_out,
    w_up,
    w_down,
    gain_attn,
    bias_attn,
    gain_ffn,
    bias_ffn,
    lengths,
    random_blocks,
    cotangent,
):
    ORDER.clear()
    size = lax.axis_size("dp")
    rank = lax.axis_index("mp")
    me = lax.axis_index("dp")
    x, core = rank // 2, rank % 2
    quarter = tokens.shape[1]
    seq = 4 * quarter
    height = w_query.shape[0]
    span = w_query.shape[1]
    heads = span // HD
    nblocks = seq // BLOCK
    fast = size == 8 and height % 16 == 0

    shift = x * (seq // 2)
    info = jnp.stack([me, x, core, shift]).astype(jnp.int32)

    blocks = (jnp.arange(nblocks) + x * (nblocks // 2)) % nblocks
    near_blocks = jnp.abs(blocks[:, None] - blocks[None, :]) <= 1
    edge = (blocks == 0) | (blocks == nblocks - 1)
    fixed = near_blocks | edge[:, None] | edge[None, :]

    def table(shard):
        chosen = lax.dynamic_slice_in_dim(random_blocks, shard * heads, heads, 0)
        chosen = jnp.roll(chosen, -x * (nblocks // 2), axis=1)
        hit = jnp.any(chosen[:, None, :, :] == blocks[None, :, None, None], axis=3)
        bias = jnp.where(fixed.T[None] | hit, 0.0, NEGATIVE)
        return jnp.concatenate(
            [
                jnp.zeros((heads, nblocks, HD), F32),
                bias,
                jnp.full((heads, nblocks, 3), -1.0, F32),
                jnp.zeros((heads, nblocks, HD - 3 - nblocks), F32),
            ],
            axis=2,
        )

    mask_own, mask_other = table(rank), table(rank ^ 2)
    mask_ends = jnp.concatenate([mask_own[2:], mask_other[2:]], axis=0)
    g_one, b_one = gain_attn[None], bias_attn[None]
    g_two, b_two = gain_ffn[None], bias_ffn[None]

    path = fast_path if fast else plain_path
    return path(
        info,
        tokens,
        cotangent,
        (w_query, w_key, w_value, w_out, w_up, w_down),
        lengths,
        (mask_own, mask_other, mask_ends),
        (g_one, b_one, g_two, b_two),
    )


def solution(mesh):
    return jax.shard_map(
        local,
        mesh=mesh,
        in_specs=(
            P("dp", "mp", None),
            P("dp", "mp"),
            P("dp", "mp"),
            P("dp", "mp"),
            P("mp", "dp"),
            P("dp", "mp"),
            P("mp", "dp"),
            P(),
            P(),
            P(),
            P(),
            P("dp"),
            P(),
            P("dp", "mp", None),
        ),
        out_specs=(
            P("dp", "mp", None),
            P("dp", "mp", None),
            P("dp", "mp"),
            P("dp", "mp"),
            P("dp", "mp"),
            P("mp", "dp"),
            P("dp", "mp"),
            P("mp", "dp"),
            P(),
            P(),
            P(),
            P(),
        ),
        check_vma=False,
    )
```

```python
import functools

import jax
import jax.numpy as jnp
from jax import lax
from jax.experimental import pallas as pl
from jax.experimental.pallas import tpu as pltpu
from jax.sharding import PartitionSpec as P

HD = 64
BLOCK = 64
LANES = 128
TILE = 256
SENT = 256
EPSILON = 1e-12
TAIL = 32
TOKEN = (8, 128)
ROOM = {
    "attend": 20,
    "attend_back": 28,
    "project": 12,
    "input_back": 24,
    "norm_one": 12,
    "norm_two": 16,
    "norm_one_back": 14,
    "feed_up": 16,
    "feed_down": 18,
    "feed_back": 32,
    "turn_rows": 12,
    "feed_grad": 24,
    "pair_grad": 16,
    "single_grad": 24,
    "join": 1,
    "join_sides": 1,
    "beside": 1,
    "pack": 2,
    "split": 4,
    "merge": 1,
    "fold": 6,
    "fold_add": 8,
    "fold_feed": 10,
    "fold_sides": 8,
    "fold_last": 6,
    "fold_z": 4,
    "halves": 1,
    "slots": 1,
    "tokens_add": 8,
    "tokens_out": 8,
    "feed_out": 6,
    "attend_out": 6,
}
SCALE = 0.125
LOG2E = 1.4426950408889634
LN2 = 0.6931471805599453
NEGATIVE = -1e30
F32 = jnp.float32
BF16 = jnp.bfloat16

CORE_SWAP = [(0, 1), (1, 0), (2, 3), (3, 2)]
CHIP_SWAP = [(0, 2), (2, 0), (1, 3), (3, 1)]


def nn(a, b):
    return lax.dot_general(a, b, (((1,), (0,)), ((), ())), preferred_element_type=F32)


def nt(a, b):
    return lax.dot_general(a, b, (((1,), (1,)), ((), ())), preferred_element_type=F32)


def tn(a, b):
    return lax.dot_general(a, b, (((0,), (0,)), ((), ())), preferred_element_type=F32)


def vmem():
    return pl.BlockSpec(memory_space=pltpu.VMEM)


def smem():
    return pl.BlockSpec(memory_space=pltpu.SMEM)


def anywhere():
    return pl.BlockSpec(memory_space=pl.ANY)


def in_hbm(values):
    return tuple(pltpu.with_memory_space_constraint(v, pltpu.HBM) for v in values)


def array(shape, dtype):
    return jax.ShapeDtypeStruct(shape, dtype)


ORDER = []


def run(kernel, name, args, specs, outs, out_specs, scratch=()):
    given, made = len(args), len(outs)
    extra = tuple(ORDER)

    def body(*refs):
        ins, rest = refs[:given], refs[given + len(extra) :]
        rest[made][...] = jnp.zeros(TOKEN, F32)
        kernel(*ins, *rest[:made], *rest[made + 1 :])

    results = pl.pallas_call(
        body,
        out_shape=tuple(outs) + (array(TOKEN, F32),),
        in_specs=list(specs) + [anywhere()] * len(extra),
        out_specs=tuple(out_specs) + (vmem(),),
        scratch_shapes=list(scratch),
        compiler_params=pltpu.CompilerParams(vmem_limit_bytes=ROOM[name] * 2**20),
        cost_estimate=pl.CostEstimate(flops=1, bytes_accessed=0, transcendentals=0),
        name=name,
    )(*args, *extra)
    ORDER[:] = [results[-1]]
    return results[:-1]


def put_rows(parts, t, value):
    height, tile = parts[0].shape[0], value.shape[0]
    if height <= tile:
        per = tile // height
        for k in range(per):
            parts[t * per + k][...] = value[k * height : (k + 1) * height]
    else:
        per = height // tile
        parts[t // per][pl.ds(t % per * tile, tile), :] = value


def get_sum(parts, more, t):
    height = parts[0].shape[0]
    if height <= TILE:
        per = TILE // height
        at = range(t * per, (t + 1) * per)
        pieces = [parts[k][...].astype(F32) + more[k][...].astype(F32) for k in at]
        return pieces[0] if per == 1 else jnp.concatenate(pieces, axis=0)
    per = height // TILE
    at = pl.ds(t % per * TILE, TILE)
    return parts[t // per][at, :].astype(F32) + more[t // per][at, :].astype(F32)


def tile_rows(ref):
    return [(t, pl.ds(t * TILE, TILE)) for t in range(ref.shape[0] // TILE)]


def far(shape, dtype):
    return pltpu.HBM(shape, dtype)


def tiles(seq, width, height):
    parts = (array((height, width), BF16),) * (seq // height)
    return parts, [vmem()] * len(parts)


def place(me, refs, slots, dst_ref, first=0, last=None, only=None, to=0):
    for ref, of in zip(refs, slots):
        height, width = ref.shape[1], ref.shape[2]
        end = width if last is None else last
        for e, (chip, j) in enumerate(of):
            if only is not None and chip != only:
                continue
            at = 0 if height == dst_ref.shape[0] else pl.multiple_of((me ^ j) * height, height)
            at_column = to + (0 if only is not None else chip * (end - first))
            dst_ref[pl.ds(at, height), pl.ds(at_column, end - first)] = ref[e, :, first:end]


def pick(me, fulls, out_ref, slots, first):
    _, height, width = out_ref.shape
    for e, (chip, j) in enumerate(slots):
        full = fulls[chip]
        at = 0 if height == full.shape[0] else pl.multiple_of((me ^ j) * height, height)
        out_ref[e] = full[pl.ds(at, height), pl.ds(first, width)].astype(BF16)


def attend_kernel(slots, columns, only, places, info, lengths, tok, mask, *rest):
    refs, (qa, ka, va, ctx, wfull) = rest[: len(slots)], rest[len(slots) :]
    seq = tok.shape[0]
    place(info[0], refs, slots, wfull, *columns, only)
    lane = lax.broadcasted_iota(jnp.int32, (TILE, LANES), 1)
    row0 = lax.broadcasted_iota(jnp.int32, (TILE, LANES), 0)
    for t in range(seq // TILE):
        at = pl.ds(t * TILE, TILE)
        row = row0 + t * TILE
        made = nn(tok[at, :], wfull[...])
        onehot = jnp.where(lane - HD == row // BLOCK, 1.0, 0.0)[:, HD:]
        position = row + info[3]
        position = jnp.where(position >= seq, position - seq, position)
        dead = (position >= lengths[info[1]]) & (lane >= HD) & (lane < HD + 16)
        for h, (q_at, k_at, v_at) in enumerate(places):
            q = made[:, q_at : q_at + HD] * (SCALE * LOG2E)
            k = made[:, k_at : k_at + HD]
            v = made[:, v_at : v_at + HD]
            qa[h, at, :] = jnp.concatenate([q, onehot], axis=1).astype(BF16)
            per = TILE // BLOCK
            table = jnp.concatenate(
                [
                    jnp.broadcast_to(mask[h, t * per + b : t * per + b + 1, :], (BLOCK, LANES))
                    for b in range(per)
                ],
                axis=0,
            )
            table = jnp.where(dead, NEGATIVE, table)
            ka[h, at, :] = jnp.concatenate([k, table[:, HD:]], axis=1).astype(BF16)
            va[h, at, :] = jnp.concatenate([v, jnp.full((TILE, HD), -1.0, F32)], axis=1).astype(BF16)
    for t in range(seq // TILE):
        at = pl.ds(t * TILE, TILE)
        pieces = []
        for h in range(len(places)):
            q = qa[h, at, :]
            s = nt(q, ka[h])
            top = jnp.max(s, axis=1, keepdims=True)
            p = jnp.exp2(s - top).astype(BF16)
            got = nn(p, va[h])
            total = -got[:, HD:]
            pieces.append(got[:, :HD] / total)
            log = top + jnp.log2(-got)
            hi = log.astype(BF16).astype(F32)
            mid = (log - hi).astype(BF16).astype(F32)
            low = log - hi - mid
            new = jnp.where(
                lane == HD + 16,
                hi,
                jnp.where(lane == HD + 17, mid, jnp.where(lane == HD + 18, low, q.astype(F32))),
            )
            qa[h, at, :] = new.astype(BF16)
        ctx[at, :] = jnp.concatenate(pieces, axis=1).astype(BF16)


PAIR = ((0, 2 * HD, 4 * HD), (HD, 3 * HD, 5 * HD))
SINGLES = ((HD, 2 * HD, 3 * HD), (5 * HD, 6 * HD, 7 * HD))


def attend(info, lengths, tok, gathered, pair, mask):
    arrays, slots = gathered
    seq, width = tok.shape
    aug = far((2, seq, LANES), BF16)
    columns, only, cols = ((0, 6 * HD), 0, 6 * HD) if pair else ((2 * HD, 6 * HD), None, 8 * HD)
    return run(
        functools.partial(attend_kernel, slots, columns, only, PAIR if pair else SINGLES),
        "attend",
        (info, lengths, tok, mask) + arrays,
        [smem()] * 2 + [vmem()] * (2 + len(arrays)),
        (aug, aug, aug, array((seq, LANES), BF16)),
        [vmem()] * 4,
        [pltpu.VMEM((width, cols), BF16)],
    )


def place_out(me, refs, slots, pairs, ends):
    place(me, refs, slots, pairs, 0, 2 * HD)
    place(me, refs, slots, ends, 2 * HD, 4 * HD)
    both = ends[...]
    ends[:, :LANES] = jnp.concatenate([both[:, :HD], both[:, LANES : LANES + HD]], axis=1)


def project_kernel(slots, info, own, other, ends, *rest):
    refs, parts, (w1, w2) = rest[: len(slots)], rest[len(slots) : -2], rest[-2:]
    place_out(info[0], refs, slots, w1, w2)
    for t, at in tile_rows(own):
        both = jnp.concatenate([own[at, :], other[at, :]], axis=1)
        out = nt(both, w1[...]) + nt(ends[at, :], w2[:, :LANES])
        put_rows(parts, t, out.astype(BF16))


def project(info, contexts, gathered, width):
    arrays, slots = gathered
    seq = contexts[0].shape[0]
    return run(
        functools.partial(project_kernel, slots),
        "project",
        (info,) + contexts + arrays,
        [smem()] + [vmem()] * (3 + len(arrays)),
        *tiles(seq, width, 2 * TILE),
        [pltpu.VMEM((width, 2 * LANES), BF16)] * 2,
    )


def attend_back_kernel(slots, chip, info, dz, qa, ka, va, ctx, *rest):
    refs, (dqkv, pairs, ends, da) = rest[: len(slots)], rest[len(slots) :]
    seq = dz.shape[0]
    heads = qa.shape[0]
    if chip is None:
        place_out(info[0], refs, slots, pairs, ends)
        wfull = ends.at[:, pl.ds(0, LANES)]
    else:
        place(info[0], refs, slots, pairs, 0, 2 * HD, chip)
        wfull = pairs.at[:, pl.ds(0, LANES)]
    lane = lax.broadcasted_iota(jnp.int32, (TILE, LANES), 1)
    for t in range(seq // TILE):
        at = pl.ds(t * TILE, TILE)
        dctx = nn(dz[at, :], wfull[...]).astype(BF16).astype(F32)
        both = dctx * ctx[at, :].astype(F32)
        for h in range(heads):
            inner = jnp.sum(both[:, h * HD : (h + 1) * HD], axis=1, keepdims=True)
            hi = inner.astype(BF16).astype(F32)
            mid = (inner - hi).astype(BF16).astype(F32)
            low = inner - hi - mid
            one = jnp.concatenate(
                [dctx[:, h * HD : (h + 1) * HD], jnp.zeros((TILE, HD), F32)], axis=1
            )
            one = jnp.where(lane == HD, hi, one)
            one = jnp.where(lane == HD + 1, mid, one)
            one = jnp.where(lane == HD + 2, low, one)
            da[h, at, :] = one.astype(BF16)

    def turned(values):
        return jnp.transpose(values.astype(F32))[:HD].astype(BF16)

    grads = []
    for h in range(heads):
        k_turned, q_turned, d_turned = turned(ka[h]), turned(qa[h]), turned(da[h])
        dq, dk, dv = None, [], []
        for t in range(seq // TILE):
            at = pl.ds(t * TILE, TILE)
            p = jnp.exp2(nt(ka[h, at, :], qa[h]))
            ds = (p * nt(va[h, at, :], da[h])).astype(BF16)
            dv.append(nt(d_turned, p.astype(BF16)))
            dk.append(nt(q_turned, ds))
            more = nn(k_turned[:, t * TILE : (t + 1) * TILE], ds)
            dq = more if dq is None else dq + more
        dk = jnp.concatenate(dk, axis=1) * LN2
        grads.append((dq * SCALE, dk, jnp.concatenate(dv, axis=1)))
    (dq0, dk0, dv0), (dq1, dk1, dv1) = grads
    if chip is None:
        blank = jnp.zeros_like(dq0)
        stacks = ((blank, dq0), (dk0, dv0), (blank, dq1), (dk1, dv1))
    else:
        stacks = ((dq0, dq1), (dk0, dk1), (dv0, dv1))
    for i, stack in enumerate(stacks):
        both = jnp.transpose(jnp.concatenate(stack, axis=0))
        dqkv[:, i * LANES : (i + 1) * LANES] = both.astype(BF16)


def attend_back(info, dz, gathered, chip, saved):
    arrays, slots = gathered
    qa, ka, va, ctx = saved
    seq, width = dz.shape
    cols = 8 * HD if chip is None else 6 * HD
    return run(
        functools.partial(attend_back_kernel, slots, chip),
        "attend_back",
        (info, dz, qa, ka, va, ctx) + arrays,
        [smem()] + [vmem()] * (5 + len(arrays)),
        (array((seq, cols), BF16),),
        [vmem()],
        [
            pltpu.VMEM((width, 2 * LANES), BF16),
            pltpu.VMEM((width, 2 * LANES), BF16),
            pltpu.VMEM((2, seq, LANES), BF16),
        ],
    )[0]


def input_back_kernel(slots1, slots2, info, own, other, ends, dz, *rest):
    n1, n2 = len(slots1), len(slots2)
    refs1, refs2, (mine, *sent, w1, w2) = rest[:n1], rest[n1 : n1 + n2], rest[n1 + n2 :]
    place(info[0], refs1, slots1, w1)
    place(info[0], refs2, slots2, w2, 2 * HD, 6 * HD)
    per = len(sent) // 2
    height = sent[0].shape[0]
    for half in range(dz.shape[0] // TILE // 2):
        for whose in range(2):
            tile = 2 * half + (info[2] if whose == 0 else 1 - info[2])
            at = pl.ds(pl.multiple_of(tile * TILE, TILE), TILE)
            pairs = jnp.concatenate([own[at, :], other[at, :]], axis=1)
            back = nt(pairs, w1[...]) + nt(ends[at, :], w2[...])
            if whose == 0:
                mine[half] = back + dz[at, :].astype(F32)
                continue
            for k in range(per):
                part = back[k * height : (k + 1) * height]
                sent[half * per + k][...] = part.astype(BF16)


def input_back(info, own, other, ends, dz, gathered1, gathered2):
    seq, width = dz.shape
    arrays = gathered1[0] + gathered2[0]
    halves = (seq // TILE // 2, TILE, width)
    grads = (own, other, ends, dz)
    return run(
        functools.partial(input_back_kernel, gathered1[1], gathered2[1]),
        "input_back",
        (info,) + grads + arrays,
        [smem()] + [vmem()] * (len(grads) + len(arrays)),
        (array(halves, F32),) + (array((SENT, width), BF16),) * (seq // 2 // SENT),
        [vmem()] * (1 + seq // 2 // SENT),
        [pltpu.VMEM((width, 12 * HD), BF16), pltpu.VMEM((width, 8 * HD), BF16)],
    )


def center(z):
    mean = jnp.mean(z, axis=1, keepdims=True)
    moved = z - mean
    spread = jnp.mean(moved * moved, axis=1, keepdims=True)
    scale = lax.rsqrt(spread + EPSILON)
    return moved * scale, scale


def norm_back(n, scale, gy, gain):
    dn = gy * gain
    return scale * (
        dn - jnp.mean(dn, axis=1, keepdims=True) - n * jnp.mean(dn * n, axis=1, keepdims=True)
    )


def add_sums(gy, n, sums):
    more = [jnp.sum(v, axis=0, keepdims=True) for v in (gy * n, gy)]
    return more if sums is None else [a + b for a, b in zip(sums, more)]


def norm_one_kernel(tok, gain, bias, *rest):
    *parts, normal, scale, hn = rest
    count = len(parts) // 2
    for t, at in tile_rows(tok):
        value = tok[at, :].astype(F32) + get_sum(parts[:count], parts[count:], t)
        n, r = center(value)
        normal[at, :] = n.astype(BF16)
        scale[at, :] = r
        hn[at, :] = (n * gain[...] + bias[...]).astype(BF16)


def norm_one(tok, p0, p1, gain, bias):
    seq, width = tok.shape
    return run(
        norm_one_kernel,
        "norm_one",
        (tok, gain, bias, *p0, *p1),
        [vmem()] * (3 + len(p0) + len(p1)),
        (array((seq, width), BF16), array((seq, 1), F32), array((seq, width), BF16)),
        [vmem()] * 3,
    )


def norm_two_kernel(info, lengths, hn, own, got, core_own, core_got, gain, bias, *rest):
    *parts, out, dzb, sums = rest
    count = len(parts) // 2
    seq = hn.shape[0]
    total = None
    for t, at in tile_rows(hn):
        value = hn[at, :].astype(F32) + get_sum(parts[:count], parts[count:], t)
        n, scale = center(value)
        out[at, :] = (n * gain[...] + bias[...]).astype(BF16)
        position = lax.broadcasted_iota(jnp.int32, value.shape, 0) + t * TILE + info[3]
        position = jnp.where(position >= seq, position - seq, position)
        mine, others = ((own, core_own), (got, core_got))[t // 2]
        cot = jnp.where(info[2] == t % 2, mine[1].astype(F32), others[1].astype(F32))
        gy = jnp.where(position < lengths[info[1]], cot, 0.0)
        dzb[at, :] = norm_back(n, scale, gy, gain[...]).astype(BF16)
        total = add_sums(gy, n, total)
    sums[...] = jnp.concatenate(total, axis=0)


def norm_two(info, lengths, hn, m0, m1, cot, gain, bias):
    seq, width = hn.shape
    return run(
        norm_two_kernel,
        "norm_two",
        (info, lengths, hn, *cot, gain, bias, *m0, *m1),
        [smem()] * 2 + [vmem()] * (3 + len(cot) + len(m0) + len(m1)),
        (
            array((seq, width), BF16),
            array((seq, width), BF16),
            array((2, width), F32),
        ),
        [vmem()] * 3,
    )


def norm_one_back_kernel(normal, scale, dz2, gain, *rest):
    *parts, dzb, sums = rest
    count = len(parts) // 2
    total = None
    for t, at in tile_rows(dz2):
        n = normal[at, :].astype(F32)
        gy = dz2[at, :].astype(F32) + get_sum(parts[:count], parts[count:], t)
        dzb[at, :] = norm_back(n, scale[at, :], gy, gain[...]).astype(BF16)
        total = add_sums(gy, n, total)
    sums[...] = jnp.concatenate(total, axis=0)


def norm_one_back(normal, scale, dz2, p0, p1, gain):
    seq, width = normal.shape
    return run(
        norm_one_back_kernel,
        "norm_one_back",
        (normal, scale, dz2, gain, *p0, *p1),
        [vmem()] * (4 + len(p0) + len(p1)),
        (array((seq, width), BF16), array((2, width), F32)),
        [vmem()] * 2,
    )


def gelu_pair(u):
    phi = 0.5 + 0.5 * lax.erf(u * 0.7071067811865476)
    return u * phi, phi + u * (jnp.exp(-0.5 * u * u) * 0.3989422804014327)


def feed_up_kernel(slots, info, hn, *rest):
    refs, (active, slope, wfull) = rest[: len(slots)], rest[len(slots) :]
    place(info[0], refs, slots, wfull)
    for _, at in tile_rows(hn):
        a, g = gelu_pair(nn(hn[at, :], wfull[...]))
        active[at, :] = a.astype(BF16)
        slope[at, :] = g.astype(BF16)


def feed_up(info, hn, gathered, units):
    arrays, slots = gathered
    seq, width = hn.shape
    return run(
        functools.partial(feed_up_kernel, slots),
        "feed_up",
        (info, hn) + arrays,
        [smem()] + [vmem()] * (1 + len(arrays)),
        (array((seq, units), BF16), array((seq, units), BF16)),
        [vmem()] * 2,
        [pltpu.VMEM((width, units), BF16)],
    )


def feed_down_kernel(slots, info, act1, act2, *rest):
    refs, parts, wfull = rest[: len(slots)], rest[len(slots) : -1], rest[-1]
    place(info[0], refs, slots, wfull)
    for t, at in tile_rows(act1):
        both = jnp.concatenate([act1[at, :], act2[at, :]], axis=1)
        put_rows(parts, t, nt(both, wfull[...]).astype(BF16))


def feed_down(info, act1, act2, gathered, width):
    seq, units = act1.shape
    arrays, slots = gathered
    return run(
        functools.partial(feed_down_kernel, slots),
        "feed_down",
        (info, act1, act2) + arrays,
        [smem()] + [vmem()] * (2 + len(arrays)),
        *tiles(seq, width, seq),
        [pltpu.VMEM((width, 2 * units), BF16)],
    )


def feed_back_kernel(slots_up, slots_down, info, dzb, slope1, slope2, *rest):
    n1, n2 = len(slots_up), len(slots_down)
    ups, downs, (du1, du2, *parts, up, down) = rest[:n1], rest[n1 : n1 + n2], rest[n1 + n2 :]
    place(info[0], ups, slots_up, up)
    place(info[0], downs, slots_down, down)
    units = du1.shape[1]
    for t, at in tile_rows(dzb):
        out = None
        for i, (slope, du) in enumerate(((slope1, du1), (slope2, du2))):
            cols = pl.ds(i * units, units)
            grad = (nn(dzb[at, :], down[:, cols]) * slope[at, :].astype(F32)).astype(BF16)
            du[at, :] = grad
            more = nt(grad, up[:, cols])
            out = more if out is None else out + more
        put_rows(parts, t, out.astype(BF16))


def feed_back(info, dzb, slope1, slope2, up, down):
    seq, width = dzb.shape
    units = slope1.shape[1]
    arrays = up[0] + down[0]
    parts, part_specs = tiles(seq, width, TILE)
    return run(
        functools.partial(feed_back_kernel, up[1], down[1]),
        "feed_back",
        (info, dzb, slope1, slope2) + arrays,
        [smem()] + [vmem()] * (3 + len(arrays)),
        (array((seq, units), BF16),) * 2 + parts,
        [vmem()] * 2 + part_specs,
        [pltpu.VMEM((width, 2 * units), BF16)] * 2,
    )


def turn_rows_kernel(first, second, out1, out2):
    for values, out in ((first, out1), (second, out2)):
        for t, at in tile_rows(values):
            out[:, t * TILE : (t + 1) * TILE] = jnp.transpose(values[at, :])


def turn_rows(first, second):
    out = array(first.shape[::-1], BF16)
    return run(
        turn_rows_kernel,
        "turn_rows",
        (first, second),
        [vmem()] * 2,
        (out, out),
        [vmem()] * 2,
    )


def feed_grad_kernel(product, places, info, a, d1, d2, *rest):
    outs, full = rest[:4], rest[4]
    half = outs[0].shape[2]
    full[...] = product(a[...], jnp.concatenate([d1[...], d2[...]], axis=1))
    fulls = [full.at[:, pl.ds(2 * chip * half, 2 * half)] for chip in range(2)]
    for i, out in enumerate(outs):
        pick(info[0], fulls, out, places[i], (i // 2) * half)


def feed_grad(info, a, d1, d2, places, product):
    seq, units = d1.shape
    width = a.shape[0] if product is nn else a.shape[1]
    count = len(places[0])
    out = array((count, width // count, units // 2), BF16)
    return run(
        functools.partial(feed_grad_kernel, product, places),
        "feed_grad",
        (info, a, d1, d2),
        [smem()] + [vmem()] * 3,
        (out,) * 4,
        [vmem()] * 4,
        [pltpu.VMEM((width, 2 * units), F32)],
    )


def pair_grad_kernel(slots, info, tok_turned, d, out, full):
    full[...] = nn(tok_turned[...], d[...])
    pick(info[0], (full,), out, slots, 0)


def pair_grad(info, tok_turned, d, slots):
    width = tok_turned.shape[0]
    cols = d.shape[1]
    return run(
        functools.partial(pair_grad_kernel, slots),
        "pair_grad",
        (info, tok_turned, d),
        [smem()] + [vmem()] * 2,
        (array((len(slots), width // len(slots), cols), BF16),),
        [vmem()],
        [pltpu.VMEM((width, cols), F32)],
    )[0]


def encode(sums):
    hi = sums.astype(BF16).astype(F32)
    mid = (sums - hi).astype(BF16).astype(F32)
    low = sums - hi - mid
    return jnp.concatenate([hi, mid, low, jnp.zeros_like(low)], axis=0).astype(BF16)


def decode(coded):
    values = coded.astype(F32)
    n = values.shape[0] // 4
    return values[:n] + values[n : 2 * n] + values[2 * n : 3 * n]


def single_grad_kernel(
    places, info, tok_turned, d, dz, own, other, ends, sums_one, sums_two, keep, send, full
):
    mine = nn(tok_turned[...], d[...])
    heads = tn(dz[...], jnp.concatenate([ends[...], own[...], other[...]], axis=1))
    third = heads[:, :LANES]
    blank = jnp.zeros((third.shape[0], HD), F32)
    width = full.shape[2]
    both = jnp.concatenate([sums_one[...], sums_two[...]], axis=0)
    both = encode(jnp.concatenate([both[:, :width], both[:, width:]], axis=0))
    for chip in range(2):
        full[chip, :, :LANES] = heads[:, (chip + 1) * LANES : (chip + 2) * LANES]
        at = chip * 4 * HD
        o_third = jnp.concatenate([third[:, chip * HD : (chip + 1) * HD], blank], axis=1)
        full[chip, :, LANES : 2 * LANES] = o_third + mine[:, at : at + LANES]
        full[chip, :, 2 * LANES :] = mine[:, at + LANES : at + 2 * LANES]
    for out, slots in zip((keep, send), places):
        count = len(slots)
        height = full.shape[1] // count
        for e, (chip, j) in enumerate(slots):
            at = 0 if count == 1 else pl.multiple_of((info[0] ^ j) * height, height)
            out[pl.ds(e * height, height), :] = full[chip, pl.ds(at, height), :].astype(BF16)
        out[pl.ds(count * height, TAIL), :] = both


def single_grad(info, tok_turned, d, dz, contexts, sums_one, sums_two, places):
    width = tok_turned.shape[0]
    cols = 6 * HD
    out = array((width + TAIL, cols), BF16)
    return run(
        functools.partial(single_grad_kernel, places),
        "single_grad",
        (info, tok_turned, d, dz, *contexts, sums_one, sums_two),
        [smem()] + [vmem()] * 8,
        (out, out),
        [vmem()] * 2,
        [pltpu.VMEM((2, width, cols), F32)],
    )


def across(values, axis, pairs):
    return lax.ppermute(values, axis, pairs)


def flip_chip(values):
    return across(values, "mp", CHIP_SWAP)


def flip_core(values):
    return across(values, "mp", CORE_SWAP)


def flip_cores(parts):
    return [flip_core(p) for p in parts]


def flip_dp(values, distance):
    size = lax.axis_size("dp")
    return across(values, "dp", [(i, i ^ distance) for i in range(size)])


def join_kernel(groups, *refs):
    count = sum(groups)
    parts, outs, sems = refs[:count], refs[count:-1], refs[-1]
    copies = []
    for out, number in zip(outs, groups):
        first = 0
        for part in parts[len(copies) : len(copies) + number]:
            to = out.at[pl.ds(first, part.shape[0])]
            copies.append(pltpu.make_async_copy(part, to, sems.at[len(copies)]))
            first += part.shape[0]
    for copy in copies:
        copy.start()
    for copy in copies:
        copy.wait()


def join(*groups):
    parts = sum((tuple(g) for g in groups), ())
    outs = [array((sum(p.shape[0] for p in g),) + g[0].shape[1:], g[0].dtype) for g in groups]
    return run(
        functools.partial(join_kernel, tuple(len(g) for g in groups)),
        "join",
        parts,
        [anywhere()] * len(parts),
        outs,
        [anywhere()] * len(outs),
        [pltpu.SemaphoreType.DMA((len(parts),))],
    )


def pack_kernel(w_query, w_key, w_value, w_out, out, rows_in, out_in, sems):
    copies = [
        pltpu.make_async_copy(w, rows_in.at[i], sems.at[i])
        for i, w in enumerate((w_query, w_key, w_value))
    ]
    copies.append(pltpu.make_async_copy(w_out, out_in, sems.at[3]))
    for copy in copies:
        copy.start()
    for copy in copies:
        copy.wait()
    for i in range(3):
        out[0, :, 2 * i * HD : 2 * (i + 1) * HD] = rows_in[i, :, : 2 * HD]
    parts = [jnp.transpose(out_in[...].astype(F32))]
    parts += [rows_in[i, :, 2 * HD :].astype(F32) for i in range(3)]
    out[0, :, 6 * HD :] = jnp.concatenate(parts, axis=1).astype(BF16)


def pack(w_query, w_key, w_value, w_out):
    height, span = w_query.shape
    return run(
        pack_kernel,
        "pack",
        in_hbm((w_query, w_key, w_value, w_out)),
        [anywhere()] * 4,
        (array((1, height, 4 * span), BF16),),
        [vmem()],
        [
            pltpu.VMEM((3, height, span), BF16),
            pltpu.VMEM(w_out.shape, BF16),
            pltpu.SemaphoreType.DMA((4,)),
        ],
    )[0]


def beside_kernel(first, second, out, sems):
    width = first.shape[1]
    copies = [
        pltpu.make_async_copy(ref, out.at[0, :, pl.ds(i * width, width)], sems.at[i])
        for i, ref in enumerate((first, second))
    ]
    for copy in copies:
        copy.start()
    for copy in copies:
        copy.wait()


def beside(first, second):
    height, width = first.shape
    return run(
        beside_kernel,
        "beside",
        in_hbm((first, second)),
        [anywhere()] * 2,
        (array((1, height, 2 * width), BF16),),
        [anywhere()],
        [pltpu.SemaphoreType.DMA((2,))],
    )[0]


def join_sides_kernel(count, *refs):
    parts, outs, sems = refs[:count], refs[count : count + 2], refs[count + 2]
    width = outs[0].shape[2]
    copies = []
    each = parts[0].shape[0]
    for i, part in enumerate(parts):
        for side, out in enumerate(outs):
            copies.append(
                pltpu.make_async_copy(
                    part.at[:, :, pl.ds(side * width, width)],
                    out.at[pl.ds(i * each, each)],
                    sems.at[2 * i + side],
                )
            )
    for copy in copies:
        copy.start()
    for copy in copies:
        copy.wait()


def join_sides(parts):
    count = len(parts)
    each, height, width = parts[0].shape
    out = array((count * each, height, width // 2), BF16)
    return run(
        functools.partial(join_sides_kernel, count),
        "join_sides",
        tuple(parts),
        [anywhere()] * count,
        (out, out),
        [anywhere()] * 2,
        [pltpu.SemaphoreType.DMA((2 * count,))],
    )


def fold_kernel(tail, own, got, *outs):
    body = own.shape[0] - tail
    each = body // len(outs)
    for i, out in enumerate(outs):
        at = pl.ds(i * each, each)
        total = (own[at].astype(F32) + got[at].astype(F32)).astype(BF16)
        if tail:
            out[:each] = total
        else:
            out[...] = total
    if tail:
        coded = encode(decode(own[body:]) + decode(got[body:]))
        for out in outs:
            out[each:] = coded


def fold(own, got, parts, tail=0):
    shape = ((own.shape[0] - tail) // parts + tail,) + own.shape[1:]
    return run(
        functools.partial(fold_kernel, tail),
        "fold",
        (own, got),
        [vmem()] * 2,
        (array(shape, BF16),) * parts,
        [vmem()] * parts,
    )


def fold_last_kernel(own1, got1, own2, got2, keep1, send1, keep2, send2):
    height = own2.shape[1]
    each = height + TAIL
    body = own1.shape[0] - TAIL
    coded = encode(decode(own1[body:]) + decode(got1[body:]))
    half = own2.shape[0] // 2
    for i in range(2 * half):
        out, first = (keep1, send1)[i // half], i % half * each
        at = pl.ds(i * height, height)
        out[first : first + height] = (own1[at].astype(F32) + got1[at].astype(F32)).astype(BF16)
        out[first + height : first + each] = coded
        total = own2[i].astype(F32) + got2[i].astype(F32)
        (keep2, send2)[i // half][i % half] = total.astype(BF16)


def fold_last(own1, got1, own2, got2):
    count, height, width = own2.shape
    first = array((count // 2 * (height + TAIL), width), BF16)
    second = array((count // 2, height, width), BF16)
    return run(
        fold_last_kernel,
        "fold_last",
        (own1, got1, own2, got2),
        [vmem()] * 4,
        (first, first, second, second),
        [vmem()] * 4,
    )


def fold_z_kernel(own1, got1, own2, got2, keep, send):
    height = own2.shape[1]
    each = height + TAIL
    for i, out in enumerate((keep, send)):
        at = pl.ds(i * each, height)
        out[:height] = (own1[at].astype(F32) + got1[at].astype(F32)).astype(BF16)
        at = pl.ds(i * each + height, TAIL)
        out[height:each] = encode(decode(own1[at]) + decode(got1[at]))
        out[each:] = (own2[i].astype(F32) + got2[i].astype(F32)).astype(BF16)


def fold_z(own1, got1, own2, got2):
    _, height, width = own2.shape
    out = array((2 * height + TAIL, width), BF16)
    return run(
        fold_z_kernel,
        "fold_z",
        (own1, got1, own2, got2),
        [vmem()] * 4,
        (out, out),
        [vmem()] * 2,
    )


def fold_add_kernel(own1, got1, own2, got2, out1, out2):
    for own, got, out in ((own1, got1, out1), (own2, got2, out2)):
        out[...] = (own[...].astype(F32) + got[...].astype(F32)).astype(BF16)


def fold_add(own1, got1, own2, got2):
    out = array(own1.shape, BF16)
    return run(
        fold_add_kernel,
        "fold_add",
        (own1, got1, own2, got2),
        [vmem()] * 4,
        (out, out),
        [vmem()] * 2,
    )


def fold_feed_kernel(first1, own1, got1, first2, own2, got2, keep1, send1, keep2, send2):
    width = own1.shape[2]
    half = keep1.shape[0]
    for first, own, got, outs in (
        (first1, own1, got1, (keep1, send1)),
        (first2, own2, got2, (keep2, send2)),
    ):
        for i, out in enumerate(outs):
            at = pl.ds(i * half, half)
            out[:, :, :width] = first[at]
            out[:, :, width:] = (own[at].astype(F32) + got[at].astype(F32)).astype(BF16)


def fold_feed(first1, own1, got1, first2, own2, got2):
    count, height, width = own1.shape
    out = array((count // 2, height, 2 * width), BF16)
    return run(
        fold_feed_kernel,
        "fold_feed",
        (first1, own1, got1, first2, own2, got2),
        [vmem()] * 6,
        (out,) * 4,
        [vmem()] * 4,
    )


def fold_sides_kernel(own1, got1, own2, got2, keep, send):
    width = own1.shape[2]
    half = keep.shape[0]
    for side, (own, got) in enumerate(((own1, got1), (own2, got2))):
        for i, out in enumerate((keep, send)):
            at = pl.ds(i * half, half)
            total = own[at].astype(F32) + got[at].astype(F32)
            out[:, :, side * width : (side + 1) * width] = total.astype(BF16)


def fold_sides(own1, got1, own2, got2):
    count, height, width = own1.shape
    out = array((count // 2, height, 2 * width), BF16)
    return run(
        fold_sides_kernel,
        "fold_sides",
        (own1, got1, own2, got2),
        [vmem()] * 4,
        (out, out),
        [vmem()] * 2,
    )


BY_Z = (0, 4, 2, 6)
Y_MAJOR = BY_Z + tuple(z + 1 for z in BY_Z)
OWN = tuple((0, j) for j in Y_MAJOR)
OTHER = tuple((1, j) for j in Y_MAJOR)
CHIP_NEAR = tuple((chip, z) for chip in range(2) for z in BY_Z)
CHIP_FAR = tuple((chip, z + 1) for chip in range(2) for z in BY_Z)


def split_kernel(other, info, first, second, out, sems):
    slot = 1 - info[1] if other else info[1]
    half = first.shape[1] // 2
    copies = []
    for i, values in enumerate((first, second)):
        for j in range(2):
            at = pl.ds(j * half, half)
            copies.append(
                pltpu.make_async_copy(values.at[slot, at], out.at[i, at], sems.at[2 * i + j])
            )
    for copy in copies:
        copy.start()
    for copy in copies:
        copy.wait()


def split(info, first, second, other):
    return run(
        functools.partial(split_kernel, other),
        "split",
        (info, *in_hbm((first, second))),
        [smem()] + [anywhere()] * 2,
        (array((2,) + first.shape[1:], first.dtype),),
        [vmem()],
        [pltpu.SemaphoreType.DMA((4,))],
    )[0]


def merge_kernel(info, own, got, core_own, core_got, out, sems):
    core = info[2]
    copies = []
    for half, (mine, other) in enumerate(((own, core_own), (got, core_got))):
        copies += [
            pltpu.make_async_copy(mine.at[0], out.at[half, core], sems.at[2 * half]),
            pltpu.make_async_copy(other.at[0], out.at[half, 1 - core], sems.at[2 * half + 1]),
        ]
    for copy in copies:
        copy.start()
    for copy in copies:
        copy.wait()


def merge(info, quarters):
    _, quarter, width = quarters[0].shape
    out = run(
        merge_kernel,
        "merge",
        (info, *quarters),
        [smem()] + [anywhere()] * 4,
        (array((2, 2, quarter, width), quarters[0].dtype),),
        [anywhere()],
        [pltpu.SemaphoreType.DMA((4,))],
    )[0]
    return out.reshape(4 * quarter, width)


def halves_kernel(info, rows_ref, own, send, sems):
    quarter = own.shape[0]
    copies = []
    for half, out in enumerate((own, send)):
        at = pl.multiple_of((2 * half + info[2]) * quarter, quarter)
        copies.append(pltpu.make_async_copy(rows_ref.at[pl.ds(at, quarter)], out, sems.at[half]))
    for copy in copies:
        copy.start()
    for copy in copies:
        copy.wait()


def halves(info, values):
    seq, width = values.shape
    out = array((seq // 4, width), values.dtype)
    return run(
        halves_kernel,
        "halves",
        (info, values),
        [smem(), anywhere()],
        (out, out),
        [anywhere()] * 2,
        [pltpu.SemaphoreType.DMA((2,))],
    )


def slots_kernel(info, own, other, out, sems):
    copies = [
        pltpu.make_async_copy(own, out.at[info[1]], sems.at[0]),
        pltpu.make_async_copy(other, out.at[1 - info[1]], sems.at[1]),
    ]
    for copy in copies:
        copy.start()
    for copy in copies:
        copy.wait()


def slots_of(info, own, other):
    return run(
        slots_kernel,
        "slots",
        (info, own, other),
        [smem()] + [anywhere()] * 2,
        (array((2,) + own.shape, own.dtype),),
        [anywhere()],
        [pltpu.SemaphoreType.DMA((2,))],
    )[0]


def tokens_add_kernel(count, mine, *rest):
    got, own, sends = rest[:count], rest[count], rest[count + 1 :]
    per = count // 2
    height = got[0].shape[0]
    for k, part in enumerate(got):
        at = k % per * height
        total = mine[k // per, pl.ds(at, height)] + part[...].astype(F32)
        if k < per:
            own[pl.ds(at, height)] = total
        else:
            each = sends[0].shape[0]
            for first in range(0, height, each):
                sends[(at + first) // each][...] = total[first : first + each].astype(BF16)


def tokens_add(mine, got):
    _, quarter, width = mine.shape
    send = array((quarter // 2, width), BF16)
    return run(
        functools.partial(tokens_add_kernel, len(got)),
        "tokens_add",
        (mine, *got),
        [vmem()] * (1 + len(got)),
        (array((quarter, width), F32), send, send),
        [vmem()] * 3,
    )


def tokens_out_kernel(info, own, *rest):
    *got, out = rest
    out[info[1]] = own[...]
    height = got[0].shape[0]
    for k, part in enumerate(got):
        out[1 - info[1], pl.ds(k * height, height), :] = part[...].astype(F32)


def tokens_out(info, own, got):
    return run(
        tokens_out_kernel,
        "tokens_out",
        (info, own, *got),
        [smem()] + [vmem()] * (1 + len(got)),
        (array((2,) + own.shape, F32),),
        [vmem()],
    )[0]


def feed_out_kernel(own, got, up, down):
    half = up.shape[1] // 2
    for i in range(4):
        at = pl.ds(i * half, half)
        total = own[0, :, at].astype(F32) + got[0, :, at].astype(F32)
        out = (down, up)[i % 2]
        out[:, pl.ds(i // 2 * half, half)] = total


def feed_out(own, got):
    _, height, width = own.shape
    out = array((height, width // 2), F32)
    return run(
        feed_out_kernel,
        "feed_out",
        (own, got),
        [vmem()] * 2,
        (out, out),
        [vmem()] * 2,
    )


def attend_out_kernel(a, b, query, key, value, out, gain1, bias1, gain2, bias2):
    height = query.shape[0]

    def both(first, last):
        return a[first:last].astype(F32) + b[first:last].astype(F32)

    one = both(0, height)
    two = both(height + TAIL, 2 * height + TAIL)
    at = pl.ds(height, TAIL)
    sums = decode(a[at]) + decode(b[at])
    for i, ref in enumerate((query, key, value)):
        ref[...] = jnp.concatenate(
            [two[:, 2 * i * HD : 2 * (i + 1) * HD], one[:, (3 + i) * HD : (4 + i) * HD]], axis=1
        )
    out[...] = jnp.transpose(one[:, : 3 * HD])
    for i, ref in enumerate((gain1, bias1, gain2, bias2)):
        ref[...] = jnp.concatenate([sums[i], sums[4 + i]], axis=0)


def attend_out(pieces, height):
    cols = pieces[0].shape[1]
    span = cols // 2
    return run(
        attend_out_kernel,
        "attend_out",
        tuple(pieces),
        [vmem()] * 2,
        (array((height, span), F32),) * 3
        + (array((span, height), F32),)
        + (array((2 * cols,), F32),) * 4,
        [vmem()] * 8,
    )


def fast_path(info, tokens, cotangent, weights, lengths, masks, norms):
    w_query, w_key, w_value, w_out, w_up, w_down = weights
    mask_own, mask_other, mask_ends = masks
    g_one, b_one, g_two, b_two = norms
    height, features, units = w_query.shape[0], tokens.shape[2], w_up.shape[1]
    flat = (tuple((0, j) for j in Y_MAJOR),)
    got_rows = flip_chip(split(info, tokens, cotangent, True))
    piece = pack(w_query, w_key, w_value, w_out)
    got_piece = flip_dp(piece, 4)
    own_rows = split(info, tokens, cotangent, False)
    (two_attn,) = join([piece, got_piece])
    got_attn = flip_dp(two_attn, 2)
    feed_piece = beside(w_up, w_down.T)
    got_feed = flip_dp(feed_piece, 4)
    z_pair, z_single = join_sides([two_attn, got_attn])
    y_pair, x_single = flip_dp(z_pair, 1), flip_chip(z_single)
    own_pair, near_single = join([z_pair, y_pair], [z_single, x_single])
    other_pair, far_single = flip_chip(own_pair), flip_dp(near_single, 1)
    single_w = ((near_single, far_single), (CHIP_NEAR, CHIP_FAR))
    two_up, two_down = join_sides([feed_piece, got_feed])
    got_up, got_down = flip_dp(two_up, 2), flip_dp(two_down, 2)
    quarters = (own_rows, got_rows, flip_core(own_rows), flip_core(got_rows))
    tok = merge(info, quarters)
    own01 = attend(info, lengths, tok, ((own_pair,), flat), True, mask_own[:2])
    z_up, z_down = join([two_up, got_up], [two_down, got_down])
    y_up, x_down = flip_dp(z_up, 1), flip_chip(z_down)
    other01 = attend(info, lengths, tok, ((other_pair,), flat), True, mask_other[:2])
    ends = attend(info, lengths, tok, single_w, False, mask_ends)
    own_up, near_down = join([z_up, y_up], [z_down, x_down])
    other_up, far_down = flip_chip(own_up), flip_dp(near_down, 1)
    up = ((own_up, other_up), (OWN, OTHER))
    down = ((near_down, far_down), (CHIP_NEAR, CHIP_FAR))
    contexts = (own01[3], other01[3], ends[3])
    attn_part = project(info, contexts, single_w, features)
    attn_got = flip_cores(attn_part)
    normal, scale_one, hn = norm_one(tok, attn_part, attn_got, g_one, b_one)
    act1, slope1 = feed_up(info, hn, ((own_up,), flat), units)
    tok_turned, hn_turned = turn_rows(tok, hn)
    act2, slope2 = feed_up(info, hn, ((other_up,), flat), units)
    mixed = feed_down(info, act1, act2, down, features)
    mixed_got = flip_cores(mixed)
    out, dzb_two, sums_two = norm_two(
        info, lengths, hn, mixed, mixed_got, quarters, g_two, b_two
    )
    keep_d1, send_d1, keep_d2, send_d2 = feed_grad(
        info, dzb_two, act1, act2, (OWN, OTHER, CHIP_NEAR, CHIP_FAR), tn
    )
    got_d1, got_d2 = flip_chip(send_d1), flip_dp(send_d2, 1)
    du1, du2, *back = feed_back(info, dzb_two, slope1, slope2, up, down)
    back_got = flip_cores(back)
    keep_u1, send_u1, keep_u2, send_u2 = feed_grad(
        info, hn_turned, du1, du2, (OWN, OTHER, CHIP_NEAR, CHIP_FAR), nn
    )
    got_u1, got_u2 = flip_chip(send_u1), flip_dp(send_u2, 1)
    sum_d1, sum_d2 = fold_add(keep_d1, got_d1, keep_d2, got_d2)
    dzb_one, sums_one = norm_one_back(normal, scale_one, dzb_two, back, back_got, g_one)
    d_ends = attend_back(info, dzb_one, single_w, None, ends)
    keep_f1, send_f1, keep_f2, send_f2 = fold_feed(
        sum_d1, keep_u1, got_u1, sum_d2, keep_u2, got_u2
    )
    got_f1, got_f2 = flip_dp(send_f1, 1), flip_chip(send_f2)
    keep_s, send_s = single_grad(
        info, tok_turned, d_ends, dzb_one, contexts, sums_one, sums_two, (CHIP_NEAR, CHIP_FAR)
    )
    got_s = flip_dp(send_s, 1)
    d_other = attend_back(info, dzb_one, single_w, 1, other01)
    grad_b = pair_grad(info, tok_turned, d_other, OWN)
    got_b = flip_chip(grad_b)
    keep_f, send_f = fold_sides(keep_f1, got_f1, keep_f2, got_f2)
    got_f = flip_dp(send_f, 2)
    d_own = attend_back(info, dzb_one, single_w, 0, own01)
    grad_a = pair_grad(info, tok_turned, d_own, OWN)
    keep_a, send_a = fold(grad_a, got_b, 2, 0)
    got_a = flip_dp(send_a, 1)
    mine, *sent = input_back(
        info, d_own, d_other, d_ends, dzb_one, ((own_pair, other_pair), (OWN, OTHER)), single_w
    )
    sent_got = flip_cores(sent)
    keep_s2, send_s2 = fold(keep_s, got_s, 2, TAIL)
    got_s2 = flip_chip(send_s2)
    keep_f3, send_f3 = fold(keep_f, got_f, 2, 0)
    got_f3 = flip_dp(send_f3, 4)
    own_tok, *send_tok = tokens_add(mine, sent_got)
    got_tok = [flip_chip(v) for v in send_tok]
    keep_s3, send_s3, keep_a3, send_a3 = fold_last(keep_s2, got_s2, keep_a, got_a)
    got_s3, got_a3 = flip_dp(send_s3, 2), flip_dp(send_a3, 2)
    own_out, send_out = halves(info, out)
    got_out = flip_chip(send_out)
    grad_up, grad_down = feed_out(keep_f3, got_f3)
    keep_z, send_z = fold_z(keep_s3, got_s3, keep_a3, got_a3)
    got_z = flip_dp(send_z, 4)
    grad_tokens = tokens_out(info, own_tok, got_tok)
    output = slots_of(info, own_out, got_out)
    grads = attend_out((keep_z, got_z), height)
    return (output, grad_tokens, *grads[:4], grad_up, grad_down.T, *grads[4:])


def plain_path(info, tokens, cotangent, weights, lengths, masks, norms):
    w_query, w_key, w_value, w_out, w_up, w_down = weights
    mask_own, mask_other, mask_ends = masks
    g_one, b_one, g_two, b_two = norms
    features, units = tokens.shape[2], w_up.shape[1]
    flat = (((0, 0),),)
    two = (((0, 0),), ((1, 0),))

    def gathered(piece):
        own = lax.all_gather(piece, "dp", axis=0, tiled=True)[None]
        return own, flip_chip(own)

    got_rows = flip_chip(split(info, tokens, cotangent, True))
    own_rows = split(info, tokens, cotangent, False)
    quarters = (own_rows, got_rows, flip_core(own_rows), flip_core(got_rows))
    tok = merge(info, quarters)
    firsts = [w[:, : 2 * HD] for w in (w_query, w_key, w_value)]
    thirds = [w_out.T] + [w[:, 2 * HD :] for w in (w_query, w_key, w_value)]
    pair_w = (gathered(jnp.concatenate(firsts, axis=1)), two)
    single_w = (gathered(jnp.concatenate(thirds, axis=1)), two)
    up, down = (gathered(w_up), two), (gathered(w_down.T), two)
    own01 = attend(info, lengths, tok, ((pair_w[0][0],), flat), True, mask_own[:2])
    other01 = attend(info, lengths, tok, ((pair_w[0][1],), flat), True, mask_other[:2])
    ends = attend(info, lengths, tok, single_w, False, mask_ends)
    contexts = (own01[3], other01[3], ends[3])
    part = project(info, contexts, single_w, features)
    normal, scale_one, hn = norm_one(tok, part, flip_cores(part), g_one, b_one)
    act1, slope1 = feed_up(info, hn, ((up[0][0],), flat), units)
    act2, slope2 = feed_up(info, hn, ((up[0][1],), flat), units)
    tok_turned, hn_turned = turn_rows(tok, hn)
    part = feed_down(info, act1, act2, down, features)
    out, dzb_two, sums_two = norm_two(
        info, lengths, hn, part, flip_cores(part), quarters, g_two, b_two
    )
    places = (((0, 0),), ((1, 0),)) * 2
    grad_d = feed_grad(info, dzb_two, act1, act2, places, tn)
    du1, du2, *part = feed_back(info, dzb_two, slope1, slope2, up, down)
    grad_u = feed_grad(info, hn_turned, du1, du2, places, nn)
    dzb_one, sums_one = norm_one_back(
        normal, scale_one, dzb_two, part, flip_cores(part), g_one
    )
    d_ends = attend_back(info, dzb_one, single_w, None, ends)
    keep_s, send_s = single_grad(
        info, tok_turned, d_ends, dzb_one, contexts, sums_one, sums_two, places[2:]
    )
    d_other = attend_back(info, dzb_one, single_w, 1, other01)
    grad_b = pair_grad(info, tok_turned, d_other, places[0])
    d_own = attend_back(info, dzb_one, single_w, 0, own01)
    grad_a = pair_grad(info, tok_turned, d_own, places[0])
    mine, *sent = input_back(info, d_own, d_other, d_ends, dzb_one, pair_w, single_w)
    own_tok, *send_tok = tokens_add(mine, flip_cores(sent))
    own_out, send_out = halves(info, out)
    output = slots_of(info, own_out, flip_chip(send_out))
    grad_tokens = tokens_out(info, own_tok, [flip_chip(v) for v in send_tok])

    def summed(own, other):
        total = own.astype(F32) + flip_chip(other).astype(F32)
        return lax.psum_scatter(total, "dp", scatter_dimension=0, tiled=True)

    def wide(keep1, send1, keep2, send2):
        return jnp.concatenate([summed(keep1[0], send1[0]), summed(keep2[0], send2[0])], axis=1)

    single = summed(keep_s[:features], send_s[:features])
    pair = summed(grad_a[0], grad_b[0])
    grads = [
        jnp.concatenate(
            [pair[:, 2 * i * HD : 2 * (i + 1) * HD], single[:, (3 + i) * HD : (4 + i) * HD]],
            axis=1,
        )
        for i in range(3)
    ] + [single[:, : 3 * HD].T]
    sums = decode(keep_s[features:])
    sums = lax.psum(sums + flip_chip(sums), "dp")
    sums = [jnp.concatenate([sums[i], sums[4 + i]]) for i in range(4)]
    return (output, grad_tokens, *grads, wide(*grad_u), wide(*grad_d).T, *sums)


def local(
    tokens,
    w_query,
    w_key,
    w_value,
    w_out,
    w_up,
    w_down,
    gain_attn,
    bias_attn,
    gain_ffn,
    bias_ffn,
    lengths,
    random_blocks,
    cotangent,
):
    ORDER.clear()
    size = lax.axis_size("dp")
    rank = lax.axis_index("mp")
    me = lax.axis_index("dp")
    x, core = rank // 2, rank % 2
    quarter = tokens.shape[1]
    seq = 4 * quarter
    height = w_query.shape[0]
    span = w_query.shape[1]
    heads = span // HD
    nblocks = seq // BLOCK
    fast = size == 8 and height % 16 == 0

    shift = x * (seq // 2)
    info = jnp.stack([me, x, core, shift]).astype(jnp.int32)

    blocks = (jnp.arange(nblocks) + x * (nblocks // 2)) % nblocks
    near_blocks = jnp.abs(blocks[:, None] - blocks[None, :]) <= 1
    edge = (blocks == 0) | (blocks == nblocks - 1)
    fixed = near_blocks | edge[:, None] | edge[None, :]

    def table(shard):
        chosen = lax.dynamic_slice_in_dim(random_blocks, shard * heads, heads, 0)
        chosen = jnp.roll(chosen, -x * (nblocks // 2), axis=1)
        hit = jnp.any(chosen[:, None, :, :] == blocks[None, :, None, None], axis=3)
        bias = jnp.where(fixed.T[None] | hit, 0.0, NEGATIVE)
        return jnp.concatenate(
            [
                jnp.zeros((heads, nblocks, HD), F32),
                bias,
                jnp.full((heads, nblocks, 3), -1.0, F32),
                jnp.zeros((heads, nblocks, HD - 3 - nblocks), F32),
            ],
            axis=2,
        )

    mask_own, mask_other = table(rank), table(rank ^ 2)
    mask_ends = jnp.concatenate([mask_own[2:], mask_other[2:]], axis=0)
    g_one, b_one = gain_attn[None], bias_attn[None]
    g_two, b_two = gain_ffn[None], bias_ffn[None]

    path = fast_path if fast else plain_path
    return path(
        info,
        tokens,
        cotangent,
        (w_query, w_key, w_value, w_out, w_up, w_down),
        lengths,
        (mask_own, mask_other, mask_ends),
        (g_one, b_one, g_two, b_two),
    )


def solution(mesh):
    return jax.shard_map(
        local,
        mesh=mesh,
        in_specs=(
            P("dp", "mp", None),
            P("dp", "mp"),
            P("dp", "mp"),
            P("dp", "mp"),
            P("mp", "dp"),
            P("dp", "mp"),
            P("mp", "dp"),
            P(),
            P(),
            P(),
            P(),
            P("dp"),
            P(),
            P("dp", "mp", None),
        ),
        out_specs=(
            P("dp", "mp", None),
            P("dp", "mp", None),
            P("dp", "mp"),
            P("dp", "mp"),
            P("dp", "mp"),
            P("mp", "dp"),
            P("dp", "mp"),
            P("mp", "dp"),
            P(),
            P(),
            P(),
            P(),
        ),
        check_vma=False,
    )
```

```python
import functools

import jax
import jax.numpy as jnp
from jax import lax
from jax.experimental import pallas as pl
from jax.experimental.pallas import tpu as pltpu
from jax.sharding import PartitionSpec as P

HD = 64
BLOCK = 64
LANES = 128
TILE = 256
SENT = 256
EPSILON = 1e-12
TAIL = 32
TOKEN = (8, 128)
ROOM = {
    "attend": 20,
    "attend_back": 28,
    "project": 12,
    "input_back": 24,
    "norm_one": 12,
    "norm_two": 18,
    "norm_one_back": 14,
    "feed_up": 16,
    "feed_down": 18,
    "feed_back": 32,
    "turn_rows": 12,
    "feed_grad": 24,
    "pair_grad": 16,
    "single_grad": 24,
    "join": 1,
    "join_sides": 1,
    "beside": 1,
    "pack": 2,
    "split": 4,
    "merge": 1,
    "fold": 6,
    "fold_add": 8,
    "fold_feed": 10,
    "fold_sides": 8,
    "fold_last": 6,
    "fold_z": 4,
    "slots": 1,
    "tokens_add": 8,
    "tokens_out": 8,
    "feed_out": 6,
    "attend_out": 6,
}
SCALE = 0.125
LOG2E = 1.4426950408889634
LN2 = 0.6931471805599453
NEGATIVE = -1e30
F32 = jnp.float32
BF16 = jnp.bfloat16

CORE_SWAP = [(0, 1), (1, 0), (2, 3), (3, 2)]
CHIP_SWAP = [(0, 2), (2, 0), (1, 3), (3, 1)]


def nn(a, b):
    return lax.dot_general(a, b, (((1,), (0,)), ((), ())), preferred_element_type=F32)


def nt(a, b):
    return lax.dot_general(a, b, (((1,), (1,)), ((), ())), preferred_element_type=F32)


def tn(a, b):
    return lax.dot_general(a, b, (((0,), (0,)), ((), ())), preferred_element_type=F32)


def vmem():
    return pl.BlockSpec(memory_space=pltpu.VMEM)


def smem():
    return pl.BlockSpec(memory_space=pltpu.SMEM)


def anywhere():
    return pl.BlockSpec(memory_space=pl.ANY)


def in_hbm(values):
    return tuple(pltpu.with_memory_space_constraint(v, pltpu.HBM) for v in values)


def array(shape, dtype):
    return jax.ShapeDtypeStruct(shape, dtype)


ORDER = []


def run(kernel, name, args, specs, outs, out_specs, scratch=()):
    given, made = len(args), len(outs)
    extra = tuple(ORDER)

    def body(*refs):
        ins, rest = refs[:given], refs[given + len(extra) :]
        rest[made][...] = jnp.zeros(TOKEN, F32)
        kernel(*ins, *rest[:made], *rest[made + 1 :])

    results = pl.pallas_call(
        body,
        out_shape=tuple(outs) + (array(TOKEN, F32),),
        in_specs=list(specs) + [anywhere()] * len(extra),
        out_specs=tuple(out_specs) + (vmem(),),
        scratch_shapes=list(scratch),
        compiler_params=pltpu.CompilerParams(vmem_limit_bytes=ROOM[name] * 2**20),
        cost_estimate=pl.CostEstimate(flops=1, bytes_accessed=0, transcendentals=0),
        name=name,
    )(*args, *extra)
    ORDER[:] = [results[-1]]
    return results[:-1]


def put_rows(parts, t, value):
    height, tile = parts[0].shape[0], value.shape[0]
    if height <= tile:
        per = tile // height
        for k in range(per):
            parts[t * per + k][...] = value[k * height : (k + 1) * height]
    else:
        per = height // tile
        parts[t // per][pl.ds(t % per * tile, tile), :] = value


def get_sum(parts, more, t):
    height = parts[0].shape[0]
    if height <= TILE:
        per = TILE // height
        at = range(t * per, (t + 1) * per)
        pieces = [parts[k][...].astype(F32) + more[k][...].astype(F32) for k in at]
        return pieces[0] if per == 1 else jnp.concatenate(pieces, axis=0)
    per = height // TILE
    at = pl.ds(t % per * TILE, TILE)
    return parts[t // per][at, :].astype(F32) + more[t // per][at, :].astype(F32)


def tile_rows(ref):
    return [(t, pl.ds(t * TILE, TILE)) for t in range(ref.shape[0] // TILE)]


def far(shape, dtype):
    return pltpu.HBM(shape, dtype)


def tiles(seq, width, height):
    parts = (array((height, width), BF16),) * (seq // height)
    return parts, [vmem()] * len(parts)


def place(me, refs, slots, dst_ref, first=0, last=None, only=None, to=0):
    for ref, of in zip(refs, slots):
        height, width = ref.shape[1], ref.shape[2]
        end = width if last is None else last
        for e, (chip, j) in enumerate(of):
            if only is not None and chip != only:
                continue
            at = 0 if height == dst_ref.shape[0] else pl.multiple_of((me ^ j) * height, height)
            at_column = to + (0 if only is not None else chip * (end - first))
            dst_ref[pl.ds(at, height), pl.ds(at_column, end - first)] = ref[e, :, first:end]


def pick(me, fulls, out_ref, slots, first):
    _, height, width = out_ref.shape
    for e, (chip, j) in enumerate(slots):
        full = fulls[chip]
        at = 0 if height == full.shape[0] else pl.multiple_of((me ^ j) * height, height)
        out_ref[e] = full[pl.ds(at, height), pl.ds(first, width)]


def attend_kernel(slots, columns, only, places, info, lengths, tok, mask, *rest):
    refs, (qa, ka, va, ctx, wfull) = rest[: len(slots)], rest[len(slots) :]
    seq = tok.shape[0]
    place(info[0], refs, slots, wfull, *columns, only)
    lane = lax.broadcasted_iota(jnp.int32, (TILE, LANES), 1)
    row0 = lax.broadcasted_iota(jnp.int32, (TILE, LANES), 0)
    for t in range(seq // TILE):
        at = pl.ds(t * TILE, TILE)
        row = row0 + t * TILE
        made = nn(tok[at, :], wfull[...])
        onehot = jnp.where(lane - HD == row // BLOCK, 1.0, 0.0)[:, HD:]
        position = row + info[3]
        position = jnp.where(position >= seq, position - seq, position)
        dead = (position >= lengths[info[1]]) & (lane >= HD) & (lane < HD + 16)
        for h, (q_at, k_at, v_at) in enumerate(places):
            q = made[:, q_at : q_at + HD] * (SCALE * LOG2E)
            k = made[:, k_at : k_at + HD]
            v = made[:, v_at : v_at + HD]
            qa[h, at, :] = jnp.concatenate([q, onehot], axis=1).astype(BF16)
            per = TILE // BLOCK
            table = jnp.concatenate(
                [
                    jnp.broadcast_to(mask[h, t * per + b : t * per + b + 1, :], (BLOCK, LANES))
                    for b in range(per)
                ],
                axis=0,
            )
            table = jnp.where(dead, NEGATIVE, table)
            ka[h, at, :] = jnp.concatenate([k, table[:, HD:]], axis=1).astype(BF16)
            va[h, at, :] = jnp.concatenate([v, jnp.full((TILE, HD), -1.0, F32)], axis=1).astype(BF16)
    for t in range(seq // TILE):
        at = pl.ds(t * TILE, TILE)
        pieces = []
        for h in range(len(places)):
            q = qa[h, at, :]
            s = nt(q, ka[h])
            top = jnp.max(s, axis=1, keepdims=True)
            p = jnp.exp2(s - top).astype(BF16)
            got = nn(p, va[h])
            total = -got[:, HD:]
            pieces.append(got[:, :HD] / total)
            log = top + jnp.log2(-got)
            hi = log.astype(BF16).astype(F32)
            mid = (log - hi).astype(BF16).astype(F32)
            low = log - hi - mid
            new = jnp.where(
                lane == HD + 16,
                hi,
                jnp.where(lane == HD + 17, mid, jnp.where(lane == HD + 18, low, q.astype(F32))),
            )
            qa[h, at, :] = new.astype(BF16)
        ctx[at, :] = jnp.concatenate(pieces, axis=1).astype(BF16)


PAIR = ((0, 2 * HD, 4 * HD), (HD, 3 * HD, 5 * HD))
SINGLES = ((HD, 2 * HD, 3 * HD), (5 * HD, 6 * HD, 7 * HD))


def attend(info, lengths, tok, gathered, pair, mask):
    arrays, slots = gathered
    seq, width = tok.shape
    aug = far((2, seq, LANES), BF16)
    columns, only, cols = ((0, 6 * HD), 0, 6 * HD) if pair else ((2 * HD, 6 * HD), None, 8 * HD)
    return run(
        functools.partial(attend_kernel, slots, columns, only, PAIR if pair else SINGLES),
        "attend",
        (info, lengths, tok, mask) + arrays,
        [smem()] * 2 + [vmem()] * (2 + len(arrays)),
        (aug, aug, aug, array((seq, LANES), BF16)),
        [vmem()] * 4,
        [pltpu.VMEM((width, cols), BF16)],
    )


def place_out(me, refs, slots, pairs, ends):
    place(me, refs, slots, pairs, 0, 2 * HD)
    place(me, refs, slots, ends, 2 * HD, 4 * HD)
    both = ends[...]
    ends[:, :LANES] = jnp.concatenate([both[:, :HD], both[:, LANES : LANES + HD]], axis=1)


def project_kernel(slots, info, own, other, ends, *rest):
    refs, parts, (w1, w2) = rest[: len(slots)], rest[len(slots) : -2], rest[-2:]
    place_out(info[0], refs, slots, w1, w2)
    for t, at in tile_rows(own):
        both = jnp.concatenate([own[at, :], other[at, :]], axis=1)
        out = nt(both, w1[...]) + nt(ends[at, :], w2[:, :LANES])
        put_rows(parts, t, out.astype(BF16))


def project(info, contexts, gathered, width):
    arrays, slots = gathered
    seq = contexts[0].shape[0]
    return run(
        functools.partial(project_kernel, slots),
        "project",
        (info,) + contexts + arrays,
        [smem()] + [vmem()] * (3 + len(arrays)),
        *tiles(seq, width, 2 * TILE),
        [pltpu.VMEM((width, 2 * LANES), BF16)] * 2,
    )


def attend_back_kernel(slots, chip, info, dz, qa, ka, va, ctx, *rest):
    refs, (dqkv, pairs, ends, da) = rest[: len(slots)], rest[len(slots) :]
    seq = dz.shape[0]
    heads = qa.shape[0]
    if chip is None:
        place_out(info[0], refs, slots, pairs, ends)
        wfull = ends.at[:, pl.ds(0, LANES)]
    else:
        place(info[0], refs, slots, pairs, 0, 2 * HD, chip)
        wfull = pairs.at[:, pl.ds(0, LANES)]
    lane = lax.broadcasted_iota(jnp.int32, (TILE, LANES), 1)
    for t in range(seq // TILE):
        at = pl.ds(t * TILE, TILE)
        dctx = nn(dz[at, :], wfull[...]).astype(BF16).astype(F32)
        both = dctx * ctx[at, :].astype(F32)
        for h in range(heads):
            inner = jnp.sum(both[:, h * HD : (h + 1) * HD], axis=1, keepdims=True)
            hi = inner.astype(BF16).astype(F32)
            mid = (inner - hi).astype(BF16).astype(F32)
            low = inner - hi - mid
            one = jnp.concatenate(
                [dctx[:, h * HD : (h + 1) * HD], jnp.zeros((TILE, HD), F32)], axis=1
            )
            one = jnp.where(lane == HD, hi, one)
            one = jnp.where(lane == HD + 1, mid, one)
            one = jnp.where(lane == HD + 2, low, one)
            da[h, at, :] = one.astype(BF16)

    def turned(values):
        return jnp.transpose(values.astype(F32))[:HD].astype(BF16)

    grads = []
    for h in range(heads):
        k_turned, q_turned, d_turned = turned(ka[h]), turned(qa[h]), turned(da[h])
        dq, dk, dv = None, [], []
        for t in range(seq // TILE):
            at = pl.ds(t * TILE, TILE)
            p = jnp.exp2(nt(ka[h, at, :], qa[h]))
            ds = (p * nt(va[h, at, :], da[h])).astype(BF16)
            dv.append(nt(d_turned, p.astype(BF16)))
            dk.append(nt(q_turned, ds))
            more = nn(k_turned[:, t * TILE : (t + 1) * TILE], ds)
            dq = more if dq is None else dq + more
        dk = jnp.concatenate(dk, axis=1) * LN2
        grads.append((dq * SCALE, dk, jnp.concatenate(dv, axis=1)))
    (dq0, dk0, dv0), (dq1, dk1, dv1) = grads
    if chip is None:
        blank = jnp.zeros_like(dq0)
        stacks = ((blank, dq0), (dk0, dv0), (blank, dq1), (dk1, dv1))
    else:
        stacks = ((dq0, dq1), (dk0, dk1), (dv0, dv1))
    for i, stack in enumerate(stacks):
        both = jnp.transpose(jnp.concatenate(stack, axis=0))
        dqkv[:, i * LANES : (i + 1) * LANES] = both.astype(BF16)


def attend_back(info, dz, gathered, chip, saved):
    arrays, slots = gathered
    qa, ka, va, ctx = saved
    seq, width = dz.shape
    cols = 8 * HD if chip is None else 6 * HD
    return run(
        functools.partial(attend_back_kernel, slots, chip),
        "attend_back",
        (info, dz, qa, ka, va, ctx) + arrays,
        [smem()] + [vmem()] * (5 + len(arrays)),
        (array((seq, cols), BF16),),
        [vmem()],
        [
            pltpu.VMEM((width, 2 * LANES), BF16),
            pltpu.VMEM((width, 2 * LANES), BF16),
            pltpu.VMEM((2, seq, LANES), BF16),
        ],
    )[0]


def input_back_kernel(slots1, slots2, info, own, other, ends, dz, *rest):
    n1, n2 = len(slots1), len(slots2)
    refs1, refs2, (mine, *sent, w1, w2) = rest[:n1], rest[n1 : n1 + n2], rest[n1 + n2 :]
    place(info[0], refs1, slots1, w1)
    place(info[0], refs2, slots2, w2, 2 * HD, 6 * HD)
    per = len(sent) // 2
    height = sent[0].shape[0]
    for half in range(dz.shape[0] // TILE // 2):
        for whose in range(2):
            tile = 2 * half + (info[2] if whose == 0 else 1 - info[2])
            at = pl.ds(pl.multiple_of(tile * TILE, TILE), TILE)
            pairs = jnp.concatenate([own[at, :], other[at, :]], axis=1)
            back = nt(pairs, w1[...]) + nt(ends[at, :], w2[...])
            if whose == 0:
                mine[half] = back + dz[at, :].astype(F32)
                continue
            for k in range(per):
                part = back[k * height : (k + 1) * height]
                sent[half * per + k][...] = part.astype(BF16)


def input_back(info, own, other, ends, dz, gathered1, gathered2):
    seq, width = dz.shape
    arrays = gathered1[0] + gathered2[0]
    halves = (seq // TILE // 2, TILE, width)
    grads = (own, other, ends, dz)
    return run(
        functools.partial(input_back_kernel, gathered1[1], gathered2[1]),
        "input_back",
        (info,) + grads + arrays,
        [smem()] + [vmem()] * (len(grads) + len(arrays)),
        (array(halves, F32),) + (array((SENT, width), BF16),) * (seq // 2 // SENT),
        [vmem()] * (1 + seq // 2 // SENT),
        [pltpu.VMEM((width, 12 * HD), BF16), pltpu.VMEM((width, 8 * HD), BF16)],
    )


def center(z):
    mean = jnp.mean(z, axis=1, keepdims=True)
    moved = z - mean
    spread = jnp.mean(moved * moved, axis=1, keepdims=True)
    scale = lax.rsqrt(spread + EPSILON)
    return moved * scale, scale


def norm_back(n, scale, gy, gain):
    dn = gy * gain
    return scale * (
        dn - jnp.mean(dn, axis=1, keepdims=True) - n * jnp.mean(dn * n, axis=1, keepdims=True)
    )


def add_sums(gy, n, sums):
    more = [jnp.sum(v, axis=0, keepdims=True) for v in (gy * n, gy)]
    return more if sums is None else [a + b for a, b in zip(sums, more)]


def norm_one_kernel(tok, gain, bias, *rest):
    *parts, normal, scale, hn = rest
    count = len(parts) // 2
    for t, at in tile_rows(tok):
        value = tok[at, :].astype(F32) + get_sum(parts[:count], parts[count:], t)
        n, r = center(value)
        normal[at, :] = n.astype(BF16)
        scale[at, :] = r
        hn[at, :] = (n * gain[...] + bias[...]).astype(BF16)


def norm_one(tok, p0, p1, gain, bias):
    seq, width = tok.shape
    return run(
        norm_one_kernel,
        "norm_one",
        (tok, gain, bias, *p0, *p1),
        [vmem()] * (3 + len(p0) + len(p1)),
        (array((seq, width), BF16), array((seq, 1), F32), array((seq, width), BF16)),
        [vmem()] * 3,
    )


def norm_two_kernel(info, lengths, hn, own, got, core_own, core_got, gain, bias, *rest):
    *parts, own_out, send_out, dzb, sums, out = rest
    count = len(parts) // 2
    seq = hn.shape[0]
    total = None
    for t, at in tile_rows(hn):
        value = hn[at, :].astype(F32) + get_sum(parts[:count], parts[count:], t)
        n, scale = center(value)
        out[at, :] = (n * gain[...] + bias[...]).astype(BF16)
        position = lax.broadcasted_iota(jnp.int32, (TILE, 1), 0) + t * TILE + info[3]
        position = jnp.where(position >= seq, position - seq, position)
        valid = jnp.where(position < lengths[info[1]], 1.0, 0.0)
        mine, others = ((own, core_own), (got, core_got))[t // 2]
        cot = jnp.where(info[2] == t % 2, mine[1].astype(F32), others[1].astype(F32))
        gy = cot * valid
        dzb[at, :] = norm_back(n, scale, gy, gain[...]).astype(BF16)
        total = add_sums(gy, n, total)
    sums[...] = jnp.concatenate(total, axis=0)
    for half, ref in enumerate((own_out, send_out)):
        at = pl.multiple_of((2 * half + info[2]) * TILE, TILE)
        ref[...] = out[pl.ds(at, TILE), :]


def norm_two(info, lengths, hn, m0, m1, cot, gain, bias):
    seq, width = hn.shape
    return run(
        norm_two_kernel,
        "norm_two",
        (info, lengths, hn, *cot, gain, bias, *m0, *m1),
        [smem()] * 2 + [vmem()] * (3 + len(cot) + len(m0) + len(m1)),
        (
            array((TILE, width), BF16),
            array((TILE, width), BF16),
            array((seq, width), BF16),
            array((2, width), F32),
        ),
        [vmem()] * 4,
        [pltpu.VMEM((seq, width), BF16)],
    )


def norm_one_back_kernel(normal, scale, dz2, gain, *rest):
    *parts, dzb, sums = rest
    count = len(parts) // 2
    total = None
    for t, at in tile_rows(dz2):
        n = normal[at, :].astype(F32)
        gy = dz2[at, :].astype(F32) + get_sum(parts[:count], parts[count:], t)
        dzb[at, :] = norm_back(n, scale[at, :], gy, gain[...]).astype(BF16)
        total = add_sums(gy, n, total)
    sums[...] = jnp.concatenate(total, axis=0)


def norm_one_back(normal, scale, dz2, p0, p1, gain):
    seq, width = normal.shape
    return run(
        norm_one_back_kernel,
        "norm_one_back",
        (normal, scale, dz2, gain, *p0, *p1),
        [vmem()] * (4 + len(p0) + len(p1)),
        (array((seq, width), BF16), array((2, width), F32)),
        [vmem()] * 2,
    )


def gelu_pair(u):
    phi = 0.5 + 0.5 * lax.erf(u * 0.7071067811865476)
    return u * phi, phi + u * (jnp.exp(-0.5 * u * u) * 0.3989422804014327)


def feed_up_kernel(slots, info, hn, *rest):
    refs, (active, slope, wfull) = rest[: len(slots)], rest[len(slots) :]
    place(info[0], refs, slots, wfull)
    for _, at in tile_rows(hn):
        a, g = gelu_pair(nn(hn[at, :], wfull[...]))
        active[at, :] = a.astype(BF16)
        slope[at, :] = g.astype(BF16)


def feed_up(info, hn, gathered, units):
    arrays, slots = gathered
    seq, width = hn.shape
    return run(
        functools.partial(feed_up_kernel, slots),
        "feed_up",
        (info, hn) + arrays,
        [smem()] + [vmem()] * (1 + len(arrays)),
        (array((seq, units), BF16), array((seq, units), BF16)),
        [vmem()] * 2,
        [pltpu.VMEM((width, units), BF16)],
    )


def feed_down_kernel(slots, info, act1, act2, *rest):
    refs, parts, wfull = rest[: len(slots)], rest[len(slots) : -1], rest[-1]
    place(info[0], refs, slots, wfull)
    for t, at in tile_rows(act1):
        both = jnp.concatenate([act1[at, :], act2[at, :]], axis=1)
        put_rows(parts, t, nt(both, wfull[...]).astype(BF16))


def feed_down(info, act1, act2, gathered, width):
    seq, units = act1.shape
    arrays, slots = gathered
    return run(
        functools.partial(feed_down_kernel, slots),
        "feed_down",
        (info, act1, act2) + arrays,
        [smem()] + [vmem()] * (2 + len(arrays)),
        *tiles(seq, width, seq),
        [pltpu.VMEM((width, 2 * units), BF16)],
    )


def feed_back_kernel(slots_up, slots_down, info, dzb, slope1, slope2, *rest):
    n1, n2 = len(slots_up), len(slots_down)
    ups, downs, (du1, du2, *parts, up, down) = rest[:n1], rest[n1 : n1 + n2], rest[n1 + n2 :]
    place(info[0], ups, slots_up, up)
    place(info[0], downs, slots_down, down)
    units = du1.shape[1]
    for t, at in tile_rows(dzb):
        out = None
        for i, (slope, du) in enumerate(((slope1, du1), (slope2, du2))):
            cols = pl.ds(i * units, units)
            grad = (nn(dzb[at, :], down[:, cols]) * slope[at, :].astype(F32)).astype(BF16)
            du[at, :] = grad
            more = nt(grad, up[:, cols])
            out = more if out is None else out + more
        put_rows(parts, t, out.astype(BF16))


def feed_back(info, dzb, slope1, slope2, up, down):
    seq, width = dzb.shape
    units = slope1.shape[1]
    arrays = up[0] + down[0]
    parts, part_specs = tiles(seq, width, TILE)
    return run(
        functools.partial(feed_back_kernel, up[1], down[1]),
        "feed_back",
        (info, dzb, slope1, slope2) + arrays,
        [smem()] + [vmem()] * (3 + len(arrays)),
        (array((seq, units), BF16),) * 2 + parts,
        [vmem()] * 2 + part_specs,
        [pltpu.VMEM((width, 2 * units), BF16)] * 2,
    )


def turn_rows_kernel(order, info, first, second, out1, out2, full):
    count = len(order)
    height = full.shape[0] // count
    for values, out in ((first, out1), (second, out2)):
        for t, at in tile_rows(values):
            full[:, t * TILE : (t + 1) * TILE] = jnp.transpose(values[at, :])
        for e, j in enumerate(order):
            at = 0 if count == 1 else pl.multiple_of((info[0] ^ j) * height, height)
            out[pl.ds(e * height, height), :] = full[pl.ds(at, height), :]


def turn_rows(info, first, second, order):
    shape = first.shape[::-1]
    out = array(shape, BF16)
    return run(
        functools.partial(turn_rows_kernel, order),
        "turn_rows",
        (info, first, second),
        [smem()] + [vmem()] * 2,
        (out, out),
        [vmem()] * 2,
        [pltpu.VMEM(shape, BF16)],
    )


def feed_grad_kernel(turned, places, info, a, d1, d2, *rest):
    outs, full = rest[:4], rest[4]
    half = outs[0].shape[2]
    product = nn if turned else tn
    made = product(a[...], jnp.concatenate([d1[...], d2[...]], axis=1)).astype(BF16)
    if turned:
        height = outs[0].shape[1]
        order = [j for chip, j in places[0] if chip == 0]
        for i, out in enumerate(outs):
            for e, (chip, j) in enumerate(places[i]):
                row = order.index(j) * height
                first = 2 * chip * half + (i // 2) * half
                out[e] = made[row : row + height, first : first + half]
        return
    full[...] = made
    fulls = [full.at[:, pl.ds(2 * chip * half, 2 * half)] for chip in range(2)]
    for i, out in enumerate(outs):
        pick(info[0], fulls, out, places[i], (i // 2) * half)


def feed_grad(info, a, d1, d2, places, turned):
    seq, units = d1.shape
    width = a.shape[0] if turned else a.shape[1]
    count = len(places[0])
    out = array((count, width // count, units // 2), BF16)
    return run(
        functools.partial(feed_grad_kernel, turned, places),
        "feed_grad",
        (info, a, d1, d2),
        [smem()] + [vmem()] * 3,
        (out,) * 4,
        [vmem()] * 4,
        [pltpu.VMEM((width, 2 * units), BF16)],
    )


def pair_grad_kernel(tok_turned, d, out):
    made = nn(tok_turned[...], d[...]).astype(BF16)
    height = out.shape[1]
    for e in range(out.shape[0]):
        out[e] = made[e * height : (e + 1) * height]


def pair_grad(tok_turned, d, count):
    width = tok_turned.shape[0]
    cols = d.shape[1]
    return run(
        pair_grad_kernel,
        "pair_grad",
        (tok_turned, d),
        [vmem()] * 2,
        (array((count, width // count, cols), BF16),),
        [vmem()],
    )[0]


def encode(sums):
    hi = sums.astype(BF16).astype(F32)
    mid = (sums - hi).astype(BF16).astype(F32)
    low = sums - hi - mid
    return jnp.concatenate([hi, mid, low, jnp.zeros_like(low)], axis=0).astype(BF16)


def decode(coded):
    values = coded.astype(F32)
    n = values.shape[0] // 4
    return values[:n] + values[n : 2 * n] + values[2 * n : 3 * n]


def single_grad_kernel(
    order, info, tok_turned, d, dz, own, other, ends, sums_one, sums_two, keep, send, full
):
    mine = nn(tok_turned[...], d[...])
    full[...] = tn(dz[...], jnp.concatenate([ends[...], own[...], other[...]], axis=1))
    count = len(order)
    height = full.shape[0] // count
    width = keep.shape[1]
    blank = jnp.zeros((height, HD), F32)
    both = jnp.concatenate([sums_one[...], sums_two[...]], axis=0)
    both = encode(jnp.concatenate([both[:, :width], both[:, width:]], axis=0))
    half = max(1, count // 2)
    for e, j in enumerate(order):
        at = 0 if count == 1 else pl.multiple_of((info[0] ^ j) * height, height)
        heads = full[pl.ds(at, height), :]
        rows_in = mine[e * height : (e + 1) * height]
        for chip in range(2):
            first = chip * 4 * HD
            third = jnp.concatenate([heads[:, chip * HD : (chip + 1) * HD], blank], axis=1)
            made = [
                heads[:, (chip + 1) * LANES : (chip + 2) * LANES],
                third + rows_in[:, first : first + LANES],
                rows_in[:, first + LANES : first + 2 * LANES],
            ]
            if count == 1:
                out, row = (keep, send)[chip], 0
            else:
                out, row = (keep, send)[e // half], (chip * half + e % half) * height
            out[pl.ds(row, height), :] = jnp.concatenate(made, axis=1).astype(BF16)
    for out in (keep, send):
        out[pl.ds(out.shape[0] - TAIL, TAIL), :] = both


def single_grad(info, tok_turned, d, dz, contexts, sums_one, sums_two, order):
    width = tok_turned.shape[0]
    cols = 6 * HD
    out = array((width + TAIL, cols), BF16)
    return run(
        functools.partial(single_grad_kernel, order),
        "single_grad",
        (info, tok_turned, d, dz, *contexts, sums_one, sums_two),
        [smem()] + [vmem()] * 8,
        (out, out),
        [vmem()] * 2,
        [pltpu.VMEM((width, 3 * LANES), F32)],
    )


def across(values, axis, pairs):
    return lax.ppermute(values, axis, pairs)


def flip_chip(values):
    return across(values, "mp", CHIP_SWAP)


def flip_core(values):
    return across(values, "mp", CORE_SWAP)


def flip_cores(parts):
    return [flip_core(p) for p in parts]


def flip_dp(values, distance):
    size = lax.axis_size("dp")
    return across(values, "dp", [(i, i ^ distance) for i in range(size)])


def join_kernel(groups, *refs):
    count = sum(groups)
    parts, outs, sems = refs[:count], refs[count:-1], refs[-1]
    copies = []
    for out, number in zip(outs, groups):
        first = 0
        for part in parts[len(copies) : len(copies) + number]:
            to = out.at[pl.ds(first, part.shape[0])]
            copies.append(pltpu.make_async_copy(part, to, sems.at[len(copies)]))
            first += part.shape[0]
    for copy in copies:
        copy.start()
    for copy in copies:
        copy.wait()


def join(*groups):
    parts = sum((tuple(g) for g in groups), ())
    outs = [array((sum(p.shape[0] for p in g),) + g[0].shape[1:], g[0].dtype) for g in groups]
    return run(
        functools.partial(join_kernel, tuple(len(g) for g in groups)),
        "join",
        parts,
        [anywhere()] * len(parts),
        outs,
        [anywhere()] * len(outs),
        [pltpu.SemaphoreType.DMA((len(parts),))],
    )


def pack_kernel(w_query, w_key, w_value, w_out, out, rows_in, out_in, sems):
    copies = [
        pltpu.make_async_copy(w, rows_in.at[i], sems.at[i])
        for i, w in enumerate((w_query, w_key, w_value))
    ]
    copies.append(pltpu.make_async_copy(w_out, out_in, sems.at[3]))
    for copy in copies:
        copy.start()
    for copy in copies:
        copy.wait()
    for i in range(3):
        out[0, :, 2 * i * HD : 2 * (i + 1) * HD] = rows_in[i, :, : 2 * HD]
    parts = [jnp.transpose(out_in[...].astype(F32))]
    parts += [rows_in[i, :, 2 * HD :].astype(F32) for i in range(3)]
    out[0, :, 6 * HD :] = jnp.concatenate(parts, axis=1).astype(BF16)


def pack(w_query, w_key, w_value, w_out):
    height, span = w_query.shape
    return run(
        pack_kernel,
        "pack",
        in_hbm((w_query, w_key, w_value, w_out)),
        [anywhere()] * 4,
        (array((1, height, 4 * span), BF16),),
        [vmem()],
        [
            pltpu.VMEM((3, height, span), BF16),
            pltpu.VMEM(w_out.shape, BF16),
            pltpu.SemaphoreType.DMA((4,)),
        ],
    )[0]


def beside_kernel(first, second, out, sems):
    width = first.shape[1]
    copies = [
        pltpu.make_async_copy(ref, out.at[0, :, pl.ds(i * width, width)], sems.at[i])
        for i, ref in enumerate((first, second))
    ]
    for copy in copies:
        copy.start()
    for copy in copies:
        copy.wait()


def beside(first, second):
    height, width = first.shape
    return run(
        beside_kernel,
        "beside",
        in_hbm((first, second)),
        [anywhere()] * 2,
        (array((1, height, 2 * width), BF16),),
        [anywhere()],
        [pltpu.SemaphoreType.DMA((2,))],
    )[0]


def join_sides_kernel(count, *refs):
    parts, outs, sems = refs[:count], refs[count : count + 2], refs[count + 2]
    width = outs[0].shape[2]
    copies = []
    each = parts[0].shape[0]
    for i, part in enumerate(parts):
        for side, out in enumerate(outs):
            copies.append(
                pltpu.make_async_copy(
                    part.at[:, :, pl.ds(side * width, width)],
                    out.at[pl.ds(i * each, each)],
                    sems.at[2 * i + side],
                )
            )
    for copy in copies:
        copy.start()
    for copy in copies:
        copy.wait()


def join_sides(parts):
    count = len(parts)
    each, height, width = parts[0].shape
    out = array((count * each, height, width // 2), BF16)
    return run(
        functools.partial(join_sides_kernel, count),
        "join_sides",
        tuple(parts),
        [anywhere()] * count,
        (out, out),
        [anywhere()] * 2,
        [pltpu.SemaphoreType.DMA((2 * count,))],
    )


def fold_kernel(tail, own, got, *outs):
    body = own.shape[0] - tail
    each = body // len(outs)
    for i, out in enumerate(outs):
        at = pl.ds(i * each, each)
        total = (own[at].astype(F32) + got[at].astype(F32)).astype(BF16)
        if tail:
            out[:each] = total
        else:
            out[...] = total
    if tail:
        coded = encode(decode(own[body:]) + decode(got[body:]))
        for out in outs:
            out[each:] = coded


def fold(own, got, parts, tail=0):
    shape = ((own.shape[0] - tail) // parts + tail,) + own.shape[1:]
    return run(
        functools.partial(fold_kernel, tail),
        "fold",
        (own, got),
        [vmem()] * 2,
        (array(shape, BF16),) * parts,
        [vmem()] * parts,
    )


def fold_last_kernel(own1, got1, own2, got2, keep1, send1, keep2, send2):
    height = own2.shape[1]
    each = height + TAIL
    body = own1.shape[0] - TAIL
    coded = encode(decode(own1[body:]) + decode(got1[body:]))
    half = own2.shape[0] // 2
    for i in range(2 * half):
        out, first = (keep1, send1)[i // half], i % half * each
        at = pl.ds(i * height, height)
        out[first : first + height] = (own1[at].astype(F32) + got1[at].astype(F32)).astype(BF16)
        out[first + height : first + each] = coded
        total = own2[i].astype(F32) + got2[i].astype(F32)
        (keep2, send2)[i // half][i % half] = total.astype(BF16)


def fold_last(own1, got1, own2, got2):
    count, height, width = own2.shape
    first = array((count // 2 * (height + TAIL), width), BF16)
    second = array((count // 2, height, width), BF16)
    return run(
        fold_last_kernel,
        "fold_last",
        (own1, got1, own2, got2),
        [vmem()] * 4,
        (first, first, second, second),
        [vmem()] * 4,
    )


def fold_z_kernel(own1, got1, own2, got2, keep, send):
    height = own2.shape[1]
    each = height + TAIL
    for i, out in enumerate((keep, send)):
        at = pl.ds(i * each, height)
        out[:height] = (own1[at].astype(F32) + got1[at].astype(F32)).astype(BF16)
        at = pl.ds(i * each + height, TAIL)
        out[height:each] = encode(decode(own1[at]) + decode(got1[at]))
        out[each:] = (own2[i].astype(F32) + got2[i].astype(F32)).astype(BF16)


def fold_z(own1, got1, own2, got2):
    _, height, width = own2.shape
    out = array((2 * height + TAIL, width), BF16)
    return run(
        fold_z_kernel,
        "fold_z",
        (own1, got1, own2, got2),
        [vmem()] * 4,
        (out, out),
        [vmem()] * 2,
    )


def fold_add_kernel(own1, got1, own2, got2, out1, out2):
    for own, got, out in ((own1, got1, out1), (own2, got2, out2)):
        out[...] = (own[...].astype(F32) + got[...].astype(F32)).astype(BF16)


def fold_add(own1, got1, own2, got2):
    out = array(own1.shape, BF16)
    return run(
        fold_add_kernel,
        "fold_add",
        (own1, got1, own2, got2),
        [vmem()] * 4,
        (out, out),
        [vmem()] * 2,
    )


def fold_feed_kernel(first1, own1, got1, first2, own2, got2, keep1, send1, keep2, send2):
    width = own1.shape[2]
    half = keep1.shape[0]
    for first, own, got, outs in (
        (first1, own1, got1, (keep1, send1)),
        (first2, own2, got2, (keep2, send2)),
    ):
        for i, out in enumerate(outs):
            at = pl.ds(i * half, half)
            out[:, :, :width] = first[at]
            out[:, :, width:] = (own[at].astype(F32) + got[at].astype(F32)).astype(BF16)


def fold_feed(first1, own1, got1, first2, own2, got2):
    count, height, width = own1.shape
    out = array((count // 2, height, 2 * width), BF16)
    return run(
        fold_feed_kernel,
        "fold_feed",
        (first1, own1, got1, first2, own2, got2),
        [vmem()] * 6,
        (out,) * 4,
        [vmem()] * 4,
    )


def fold_sides_kernel(own1, got1, own2, got2, keep, send):
    width = own1.shape[2]
    half = keep.shape[0]
    for side, (own, got) in enumerate(((own1, got1), (own2, got2))):
        for i, out in enumerate((keep, send)):
            at = pl.ds(i * half, half)
            total = own[at].astype(F32) + got[at].astype(F32)
            out[:, :, side * width : (side + 1) * width] = total.astype(BF16)


def fold_sides(own1, got1, own2, got2):
    count, height, width = own1.shape
    out = array((count // 2, height, 2 * width), BF16)
    return run(
        fold_sides_kernel,
        "fold_sides",
        (own1, got1, own2, got2),
        [vmem()] * 4,
        (out, out),
        [vmem()] * 2,
    )


BY_Z = (0, 4, 2, 6)
Y_MAJOR = BY_Z + tuple(z + 1 for z in BY_Z)
OWN = tuple((0, j) for j in Y_MAJOR)
OTHER = tuple((1, j) for j in Y_MAJOR)
CHIP_NEAR = tuple((chip, z) for chip in range(2) for z in BY_Z)
CHIP_FAR = tuple((chip, z + 1) for chip in range(2) for z in BY_Z)


def split_kernel(other, info, first, second, out, sems):
    slot = 1 - info[1] if other else info[1]
    half = first.shape[1] // 2
    copies = []
    for i, values in enumerate((first, second)):
        for j in range(2):
            at = pl.ds(j * half, half)
            copies.append(
                pltpu.make_async_copy(values.at[slot, at], out.at[i, at], sems.at[2 * i + j])
            )
    for copy in copies:
        copy.start()
    for copy in copies:
        copy.wait()


def split(info, first, second, other):
    return run(
        functools.partial(split_kernel, other),
        "split",
        (info, *in_hbm((first, second))),
        [smem()] + [anywhere()] * 2,
        (array((2,) + first.shape[1:], first.dtype),),
        [vmem()],
        [pltpu.SemaphoreType.DMA((4,))],
    )[0]


def merge_kernel(info, own, got, core_own, core_got, out, sems):
    core = info[2]
    copies = []
    for half, (mine, other) in enumerate(((own, core_own), (got, core_got))):
        copies += [
            pltpu.make_async_copy(mine.at[0], out.at[half, core], sems.at[2 * half]),
            pltpu.make_async_copy(other.at[0], out.at[half, 1 - core], sems.at[2 * half + 1]),
        ]
    for copy in copies:
        copy.start()
    for copy in copies:
        copy.wait()


def merge(info, quarters):
    _, quarter, width = quarters[0].shape
    out = run(
        merge_kernel,
        "merge",
        (info, *quarters),
        [smem()] + [anywhere()] * 4,
        (array((2, 2, quarter, width), quarters[0].dtype),),
        [anywhere()],
        [pltpu.SemaphoreType.DMA((4,))],
    )[0]
    return out.reshape(4 * quarter, width)


def slots_kernel(info, own, other, out, sems):
    copies = [
        pltpu.make_async_copy(own, out.at[info[1]], sems.at[0]),
        pltpu.make_async_copy(other, out.at[1 - info[1]], sems.at[1]),
    ]
    for copy in copies:
        copy.start()
    for copy in copies:
        copy.wait()


def slots_of(info, own, other):
    return run(
        slots_kernel,
        "slots",
        (info, own, other),
        [smem()] + [anywhere()] * 2,
        (array((2,) + own.shape, own.dtype),),
        [anywhere()],
        [pltpu.SemaphoreType.DMA((2,))],
    )[0]


def tokens_add_kernel(count, mine, *rest):
    got, own, sends = rest[:count], rest[count], rest[count + 1 :]
    per = count // 2
    height = got[0].shape[0]
    for k, part in enumerate(got):
        at = k % per * height
        total = mine[k // per, pl.ds(at, height)] + part[...].astype(F32)
        if k < per:
            own[pl.ds(at, height)] = total
        else:
            each = sends[0].shape[0]
            for first in range(0, height, each):
                sends[(at + first) // each][...] = total[first : first + each].astype(BF16)


def tokens_add(mine, got):
    _, quarter, width = mine.shape
    send = array((quarter // 2, width), BF16)
    return run(
        functools.partial(tokens_add_kernel, len(got)),
        "tokens_add",
        (mine, *got),
        [vmem()] * (1 + len(got)),
        (array((quarter, width), F32), send, send),
        [vmem()] * 3,
    )


def tokens_out_kernel(info, own, *rest):
    *got, out = rest
    out[info[1]] = own[...]
    height = got[0].shape[0]
    for k, part in enumerate(got):
        out[1 - info[1], pl.ds(k * height, height), :] = part[...].astype(F32)


def tokens_out(info, own, got):
    return run(
        tokens_out_kernel,
        "tokens_out",
        (info, own, *got),
        [smem()] + [vmem()] * (1 + len(got)),
        (array((2,) + own.shape, F32),),
        [vmem()],
    )[0]


def feed_out_kernel(own, got, up, down):
    half = up.shape[1] // 2
    for i in range(4):
        at = pl.ds(i * half, half)
        total = own[0, :, at].astype(F32) + got[0, :, at].astype(F32)
        out = (down, up)[i % 2]
        out[:, pl.ds(i // 2 * half, half)] = total


def feed_out(own, got):
    _, height, width = own.shape
    out = array((height, width // 2), F32)
    return run(
        feed_out_kernel,
        "feed_out",
        (own, got),
        [vmem()] * 2,
        (out, out),
        [vmem()] * 2,
    )


def attend_out_kernel(a, b, query, key, value, out, gain1, bias1, gain2, bias2):
    height = query.shape[0]

    def both(first, last):
        return a[first:last].astype(F32) + b[first:last].astype(F32)

    one = both(0, height)
    two = both(height + TAIL, 2 * height + TAIL)
    at = pl.ds(height, TAIL)
    sums = decode(a[at]) + decode(b[at])
    for i, ref in enumerate((query, key, value)):
        ref[...] = jnp.concatenate(
            [two[:, 2 * i * HD : 2 * (i + 1) * HD], one[:, (3 + i) * HD : (4 + i) * HD]], axis=1
        )
    out[...] = jnp.transpose(one[:, : 3 * HD])
    for i, ref in enumerate((gain1, bias1, gain2, bias2)):
        ref[...] = jnp.concatenate([sums[i], sums[4 + i]], axis=0)


def attend_out(pieces, height):
    cols = pieces[0].shape[1]
    span = cols // 2
    return run(
        attend_out_kernel,
        "attend_out",
        tuple(pieces),
        [vmem()] * 2,
        (array((height, span), F32),) * 3
        + (array((span, height), F32),)
        + (array((2 * cols,), F32),) * 4,
        [vmem()] * 8,
    )


def fast_path(info, tokens, cotangent, weights, lengths, masks, norms):
    w_query, w_key, w_value, w_out, w_up, w_down = weights
    mask_own, mask_other, mask_ends = masks
    g_one, b_one, g_two, b_two = norms
    height, features, units = w_query.shape[0], tokens.shape[2], w_up.shape[1]
    flat = (tuple((0, j) for j in Y_MAJOR),)
    got_rows = flip_chip(split(info, tokens, cotangent, True))
    piece = pack(w_query, w_key, w_value, w_out)
    got_piece = flip_dp(piece, 4)
    own_rows = split(info, tokens, cotangent, False)
    (two_attn,) = join([piece, got_piece])
    got_attn = flip_dp(two_attn, 2)
    feed_piece = beside(w_up, w_down.T)
    got_feed = flip_dp(feed_piece, 4)
    z_pair, z_single = join_sides([two_attn, got_attn])
    y_pair, x_single = flip_dp(z_pair, 1), flip_chip(z_single)
    own_pair, near_single = join([z_pair, y_pair], [z_single, x_single])
    other_pair, far_single = flip_chip(own_pair), flip_dp(near_single, 1)
    single_w = ((near_single, far_single), (CHIP_NEAR, CHIP_FAR))
    two_up, two_down = join_sides([feed_piece, got_feed])
    got_up, got_down = flip_dp(two_up, 2), flip_dp(two_down, 2)
    quarters = (own_rows, got_rows, flip_core(own_rows), flip_core(got_rows))
    tok = merge(info, quarters)
    own01 = attend(info, lengths, tok, ((own_pair,), flat), True, mask_own[:2])
    z_up, z_down = join([two_up, got_up], [two_down, got_down])
    y_up, x_down = flip_dp(z_up, 1), flip_chip(z_down)
    other01 = attend(info, lengths, tok, ((other_pair,), flat), True, mask_other[:2])
    ends = attend(info, lengths, tok, single_w, False, mask_ends)
    own_up, near_down = join([z_up, y_up], [z_down, x_down])
    other_up, far_down = flip_chip(own_up), flip_dp(near_down, 1)
    up = ((own_up, other_up), (OWN, OTHER))
    down = ((near_down, far_down), (CHIP_NEAR, CHIP_FAR))
    contexts = (own01[3], other01[3], ends[3])
    attn_part = project(info, contexts, single_w, features)
    attn_got = flip_cores(attn_part)
    normal, scale_one, hn = norm_one(tok, attn_part, attn_got, g_one, b_one)
    act1, slope1 = feed_up(info, hn, ((own_up,), flat), units)
    tok_turned, hn_turned = turn_rows(info, tok, hn, Y_MAJOR)
    act2, slope2 = feed_up(info, hn, ((other_up,), flat), units)
    mixed = feed_down(info, act1, act2, down, features)
    mixed_got = flip_cores(mixed)
    own_out, send_out, dzb_two, sums_two = norm_two(
        info, lengths, hn, mixed, mixed_got, quarters, g_two, b_two
    )
    keep_d1, send_d1, keep_d2, send_d2 = feed_grad(
        info, dzb_two, act1, act2, (OWN, OTHER, CHIP_NEAR, CHIP_FAR), False
    )
    got_d1, got_d2 = flip_chip(send_d1), flip_dp(send_d2, 1)
    du1, du2, *back = feed_back(info, dzb_two, slope1, slope2, up, down)
    back_got = flip_cores(back)
    keep_u1, send_u1, keep_u2, send_u2 = feed_grad(
        info, hn_turned, du1, du2, (OWN, OTHER, CHIP_NEAR, CHIP_FAR), True
    )
    got_u1, got_u2 = flip_chip(send_u1), flip_dp(send_u2, 1)
    sum_d1, sum_d2 = fold_add(keep_d1, got_d1, keep_d2, got_d2)
    dzb_one, sums_one = norm_one_back(normal, scale_one, dzb_two, back, back_got, g_one)
    d_ends = attend_back(info, dzb_one, single_w, None, ends)
    keep_f1, send_f1, keep_f2, send_f2 = fold_feed(
        sum_d1, keep_u1, got_u1, sum_d2, keep_u2, got_u2
    )
    got_f1, got_f2 = flip_dp(send_f1, 1), flip_chip(send_f2)
    keep_s, send_s = single_grad(
        info, tok_turned, d_ends, dzb_one, contexts, sums_one, sums_two, Y_MAJOR
    )
    got_s = flip_dp(send_s, 1)
    d_other = attend_back(info, dzb_one, single_w, 1, other01)
    grad_b = pair_grad(tok_turned, d_other, len(OWN))
    got_b = flip_chip(grad_b)
    keep_f, send_f = fold_sides(keep_f1, got_f1, keep_f2, got_f2)
    got_f = flip_dp(send_f, 2)
    d_own = attend_back(info, dzb_one, single_w, 0, own01)
    grad_a = pair_grad(tok_turned, d_own, len(OWN))
    keep_a, send_a = fold(grad_a, got_b, 2, 0)
    got_a = flip_dp(send_a, 1)
    mine, *sent = input_back(
        info, d_own, d_other, d_ends, dzb_one, ((own_pair, other_pair), (OWN, OTHER)), single_w
    )
    sent_got = flip_cores(sent)
    keep_s2, send_s2 = fold(keep_s, got_s, 2, TAIL)
    got_s2 = flip_chip(send_s2)
    keep_f3, send_f3 = fold(keep_f, got_f, 2, 0)
    got_f3 = flip_dp(send_f3, 4)
    own_tok, *send_tok = tokens_add(mine, sent_got)
    got_tok = [flip_chip(v) for v in send_tok]
    keep_s3, send_s3, keep_a3, send_a3 = fold_last(keep_s2, got_s2, keep_a, got_a)
    got_s3, got_a3 = flip_dp(send_s3, 2), flip_dp(send_a3, 2)
    got_out = flip_chip(send_out)
    grad_up, grad_down = feed_out(keep_f3, got_f3)
    keep_z, send_z = fold_z(keep_s3, got_s3, keep_a3, got_a3)
    got_z = flip_dp(send_z, 4)
    grad_tokens = tokens_out(info, own_tok, got_tok)
    output = slots_of(info, own_out, got_out)
    grads = attend_out((keep_z, got_z), height)
    return (output, grad_tokens, *grads[:4], grad_up, grad_down.T, *grads[4:])


def plain_path(info, tokens, cotangent, weights, lengths, masks, norms):
    w_query, w_key, w_value, w_out, w_up, w_down = weights
    mask_own, mask_other, mask_ends = masks
    g_one, b_one, g_two, b_two = norms
    features, units = tokens.shape[2], w_up.shape[1]
    flat = (((0, 0),),)
    two = (((0, 0),), ((1, 0),))

    def gathered(piece):
        own = lax.all_gather(piece, "dp", axis=0, tiled=True)[None]
        return own, flip_chip(own)

    got_rows = flip_chip(split(info, tokens, cotangent, True))
    own_rows = split(info, tokens, cotangent, False)
    quarters = (own_rows, got_rows, flip_core(own_rows), flip_core(got_rows))
    tok = merge(info, quarters)
    firsts = [w[:, : 2 * HD] for w in (w_query, w_key, w_value)]
    thirds = [w_out.T] + [w[:, 2 * HD :] for w in (w_query, w_key, w_value)]
    pair_w = (gathered(jnp.concatenate(firsts, axis=1)), two)
    single_w = (gathered(jnp.concatenate(thirds, axis=1)), two)
    up, down = (gathered(w_up), two), (gathered(w_down.T), two)
    own01 = attend(info, lengths, tok, ((pair_w[0][0],), flat), True, mask_own[:2])
    other01 = attend(info, lengths, tok, ((pair_w[0][1],), flat), True, mask_other[:2])
    ends = attend(info, lengths, tok, single_w, False, mask_ends)
    contexts = (own01[3], other01[3], ends[3])
    part = project(info, contexts, single_w, features)
    normal, scale_one, hn = norm_one(tok, part, flip_cores(part), g_one, b_one)
    act1, slope1 = feed_up(info, hn, ((up[0][0],), flat), units)
    act2, slope2 = feed_up(info, hn, ((up[0][1],), flat), units)
    tok_turned, hn_turned = turn_rows(info, tok, hn, (0,))
    part = feed_down(info, act1, act2, down, features)
    own_out, send_out, dzb_two, sums_two = norm_two(
        info, lengths, hn, part, flip_cores(part), quarters, g_two, b_two
    )
    places = (((0, 0),), ((1, 0),)) * 2
    grad_d = feed_grad(info, dzb_two, act1, act2, places, False)
    du1, du2, *part = feed_back(info, dzb_two, slope1, slope2, up, down)
    grad_u = feed_grad(info, hn_turned, du1, du2, places, True)
    dzb_one, sums_one = norm_one_back(
        normal, scale_one, dzb_two, part, flip_cores(part), g_one
    )
    d_ends = attend_back(info, dzb_one, single_w, None, ends)
    keep_s, send_s = single_grad(
        info, tok_turned, d_ends, dzb_one, contexts, sums_one, sums_two, (0,)
    )
    d_other = attend_back(info, dzb_one, single_w, 1, other01)
    grad_b = pair_grad(tok_turned, d_other, 1)
    d_own = attend_back(info, dzb_one, single_w, 0, own01)
    grad_a = pair_grad(tok_turned, d_own, 1)
    mine, *sent = input_back(info, d_own, d_other, d_ends, dzb_one, pair_w, single_w)
    own_tok, *send_tok = tokens_add(mine, flip_cores(sent))
    output = slots_of(info, own_out, flip_chip(send_out))
    grad_tokens = tokens_out(info, own_tok, [flip_chip(v) for v in send_tok])

    def summed(own, other):
        total = own.astype(F32) + flip_chip(other).astype(F32)
        return lax.psum_scatter(total, "dp", scatter_dimension=0, tiled=True)

    def wide(keep1, send1, keep2, send2):
        return jnp.concatenate([summed(keep1[0], send1[0]), summed(keep2[0], send2[0])], axis=1)

    single = summed(keep_s[:features], send_s[:features])
    pair = summed(grad_a[0], grad_b[0])
    grads = [
        jnp.concatenate(
            [pair[:, 2 * i * HD : 2 * (i + 1) * HD], single[:, (3 + i) * HD : (4 + i) * HD]],
            axis=1,
        )
        for i in range(3)
    ] + [single[:, : 3 * HD].T]
    sums = decode(keep_s[features:])
    sums = lax.psum(sums + flip_chip(sums), "dp")
    sums = [jnp.concatenate([sums[i], sums[4 + i]]) for i in range(4)]
    return (output, grad_tokens, *grads, wide(*grad_u), wide(*grad_d).T, *sums)


def local(
    tokens,
    w_query,
    w_key,
    w_value,
    w_out,
    w_up,
    w_down,
    gain_attn,
    bias_attn,
    gain_ffn,
    bias_ffn,
    lengths,
    random_blocks,
    cotangent,
):
    ORDER.clear()
    size = lax.axis_size("dp")
    rank = lax.axis_index("mp")
    me = lax.axis_index("dp")
    x, core = rank // 2, rank % 2
    quarter = tokens.shape[1]
    seq = 4 * quarter
    height = w_query.shape[0]
    span = w_query.shape[1]
    heads = span // HD
    nblocks = seq // BLOCK
    fast = size == 8 and height % 16 == 0

    shift = x * (seq // 2)
    info = jnp.stack([me, x, core, shift]).astype(jnp.int32)

    blocks = (jnp.arange(nblocks) + x * (nblocks // 2)) % nblocks
    near_blocks = jnp.abs(blocks[:, None] - blocks[None, :]) <= 1
    edge = (blocks == 0) | (blocks == nblocks - 1)
    fixed = near_blocks | edge[:, None] | edge[None, :]

    def table(shard):
        chosen = lax.dynamic_slice_in_dim(random_blocks, shard * heads, heads, 0)
        chosen = jnp.roll(chosen, -x * (nblocks // 2), axis=1)
        hit = jnp.any(chosen[:, None, :, :] == blocks[None, :, None, None], axis=3)
        bias = jnp.where(fixed.T[None] | hit, 0.0, NEGATIVE)
        return jnp.concatenate(
            [
                jnp.zeros((heads, nblocks, HD), F32),
                bias,
                jnp.full((heads, nblocks, 3), -1.0, F32),
                jnp.zeros((heads, nblocks, HD - 3 - nblocks), F32),
            ],
            axis=2,
        )

    mask_own, mask_other = table(rank), table(rank ^ 2)
    mask_ends = jnp.concatenate([mask_own[2:], mask_other[2:]], axis=0)
    g_one, b_one = gain_attn[None], bias_attn[None]
    g_two, b_two = gain_ffn[None], bias_ffn[None]

    path = fast_path if fast else plain_path
    return path(
        info,
        tokens,
        cotangent,
        (w_query, w_key, w_value, w_out, w_up, w_down),
        lengths,
        (mask_own, mask_other, mask_ends),
        (g_one, b_one, g_two, b_two),
    )


def solution(mesh):
    return jax.shard_map(
        local,
        mesh=mesh,
        in_specs=(
            P("dp", "mp", None),
            P("dp", "mp"),
            P("dp", "mp"),
            P("dp", "mp"),
            P("mp", "dp"),
            P("dp", "mp"),
            P("mp", "dp"),
            P(),
            P(),
            P(),
            P(),
            P("dp"),
            P(),
            P("dp", "mp", None),
        ),
        out_specs=(
            P("dp", "mp", None),
            P("dp", "mp", None),
            P("dp", "mp"),
            P("dp", "mp"),
            P("dp", "mp"),
            P("mp", "dp"),
            P("dp", "mp"),
            P("mp", "dp"),
            P(),
            P(),
            P(),
            P(),
        ),
        check_vma=False,
    )
```

```python
import functools

import jax
import jax.numpy as jnp
from jax import lax
from jax.experimental import pallas as pl
from jax.experimental.pallas import tpu as pltpu
from jax.sharding import PartitionSpec as P

HD = 64
BLOCK = 64
LANES = 128
TILE = 256
SENT = 256
EPSILON = 1e-12
TAIL = 32
TOKEN = (8, 128)
ROOM = {
    "attend": 20,
    "attend_back": 28,
    "project": 12,
    "input_back": 24,
    "norm_one": 12,
    "norm_two": 18,
    "norm_one_back": 14,
    "feed_up": 16,
    "feed_down": 18,
    "feed_back": 32,
    "turn_rows": 12,
    "feed_grad": 24,
    "pair_grad": 16,
    "single_grad": 24,
    "join": 1,
    "join_sides": 1,
    "beside": 1,
    "pack": 2,
    "split": 4,
    "merge": 1,
    "fold": 6,
    "fold_add": 8,
    "fold_feed": 10,
    "fold_sides": 8,
    "fold_last": 6,
    "fold_z": 4,
    "slots": 1,
    "tokens_add": 8,
    "tokens_out": 8,
    "feed_out": 6,
    "attend_out": 6,
}
SCALE = 0.125
LOG2E = 1.4426950408889634
LN2 = 0.6931471805599453
NEGATIVE = -1e30
F32 = jnp.float32
BF16 = jnp.bfloat16

CORE_SWAP = [(0, 1), (1, 0), (2, 3), (3, 2)]
CHIP_SWAP = [(0, 2), (2, 0), (1, 3), (3, 1)]


def nn(a, b):
    return lax.dot_general(a, b, (((1,), (0,)), ((), ())), preferred_element_type=F32)


def nt(a, b):
    return lax.dot_general(a, b, (((1,), (1,)), ((), ())), preferred_element_type=F32)


def tn(a, b):
    return lax.dot_general(a, b, (((0,), (0,)), ((), ())), preferred_element_type=F32)


def vmem():
    return pl.BlockSpec(memory_space=pltpu.VMEM)


def smem():
    return pl.BlockSpec(memory_space=pltpu.SMEM)


def anywhere():
    return pl.BlockSpec(memory_space=pl.ANY)


def in_hbm(values):
    return tuple(pltpu.with_memory_space_constraint(v, pltpu.HBM) for v in values)


def array(shape, dtype):
    return jax.ShapeDtypeStruct(shape, dtype)


ORDER = []


def run(kernel, name, args, specs, outs, out_specs, scratch=()):
    given, made = len(args), len(outs)
    extra = tuple(ORDER)

    def body(*refs):
        ins, rest = refs[:given], refs[given + len(extra) :]
        rest[made][...] = jnp.zeros(TOKEN, F32)
        kernel(*ins, *rest[:made], *rest[made + 1 :])

    results = pl.pallas_call(
        body,
        out_shape=tuple(outs) + (array(TOKEN, F32),),
        in_specs=list(specs) + [anywhere()] * len(extra),
        out_specs=tuple(out_specs) + (vmem(),),
        scratch_shapes=list(scratch),
        compiler_params=pltpu.CompilerParams(vmem_limit_bytes=ROOM[name] * 2**20),
        cost_estimate=pl.CostEstimate(flops=1, bytes_accessed=0, transcendentals=0),
        name=name,
    )(*args, *extra)
    ORDER[:] = [results[-1]]
    return results[:-1]


def put_rows(parts, t, value):
    height, tile = parts[0].shape[0], value.shape[0]
    if height <= tile:
        per = tile // height
        for k in range(per):
            parts[t * per + k][...] = value[k * height : (k + 1) * height]
    else:
        per = height // tile
        parts[t // per][pl.ds(t % per * tile, tile), :] = value


def get_sum(parts, more, t):
    height = parts[0].shape[0]
    if height <= TILE:
        per = TILE // height
        at = range(t * per, (t + 1) * per)
        pieces = [parts[k][...].astype(F32) + more[k][...].astype(F32) for k in at]
        return pieces[0] if per == 1 else jnp.concatenate(pieces, axis=0)
    per = height // TILE
    at = pl.ds(t % per * TILE, TILE)
    return parts[t // per][at, :].astype(F32) + more[t // per][at, :].astype(F32)


def tile_rows(ref):
    return [(t, pl.ds(t * TILE, TILE)) for t in range(ref.shape[0] // TILE)]


def far(shape, dtype):
    return pltpu.HBM(shape, dtype)


def tiles(seq, width, height):
    parts = (array((height, width), BF16),) * (seq // height)
    return parts, [vmem()] * len(parts)


def place(me, refs, slots, dst_ref, first=0, last=None, only=None, to=0):
    for ref, of in zip(refs, slots):
        height, width = ref.shape[1], ref.shape[2]
        end = width if last is None else last
        for e, (chip, j) in enumerate(of):
            if only is not None and chip != only:
                continue
            at = 0 if height == dst_ref.shape[0] else pl.multiple_of((me ^ j) * height, height)
            at_column = to + (0 if only is not None else chip * (end - first))
            dst_ref[pl.ds(at, height), pl.ds(at_column, end - first)] = ref[e, :, first:end]


def pick(me, fulls, out_ref, slots, first):
    _, height, width = out_ref.shape
    for e, (chip, j) in enumerate(slots):
        full = fulls[chip]
        at = 0 if height == full.shape[0] else pl.multiple_of((me ^ j) * height, height)
        out_ref[e] = full[pl.ds(at, height), pl.ds(first, width)]


def attend_kernel(slots, columns, only, places, info, lengths, tok, mask, *rest):
    refs, (qa, ka, va, ctx, wfull) = rest[: len(slots)], rest[len(slots) :]
    seq = tok.shape[0]
    place(info[0], refs, slots, wfull, *columns, only)
    lane = lax.broadcasted_iota(jnp.int32, (TILE, LANES), 1)
    row0 = lax.broadcasted_iota(jnp.int32, (TILE, LANES), 0)
    for t in range(seq // TILE):
        at = pl.ds(t * TILE, TILE)
        row = row0 + t * TILE
        made = nn(tok[at, :], wfull[...])
        onehot = jnp.where(lane - HD == row // BLOCK, 1.0, 0.0)[:, HD:]
        position = row + info[3]
        position = jnp.where(position >= seq, position - seq, position)
        dead = (position >= lengths[info[1]]) & (lane >= HD) & (lane < HD + 16)
        for h, (q_at, k_at, v_at) in enumerate(places):
            q = made[:, q_at : q_at + HD] * (SCALE * LOG2E)
            k = made[:, k_at : k_at + HD]
            v = made[:, v_at : v_at + HD]
            qa[h, at, :] = jnp.concatenate([q, onehot], axis=1).astype(BF16)
            per = TILE // BLOCK
            table = jnp.concatenate(
                [
                    jnp.broadcast_to(mask[h, t * per + b : t * per + b + 1, :], (BLOCK, LANES))
                    for b in range(per)
                ],
                axis=0,
            )
            table = jnp.where(dead, NEGATIVE, table)
            ka[h, at, :] = jnp.concatenate([k, table[:, HD:]], axis=1).astype(BF16)
            va[h, at, :] = jnp.concatenate([v, jnp.full((TILE, HD), -1.0, F32)], axis=1).astype(BF16)
    for t in range(seq // TILE):
        at = pl.ds(t * TILE, TILE)
        pieces = []
        for h in range(len(places)):
            q = qa[h, at, :]
            s = nt(q, ka[h])
            top = jnp.max(s, axis=1, keepdims=True)
            p = jnp.exp2(s - top).astype(BF16)
            got = nn(p, va[h])
            total = -got[:, HD:]
            pieces.append(got[:, :HD] / total)
            log = top + jnp.log2(-got)
            hi = log.astype(BF16).astype(F32)
            mid = (log - hi).astype(BF16).astype(F32)
            low = log - hi - mid
            new = jnp.where(
                lane == HD + 16,
                hi,
                jnp.where(lane == HD + 17, mid, jnp.where(lane == HD + 18, low, q.astype(F32))),
            )
            qa[h, at, :] = new.astype(BF16)
        ctx[at, :] = jnp.concatenate(pieces, axis=1).astype(BF16)


PAIR = ((0, 2 * HD, 4 * HD), (HD, 3 * HD, 5 * HD))
SINGLES = ((HD, 2 * HD, 3 * HD), (5 * HD, 6 * HD, 7 * HD))


def attend(info, lengths, tok, gathered, pair, mask):
    arrays, slots = gathered
    seq, width = tok.shape
    aug = far((2, seq, LANES), BF16)
    columns, only, cols = ((0, 6 * HD), 0, 6 * HD) if pair else ((2 * HD, 6 * HD), None, 8 * HD)
    return run(
        functools.partial(attend_kernel, slots, columns, only, PAIR if pair else SINGLES),
        "attend",
        (info, lengths, tok, mask) + arrays,
        [smem()] * 2 + [vmem()] * (2 + len(arrays)),
        (aug, aug, aug, array((seq, LANES), BF16)),
        [vmem()] * 4,
        [pltpu.VMEM((width, cols), BF16)],
    )


def place_out(me, refs, slots, pairs, ends):
    place(me, refs, slots, pairs, 0, 2 * HD)
    place(me, refs, slots, ends, 2 * HD, 4 * HD)
    both = ends[...]
    ends[:, :LANES] = jnp.concatenate([both[:, :HD], both[:, LANES : LANES + HD]], axis=1)


def project_kernel(slots, info, own, other, ends, *rest):
    refs, parts, (w1, w2) = rest[: len(slots)], rest[len(slots) : -2], rest[-2:]
    place_out(info[0], refs, slots, w1, w2)
    for t, at in tile_rows(own):
        both = jnp.concatenate([own[at, :], other[at, :]], axis=1)
        out = nt(both, w1[...]) + nt(ends[at, :], w2[:, :LANES])
        put_rows(parts, t, out.astype(BF16))


def project(info, contexts, gathered, width):
    arrays, slots = gathered
    seq = contexts[0].shape[0]
    return run(
        functools.partial(project_kernel, slots),
        "project",
        (info,) + contexts + arrays,
        [smem()] + [vmem()] * (3 + len(arrays)),
        *tiles(seq, width, 2 * TILE),
        [pltpu.VMEM((width, 2 * LANES), BF16)] * 2,
    )


def attend_back_kernel(slots, chip, info, dz, qa, ka, va, ctx, *rest):
    refs, (dqkv, pairs, ends, da) = rest[: len(slots)], rest[len(slots) :]
    seq = dz.shape[0]
    heads = qa.shape[0]
    if chip is None:
        place_out(info[0], refs, slots, pairs, ends)
        wfull = ends.at[:, pl.ds(0, LANES)]
    else:
        place(info[0], refs, slots, pairs, 0, 2 * HD, chip)
        wfull = pairs.at[:, pl.ds(0, LANES)]
    lane = lax.broadcasted_iota(jnp.int32, (TILE, LANES), 1)
    for t in range(seq // TILE):
        at = pl.ds(t * TILE, TILE)
        dctx = nn(dz[at, :], wfull[...]).astype(BF16).astype(F32)
        both = dctx * ctx[at, :].astype(F32)
        for h in range(heads):
            inner = jnp.sum(both[:, h * HD : (h + 1) * HD], axis=1, keepdims=True)
            hi = inner.astype(BF16).astype(F32)
            mid = (inner - hi).astype(BF16).astype(F32)
            low = inner - hi - mid
            one = jnp.concatenate(
                [dctx[:, h * HD : (h + 1) * HD], jnp.zeros((TILE, HD), F32)], axis=1
            )
            one = jnp.where(lane == HD, hi, one)
            one = jnp.where(lane == HD + 1, mid, one)
            one = jnp.where(lane == HD + 2, low, one)
            da[h, at, :] = one.astype(BF16)

    def turned(values):
        return jnp.transpose(values.astype(F32))[:HD].astype(BF16)

    grads = []
    for h in range(heads):
        k_turned, q_turned, d_turned = turned(ka[h]), turned(qa[h]), turned(da[h])
        dq, dk, dv = None, [], []
        for t in range(seq // TILE):
            at = pl.ds(t * TILE, TILE)
            p = jnp.exp2(nt(ka[h, at, :], qa[h]))
            ds = (p * nt(va[h, at, :], da[h])).astype(BF16)
            dv.append(nt(d_turned, p.astype(BF16)))
            dk.append(nt(q_turned, ds))
            more = nn(k_turned[:, t * TILE : (t + 1) * TILE], ds)
            dq = more if dq is None else dq + more
        dk = jnp.concatenate(dk, axis=1) * LN2
        grads.append((dq * SCALE, dk, jnp.concatenate(dv, axis=1)))
    (dq0, dk0, dv0), (dq1, dk1, dv1) = grads
    if chip is None:
        blank = jnp.zeros_like(dq0)
        stacks = ((blank, dq0), (dk0, dv0), (blank, dq1), (dk1, dv1))
    else:
        stacks = ((dq0, dq1), (dk0, dk1), (dv0, dv1))
    for i, stack in enumerate(stacks):
        both = jnp.transpose(jnp.concatenate(stack, axis=0))
        dqkv[:, i * LANES : (i + 1) * LANES] = both.astype(BF16)


def attend_back(info, dz, gathered, chip, saved):
    arrays, slots = gathered
    qa, ka, va, ctx = saved
    seq, width = dz.shape
    cols = 8 * HD if chip is None else 6 * HD
    return run(
        functools.partial(attend_back_kernel, slots, chip),
        "attend_back",
        (info, dz, qa, ka, va, ctx) + arrays,
        [smem()] + [vmem()] * (5 + len(arrays)),
        (array((seq, cols), BF16),),
        [vmem()],
        [
            pltpu.VMEM((width, 2 * LANES), BF16),
            pltpu.VMEM((width, 2 * LANES), BF16),
            pltpu.VMEM((2, seq, LANES), BF16),
        ],
    )[0]


def input_back_kernel(slots1, slots2, info, own, other, ends, dz, *rest):
    n1, n2 = len(slots1), len(slots2)
    refs1, refs2, (mine, *sent, w1, w2) = rest[:n1], rest[n1 : n1 + n2], rest[n1 + n2 :]
    place(info[0], refs1, slots1, w1)
    place(info[0], refs2, slots2, w2, 2 * HD, 6 * HD)
    per = len(sent) // 2
    height = sent[0].shape[0]
    for half in range(dz.shape[0] // TILE // 2):
        for whose in range(2):
            tile = 2 * half + (info[2] if whose == 0 else 1 - info[2])
            at = pl.ds(pl.multiple_of(tile * TILE, TILE), TILE)
            pairs = jnp.concatenate([own[at, :], other[at, :]], axis=1)
            back = nt(pairs, w1[...]) + nt(ends[at, :], w2[...])
            if whose == 0:
                mine[half] = back + dz[at, :].astype(F32)
                continue
            for k in range(per):
                part = back[k * height : (k + 1) * height]
                sent[half * per + k][...] = part.astype(BF16)


def input_back(info, own, other, ends, dz, gathered1, gathered2):
    seq, width = dz.shape
    arrays = gathered1[0] + gathered2[0]
    halves = (seq // TILE // 2, TILE, width)
    grads = (own, other, ends, dz)
    return run(
        functools.partial(input_back_kernel, gathered1[1], gathered2[1]),
        "input_back",
        (info,) + grads + arrays,
        [smem()] + [vmem()] * (len(grads) + len(arrays)),
        (array(halves, F32),) + (array((SENT, width), BF16),) * (seq // 2 // SENT),
        [vmem()] * (1 + seq // 2 // SENT),
        [pltpu.VMEM((width, 12 * HD), BF16), pltpu.VMEM((width, 8 * HD), BF16)],
    )


def center(z):
    mean = jnp.mean(z, axis=1, keepdims=True)
    moved = z - mean
    spread = jnp.mean(moved * moved, axis=1, keepdims=True)
    scale = lax.rsqrt(spread + EPSILON)
    return moved * scale, scale


def norm_back(n, scale, gy, gain):
    dn = gy * gain
    return scale * (
        dn - jnp.mean(dn, axis=1, keepdims=True) - n * jnp.mean(dn * n, axis=1, keepdims=True)
    )


def add_sums(gy, n, sums):
    more = [jnp.sum(v, axis=0, keepdims=True) for v in (gy * n, gy)]
    return more if sums is None else [a + b for a, b in zip(sums, more)]


def norm_one_kernel(tok, gain, bias, *rest):
    *parts, normal, scale, hn = rest
    count = len(parts) // 2
    for t, at in tile_rows(tok):
        value = tok[at, :].astype(F32) + get_sum(parts[:count], parts[count:], t)
        n, r = center(value)
        normal[at, :] = n.astype(BF16)
        scale[at, :] = r
        hn[at, :] = (n * gain[...] + bias[...]).astype(BF16)


def norm_one(tok, p0, p1, gain, bias):
    seq, width = tok.shape
    return run(
        norm_one_kernel,
        "norm_one",
        (tok, gain, bias, *p0, *p1),
        [vmem()] * (3 + len(p0) + len(p1)),
        (array((seq, width), BF16), array((seq, 1), F32), array((seq, width), BF16)),
        [vmem()] * 3,
    )


def norm_two_kernel(info, lengths, hn, own, got, core_own, core_got, gain, bias, *rest):
    *parts, own_out, send_out, dzb, sums, out = rest
    count = len(parts) // 2
    seq = hn.shape[0]
    total = None
    for t, at in tile_rows(hn):
        value = hn[at, :].astype(F32) + get_sum(parts[:count], parts[count:], t)
        n, scale = center(value)
        out[at, :] = (n * gain[...] + bias[...]).astype(BF16)
        position = lax.broadcasted_iota(jnp.int32, (TILE, 1), 0) + t * TILE + info[3]
        position = jnp.where(position >= seq, position - seq, position)
        valid = jnp.where(position < lengths[info[1]], 1.0, 0.0)
        mine, others = ((own, core_own), (got, core_got))[t // 2]
        cot = jnp.where(info[2] == t % 2, mine[1].astype(F32), others[1].astype(F32))
        gy = cot * valid
        dzb[at, :] = norm_back(n, scale, gy, gain[...]).astype(BF16)
        total = add_sums(gy, n, total)
    sums[...] = jnp.concatenate(total, axis=0)
    for half, ref in enumerate((own_out, send_out)):
        at = pl.multiple_of((2 * half + info[2]) * TILE, TILE)
        ref[...] = out[pl.ds(at, TILE), :]


def norm_two(info, lengths, hn, m0, m1, cot, gain, bias):
    seq, width = hn.shape
    return run(
        norm_two_kernel,
        "norm_two",
        (info, lengths, hn, *cot, gain, bias, *m0, *m1),
        [smem()] * 2 + [vmem()] * (3 + len(cot) + len(m0) + len(m1)),
        (
            array((TILE, width), BF16),
            array((TILE, width), BF16),
            array((seq, width), BF16),
            array((2, width), F32),
        ),
        [vmem()] * 4,
        [pltpu.VMEM((seq, width), BF16)],
    )


def norm_one_back_kernel(normal, scale, dz2, gain, *rest):
    *parts, dzb, sums = rest
    count = len(parts) // 2
    total = None
    for t, at in tile_rows(dz2):
        n = normal[at, :].astype(F32)
        gy = dz2[at, :].astype(F32) + get_sum(parts[:count], parts[count:], t)
        dzb[at, :] = norm_back(n, scale[at, :], gy, gain[...]).astype(BF16)
        total = add_sums(gy, n, total)
    sums[...] = jnp.concatenate(total, axis=0)


def norm_one_back(normal, scale, dz2, p0, p1, gain):
    seq, width = normal.shape
    return run(
        norm_one_back_kernel,
        "norm_one_back",
        (normal, scale, dz2, gain, *p0, *p1),
        [vmem()] * (4 + len(p0) + len(p1)),
        (array((seq, width), BF16), array((2, width), F32)),
        [vmem()] * 2,
    )


def gelu_pair(u):
    phi = 0.5 + 0.5 * lax.erf(u * 0.7071067811865476)
    return u * phi, phi + u * (jnp.exp(-0.5 * u * u) * 0.3989422804014327)


def feed_up_kernel(slots, info, hn, *rest):
    refs, (active, slope, wfull) = rest[: len(slots)], rest[len(slots) :]
    place(info[0], refs, slots, wfull)
    for _, at in tile_rows(hn):
        a, g = gelu_pair(nn(hn[at, :], wfull[...]))
        active[at, :] = a.astype(BF16)
        slope[at, :] = g.astype(BF16)


def feed_up(info, hn, gathered, units):
    arrays, slots = gathered
    seq, width = hn.shape
    return run(
        functools.partial(feed_up_kernel, slots),
        "feed_up",
        (info, hn) + arrays,
        [smem()] + [vmem()] * (1 + len(arrays)),
        (array((seq, units), BF16), array((seq, units), BF16)),
        [vmem()] * 2,
        [pltpu.VMEM((width, units), BF16)],
    )


def feed_down_kernel(slots, info, act1, act2, *rest):
    refs, parts, wfull = rest[: len(slots)], rest[len(slots) : -1], rest[-1]
    place(info[0], refs, slots, wfull)
    for t, at in tile_rows(act1):
        both = jnp.concatenate([act1[at, :], act2[at, :]], axis=1)
        put_rows(parts, t, nt(both, wfull[...]).astype(BF16))


def feed_down(info, act1, act2, gathered, width):
    seq, units = act1.shape
    arrays, slots = gathered
    return run(
        functools.partial(feed_down_kernel, slots),
        "feed_down",
        (info, act1, act2) + arrays,
        [smem()] + [vmem()] * (2 + len(arrays)),
        *tiles(seq, width, seq),
        [pltpu.VMEM((width, 2 * units), BF16)],
    )


def feed_back_kernel(slots_up, slots_down, info, dzb, slope1, slope2, *rest):
    n1, n2 = len(slots_up), len(slots_down)
    ups, downs, (du1, du2, *parts, up, down) = rest[:n1], rest[n1 : n1 + n2], rest[n1 + n2 :]
    place(info[0], ups, slots_up, up)
    place(info[0], downs, slots_down, down)
    units = du1.shape[1]
    for t, at in tile_rows(dzb):
        out = None
        for i, (slope, du) in enumerate(((slope1, du1), (slope2, du2))):
            cols = pl.ds(i * units, units)
            grad = (nn(dzb[at, :], down[:, cols]) * slope[at, :].astype(F32)).astype(BF16)
            du[at, :] = grad
            more = nt(grad, up[:, cols])
            out = more if out is None else out + more
        put_rows(parts, t, out.astype(BF16))


def feed_back(info, dzb, slope1, slope2, up, down):
    seq, width = dzb.shape
    units = slope1.shape[1]
    arrays = up[0] + down[0]
    parts, part_specs = tiles(seq, width, TILE)
    return run(
        functools.partial(feed_back_kernel, up[1], down[1]),
        "feed_back",
        (info, dzb, slope1, slope2) + arrays,
        [smem()] + [vmem()] * (3 + len(arrays)),
        (array((seq, units), BF16),) * 2 + parts,
        [vmem()] * 2 + part_specs,
        [pltpu.VMEM((width, 2 * units), BF16)] * 2,
    )


def turn_rows_kernel(order, info, first, second, out1, out2, full):
    count = len(order)
    height = full.shape[0] // count
    for values, out in ((first, out1), (second, out2)):
        for t, at in tile_rows(values):
            full[:, t * TILE : (t + 1) * TILE] = jnp.transpose(values[at, :])
        for e, j in enumerate(order):
            at = 0 if count == 1 else pl.multiple_of((info[0] ^ j) * height, height)
            out[pl.ds(e * height, height), :] = full[pl.ds(at, height), :]


def turn_rows(info, first, second, order):
    shape = first.shape[::-1]
    out = array(shape, BF16)
    return run(
        functools.partial(turn_rows_kernel, order),
        "turn_rows",
        (info, first, second),
        [smem()] + [vmem()] * 2,
        (out, out),
        [vmem()] * 2,
        [pltpu.VMEM(shape, BF16)],
    )


def feed_grad_kernel(turned, places, info, a, d1, d2, *rest):
    outs, full = rest[:4], rest[4]
    half = outs[0].shape[2]
    product = nn if turned else tn
    made = product(a[...], jnp.concatenate([d1[...], d2[...]], axis=1)).astype(BF16)
    if turned:
        height = outs[0].shape[1]
        order = [j for chip, j in places[0] if chip == 0]
        for i, out in enumerate(outs):
            for e, (chip, j) in enumerate(places[i]):
                row = order.index(j) * height
                first = 2 * chip * half + (i // 2) * half
                out[e] = made[row : row + height, first : first + half]
        return
    full[...] = made
    fulls = [full.at[:, pl.ds(2 * chip * half, 2 * half)] for chip in range(2)]
    for i, out in enumerate(outs):
        pick(info[0], fulls, out, places[i], (i // 2) * half)


def feed_grad(info, a, d1, d2, places, turned):
    seq, units = d1.shape
    width = a.shape[0] if turned else a.shape[1]
    count = len(places[0])
    out = array((count, width // count, units // 2), BF16)
    return run(
        functools.partial(feed_grad_kernel, turned, places),
        "feed_grad",
        (info, a, d1, d2),
        [smem()] + [vmem()] * 3,
        (out,) * 4,
        [vmem()] * 4,
        [pltpu.VMEM((width, 2 * units), BF16)],
    )


def pair_grad_kernel(tok_turned, d, out):
    made = nn(tok_turned[...], d[...]).astype(BF16)
    height = out.shape[1]
    for e in range(out.shape[0]):
        out[e] = made[e * height : (e + 1) * height]


def pair_grad(tok_turned, d, count):
    width = tok_turned.shape[0]
    cols = d.shape[1]
    return run(
        pair_grad_kernel,
        "pair_grad",
        (tok_turned, d),
        [vmem()] * 2,
        (array((count, width // count, cols), BF16),),
        [vmem()],
    )[0]


def encode(sums):
    hi = sums.astype(BF16).astype(F32)
    mid = (sums - hi).astype(BF16).astype(F32)
    low = sums - hi - mid
    return jnp.concatenate([hi, mid, low, jnp.zeros_like(low)], axis=0).astype(BF16)


def decode(coded):
    values = coded.astype(F32)
    n = values.shape[0] // 4
    return values[:n] + values[n : 2 * n] + values[2 * n : 3 * n]


def single_grad_kernel(
    order, info, tok_turned, d, dz, own, other, ends, sums_one, sums_two, keep, send, full
):
    mine = nn(tok_turned[...], d[...])
    full[...] = tn(dz[...], jnp.concatenate([ends[...], own[...], other[...]], axis=1))
    count = len(order)
    height = full.shape[0] // count
    width = keep.shape[1]
    blank = jnp.zeros((height, HD), F32)
    both = jnp.concatenate([sums_one[...], sums_two[...]], axis=0)
    both = encode(jnp.concatenate([both[:, :width], both[:, width:]], axis=0))
    half = max(1, count // 2)
    for e, j in enumerate(order):
        at = 0 if count == 1 else pl.multiple_of((info[0] ^ j) * height, height)
        heads = full[pl.ds(at, height), :]
        rows_in = mine[e * height : (e + 1) * height]
        for chip in range(2):
            first = chip * 4 * HD
            third = jnp.concatenate([heads[:, chip * HD : (chip + 1) * HD], blank], axis=1)
            made = [
                heads[:, (chip + 1) * LANES : (chip + 2) * LANES],
                third + rows_in[:, first : first + LANES],
                rows_in[:, first + LANES : first + 2 * LANES],
            ]
            if count == 1:
                out, row = (keep, send)[chip], 0
            else:
                out, row = (keep, send)[e // half], (chip * half + e % half) * height
            out[pl.ds(row, height), :] = jnp.concatenate(made, axis=1).astype(BF16)
    for out in (keep, send):
        out[pl.ds(out.shape[0] - TAIL, TAIL), :] = both


def single_grad(info, tok_turned, d, dz, contexts, sums_one, sums_two, order):
    width = tok_turned.shape[0]
    cols = 6 * HD
    out = array((width + TAIL, cols), BF16)
    return run(
        functools.partial(single_grad_kernel, order),
        "single_grad",
        (info, tok_turned, d, dz, *contexts, sums_one, sums_two),
        [smem()] + [vmem()] * 8,
        (out, out),
        [vmem()] * 2,
        [pltpu.VMEM((width, 3 * LANES), F32)],
    )


def across(values, axis, pairs):
    return lax.ppermute(values, axis, pairs)


def flip_chip(values):
    return across(values, "mp", CHIP_SWAP)


def flip_core(values):
    return across(values, "mp", CORE_SWAP)


def flip_cores(parts):
    return [flip_core(p) for p in parts]


def flip_dp(values, distance):
    size = lax.axis_size("dp")
    return across(values, "dp", [(i, i ^ distance) for i in range(size)])


def join_kernel(groups, *refs):
    count = sum(groups)
    parts, outs, sems = refs[:count], refs[count:-1], refs[-1]
    copies = []
    for out, number in zip(outs, groups):
        first = 0
        for part in parts[len(copies) : len(copies) + number]:
            to = out.at[pl.ds(first, part.shape[0])]
            copies.append(pltpu.make_async_copy(part, to, sems.at[len(copies)]))
            first += part.shape[0]
    for copy in copies:
        copy.start()
    for copy in copies:
        copy.wait()


def join(*groups):
    parts = sum((tuple(g) for g in groups), ())
    outs = [array((sum(p.shape[0] for p in g),) + g[0].shape[1:], g[0].dtype) for g in groups]
    return run(
        functools.partial(join_kernel, tuple(len(g) for g in groups)),
        "join",
        parts,
        [anywhere()] * len(parts),
        outs,
        [anywhere()] * len(outs),
        [pltpu.SemaphoreType.DMA((len(parts),))],
    )


def pack_kernel(w_query, w_key, w_value, w_out, out, rows_in, out_in, sems):
    copies = [
        pltpu.make_async_copy(w, rows_in.at[i], sems.at[i])
        for i, w in enumerate((w_query, w_key, w_value))
    ]
    copies.append(pltpu.make_async_copy(w_out, out_in, sems.at[3]))
    for copy in copies:
        copy.start()
    for copy in copies:
        copy.wait()
    for i in range(3):
        out[0, :, 2 * i * HD : 2 * (i + 1) * HD] = rows_in[i, :, : 2 * HD]
    parts = [jnp.transpose(out_in[...].astype(F32))]
    parts += [rows_in[i, :, 2 * HD :].astype(F32) for i in range(3)]
    out[0, :, 6 * HD :] = jnp.concatenate(parts, axis=1).astype(BF16)


def pack(w_query, w_key, w_value, w_out):
    height, span = w_query.shape
    return run(
        pack_kernel,
        "pack",
        in_hbm((w_query, w_key, w_value, w_out)),
        [anywhere()] * 4,
        (array((1, height, 4 * span), BF16),),
        [vmem()],
        [
            pltpu.VMEM((3, height, span), BF16),
            pltpu.VMEM(w_out.shape, BF16),
            pltpu.SemaphoreType.DMA((4,)),
        ],
    )[0]


def beside_kernel(first, second, out, sems):
    width = first.shape[1]
    copies = [
        pltpu.make_async_copy(ref, out.at[0, :, pl.ds(i * width, width)], sems.at[i])
        for i, ref in enumerate((first, second))
    ]
    for copy in copies:
        copy.start()
    for copy in copies:
        copy.wait()


def beside(first, second):
    height, width = first.shape
    return run(
        beside_kernel,
        "beside",
        in_hbm((first, second)),
        [anywhere()] * 2,
        (array((1, height, 2 * width), BF16),),
        [anywhere()],
        [pltpu.SemaphoreType.DMA((2,))],
    )[0]


def join_sides_kernel(count, *refs):
    parts, outs, sems = refs[:count], refs[count : count + 2], refs[count + 2]
    width = outs[0].shape[2]
    copies = []
    each = parts[0].shape[0]
    for i, part in enumerate(parts):
        for side, out in enumerate(outs):
            copies.append(
                pltpu.make_async_copy(
                    part.at[:, :, pl.ds(side * width, width)],
                    out.at[pl.ds(i * each, each)],
                    sems.at[2 * i + side],
                )
            )
    for copy in copies:
        copy.start()
    for copy in copies:
        copy.wait()


def join_sides(parts):
    count = len(parts)
    each, height, width = parts[0].shape
    out = array((count * each, height, width // 2), BF16)
    return run(
        functools.partial(join_sides_kernel, count),
        "join_sides",
        tuple(parts),
        [anywhere()] * count,
        (out, out),
        [anywhere()] * 2,
        [pltpu.SemaphoreType.DMA((2 * count,))],
    )


def fold_kernel(tail, own, got, *outs):
    body = own.shape[0] - tail
    each = body // len(outs)
    for i, out in enumerate(outs):
        at = pl.ds(i * each, each)
        total = (own[at].astype(F32) + got[at].astype(F32)).astype(BF16)
        if tail:
            out[:each] = total
        else:
            out[...] = total
    if tail:
        coded = encode(decode(own[body:]) + decode(got[body:]))
        for out in outs:
            out[each:] = coded


def fold(own, got, parts, tail=0):
    shape = ((own.shape[0] - tail) // parts + tail,) + own.shape[1:]
    return run(
        functools.partial(fold_kernel, tail),
        "fold",
        (own, got),
        [vmem()] * 2,
        (array(shape, BF16),) * parts,
        [vmem()] * parts,
    )


def fold_last_kernel(own1, got1, own2, got2, keep1, send1, keep2, send2):
    height = own2.shape[1]
    each = height + TAIL
    body = own1.shape[0] - TAIL
    coded = encode(decode(own1[body:]) + decode(got1[body:]))
    half = own2.shape[0] // 2
    for i in range(2 * half):
        out, first = (keep1, send1)[i // half], i % half * each
        at = pl.ds(i * height, height)
        out[first : first + height] = (own1[at].astype(F32) + got1[at].astype(F32)).astype(BF16)
        out[first + height : first + each] = coded
        total = own2[i].astype(F32) + got2[i].astype(F32)
        (keep2, send2)[i // half][i % half] = total.astype(BF16)


def fold_last(own1, got1, own2, got2):
    count, height, width = own2.shape
    first = array((count // 2 * (height + TAIL), width), BF16)
    second = array((count // 2, height, width), BF16)
    return run(
        fold_last_kernel,
        "fold_last",
        (own1, got1, own2, got2),
        [vmem()] * 4,
        (first, first, second, second),
        [vmem()] * 4,
    )


def fold_z_kernel(own1, got1, own2, got2, keep, send):
    height = own2.shape[1]
    each = height + TAIL
    for i, out in enumerate((keep, send)):
        at = pl.ds(i * each, height)
        out[:height] = (own1[at].astype(F32) + got1[at].astype(F32)).astype(BF16)
        at = pl.ds(i * each + height, TAIL)
        out[height:each] = encode(decode(own1[at]) + decode(got1[at]))
        out[each:] = (own2[i].astype(F32) + got2[i].astype(F32)).astype(BF16)


def fold_z(own1, got1, own2, got2):
    _, height, width = own2.shape
    out = array((2 * height + TAIL, width), BF16)
    return run(
        fold_z_kernel,
        "fold_z",
        (own1, got1, own2, got2),
        [vmem()] * 4,
        (out, out),
        [vmem()] * 2,
    )


def fold_add_kernel(own1, got1, own2, got2, out1, out2):
    for own, got, out in ((own1, got1, out1), (own2, got2, out2)):
        out[...] = (own[...].astype(F32) + got[...].astype(F32)).astype(BF16)


def fold_add(own1, got1, own2, got2):
    out = array(own1.shape, BF16)
    return run(
        fold_add_kernel,
        "fold_add",
        (own1, got1, own2, got2),
        [vmem()] * 4,
        (out, out),
        [vmem()] * 2,
    )


def fold_feed_kernel(first1, own1, got1, first2, own2, got2, keep1, send1, keep2, send2):
    width = own1.shape[2]
    half = keep1.shape[0]
    for first, own, got, outs in (
        (first1, own1, got1, (keep1, send1)),
        (first2, own2, got2, (keep2, send2)),
    ):
        for i, out in enumerate(outs):
            at = pl.ds(i * half, half)
            out[:, :, :width] = first[at]
            out[:, :, width:] = (own[at].astype(F32) + got[at].astype(F32)).astype(BF16)


def fold_feed(first1, own1, got1, first2, own2, got2):
    count, height, width = own1.shape
    out = array((count // 2, height, 2 * width), BF16)
    return run(
        fold_feed_kernel,
        "fold_feed",
        (first1, own1, got1, first2, own2, got2),
        [vmem()] * 6,
        (out,) * 4,
        [vmem()] * 4,
    )


def fold_sides_kernel(own1, got1, own2, got2, keep, send):
    width = own1.shape[2]
    half = keep.shape[0]
    for side, (own, got) in enumerate(((own1, got1), (own2, got2))):
        for i, out in enumerate((keep, send)):
            at = pl.ds(i * half, half)
            total = own[at].astype(F32) + got[at].astype(F32)
            out[:, :, side * width : (side + 1) * width] = total.astype(BF16)


def fold_sides(own1, got1, own2, got2):
    count, height, width = own1.shape
    out = array((count // 2, height, 2 * width), BF16)
    return run(
        fold_sides_kernel,
        "fold_sides",
        (own1, got1, own2, got2),
        [vmem()] * 4,
        (out, out),
        [vmem()] * 2,
    )


BY_Z = (0, 4, 2, 6)
Y_MAJOR = BY_Z + tuple(z + 1 for z in BY_Z)
OWN = tuple((0, j) for j in Y_MAJOR)
OTHER = tuple((1, j) for j in Y_MAJOR)
CHIP_NEAR = tuple((chip, z) for chip in range(2) for z in BY_Z)
CHIP_FAR = tuple((chip, z + 1) for chip in range(2) for z in BY_Z)


def split_kernel(other, info, first, second, out, sems):
    slot = 1 - info[1] if other else info[1]
    half = first.shape[1] // 2
    copies = []
    for i, values in enumerate((first, second)):
        for j in range(2):
            at = pl.ds(j * half, half)
            copies.append(
                pltpu.make_async_copy(values.at[slot, at], out.at[i, at], sems.at[2 * i + j])
            )
    for copy in copies:
        copy.start()
    for copy in copies:
        copy.wait()


def split(info, first, second, other):
    return run(
        functools.partial(split_kernel, other),
        "split",
        (info, *in_hbm((first, second))),
        [smem()] + [anywhere()] * 2,
        (array((2,) + first.shape[1:], first.dtype),),
        [vmem()],
        [pltpu.SemaphoreType.DMA((4,))],
    )[0]


def merge_kernel(info, own, got, core_own, core_got, out, sems):
    core = info[2]
    copies = []
    for half, (mine, other) in enumerate(((own, core_own), (got, core_got))):
        copies += [
            pltpu.make_async_copy(mine.at[0], out.at[half, core], sems.at[2 * half]),
            pltpu.make_async_copy(other.at[0], out.at[half, 1 - core], sems.at[2 * half + 1]),
        ]
    for copy in copies:
        copy.start()
    for copy in copies:
        copy.wait()


def merge(info, quarters):
    _, quarter, width = quarters[0].shape
    out = run(
        merge_kernel,
        "merge",
        (info, *quarters),
        [smem()] + [anywhere()] * 4,
        (array((2, 2, quarter, width), quarters[0].dtype),),
        [anywhere()],
        [pltpu.SemaphoreType.DMA((4,))],
    )[0]
    return out.reshape(4 * quarter, width)


def slots_kernel(info, own, other, out, sems):
    copies = [
        pltpu.make_async_copy(own, out.at[info[1]], sems.at[0]),
        pltpu.make_async_copy(other, out.at[1 - info[1]], sems.at[1]),
    ]
    for copy in copies:
        copy.start()
    for copy in copies:
        copy.wait()


def slots_of(info, own, other):
    return run(
        slots_kernel,
        "slots",
        (info, own, other),
        [smem()] + [anywhere()] * 2,
        (array((2,) + own.shape, own.dtype),),
        [anywhere()],
        [pltpu.SemaphoreType.DMA((2,))],
    )[0]


def tokens_add_kernel(count, mine, *rest):
    got, own, sends = rest[:count], rest[count], rest[count + 1 :]
    per = count // 2
    height = got[0].shape[0]
    for k, part in enumerate(got):
        at = k % per * height
        total = mine[k // per, pl.ds(at, height)] + part[...].astype(F32)
        if k < per:
            own[pl.ds(at, height)] = total
        else:
            each = sends[0].shape[0]
            for first in range(0, height, each):
                sends[(at + first) // each][...] = total[first : first + each].astype(BF16)


def tokens_add(mine, got):
    _, quarter, width = mine.shape
    send = array((quarter // 2, width), BF16)
    return run(
        functools.partial(tokens_add_kernel, len(got)),
        "tokens_add",
        (mine, *got),
        [vmem()] * (1 + len(got)),
        (array((quarter, width), F32), send, send),
        [vmem()] * 3,
    )


def tokens_out_kernel(info, own, *rest):
    *got, out = rest
    out[info[1]] = own[...]
    height = got[0].shape[0]
    for k, part in enumerate(got):
        out[1 - info[1], pl.ds(k * height, height), :] = part[...].astype(F32)


def tokens_out(info, own, got):
    return run(
        tokens_out_kernel,
        "tokens_out",
        (info, own, *got),
        [smem()] + [vmem()] * (1 + len(got)),
        (array((2,) + own.shape, F32),),
        [vmem()],
    )[0]


def feed_out_kernel(own, got, up, down):
    half = up.shape[1] // 2
    for i in range(4):
        at = pl.ds(i * half, half)
        total = own[0, :, at].astype(F32) + got[0, :, at].astype(F32)
        out = (down, up)[i % 2]
        out[:, pl.ds(i // 2 * half, half)] = total


def feed_out(own, got):
    _, height, width = own.shape
    out = array((height, width // 2), F32)
    return run(
        feed_out_kernel,
        "feed_out",
        (own, got),
        [vmem()] * 2,
        (out, out),
        [vmem()] * 2,
    )


def attend_out_kernel(a, b, query, key, value, out, gain1, bias1, gain2, bias2):
    height = query.shape[0]

    def both(first, last):
        return a[first:last].astype(F32) + b[first:last].astype(F32)

    one = both(0, height)
    two = both(height + TAIL, 2 * height + TAIL)
    at = pl.ds(height, TAIL)
    sums = decode(a[at]) + decode(b[at])
    for i, ref in enumerate((query, key, value)):
        ref[...] = jnp.concatenate(
            [two[:, 2 * i * HD : 2 * (i + 1) * HD], one[:, (3 + i) * HD : (4 + i) * HD]], axis=1
        )
    out[...] = jnp.transpose(one[:, : 3 * HD])
    for i, ref in enumerate((gain1, bias1, gain2, bias2)):
        ref[...] = jnp.concatenate([sums[i], sums[4 + i]], axis=0)


def attend_out(pieces, height):
    cols = pieces[0].shape[1]
    span = cols // 2
    return run(
        attend_out_kernel,
        "attend_out",
        tuple(pieces),
        [vmem()] * 2,
        (array((height, span), F32),) * 3
        + (array((span, height), F32),)
        + (array((2 * cols,), F32),) * 4,
        [vmem()] * 8,
    )


def fast_path(info, tokens, cotangent, weights, lengths, masks, norms):
    w_query, w_key, w_value, w_out, w_up, w_down = weights
    mask_own, mask_other, mask_ends = masks
    g_one, b_one, g_two, b_two = norms
    height, features, units = w_query.shape[0], tokens.shape[2], w_up.shape[1]
    flat = (tuple((0, j) for j in Y_MAJOR),)
    got_rows = flip_chip(split(info, tokens, cotangent, True))
    piece = pack(w_query, w_key, w_value, w_out)
    got_piece = flip_dp(piece, 4)
    own_rows = split(info, tokens, cotangent, False)
    (two_attn,) = join([piece, got_piece])
    got_attn = flip_dp(two_attn, 2)
    feed_piece = beside(w_up, w_down.T)
    got_feed = flip_dp(feed_piece, 4)
    z_pair, z_single = join_sides([two_attn, got_attn])
    y_pair, x_single = flip_dp(z_pair, 1), flip_chip(z_single)
    own_pair, near_single = join([z_pair, y_pair], [z_single, x_single])
    other_pair, far_single = flip_chip(own_pair), flip_dp(near_single, 1)
    single_w = ((near_single, far_single), (CHIP_NEAR, CHIP_FAR))
    two_up, two_down = join_sides([feed_piece, got_feed])
    got_up, got_down = flip_dp(two_up, 2), flip_dp(two_down, 2)
    quarters = (own_rows, got_rows, flip_core(own_rows), flip_core(got_rows))
    tok = merge(info, quarters)
    own01 = attend(info, lengths, tok, ((own_pair,), flat), True, mask_own[:2])
    z_up, z_down = join([two_up, got_up], [two_down, got_down])
    y_up, x_down = flip_dp(z_up, 1), flip_chip(z_down)
    other01 = attend(info, lengths, tok, ((other_pair,), flat), True, mask_other[:2])
    ends = attend(info, lengths, tok, single_w, False, mask_ends)
    own_up, near_down = join([z_up, y_up], [z_down, x_down])
    other_up, far_down = flip_chip(own_up), flip_dp(near_down, 1)
    up = ((own_up, other_up), (OWN, OTHER))
    down = ((near_down, far_down), (CHIP_NEAR, CHIP_FAR))
    contexts = (own01[3], other01[3], ends[3])
    attn_part = project(info, contexts, single_w, features)
    attn_got = flip_cores(attn_part)
    normal, scale_one, hn = norm_one(tok, attn_part, attn_got, g_one, b_one)
    act1, slope1 = feed_up(info, hn, ((own_up,), flat), units)
    tok_turned, hn_turned = turn_rows(info, tok, hn, Y_MAJOR)
    act2, slope2 = feed_up(info, hn, ((other_up,), flat), units)
    mixed = feed_down(info, act1, act2, down, features)
    mixed_got = flip_cores(mixed)
    own_out, send_out, dzb_two, sums_two = norm_two(
        info, lengths, hn, mixed, mixed_got, quarters, g_two, b_two
    )
    keep_d1, send_d1, keep_d2, send_d2 = feed_grad(
        info, dzb_two, act1, act2, (OWN, OTHER, CHIP_NEAR, CHIP_FAR), False
    )
    got_d1, got_d2 = flip_chip(send_d1), flip_dp(send_d2, 1)
    du1, du2, *back = feed_back(info, dzb_two, slope1, slope2, up, down)
    back_got = flip_cores(back)
    keep_u1, send_u1, keep_u2, send_u2 = feed_grad(
        info, hn_turned, du1, du2, (OWN, OTHER, CHIP_NEAR, CHIP_FAR), True
    )
    got_u1, got_u2 = flip_chip(send_u1), flip_dp(send_u2, 1)
    sum_d1, sum_d2 = fold_add(keep_d1, got_d1, keep_d2, got_d2)
    dzb_one, sums_one = norm_one_back(normal, scale_one, dzb_two, back, back_got, g_one)
    d_ends = attend_back(info, dzb_one, single_w, None, ends)
    keep_f1, send_f1, keep_f2, send_f2 = fold_feed(
        sum_d1, keep_u1, got_u1, sum_d2, keep_u2, got_u2
    )
    got_f1, got_f2 = flip_dp(send_f1, 1), flip_chip(send_f2)
    keep_s, send_s = single_grad(
        info, tok_turned, d_ends, dzb_one, contexts, sums_one, sums_two, Y_MAJOR
    )
    d_other = attend_back(info, dzb_one, single_w, 1, other01)
    grad_b = pair_grad(tok_turned, d_other, len(OWN))
    got_b = flip_chip(grad_b)
    (send_s1,) = join([send_s])
    got_s = flip_dp(send_s1, 1)
    keep_f, send_f = fold_sides(keep_f1, got_f1, keep_f2, got_f2)
    got_f = flip_dp(send_f, 2)
    d_own = attend_back(info, dzb_one, single_w, 0, own01)
    grad_a = pair_grad(tok_turned, d_own, len(OWN))
    keep_a, send_a = fold(grad_a, got_b, 2, 0)
    got_a = flip_dp(send_a, 1)
    keep_s2, send_s2 = fold(keep_s, got_s, 2, TAIL)
    got_s2 = flip_chip(send_s2)
    mine, *sent = input_back(
        info, d_own, d_other, d_ends, dzb_one, ((own_pair, other_pair), (OWN, OTHER)), single_w
    )
    keep_f3, send_f3 = fold(keep_f, got_f, 2, 0)
    got_f3 = flip_dp(send_f3, 4)
    keep_s3, send_s3, keep_a3, send_a3 = fold_last(keep_s2, got_s2, keep_a, got_a)
    got_s3, got_a3 = flip_dp(send_s3, 2), flip_dp(send_a3, 2)
    sent_parts = join([sent[0]], [sent[1]])
    sent_got = flip_cores(sent_parts)
    own_tok, *send_tok = tokens_add(mine, sent_got)
    got_tok = [flip_chip(v) for v in send_tok]
    got_out = flip_chip(send_out)
    keep_z, send_z = fold_z(keep_s3, got_s3, keep_a3, got_a3)
    got_z = flip_dp(send_z, 4)
    grad_tokens = tokens_out(info, own_tok, got_tok)
    output = slots_of(info, own_out, got_out)
    grad_up, grad_down = feed_out(keep_f3, got_f3)
    grads = attend_out((keep_z, got_z), height)
    return (output, grad_tokens, *grads[:4], grad_up, grad_down.T, *grads[4:])


def plain_path(info, tokens, cotangent, weights, lengths, masks, norms):
    w_query, w_key, w_value, w_out, w_up, w_down = weights
    mask_own, mask_other, mask_ends = masks
    g_one, b_one, g_two, b_two = norms
    features, units = tokens.shape[2], w_up.shape[1]
    flat = (((0, 0),),)
    two = (((0, 0),), ((1, 0),))

    def gathered(piece):
        own = lax.all_gather(piece, "dp", axis=0, tiled=True)[None]
        return own, flip_chip(own)

    got_rows = flip_chip(split(info, tokens, cotangent, True))
    own_rows = split(info, tokens, cotangent, False)
    quarters = (own_rows, got_rows, flip_core(own_rows), flip_core(got_rows))
    tok = merge(info, quarters)
    firsts = [w[:, : 2 * HD] for w in (w_query, w_key, w_value)]
    thirds = [w_out.T] + [w[:, 2 * HD :] for w in (w_query, w_key, w_value)]
    pair_w = (gathered(jnp.concatenate(firsts, axis=1)), two)
    single_w = (gathered(jnp.concatenate(thirds, axis=1)), two)
    up, down = (gathered(w_up), two), (gathered(w_down.T), two)
    own01 = attend(info, lengths, tok, ((pair_w[0][0],), flat), True, mask_own[:2])
    other01 = attend(info, lengths, tok, ((pair_w[0][1],), flat), True, mask_other[:2])
    ends = attend(info, lengths, tok, single_w, False, mask_ends)
    contexts = (own01[3], other01[3], ends[3])
    part = project(info, contexts, single_w, features)
    normal, scale_one, hn = norm_one(tok, part, flip_cores(part), g_one, b_one)
    act1, slope1 = feed_up(info, hn, ((up[0][0],), flat), units)
    act2, slope2 = feed_up(info, hn, ((up[0][1],), flat), units)
    tok_turned, hn_turned = turn_rows(info, tok, hn, (0,))
    part = feed_down(info, act1, act2, down, features)
    own_out, send_out, dzb_two, sums_two = norm_two(
        info, lengths, hn, part, flip_cores(part), quarters, g_two, b_two
    )
    places = (((0, 0),), ((1, 0),)) * 2
    grad_d = feed_grad(info, dzb_two, act1, act2, places, False)
    du1, du2, *part = feed_back(info, dzb_two, slope1, slope2, up, down)
    grad_u = feed_grad(info, hn_turned, du1, du2, places, True)
    dzb_one, sums_one = norm_one_back(
        normal, scale_one, dzb_two, part, flip_cores(part), g_one
    )
    d_ends = attend_back(info, dzb_one, single_w, None, ends)
    keep_s, send_s = single_grad(
        info, tok_turned, d_ends, dzb_one, contexts, sums_one, sums_two, (0,)
    )
    d_other = attend_back(info, dzb_one, single_w, 1, other01)
    grad_b = pair_grad(tok_turned, d_other, 1)
    d_own = attend_back(info, dzb_one, single_w, 0, own01)
    grad_a = pair_grad(tok_turned, d_own, 1)
    mine, *sent = input_back(info, d_own, d_other, d_ends, dzb_one, pair_w, single_w)
    own_tok, *send_tok = tokens_add(mine, flip_cores(sent))
    output = slots_of(info, own_out, flip_chip(send_out))
    grad_tokens = tokens_out(info, own_tok, [flip_chip(v) for v in send_tok])

    def summed(own, other):
        total = own.astype(F32) + flip_chip(other).astype(F32)
        return lax.psum_scatter(total, "dp", scatter_dimension=0, tiled=True)

    def wide(keep1, send1, keep2, send2):
        return jnp.concatenate([summed(keep1[0], send1[0]), summed(keep2[0], send2[0])], axis=1)

    single = summed(keep_s[:features], send_s[:features])
    pair = summed(grad_a[0], grad_b[0])
    grads = [
        jnp.concatenate(
            [pair[:, 2 * i * HD : 2 * (i + 1) * HD], single[:, (3 + i) * HD : (4 + i) * HD]],
            axis=1,
        )
        for i in range(3)
    ] + [single[:, : 3 * HD].T]
    sums = decode(keep_s[features:])
    sums = lax.psum(sums + flip_chip(sums), "dp")
    sums = [jnp.concatenate([sums[i], sums[4 + i]]) for i in range(4)]
    return (output, grad_tokens, *grads, wide(*grad_u), wide(*grad_d).T, *sums)


def local(
    tokens,
    w_query,
    w_key,
    w_value,
    w_out,
    w_up,
    w_down,
    gain_attn,
    bias_attn,
    gain_ffn,
    bias_ffn,
    lengths,
    random_blocks,
    cotangent,
):
    ORDER.clear()
    size = lax.axis_size("dp")
    rank = lax.axis_index("mp")
    me = lax.axis_index("dp")
    x, core = rank // 2, rank % 2
    quarter = tokens.shape[1]
    seq = 4 * quarter
    height = w_query.shape[0]
    span = w_query.shape[1]
    heads = span // HD
    nblocks = seq // BLOCK
    fast = size == 8 and height % 16 == 0

    shift = x * (seq // 2)
    info = jnp.stack([me, x, core, shift]).astype(jnp.int32)

    blocks = (jnp.arange(nblocks) + x * (nblocks // 2)) % nblocks
    near_blocks = jnp.abs(blocks[:, None] - blocks[None, :]) <= 1
    edge = (blocks == 0) | (blocks == nblocks - 1)
    fixed = near_blocks | edge[:, None] | edge[None, :]

    def table(shard):
        chosen = lax.dynamic_slice_in_dim(random_blocks, shard * heads, heads, 0)
        chosen = jnp.roll(chosen, -x * (nblocks // 2), axis=1)
        hit = jnp.any(chosen[:, None, :, :] == blocks[None, :, None, None], axis=3)
        bias = jnp.where(fixed.T[None] | hit, 0.0, NEGATIVE)
        return jnp.concatenate(
            [
                jnp.zeros((heads, nblocks, HD), F32),
                bias,
                jnp.full((heads, nblocks, 3), -1.0, F32),
                jnp.zeros((heads, nblocks, HD - 3 - nblocks), F32),
            ],
            axis=2,
        )

    mask_own, mask_other = table(rank), table(rank ^ 2)
    mask_ends = jnp.concatenate([mask_own[2:], mask_other[2:]], axis=0)
    g_one, b_one = gain_attn[None], bias_attn[None]
    g_two, b_two = gain_ffn[None], bias_ffn[None]

    path = fast_path if fast else plain_path
    return path(
        info,
        tokens,
        cotangent,
        (w_query, w_key, w_value, w_out, w_up, w_down),
        lengths,
        (mask_own, mask_other, mask_ends),
        (g_one, b_one, g_two, b_two),
    )


def solution(mesh):
    return jax.shard_map(
        local,
        mesh=mesh,
        in_specs=(
            P("dp", "mp", None),
            P("dp", "mp"),
            P("dp", "mp"),
            P("dp", "mp"),
            P("mp", "dp"),
            P("dp", "mp"),
            P("mp", "dp"),
            P(),
            P(),
            P(),
            P(),
            P("dp"),
            P(),
            P("dp", "mp", None),
        ),
        out_specs=(
            P("dp", "mp", None),
            P("dp", "mp", None),
            P("dp", "mp"),
            P("dp", "mp"),
            P("dp", "mp"),
            P("mp", "dp"),
            P("dp", "mp"),
            P("mp", "dp"),
            P(),
            P(),
            P(),
            P(),
        ),
        check_vma=False,
    )
```

```python
import functools

import jax
import jax.numpy as jnp
from jax import lax
from jax.experimental import pallas as pl
from jax.experimental.pallas import tpu as pltpu
from jax.sharding import PartitionSpec as P

HD = 64
BLOCK = 64
LANES = 128
TILE = 256
KEYS = 512
SENT = 256
EPSILON = 1e-12
TAIL = 32
TOKEN = (8, 128)
ROOM = {
    "attend": 28,
    "attend_back": 32,
    "project": 12,
    "input_back": 24,
    "norm_one": 12,
    "norm_two": 18,
    "norm_one_back": 14,
    "feed_up": 20,
    "feed_down": 20,
    "feed_back": 36,
    "turn_rows": 12,
    "feed_grad": 24,
    "pair_grad": 16,
    "single_grad": 24,
    "join": 1,
    "join_sides": 1,
    "beside": 1,
    "pack": 2,
    "split": 4,
    "merge": 1,
    "fold": 6,
    "fold_add": 8,
    "fold_feed": 10,
    "fold_sides": 8,
    "fold_last": 6,
    "fold_z": 4,
    "slots": 1,
    "tokens_add": 8,
    "tokens_out": 8,
    "feed_out": 6,
    "attend_out": 6,
}
SCALE = 0.125
LOG2E = 1.4426950408889634
LN2 = 0.6931471805599453
NEGATIVE = -1e30
F32 = jnp.float32
BF16 = jnp.bfloat16

CORE_SWAP = [(0, 1), (1, 0), (2, 3), (3, 2)]
CHIP_SWAP = [(0, 2), (2, 0), (1, 3), (3, 1)]


def nn(a, b):
    return lax.dot_general(a, b, (((1,), (0,)), ((), ())), preferred_element_type=F32)


def nt(a, b):
    return lax.dot_general(a, b, (((1,), (1,)), ((), ())), preferred_element_type=F32)


def tn(a, b):
    return lax.dot_general(a, b, (((0,), (0,)), ((), ())), preferred_element_type=F32)


def vmem():
    return pl.BlockSpec(memory_space=pltpu.VMEM)


def smem():
    return pl.BlockSpec(memory_space=pltpu.SMEM)


def anywhere():
    return pl.BlockSpec(memory_space=pl.ANY)


def in_hbm(values):
    return tuple(pltpu.with_memory_space_constraint(v, pltpu.HBM) for v in values)


def array(shape, dtype):
    return jax.ShapeDtypeStruct(shape, dtype)


ORDER = []


def run(kernel, name, args, specs, outs, out_specs, scratch=()):
    given, made = len(args), len(outs)
    extra = tuple(ORDER)

    def body(*refs):
        ins, rest = refs[:given], refs[given + len(extra) :]
        rest[made][...] = jnp.zeros(TOKEN, F32)
        kernel(*ins, *rest[:made], *rest[made + 1 :])

    results = pl.pallas_call(
        body,
        out_shape=tuple(outs) + (array(TOKEN, F32),),
        in_specs=list(specs) + [anywhere()] * len(extra),
        out_specs=tuple(out_specs) + (vmem(),),
        scratch_shapes=list(scratch),
        compiler_params=pltpu.CompilerParams(vmem_limit_bytes=ROOM[name] * 2**20),
        cost_estimate=pl.CostEstimate(flops=1, bytes_accessed=0, transcendentals=0),
        name=name,
    )(*args, *extra)
    ORDER[:] = [results[-1]]
    return results[:-1]


def put_rows(parts, t, value):
    height, tile = parts[0].shape[0], value.shape[0]
    if height <= tile:
        per = tile // height
        for k in range(per):
            parts[t * per + k][...] = value[k * height : (k + 1) * height]
    else:
        per = height // tile
        parts[t // per][pl.ds(t % per * tile, tile), :] = value


def get_sum(parts, more, t):
    height = parts[0].shape[0]
    if height <= TILE:
        per = TILE // height
        at = range(t * per, (t + 1) * per)
        pieces = [parts[k][...].astype(F32) + more[k][...].astype(F32) for k in at]
        return pieces[0] if per == 1 else jnp.concatenate(pieces, axis=0)
    per = height // TILE
    at = pl.ds(t % per * TILE, TILE)
    return parts[t // per][at, :].astype(F32) + more[t // per][at, :].astype(F32)


def tile_rows(ref, tile=TILE):
    return [(t, pl.ds(t * tile, tile)) for t in range(ref.shape[0] // tile)]


def far(shape, dtype):
    return pltpu.HBM(shape, dtype)


def tiles(seq, width, height):
    parts = (array((height, width), BF16),) * (seq // height)
    return parts, [vmem()] * len(parts)


def place(me, refs, slots, dst_ref, first=0, last=None, only=None, to=0):
    for ref, of in zip(refs, slots):
        height, width = ref.shape[1], ref.shape[2]
        end = width if last is None else last
        for e, (chip, j) in enumerate(of):
            if only is not None and chip != only:
                continue
            at = 0 if height == dst_ref.shape[0] else pl.multiple_of((me ^ j) * height, height)
            at_column = to + (0 if only is not None else chip * (end - first))
            dst_ref[pl.ds(at, height), pl.ds(at_column, end - first)] = ref[e, :, first:end]


def pick(me, fulls, out_ref, slots, first):
    _, height, width = out_ref.shape
    for e, (chip, j) in enumerate(slots):
        full = fulls[chip]
        at = 0 if height == full.shape[0] else pl.multiple_of((me ^ j) * height, height)
        out_ref[e] = full[pl.ds(at, height), pl.ds(first, width)]


def attend_kernel(slots, columns, only, places, info, lengths, tok, mask, *rest):
    refs, (qa, ka, va, ctx, wfull) = rest[: len(slots)], rest[len(slots) :]
    seq = tok.shape[0]
    place(info[0], refs, slots, wfull, *columns, only)
    lane = lax.broadcasted_iota(jnp.int32, (TILE, LANES), 1)
    row0 = lax.broadcasted_iota(jnp.int32, (TILE, LANES), 0)
    for t in range(seq // TILE):
        at = pl.ds(t * TILE, TILE)
        row = row0 + t * TILE
        made = nn(tok[at, :], wfull[...])
        onehot = jnp.where(lane - HD == row // BLOCK, 1.0, 0.0)[:, HD:]
        position = row + info[3]
        position = jnp.where(position >= seq, position - seq, position)
        dead = (position >= lengths[info[1]]) & (lane >= HD) & (lane < HD + 16)
        for h, (q_at, k_at, v_at) in enumerate(places):
            q = made[:, q_at : q_at + HD] * (SCALE * LOG2E)
            k = made[:, k_at : k_at + HD]
            v = made[:, v_at : v_at + HD]
            qa[h, at, :] = jnp.concatenate([q, onehot], axis=1).astype(BF16)
            per = TILE // BLOCK
            table = jnp.concatenate(
                [
                    jnp.broadcast_to(mask[h, t * per + b : t * per + b + 1, :], (BLOCK, LANES))
                    for b in range(per)
                ],
                axis=0,
            )
            table = jnp.where(dead, NEGATIVE, table)
            ka[h, at, :] = jnp.concatenate([k, table[:, HD:]], axis=1).astype(BF16)
            va[h, at, :] = jnp.concatenate([v, jnp.full((TILE, HD), -1.0, F32)], axis=1).astype(BF16)
    lane = lax.broadcasted_iota(jnp.int32, (2 * TILE, LANES), 1)
    for t in range(seq // TILE // 2):
        at = pl.ds(t * 2 * TILE, 2 * TILE)
        pieces = []
        for h in range(len(places)):
            q = qa[h, at, :]
            s = nt(q, ka[h])
            top = jnp.max(s, axis=1, keepdims=True)
            p = jnp.exp2(s - top).astype(BF16)
            got = nn(p, va[h])
            total = -got[:, HD:]
            pieces.append(got[:, :HD] / total)
            log = top + jnp.log2(-got)
            hi = log.astype(BF16).astype(F32)
            mid = (log - hi).astype(BF16).astype(F32)
            low = log - hi - mid
            new = jnp.where(
                lane == HD + 16,
                hi,
                jnp.where(lane == HD + 17, mid, jnp.where(lane == HD + 18, low, q.astype(F32))),
            )
            qa[h, at, :] = new.astype(BF16)
        ctx[at, :] = jnp.concatenate(pieces, axis=1).astype(BF16)


PAIR = ((0, 2 * HD, 4 * HD), (HD, 3 * HD, 5 * HD))
SINGLES = ((HD, 2 * HD, 3 * HD), (5 * HD, 6 * HD, 7 * HD))


def attend(info, lengths, tok, gathered, pair, mask):
    arrays, slots = gathered
    seq, width = tok.shape
    aug = far((2, seq, LANES), BF16)
    columns, only, cols = ((0, 6 * HD), 0, 6 * HD) if pair else ((2 * HD, 6 * HD), None, 8 * HD)
    return run(
        functools.partial(attend_kernel, slots, columns, only, PAIR if pair else SINGLES),
        "attend",
        (info, lengths, tok, mask) + arrays,
        [smem()] * 2 + [vmem()] * (2 + len(arrays)),
        (aug, aug, aug, array((seq, LANES), BF16)),
        [vmem()] * 4,
        [pltpu.VMEM((width, cols), BF16)],
    )


def place_out(me, refs, slots, pairs, ends):
    place(me, refs, slots, pairs, 0, 2 * HD)
    place(me, refs, slots, ends, 2 * HD, 4 * HD)
    both = ends[...]
    ends[:, :LANES] = jnp.concatenate([both[:, :HD], both[:, LANES : LANES + HD]], axis=1)


def project_kernel(slots, info, own, other, ends, *rest):
    refs, parts, (w1, w2) = rest[: len(slots)], rest[len(slots) : -2], rest[-2:]
    place_out(info[0], refs, slots, w1, w2)
    for t, at in tile_rows(own, 2 * TILE):
        both = jnp.concatenate([own[at, :], other[at, :]], axis=1)
        out = nt(both, w1[...]) + nt(ends[at, :], w2[:, :LANES])
        put_rows(parts, t, out.astype(BF16))


def project(info, contexts, gathered, width):
    arrays, slots = gathered
    seq = contexts[0].shape[0]
    return run(
        functools.partial(project_kernel, slots),
        "project",
        (info,) + contexts + arrays,
        [smem()] + [vmem()] * (3 + len(arrays)),
        *tiles(seq, width, 2 * TILE),
        [pltpu.VMEM((width, 2 * LANES), BF16)] * 2,
    )


def attend_back_kernel(slots, chip, info, dz, qa, ka, va, ctx, *rest):
    refs, (dqkv, pairs, ends, da) = rest[: len(slots)], rest[len(slots) :]
    seq = dz.shape[0]
    heads = qa.shape[0]
    if chip is None:
        place_out(info[0], refs, slots, pairs, ends)
        wfull = ends.at[:, pl.ds(0, LANES)]
    else:
        place(info[0], refs, slots, pairs, 0, 2 * HD, chip)
        wfull = pairs.at[:, pl.ds(0, LANES)]
    lane = lax.broadcasted_iota(jnp.int32, (TILE, LANES), 1)
    for t in range(seq // TILE):
        at = pl.ds(t * TILE, TILE)
        dctx = nn(dz[at, :], wfull[...]).astype(BF16).astype(F32)
        both = dctx * ctx[at, :].astype(F32)
        for h in range(heads):
            inner = jnp.sum(both[:, h * HD : (h + 1) * HD], axis=1, keepdims=True)
            hi = inner.astype(BF16).astype(F32)
            mid = (inner - hi).astype(BF16).astype(F32)
            low = inner - hi - mid
            one = jnp.concatenate(
                [dctx[:, h * HD : (h + 1) * HD], jnp.zeros((TILE, HD), F32)], axis=1
            )
            one = jnp.where(lane == HD, hi, one)
            one = jnp.where(lane == HD + 1, mid, one)
            one = jnp.where(lane == HD + 2, low, one)
            da[h, at, :] = one.astype(BF16)

    def turned(values):
        return jnp.transpose(values.astype(F32))[:HD].astype(BF16)

    grads = []
    for h in range(heads):
        k_turned, q_turned, d_turned = turned(ka[h]), turned(qa[h]), turned(da[h])
        dq, dk, dv = None, [], []
        for t in range(seq // KEYS):
            at = pl.ds(t * KEYS, KEYS)
            p = jnp.exp2(nt(ka[h, at, :], qa[h]))
            ds = (p * nt(va[h, at, :], da[h])).astype(BF16)
            dv.append(nt(d_turned, p.astype(BF16)))
            dk.append(nt(q_turned, ds))
            more = nn(k_turned[:, t * KEYS : (t + 1) * KEYS], ds)
            dq = more if dq is None else dq + more
        dk = jnp.concatenate(dk, axis=1) * LN2
        grads.append((dq * SCALE, dk, jnp.concatenate(dv, axis=1)))
    (dq0, dk0, dv0), (dq1, dk1, dv1) = grads
    if chip is None:
        blank = jnp.zeros_like(dq0)
        stacks = ((blank, dq0), (dk0, dv0), (blank, dq1), (dk1, dv1))
    else:
        stacks = ((dq0, dq1), (dk0, dk1), (dv0, dv1))
    for i, stack in enumerate(stacks):
        both = jnp.transpose(jnp.concatenate(stack, axis=0))
        dqkv[:, i * LANES : (i + 1) * LANES] = both.astype(BF16)


def attend_back(info, dz, gathered, chip, saved):
    arrays, slots = gathered
    qa, ka, va, ctx = saved
    seq, width = dz.shape
    cols = 8 * HD if chip is None else 6 * HD
    return run(
        functools.partial(attend_back_kernel, slots, chip),
        "attend_back",
        (info, dz, qa, ka, va, ctx) + arrays,
        [smem()] + [vmem()] * (5 + len(arrays)),
        (array((seq, cols), BF16),),
        [vmem()],
        [
            pltpu.VMEM((width, 2 * LANES), BF16),
            pltpu.VMEM((width, 2 * LANES), BF16),
            pltpu.VMEM((2, seq, LANES), BF16),
        ],
    )[0]


def input_back_kernel(slots1, slots2, info, own, other, ends, dz, *rest):
    n1, n2 = len(slots1), len(slots2)
    refs1, refs2, (mine, *sent, w1, w2) = rest[:n1], rest[n1 : n1 + n2], rest[n1 + n2 :]
    place(info[0], refs1, slots1, w1)
    place(info[0], refs2, slots2, w2, 2 * HD, 6 * HD)
    per = len(sent) // 2
    height = sent[0].shape[0]
    for half in range(dz.shape[0] // TILE // 2):
        for whose in range(2):
            tile = 2 * half + (info[2] if whose == 0 else 1 - info[2])
            at = pl.ds(pl.multiple_of(tile * TILE, TILE), TILE)
            pairs = jnp.concatenate([own[at, :], other[at, :]], axis=1)
            back = nt(pairs, w1[...]) + nt(ends[at, :], w2[...])
            if whose == 0:
                mine[half] = back + dz[at, :].astype(F32)
                continue
            for k in range(per):
                part = back[k * height : (k + 1) * height]
                sent[half * per + k][...] = part.astype(BF16)


def input_back(info, own, other, ends, dz, gathered1, gathered2):
    seq, width = dz.shape
    arrays = gathered1[0] + gathered2[0]
    halves = (seq // TILE // 2, TILE, width)
    grads = (own, other, ends, dz)
    return run(
        functools.partial(input_back_kernel, gathered1[1], gathered2[1]),
        "input_back",
        (info,) + grads + arrays,
        [smem()] + [vmem()] * (len(grads) + len(arrays)),
        (array(halves, F32),) + (array((SENT, width), BF16),) * (seq // 2 // SENT),
        [vmem()] * (1 + seq // 2 // SENT),
        [pltpu.VMEM((width, 12 * HD), BF16), pltpu.VMEM((width, 8 * HD), BF16)],
    )


def center(z):
    mean = jnp.mean(z, axis=1, keepdims=True)
    moved = z - mean
    spread = jnp.mean(moved * moved, axis=1, keepdims=True)
    scale = lax.rsqrt(spread + EPSILON)
    return moved * scale, scale


def norm_back(n, scale, gy, gain):
    dn = gy * gain
    return scale * (
        dn - jnp.mean(dn, axis=1, keepdims=True) - n * jnp.mean(dn * n, axis=1, keepdims=True)
    )


def add_sums(gy, n, sums):
    more = [jnp.sum(v, axis=0, keepdims=True) for v in (gy * n, gy)]
    return more if sums is None else [a + b for a, b in zip(sums, more)]


def norm_one_kernel(tok, gain, bias, *rest):
    *parts, normal, scale, hn = rest
    count = len(parts) // 2
    for t, at in tile_rows(tok):
        value = tok[at, :].astype(F32) + get_sum(parts[:count], parts[count:], t)
        n, r = center(value)
        normal[at, :] = n.astype(BF16)
        scale[at, :] = r
        hn[at, :] = (n * gain[...] + bias[...]).astype(BF16)


def norm_one(tok, p0, p1, gain, bias):
    seq, width = tok.shape
    return run(
        norm_one_kernel,
        "norm_one",
        (tok, gain, bias, *p0, *p1),
        [vmem()] * (3 + len(p0) + len(p1)),
        (array((seq, width), BF16), array((seq, 1), F32), array((seq, width), BF16)),
        [vmem()] * 3,
    )


def norm_two_kernel(info, lengths, hn, own, got, core_own, core_got, gain, bias, *rest):
    *parts, own_out, send_out, dzb, sums, out = rest
    count = len(parts) // 2
    seq = hn.shape[0]
    total = None
    for t, at in tile_rows(hn):
        value = hn[at, :].astype(F32) + get_sum(parts[:count], parts[count:], t)
        n, scale = center(value)
        out[at, :] = (n * gain[...] + bias[...]).astype(BF16)
        position = lax.broadcasted_iota(jnp.int32, (TILE, 1), 0) + t * TILE + info[3]
        position = jnp.where(position >= seq, position - seq, position)
        valid = jnp.where(position < lengths[info[1]], 1.0, 0.0)
        mine, others = ((own, core_own), (got, core_got))[t // 2]
        cot = jnp.where(info[2] == t % 2, mine[1].astype(F32), others[1].astype(F32))
        gy = cot * valid
        dzb[at, :] = norm_back(n, scale, gy, gain[...]).astype(BF16)
        total = add_sums(gy, n, total)
    sums[...] = jnp.concatenate(total, axis=0)
    for half, ref in enumerate((own_out, send_out)):
        at = pl.multiple_of((2 * half + info[2]) * TILE, TILE)
        ref[...] = out[pl.ds(at, TILE), :]


def norm_two(info, lengths, hn, m0, m1, cot, gain, bias):
    seq, width = hn.shape
    return run(
        norm_two_kernel,
        "norm_two",
        (info, lengths, hn, *cot, gain, bias, *m0, *m1),
        [smem()] * 2 + [vmem()] * (3 + len(cot) + len(m0) + len(m1)),
        (
            array((TILE, width), BF16),
            array((TILE, width), BF16),
            array((seq, width), BF16),
            array((2, width), F32),
        ),
        [vmem()] * 4,
        [pltpu.VMEM((seq, width), BF16)],
    )


def norm_one_back_kernel(normal, scale, dz2, gain, *rest):
    *parts, dzb, sums = rest
    count = len(parts) // 2
    total = None
    for t, at in tile_rows(dz2):
        n = normal[at, :].astype(F32)
        gy = dz2[at, :].astype(F32) + get_sum(parts[:count], parts[count:], t)
        dzb[at, :] = norm_back(n, scale[at, :], gy, gain[...]).astype(BF16)
        total = add_sums(gy, n, total)
    sums[...] = jnp.concatenate(total, axis=0)


def norm_one_back(normal, scale, dz2, p0, p1, gain):
    seq, width = normal.shape
    return run(
        norm_one_back_kernel,
        "norm_one_back",
        (normal, scale, dz2, gain, *p0, *p1),
        [vmem()] * (4 + len(p0) + len(p1)),
        (array((seq, width), BF16), array((2, width), F32)),
        [vmem()] * 2,
    )


def gelu_pair(u):
    phi = 0.5 + 0.5 * lax.erf(u * 0.7071067811865476)
    return u * phi, phi + u * (jnp.exp(-0.5 * u * u) * 0.3989422804014327)


def feed_up_kernel(slots, info, hn, *rest):
    refs, (active, slope, wfull) = rest[: len(slots)], rest[len(slots) :]
    place(info[0], refs, slots, wfull)
    for _, at in tile_rows(hn, 2 * TILE):
        a, g = gelu_pair(nn(hn[at, :], wfull[...]))
        active[at, :] = a.astype(BF16)
        slope[at, :] = g.astype(BF16)


def feed_up(info, hn, gathered, units):
    arrays, slots = gathered
    seq, width = hn.shape
    return run(
        functools.partial(feed_up_kernel, slots),
        "feed_up",
        (info, hn) + arrays,
        [smem()] + [vmem()] * (1 + len(arrays)),
        (array((seq, units), BF16), array((seq, units), BF16)),
        [vmem()] * 2,
        [pltpu.VMEM((width, units), BF16)],
    )


def feed_down_kernel(slots, info, act1, act2, *rest):
    refs, parts, wfull = rest[: len(slots)], rest[len(slots) : -1], rest[-1]
    place(info[0], refs, slots, wfull)
    for t, at in tile_rows(act1, 2 * TILE):
        both = jnp.concatenate([act1[at, :], act2[at, :]], axis=1)
        put_rows(parts, t, nt(both, wfull[...]).astype(BF16))


def feed_down(info, act1, act2, gathered, width):
    seq, units = act1.shape
    arrays, slots = gathered
    return run(
        functools.partial(feed_down_kernel, slots),
        "feed_down",
        (info, act1, act2) + arrays,
        [smem()] + [vmem()] * (2 + len(arrays)),
        *tiles(seq, width, seq),
        [pltpu.VMEM((width, 2 * units), BF16)],
    )


def feed_back_kernel(slots_up, slots_down, info, dzb, slope1, slope2, *rest):
    n1, n2 = len(slots_up), len(slots_down)
    ups, downs, (du1, du2, *parts, up, down) = rest[:n1], rest[n1 : n1 + n2], rest[n1 + n2 :]
    place(info[0], ups, slots_up, up)
    place(info[0], downs, slots_down, down)
    units = du1.shape[1]
    for t, at in tile_rows(dzb, 2 * TILE):
        out = None
        for i, (slope, du) in enumerate(((slope1, du1), (slope2, du2))):
            cols = pl.ds(i * units, units)
            grad = (nn(dzb[at, :], down[:, cols]) * slope[at, :].astype(F32)).astype(BF16)
            du[at, :] = grad
            more = nt(grad, up[:, cols])
            out = more if out is None else out + more
        put_rows(parts, t, out.astype(BF16))


def feed_back(info, dzb, slope1, slope2, up, down):
    seq, width = dzb.shape
    units = slope1.shape[1]
    arrays = up[0] + down[0]
    parts, part_specs = tiles(seq, width, TILE)
    return run(
        functools.partial(feed_back_kernel, up[1], down[1]),
        "feed_back",
        (info, dzb, slope1, slope2) + arrays,
        [smem()] + [vmem()] * (3 + len(arrays)),
        (array((seq, units), BF16),) * 2 + parts,
        [vmem()] * 2 + part_specs,
        [pltpu.VMEM((width, 2 * units), BF16)] * 2,
    )


def turn_rows_kernel(order, info, first, second, out1, out2, full):
    count = len(order)
    height = full.shape[0] // count
    for values, out in ((first, out1), (second, out2)):
        for t, at in tile_rows(values):
            full[:, t * TILE : (t + 1) * TILE] = jnp.transpose(values[at, :])
        for e, j in enumerate(order):
            at = 0 if count == 1 else pl.multiple_of((info[0] ^ j) * height, height)
            out[pl.ds(e * height, height), :] = full[pl.ds(at, height), :]


def turn_rows(info, first, second, order):
    shape = first.shape[::-1]
    out = array(shape, BF16)
    return run(
        functools.partial(turn_rows_kernel, order),
        "turn_rows",
        (info, first, second),
        [smem()] + [vmem()] * 2,
        (out, out),
        [vmem()] * 2,
        [pltpu.VMEM(shape, BF16)],
    )


def feed_grad_kernel(turned, places, info, a, d1, d2, *rest):
    outs, full = rest[:4], rest[4]
    half = outs[0].shape[2]
    product = nn if turned else tn
    made = product(a[...], jnp.concatenate([d1[...], d2[...]], axis=1)).astype(BF16)
    if turned:
        height = outs[0].shape[1]
        order = [j for chip, j in places[0] if chip == 0]
        for i, out in enumerate(outs):
            for e, (chip, j) in enumerate(places[i]):
                row = order.index(j) * height
                first = 2 * chip * half + (i // 2) * half
                out[e] = made[row : row + height, first : first + half]
        return
    full[...] = made
    fulls = [full.at[:, pl.ds(2 * chip * half, 2 * half)] for chip in range(2)]
    for i, out in enumerate(outs):
        pick(info[0], fulls, out, places[i], (i // 2) * half)


def feed_grad(info, a, d1, d2, places, turned):
    seq, units = d1.shape
    width = a.shape[0] if turned else a.shape[1]
    count = len(places[0])
    out = array((count, width // count, units // 2), BF16)
    return run(
        functools.partial(feed_grad_kernel, turned, places),
        "feed_grad",
        (info, a, d1, d2),
        [smem()] + [vmem()] * 3,
        (out,) * 4,
        [vmem()] * 4,
        [pltpu.VMEM((width, 2 * units), BF16)],
    )


def pair_grad_kernel(tok_turned, d, out):
    made = nn(tok_turned[...], d[...]).astype(BF16)
    height = out.shape[1]
    for e in range(out.shape[0]):
        out[e] = made[e * height : (e + 1) * height]


def pair_grad(tok_turned, d, count):
    width = tok_turned.shape[0]
    cols = d.shape[1]
    return run(
        pair_grad_kernel,
        "pair_grad",
        (tok_turned, d),
        [vmem()] * 2,
        (array((count, width // count, cols), BF16),),
        [vmem()],
    )[0]


def encode(sums):
    hi = sums.astype(BF16).astype(F32)
    mid = (sums - hi).astype(BF16).astype(F32)
    low = sums - hi - mid
    return jnp.concatenate([hi, mid, low, jnp.zeros_like(low)], axis=0).astype(BF16)


def decode(coded):
    values = coded.astype(F32)
    n = values.shape[0] // 4
    return values[:n] + values[n : 2 * n] + values[2 * n : 3 * n]


def single_grad_kernel(
    order, info, tok_turned, d, dz, own, other, ends, sums_one, sums_two, keep, send, full
):
    mine = nn(tok_turned[...], d[...])
    full[...] = tn(dz[...], jnp.concatenate([ends[...], own[...], other[...]], axis=1))
    count = len(order)
    height = full.shape[0] // count
    width = keep.shape[1]
    blank = jnp.zeros((height, HD), F32)
    both = jnp.concatenate([sums_one[...], sums_two[...]], axis=0)
    both = encode(jnp.concatenate([both[:, :width], both[:, width:]], axis=0))
    half = max(1, count // 2)
    for e, j in enumerate(order):
        at = 0 if count == 1 else pl.multiple_of((info[0] ^ j) * height, height)
        heads = full[pl.ds(at, height), :]
        rows_in = mine[e * height : (e + 1) * height]
        for chip in range(2):
            first = chip * 4 * HD
            third = jnp.concatenate([heads[:, chip * HD : (chip + 1) * HD], blank], axis=1)
            made = [
                heads[:, (chip + 1) * LANES : (chip + 2) * LANES],
                third + rows_in[:, first : first + LANES],
                rows_in[:, first + LANES : first + 2 * LANES],
            ]
            if count == 1:
                out, row = (keep, send)[chip], 0
            else:
                out, row = (keep, send)[e // half], (chip * half + e % half) * height
            out[pl.ds(row, height), :] = jnp.concatenate(made, axis=1).astype(BF16)
    for out in (keep, send):
        out[pl.ds(out.shape[0] - TAIL, TAIL), :] = both


def single_grad(info, tok_turned, d, dz, contexts, sums_one, sums_two, order):
    width = tok_turned.shape[0]
    cols = 6 * HD
    out = array((width + TAIL, cols), BF16)
    return run(
        functools.partial(single_grad_kernel, order),
        "single_grad",
        (info, tok_turned, d, dz, *contexts, sums_one, sums_two),
        [smem()] + [vmem()] * 8,
        (out, out),
        [vmem()] * 2,
        [pltpu.VMEM((width, 3 * LANES), F32)],
    )


def across(values, axis, pairs):
    return lax.ppermute(values, axis, pairs)


def flip_chip(values):
    return across(values, "mp", CHIP_SWAP)


def flip_core(values):
    return across(values, "mp", CORE_SWAP)


def flip_cores(parts):
    return [flip_core(p) for p in parts]


def flip_dp(values, distance):
    size = lax.axis_size("dp")
    return across(values, "dp", [(i, i ^ distance) for i in range(size)])


def join_kernel(groups, *refs):
    count = sum(groups)
    parts, outs, sems = refs[:count], refs[count:-1], refs[-1]
    copies = []
    for out, number in zip(outs, groups):
        first = 0
        for part in parts[len(copies) : len(copies) + number]:
            to = out.at[pl.ds(first, part.shape[0])]
            copies.append(pltpu.make_async_copy(part, to, sems.at[len(copies)]))
            first += part.shape[0]
    for copy in copies:
        copy.start()
    for copy in copies:
        copy.wait()


def join(*groups):
    parts = sum((tuple(g) for g in groups), ())
    outs = [array((sum(p.shape[0] for p in g),) + g[0].shape[1:], g[0].dtype) for g in groups]
    return run(
        functools.partial(join_kernel, tuple(len(g) for g in groups)),
        "join",
        parts,
        [anywhere()] * len(parts),
        outs,
        [anywhere()] * len(outs),
        [pltpu.SemaphoreType.DMA((len(parts),))],
    )


def pack_kernel(w_query, w_key, w_value, w_out, out, rows_in, out_in, sems):
    copies = [
        pltpu.make_async_copy(w, rows_in.at[i], sems.at[i])
        for i, w in enumerate((w_query, w_key, w_value))
    ]
    copies.append(pltpu.make_async_copy(w_out, out_in, sems.at[3]))
    for copy in copies:
        copy.start()
    for copy in copies:
        copy.wait()
    for i in range(3):
        out[0, :, 2 * i * HD : 2 * (i + 1) * HD] = rows_in[i, :, : 2 * HD]
    parts = [jnp.transpose(out_in[...].astype(F32))]
    parts += [rows_in[i, :, 2 * HD :].astype(F32) for i in range(3)]
    out[0, :, 6 * HD :] = jnp.concatenate(parts, axis=1).astype(BF16)


def pack(w_query, w_key, w_value, w_out):
    height, span = w_query.shape
    return run(
        pack_kernel,
        "pack",
        in_hbm((w_query, w_key, w_value, w_out)),
        [anywhere()] * 4,
        (array((1, height, 4 * span), BF16),),
        [vmem()],
        [
            pltpu.VMEM((3, height, span), BF16),
            pltpu.VMEM(w_out.shape, BF16),
            pltpu.SemaphoreType.DMA((4,)),
        ],
    )[0]


def beside_kernel(first, second, out, sems):
    width = first.shape[1]
    copies = [
        pltpu.make_async_copy(ref, out.at[0, :, pl.ds(i * width, width)], sems.at[i])
        for i, ref in enumerate((first, second))
    ]
    for copy in copies:
        copy.start()
    for copy in copies:
        copy.wait()


def beside(first, second):
    height, width = first.shape
    return run(
        beside_kernel,
        "beside",
        in_hbm((first, second)),
        [anywhere()] * 2,
        (array((1, height, 2 * width), BF16),),
        [anywhere()],
        [pltpu.SemaphoreType.DMA((2,))],
    )[0]


def join_sides_kernel(count, *refs):
    parts, outs, sems = refs[:count], refs[count : count + 2], refs[count + 2]
    width = outs[0].shape[2]
    copies = []
    each = parts[0].shape[0]
    for i, part in enumerate(parts):
        for side, out in enumerate(outs):
            copies.append(
                pltpu.make_async_copy(
                    part.at[:, :, pl.ds(side * width, width)],
                    out.at[pl.ds(i * each, each)],
                    sems.at[2 * i + side],
                )
            )
    for copy in copies:
        copy.start()
    for copy in copies:
        copy.wait()


def join_sides(parts):
    count = len(parts)
    each, height, width = parts[0].shape
    out = array((count * each, height, width // 2), BF16)
    return run(
        functools.partial(join_sides_kernel, count),
        "join_sides",
        tuple(parts),
        [anywhere()] * count,
        (out, out),
        [anywhere()] * 2,
        [pltpu.SemaphoreType.DMA((2 * count,))],
    )


def fold_kernel(tail, own, got, *outs):
    body = own.shape[0] - tail
    each = body // len(outs)
    for i, out in enumerate(outs):
        at = pl.ds(i * each, each)
        total = (own[at].astype(F32) + got[at].astype(F32)).astype(BF16)
        if tail:
            out[:each] = total
        else:
            out[...] = total
    if tail:
        coded = encode(decode(own[body:]) + decode(got[body:]))
        for out in outs:
            out[each:] = coded


def fold(own, got, parts, tail=0):
    shape = ((own.shape[0] - tail) // parts + tail,) + own.shape[1:]
    return run(
        functools.partial(fold_kernel, tail),
        "fold",
        (own, got),
        [vmem()] * 2,
        (array(shape, BF16),) * parts,
        [vmem()] * parts,
    )


def fold_last_kernel(own1, got1, own2, got2, keep1, send1, keep2, send2):
    height = own2.shape[1]
    each = height + TAIL
    body = own1.shape[0] - TAIL
    coded = encode(decode(own1[body:]) + decode(got1[body:]))
    half = own2.shape[0] // 2
    for i in range(2 * half):
        out, first = (keep1, send1)[i // half], i % half * each
        at = pl.ds(i * height, height)
        out[first : first + height] = (own1[at].astype(F32) + got1[at].astype(F32)).astype(BF16)
        out[first + height : first + each] = coded
        total = own2[i].astype(F32) + got2[i].astype(F32)
        (keep2, send2)[i // half][i % half] = total.astype(BF16)


def fold_last(own1, got1, own2, got2):
    count, height, width = own2.shape
    first = array((count // 2 * (height + TAIL), width), BF16)
    second = array((count // 2, height, width), BF16)
    return run(
        fold_last_kernel,
        "fold_last",
        (own1, got1, own2, got2),
        [vmem()] * 4,
        (first, first, second, second),
        [vmem()] * 4,
    )


def fold_z_kernel(own1, got1, own2, got2, keep, send):
    height = own2.shape[1]
    each = height + TAIL
    for i, out in enumerate((keep, send)):
        at = pl.ds(i * each, height)
        out[:height] = (own1[at].astype(F32) + got1[at].astype(F32)).astype(BF16)
        at = pl.ds(i * each + height, TAIL)
        out[height:each] = encode(decode(own1[at]) + decode(got1[at]))
        out[each:] = (own2[i].astype(F32) + got2[i].astype(F32)).astype(BF16)


def fold_z(own1, got1, own2, got2):
    _, height, width = own2.shape
    out = array((2 * height + TAIL, width), BF16)
    return run(
        fold_z_kernel,
        "fold_z",
        (own1, got1, own2, got2),
        [vmem()] * 4,
        (out, out),
        [vmem()] * 2,
    )


def fold_add_kernel(own1, got1, own2, got2, out1, out2):
    for own, got, out in ((own1, got1, out1), (own2, got2, out2)):
        out[...] = (own[...].astype(F32) + got[...].astype(F32)).astype(BF16)


def fold_add(own1, got1, own2, got2):
    out = array(own1.shape, BF16)
    return run(
        fold_add_kernel,
        "fold_add",
        (own1, got1, own2, got2),
        [vmem()] * 4,
        (out, out),
        [vmem()] * 2,
    )


def fold_feed_kernel(first1, own1, got1, first2, own2, got2, keep1, send1, keep2, send2):
    width = own1.shape[2]
    half = keep1.shape[0]
    for first, own, got, outs in (
        (first1, own1, got1, (keep1, send1)),
        (first2, own2, got2, (keep2, send2)),
    ):
        for i, out in enumerate(outs):
            at = pl.ds(i * half, half)
            out[:, :, :width] = first[at]
            out[:, :, width:] = (own[at].astype(F32) + got[at].astype(F32)).astype(BF16)


def fold_feed(first1, own1, got1, first2, own2, got2):
    count, height, width = own1.shape
    out = array((count // 2, height, 2 * width), BF16)
    return run(
        fold_feed_kernel,
        "fold_feed",
        (first1, own1, got1, first2, own2, got2),
        [vmem()] * 6,
        (out,) * 4,
        [vmem()] * 4,
    )


def fold_sides_kernel(own1, got1, own2, got2, keep, send):
    width = own1.shape[2]
    half = keep.shape[0]
    for side, (own, got) in enumerate(((own1, got1), (own2, got2))):
        for i, out in enumerate((keep, send)):
            at = pl.ds(i * half, half)
            total = own[at].astype(F32) + got[at].astype(F32)
            out[:, :, side * width : (side + 1) * width] = total.astype(BF16)


def fold_sides(own1, got1, own2, got2):
    count, height, width = own1.shape
    out = array((count // 2, height, 2 * width), BF16)
    return run(
        fold_sides_kernel,
        "fold_sides",
        (own1, got1, own2, got2),
        [vmem()] * 4,
        (out, out),
        [vmem()] * 2,
    )


BY_Z = (0, 4, 2, 6)
Y_MAJOR = BY_Z + tuple(z + 1 for z in BY_Z)
OWN = tuple((0, j) for j in Y_MAJOR)
OTHER = tuple((1, j) for j in Y_MAJOR)
CHIP_NEAR = tuple((chip, z) for chip in range(2) for z in BY_Z)
CHIP_FAR = tuple((chip, z + 1) for chip in range(2) for z in BY_Z)


def split_kernel(other, info, first, second, out, sems):
    slot = 1 - info[1] if other else info[1]
    half = first.shape[1] // 2
    copies = []
    for i, values in enumerate((first, second)):
        for j in range(2):
            at = pl.ds(j * half, half)
            copies.append(
                pltpu.make_async_copy(values.at[slot, at], out.at[i, at], sems.at[2 * i + j])
            )
    for copy in copies:
        copy.start()
    for copy in copies:
        copy.wait()


def split(info, first, second, other):
    return run(
        functools.partial(split_kernel, other),
        "split",
        (info, *in_hbm((first, second))),
        [smem()] + [anywhere()] * 2,
        (array((2,) + first.shape[1:], first.dtype),),
        [vmem()],
        [pltpu.SemaphoreType.DMA((4,))],
    )[0]


def merge_kernel(info, own, got, core_own, core_got, out, sems):
    core = info[2]
    copies = []
    for half, (mine, other) in enumerate(((own, core_own), (got, core_got))):
        copies += [
            pltpu.make_async_copy(mine.at[0], out.at[half, core], sems.at[2 * half]),
            pltpu.make_async_copy(other.at[0], out.at[half, 1 - core], sems.at[2 * half + 1]),
        ]
    for copy in copies:
        copy.start()
    for copy in copies:
        copy.wait()


def merge(info, quarters):
    _, quarter, width = quarters[0].shape
    out = run(
        merge_kernel,
        "merge",
        (info, *quarters),
        [smem()] + [anywhere()] * 4,
        (array((2, 2, quarter, width), quarters[0].dtype),),
        [anywhere()],
        [pltpu.SemaphoreType.DMA((4,))],
    )[0]
    return out.reshape(4 * quarter, width)


def slots_kernel(info, own, other, out, sems):
    copies = [
        pltpu.make_async_copy(own, out.at[info[1]], sems.at[0]),
        pltpu.make_async_copy(other, out.at[1 - info[1]], sems.at[1]),
    ]
    for copy in copies:
        copy.start()
    for copy in copies:
        copy.wait()


def slots_of(info, own, other):
    return run(
        slots_kernel,
        "slots",
        (info, own, other),
        [smem()] + [anywhere()] * 2,
        (array((2,) + own.shape, own.dtype),),
        [anywhere()],
        [pltpu.SemaphoreType.DMA((2,))],
    )[0]


def tokens_add_kernel(count, mine, *rest):
    got, own, sends = rest[:count], rest[count], rest[count + 1 :]
    per = count // 2
    height = got[0].shape[0]
    for k, part in enumerate(got):
        at = k % per * height
        total = mine[k // per, pl.ds(at, height)] + part[...].astype(F32)
        if k < per:
            own[pl.ds(at, height)] = total
        else:
            each = sends[0].shape[0]
            for first in range(0, height, each):
                sends[(at + first) // each][...] = total[first : first + each].astype(BF16)


def tokens_add(mine, got):
    _, quarter, width = mine.shape
    send = array((quarter // 2, width), BF16)
    return run(
        functools.partial(tokens_add_kernel, len(got)),
        "tokens_add",
        (mine, *got),
        [vmem()] * (1 + len(got)),
        (array((quarter, width), F32), send, send),
        [vmem()] * 3,
    )


def tokens_out_kernel(info, own, *rest):
    *got, out = rest
    out[info[1]] = own[...]
    height = got[0].shape[0]
    for k, part in enumerate(got):
        out[1 - info[1], pl.ds(k * height, height), :] = part[...].astype(F32)


def tokens_out(info, own, got):
    return run(
        tokens_out_kernel,
        "tokens_out",
        (info, own, *got),
        [smem()] + [vmem()] * (1 + len(got)),
        (array((2,) + own.shape, F32),),
        [vmem()],
    )[0]


def feed_out_kernel(own, got, up, down):
    half = up.shape[1] // 2
    for i in range(4):
        at = pl.ds(i * half, half)
        total = own[0, :, at].astype(F32) + got[0, :, at].astype(F32)
        out = (down, up)[i % 2]
        out[:, pl.ds(i // 2 * half, half)] = total


def feed_out(own, got):
    _, height, width = own.shape
    out = array((height, width // 2), F32)
    return run(
        feed_out_kernel,
        "feed_out",
        (own, got),
        [vmem()] * 2,
        (out, out),
        [vmem()] * 2,
    )


def attend_out_kernel(a, b, query, key, value, out, gain1, bias1, gain2, bias2):
    height = query.shape[0]

    def both(first, last):
        return a[first:last].astype(F32) + b[first:last].astype(F32)

    one = both(0, height)
    two = both(height + TAIL, 2 * height + TAIL)
    at = pl.ds(height, TAIL)
    sums = decode(a[at]) + decode(b[at])
    for i, ref in enumerate((query, key, value)):
        ref[...] = jnp.concatenate(
            [two[:, 2 * i * HD : 2 * (i + 1) * HD], one[:, (3 + i) * HD : (4 + i) * HD]], axis=1
        )
    out[...] = jnp.transpose(one[:, : 3 * HD])
    for i, ref in enumerate((gain1, bias1, gain2, bias2)):
        ref[...] = jnp.concatenate([sums[i], sums[4 + i]], axis=0)


def attend_out(pieces, height):
    cols = pieces[0].shape[1]
    span = cols // 2
    return run(
        attend_out_kernel,
        "attend_out",
        tuple(pieces),
        [vmem()] * 2,
        (array((height, span), F32),) * 3
        + (array((span, height), F32),)
        + (array((2 * cols,), F32),) * 4,
        [vmem()] * 8,
    )


def fast_path(info, tokens, cotangent, weights, lengths, masks, norms):
    w_query, w_key, w_value, w_out, w_up, w_down = weights
    mask_own, mask_other, mask_ends = masks
    g_one, b_one, g_two, b_two = norms
    height, features, units = w_query.shape[0], tokens.shape[2], w_up.shape[1]
    flat = (tuple((0, j) for j in Y_MAJOR),)
    got_rows = flip_chip(split(info, tokens, cotangent, True))
    piece = pack(w_query, w_key, w_value, w_out)
    got_piece = flip_dp(piece, 4)
    own_rows = split(info, tokens, cotangent, False)
    (two_attn,) = join([piece, got_piece])
    got_attn = flip_dp(two_attn, 2)
    feed_piece = beside(w_up, w_down.T)
    got_feed = flip_dp(feed_piece, 4)
    z_pair, z_single = join_sides([two_attn, got_attn])
    y_pair, x_single = flip_dp(z_pair, 1), flip_chip(z_single)
    own_pair, near_single = join([z_pair, y_pair], [z_single, x_single])
    other_pair, far_single = flip_chip(own_pair), flip_dp(near_single, 1)
    single_w = ((near_single, far_single), (CHIP_NEAR, CHIP_FAR))
    two_up, two_down = join_sides([feed_piece, got_feed])
    got_up, got_down = flip_dp(two_up, 2), flip_dp(two_down, 2)
    quarters = (own_rows, got_rows, flip_core(own_rows), flip_core(got_rows))
    tok = merge(info, quarters)
    own01 = attend(info, lengths, tok, ((own_pair,), flat), True, mask_own[:2])
    z_up, z_down = join([two_up, got_up], [two_down, got_down])
    y_up, x_down = flip_dp(z_up, 1), flip_chip(z_down)
    other01 = attend(info, lengths, tok, ((other_pair,), flat), True, mask_other[:2])
    ends = attend(info, lengths, tok, single_w, False, mask_ends)
    own_up, near_down = join([z_up, y_up], [z_down, x_down])
    other_up, far_down = flip_chip(own_up), flip_dp(near_down, 1)
    up = ((own_up, other_up), (OWN, OTHER))
    down = ((near_down, far_down), (CHIP_NEAR, CHIP_FAR))
    contexts = (own01[3], other01[3], ends[3])
    attn_part = project(info, contexts, single_w, features)
    attn_got = flip_cores(attn_part)
    normal, scale_one, hn = norm_one(tok, attn_part, attn_got, g_one, b_one)
    act1, slope1 = feed_up(info, hn, ((own_up,), flat), units)
    tok_turned, hn_turned = turn_rows(info, tok, hn, Y_MAJOR)
    act2, slope2 = feed_up(info, hn, ((other_up,), flat), units)
    mixed = feed_down(info, act1, act2, down, features)
    mixed_got = flip_cores(mixed)
    own_out, send_out, dzb_two, sums_two = norm_two(
        info, lengths, hn, mixed, mixed_got, quarters, g_two, b_two
    )
    keep_d1, send_d1, keep_d2, send_d2 = feed_grad(
        info, dzb_two, act1, act2, (OWN, OTHER, CHIP_NEAR, CHIP_FAR), False
    )
    got_d1, got_d2 = flip_chip(send_d1), flip_dp(send_d2, 1)
    du1, du2, *back = feed_back(info, dzb_two, slope1, slope2, up, down)
    back_got = flip_cores(back)
    keep_u1, send_u1, keep_u2, send_u2 = feed_grad(
        info, hn_turned, du1, du2, (OWN, OTHER, CHIP_NEAR, CHIP_FAR), True
    )
    got_u1, got_u2 = flip_chip(send_u1), flip_dp(send_u2, 1)
    sum_d1, sum_d2 = fold_add(keep_d1, got_d1, keep_d2, got_d2)
    dzb_one, sums_one = norm_one_back(normal, scale_one, dzb_two, back, back_got, g_one)
    d_ends = attend_back(info, dzb_one, single_w, None, ends)
    keep_f1, send_f1, keep_f2, send_f2 = fold_feed(
        sum_d1, keep_u1, got_u1, sum_d2, keep_u2, got_u2
    )
    got_f1, got_f2 = flip_dp(send_f1, 1), flip_chip(send_f2)
    keep_s, send_s = single_grad(
        info, tok_turned, d_ends, dzb_one, contexts, sums_one, sums_two, Y_MAJOR
    )
    d_other = attend_back(info, dzb_one, single_w, 1, other01)
    grad_b = pair_grad(tok_turned, d_other, len(OWN))
    got_b = flip_chip(grad_b)
    (send_s1,) = join([send_s])
    got_s = flip_dp(send_s1, 1)
    keep_f, send_f = fold_sides(keep_f1, got_f1, keep_f2, got_f2)
    got_f = flip_dp(send_f, 2)
    d_own = attend_back(info, dzb_one, single_w, 0, own01)
    grad_a = pair_grad(tok_turned, d_own, len(OWN))
    keep_a, send_a = fold(grad_a, got_b, 2, 0)
    got_a = flip_dp(send_a, 1)
    keep_s2, send_s2 = fold(keep_s, got_s, 2, TAIL)
    got_s2 = flip_chip(send_s2)
    mine, *sent = input_back(
        info, d_own, d_other, d_ends, dzb_one, ((own_pair, other_pair), (OWN, OTHER)), single_w
    )
    keep_f3, send_f3 = fold(keep_f, got_f, 2, 0)
    got_f3 = flip_dp(send_f3, 4)
    keep_s3, send_s3, keep_a3, send_a3 = fold_last(keep_s2, got_s2, keep_a, got_a)
    got_s3, got_a3 = flip_dp(send_s3, 2), flip_dp(send_a3, 2)
    sent_parts = join(*[[v] for v in sent])
    sent_got = flip_cores(sent_parts)
    own_tok, *send_tok = tokens_add(mine, sent_got)
    got_tok = [flip_chip(v) for v in send_tok]
    got_out = flip_chip(send_out)
    keep_z, send_z = fold_z(keep_s3, got_s3, keep_a3, got_a3)
    got_z = flip_dp(send_z, 4)
    grad_tokens = tokens_out(info, own_tok, got_tok)
    output = slots_of(info, own_out, got_out)
    grad_up, grad_down = feed_out(keep_f3, got_f3)
    grads = attend_out((keep_z, got_z), height)
    return (output, grad_tokens, *grads[:4], grad_up, grad_down.T, *grads[4:])


def plain_path(info, tokens, cotangent, weights, lengths, masks, norms):
    w_query, w_key, w_value, w_out, w_up, w_down = weights
    mask_own, mask_other, mask_ends = masks
    g_one, b_one, g_two, b_two = norms
    features, units = tokens.shape[2], w_up.shape[1]
    flat = (((0, 0),),)
    two = (((0, 0),), ((1, 0),))

    def gathered(piece):
        own = lax.all_gather(piece, "dp", axis=0, tiled=True)[None]
        return own, flip_chip(own)

    got_rows = flip_chip(split(info, tokens, cotangent, True))
    own_rows = split(info, tokens, cotangent, False)
    quarters = (own_rows, got_rows, flip_core(own_rows), flip_core(got_rows))
    tok = merge(info, quarters)
    firsts = [w[:, : 2 * HD] for w in (w_query, w_key, w_value)]
    thirds = [w_out.T] + [w[:, 2 * HD :] for w in (w_query, w_key, w_value)]
    pair_w = (gathered(jnp.concatenate(firsts, axis=1)), two)
    single_w = (gathered(jnp.concatenate(thirds, axis=1)), two)
    up, down = (gathered(w_up), two), (gathered(w_down.T), two)
    own01 = attend(info, lengths, tok, ((pair_w[0][0],), flat), True, mask_own[:2])
    other01 = attend(info, lengths, tok, ((pair_w[0][1],), flat), True, mask_other[:2])
    ends = attend(info, lengths, tok, single_w, False, mask_ends)
    contexts = (own01[3], other01[3], ends[3])
    part = project(info, contexts, single_w, features)
    normal, scale_one, hn = norm_one(tok, part, flip_cores(part), g_one, b_one)
    act1, slope1 = feed_up(info, hn, ((up[0][0],), flat), units)
    act2, slope2 = feed_up(info, hn, ((up[0][1],), flat), units)
    tok_turned, hn_turned = turn_rows(info, tok, hn, (0,))
    part = feed_down(info, act1, act2, down, features)
    own_out, send_out, dzb_two, sums_two = norm_two(
        info, lengths, hn, part, flip_cores(part), quarters, g_two, b_two
    )
    places = (((0, 0),), ((1, 0),)) * 2
    grad_d = feed_grad(info, dzb_two, act1, act2, places, False)
    du1, du2, *part = feed_back(info, dzb_two, slope1, slope2, up, down)
    grad_u = feed_grad(info, hn_turned, du1, du2, places, True)
    dzb_one, sums_one = norm_one_back(
        normal, scale_one, dzb_two, part, flip_cores(part), g_one
    )
    d_ends = attend_back(info, dzb_one, single_w, None, ends)
    keep_s, send_s = single_grad(
        info, tok_turned, d_ends, dzb_one, contexts, sums_one, sums_two, (0,)
    )
    d_other = attend_back(info, dzb_one, single_w, 1, other01)
    grad_b = pair_grad(tok_turned, d_other, 1)
    d_own = attend_back(info, dzb_one, single_w, 0, own01)
    grad_a = pair_grad(tok_turned, d_own, 1)
    mine, *sent = input_back(info, d_own, d_other, d_ends, dzb_one, pair_w, single_w)
    own_tok, *send_tok = tokens_add(mine, flip_cores(sent))
    output = slots_of(info, own_out, flip_chip(send_out))
    grad_tokens = tokens_out(info, own_tok, [flip_chip(v) for v in send_tok])

    def summed(own, other):
        total = own.astype(F32) + flip_chip(other).astype(F32)
        return lax.psum_scatter(total, "dp", scatter_dimension=0, tiled=True)

    def wide(keep1, send1, keep2, send2):
        return jnp.concatenate([summed(keep1[0], send1[0]), summed(keep2[0], send2[0])], axis=1)

    single = summed(keep_s[:features], send_s[:features])
    pair = summed(grad_a[0], grad_b[0])
    grads = [
        jnp.concatenate(
            [pair[:, 2 * i * HD : 2 * (i + 1) * HD], single[:, (3 + i) * HD : (4 + i) * HD]],
            axis=1,
        )
        for i in range(3)
    ] + [single[:, : 3 * HD].T]
    sums = decode(keep_s[features:])
    sums = lax.psum(sums + flip_chip(sums), "dp")
    sums = [jnp.concatenate([sums[i], sums[4 + i]]) for i in range(4)]
    return (output, grad_tokens, *grads, wide(*grad_u), wide(*grad_d).T, *sums)


def local(
    tokens,
    w_query,
    w_key,
    w_value,
    w_out,
    w_up,
    w_down,
    gain_attn,
    bias_attn,
    gain_ffn,
    bias_ffn,
    lengths,
    random_blocks,
    cotangent,
):
    ORDER.clear()
    size = lax.axis_size("dp")
    rank = lax.axis_index("mp")
    me = lax.axis_index("dp")
    x, core = rank // 2, rank % 2
    quarter = tokens.shape[1]
    seq = 4 * quarter
    height = w_query.shape[0]
    span = w_query.shape[1]
    heads = span // HD
    nblocks = seq // BLOCK
    fast = size == 8 and height % 16 == 0

    shift = x * (seq // 2)
    info = jnp.stack([me, x, core, shift]).astype(jnp.int32)

    blocks = (jnp.arange(nblocks) + x * (nblocks // 2)) % nblocks
    near_blocks = jnp.abs(blocks[:, None] - blocks[None, :]) <= 1
    edge = (blocks == 0) | (blocks == nblocks - 1)
    fixed = near_blocks | edge[:, None] | edge[None, :]

    def table(shard):
        chosen = lax.dynamic_slice_in_dim(random_blocks, shard * heads, heads, 0)
        chosen = jnp.roll(chosen, -x * (nblocks // 2), axis=1)
        hit = jnp.any(chosen[:, None, :, :] == blocks[None, :, None, None], axis=3)
        bias = jnp.where(fixed.T[None] | hit, 0.0, NEGATIVE)
        return jnp.concatenate(
            [
                jnp.zeros((heads, nblocks, HD), F32),
                bias,
                jnp.full((heads, nblocks, 3), -1.0, F32),
                jnp.zeros((heads, nblocks, HD - 3 - nblocks), F32),
            ],
            axis=2,
        )

    mask_own, mask_other = table(rank), table(rank ^ 2)
    mask_ends = jnp.concatenate([mask_own[2:], mask_other[2:]], axis=0)
    g_one, b_one = gain_attn[None], bias_attn[None]
    g_two, b_two = gain_ffn[None], bias_ffn[None]

    path = fast_path if fast else plain_path
    return path(
        info,
        tokens,
        cotangent,
        (w_query, w_key, w_value, w_out, w_up, w_down),
        lengths,
        (mask_own, mask_other, mask_ends),
        (g_one, b_one, g_two, b_two),
    )


def solution(mesh):
    return jax.shard_map(
        local,
        mesh=mesh,
        in_specs=(
            P("dp", "mp", None),
            P("dp", "mp"),
            P("dp", "mp"),
            P("dp", "mp"),
            P("mp", "dp"),
            P("dp", "mp"),
            P("mp", "dp"),
            P(),
            P(),
            P(),
            P(),
            P("dp"),
            P(),
            P("dp", "mp", None),
        ),
        out_specs=(
            P("dp", "mp", None),
            P("dp", "mp", None),
            P("dp", "mp"),
            P("dp", "mp"),
            P("dp", "mp"),
            P("mp", "dp"),
            P("dp", "mp"),
            P("mp", "dp"),
            P(),
            P(),
            P(),
            P(),
        ),
        check_vma=False,
    )
```

```python
import functools

import jax
import jax.numpy as jnp
from jax import lax
from jax.experimental import pallas as pl
from jax.experimental.pallas import tpu as pltpu
from jax.sharding import PartitionSpec as P

HD = 64
BLOCK = 64
LANES = 128
TILE = 256
KEYS = 128
SENT = 256
EPSILON = 1e-12
TAIL = 32
TOKEN = (8, 128)
ROOM = {
    "attend": 28,
    "attend_back": 28,
    "project": 12,
    "input_back": 24,
    "norm_one": 12,
    "norm_two": 18,
    "norm_one_back": 14,
    "feed_up": 16,
    "feed_down": 18,
    "feed_back": 32,
    "turn_rows": 12,
    "feed_grad": 24,
    "pair_grad": 16,
    "single_grad": 24,
    "join": 1,
    "join_sides": 1,
    "beside": 1,
    "pack": 2,
    "split": 4,
    "merge": 1,
    "fold": 6,
    "fold_add": 8,
    "fold_feed": 10,
    "fold_sides": 8,
    "fold_last": 6,
    "fold_z": 4,
    "slots": 1,
    "tokens_add": 8,
    "tokens_out": 8,
    "feed_out": 6,
    "attend_out": 6,
}
SCALE = 0.125
LOG2E = 1.4426950408889634
LN2 = 0.6931471805599453
NEGATIVE = -1e30
F32 = jnp.float32
BF16 = jnp.bfloat16

CORE_SWAP = [(0, 1), (1, 0), (2, 3), (3, 2)]
CHIP_SWAP = [(0, 2), (2, 0), (1, 3), (3, 1)]


def nn(a, b):
    return lax.dot_general(a, b, (((1,), (0,)), ((), ())), preferred_element_type=F32)


def nt(a, b):
    return lax.dot_general(a, b, (((1,), (1,)), ((), ())), preferred_element_type=F32)


def tn(a, b):
    return lax.dot_general(a, b, (((0,), (0,)), ((), ())), preferred_element_type=F32)


def vmem():
    return pl.BlockSpec(memory_space=pltpu.VMEM)


def smem():
    return pl.BlockSpec(memory_space=pltpu.SMEM)


def anywhere():
    return pl.BlockSpec(memory_space=pl.ANY)


def in_hbm(values):
    return tuple(pltpu.with_memory_space_constraint(v, pltpu.HBM) for v in values)


def array(shape, dtype):
    return jax.ShapeDtypeStruct(shape, dtype)


ORDER = []


def run(kernel, name, args, specs, outs, out_specs, scratch=()):
    given, made = len(args), len(outs)
    extra = tuple(ORDER)

    def body(*refs):
        ins, rest = refs[:given], refs[given + len(extra) :]
        rest[made][...] = jnp.zeros(TOKEN, F32)
        kernel(*ins, *rest[:made], *rest[made + 1 :])

    results = pl.pallas_call(
        body,
        out_shape=tuple(outs) + (array(TOKEN, F32),),
        in_specs=list(specs) + [anywhere()] * len(extra),
        out_specs=tuple(out_specs) + (vmem(),),
        scratch_shapes=list(scratch),
        compiler_params=pltpu.CompilerParams(vmem_limit_bytes=ROOM[name] * 2**20),
        cost_estimate=pl.CostEstimate(flops=1, bytes_accessed=0, transcendentals=0),
        name=name,
    )(*args, *extra)
    ORDER[:] = [results[-1]]
    return results[:-1]


def put_rows(parts, t, value):
    height, tile = parts[0].shape[0], value.shape[0]
    if height <= tile:
        per = tile // height
        for k in range(per):
            parts[t * per + k][...] = value[k * height : (k + 1) * height]
    else:
        per = height // tile
        parts[t // per][pl.ds(t % per * tile, tile), :] = value


def get_sum(parts, more, t):
    height = parts[0].shape[0]
    if height <= TILE:
        per = TILE // height
        at = range(t * per, (t + 1) * per)
        pieces = [parts[k][...].astype(F32) + more[k][...].astype(F32) for k in at]
        return pieces[0] if per == 1 else jnp.concatenate(pieces, axis=0)
    per = height // TILE
    at = pl.ds(t % per * TILE, TILE)
    return parts[t // per][at, :].astype(F32) + more[t // per][at, :].astype(F32)


def tile_rows(ref, tile=TILE):
    return [(t, pl.ds(t * tile, tile)) for t in range(ref.shape[0] // tile)]


def far(shape, dtype):
    return pltpu.HBM(shape, dtype)


def tiles(seq, width, height):
    parts = (array((height, width), BF16),) * (seq // height)
    return parts, [vmem()] * len(parts)


def place(me, refs, slots, dst_ref, first=0, last=None, only=None, to=0):
    for ref, of in zip(refs, slots):
        height, width = ref.shape[1], ref.shape[2]
        end = width if last is None else last
        for e, (chip, j) in enumerate(of):
            if only is not None and chip != only:
                continue
            at = 0 if height == dst_ref.shape[0] else pl.multiple_of((me ^ j) * height, height)
            at_column = to + (0 if only is not None else chip * (end - first))
            dst_ref[pl.ds(at, height), pl.ds(at_column, end - first)] = ref[e, :, first:end]


def pick(me, fulls, out_ref, slots, first):
    _, height, width = out_ref.shape
    for e, (chip, j) in enumerate(slots):
        full = fulls[chip]
        at = 0 if height == full.shape[0] else pl.multiple_of((me ^ j) * height, height)
        out_ref[e] = full[pl.ds(at, height), pl.ds(first, width)]


def attend_kernel(slots, columns, only, places, info, lengths, tok, mask, *rest):
    refs, (qa, ka, va, ctx, wfull) = rest[: len(slots)], rest[len(slots) :]
    seq = tok.shape[0]
    place(info[0], refs, slots, wfull, *columns, only)
    lane = lax.broadcasted_iota(jnp.int32, (TILE, LANES), 1)
    row0 = lax.broadcasted_iota(jnp.int32, (TILE, LANES), 0)
    for t in range(seq // TILE):
        at = pl.ds(t * TILE, TILE)
        row = row0 + t * TILE
        made = nn(tok[at, :], wfull[...])
        onehot = jnp.where(lane - HD == row // BLOCK, 1.0, 0.0)[:, HD:]
        position = row + info[3]
        position = jnp.where(position >= seq, position - seq, position)
        dead = (position >= lengths[info[1]]) & (lane >= HD) & (lane < HD + 16)
        for h, (q_at, k_at, v_at) in enumerate(places):
            q = made[:, q_at : q_at + HD] * (SCALE * LOG2E)
            k = made[:, k_at : k_at + HD]
            v = made[:, v_at : v_at + HD]
            qa[h, at, :] = jnp.concatenate([q, onehot], axis=1).astype(BF16)
            per = TILE // BLOCK
            table = jnp.concatenate(
                [
                    jnp.broadcast_to(mask[h, t * per + b : t * per + b + 1, :], (BLOCK, LANES))
                    for b in range(per)
                ],
                axis=0,
            )
            table = jnp.where(dead, NEGATIVE, table)
            ka[h, at, :] = jnp.concatenate([k, table[:, HD:]], axis=1).astype(BF16)
            va[h, at, :] = jnp.concatenate([v, jnp.full((TILE, HD), -1.0, F32)], axis=1).astype(BF16)
    lane = lax.broadcasted_iota(jnp.int32, (2 * TILE, LANES), 1)
    for t in range(seq // TILE // 2):
        at = pl.ds(t * 2 * TILE, 2 * TILE)
        pieces = []
        for h in range(len(places)):
            q = qa[h, at, :]
            s = nt(q, ka[h])
            top = jnp.max(s, axis=1, keepdims=True)
            p = jnp.exp2(s - top).astype(BF16)
            got = nn(p, va[h])
            total = -got[:, HD:]
            pieces.append(got[:, :HD] / total)
            log = top + jnp.log2(-got)
            hi = log.astype(BF16).astype(F32)
            mid = (log - hi).astype(BF16).astype(F32)
            low = log - hi - mid
            new = jnp.where(
                lane == HD + 16,
                hi,
                jnp.where(lane == HD + 17, mid, jnp.where(lane == HD + 18, low, q.astype(F32))),
            )
            qa[h, at, :] = new.astype(BF16)
        ctx[at, :] = jnp.concatenate(pieces, axis=1).astype(BF16)


PAIR = ((0, 2 * HD, 4 * HD), (HD, 3 * HD, 5 * HD))
SINGLES = ((HD, 2 * HD, 3 * HD), (5 * HD, 6 * HD, 7 * HD))


def attend(info, lengths, tok, gathered, pair, mask):
    arrays, slots = gathered
    seq, width = tok.shape
    aug = far((2, seq, LANES), BF16)
    columns, only, cols = ((0, 6 * HD), 0, 6 * HD) if pair else ((2 * HD, 6 * HD), None, 8 * HD)
    return run(
        functools.partial(attend_kernel, slots, columns, only, PAIR if pair else SINGLES),
        "attend",
        (info, lengths, tok, mask) + arrays,
        [smem()] * 2 + [vmem()] * (2 + len(arrays)),
        (aug, aug, aug, array((seq, LANES), BF16)),
        [vmem()] * 4,
        [pltpu.VMEM((width, cols), BF16)],
    )


def place_out(me, refs, slots, pairs, ends):
    place(me, refs, slots, pairs, 0, 2 * HD)
    place(me, refs, slots, ends, 2 * HD, 4 * HD)
    both = ends[...]
    ends[:, :LANES] = jnp.concatenate([both[:, :HD], both[:, LANES : LANES + HD]], axis=1)


def project_kernel(slots, info, own, other, ends, *rest):
    refs, parts, (w1, w2) = rest[: len(slots)], rest[len(slots) : -2], rest[-2:]
    place_out(info[0], refs, slots, w1, w2)
    for t, at in tile_rows(own):
        both = jnp.concatenate([own[at, :], other[at, :]], axis=1)
        out = nt(both, w1[...]) + nt(ends[at, :], w2[:, :LANES])
        put_rows(parts, t, out.astype(BF16))


def project(info, contexts, gathered, width):
    arrays, slots = gathered
    seq = contexts[0].shape[0]
    return run(
        functools.partial(project_kernel, slots),
        "project",
        (info,) + contexts + arrays,
        [smem()] + [vmem()] * (3 + len(arrays)),
        *tiles(seq, width, 2 * TILE),
        [pltpu.VMEM((width, 2 * LANES), BF16)] * 2,
    )


def attend_back_kernel(slots, chip, info, dz, qa, ka, va, ctx, *rest):
    refs, (dqkv, pairs, ends, da) = rest[: len(slots)], rest[len(slots) :]
    seq = dz.shape[0]
    heads = qa.shape[0]
    if chip is None:
        place_out(info[0], refs, slots, pairs, ends)
        wfull = ends.at[:, pl.ds(0, LANES)]
    else:
        place(info[0], refs, slots, pairs, 0, 2 * HD, chip)
        wfull = pairs.at[:, pl.ds(0, LANES)]
    lane = lax.broadcasted_iota(jnp.int32, (TILE, LANES), 1)
    for t in range(seq // TILE):
        at = pl.ds(t * TILE, TILE)
        dctx = nn(dz[at, :], wfull[...]).astype(BF16).astype(F32)
        both = dctx * ctx[at, :].astype(F32)
        for h in range(heads):
            inner = jnp.sum(both[:, h * HD : (h + 1) * HD], axis=1, keepdims=True)
            hi = inner.astype(BF16).astype(F32)
            mid = (inner - hi).astype(BF16).astype(F32)
            low = inner - hi - mid
            one = jnp.concatenate(
                [dctx[:, h * HD : (h + 1) * HD], jnp.zeros((TILE, HD), F32)], axis=1
            )
            one = jnp.where(lane == HD, hi, one)
            one = jnp.where(lane == HD + 1, mid, one)
            one = jnp.where(lane == HD + 2, low, one)
            da[h, at, :] = one.astype(BF16)

    def turned(values):
        return jnp.transpose(values.astype(F32))[:HD].astype(BF16)

    grads = []
    for h in range(heads):
        k_turned, q_turned, d_turned = turned(ka[h]), turned(qa[h]), turned(da[h])
        dq, dk, dv = None, [], []
        for t in range(seq // KEYS):
            at = pl.ds(t * KEYS, KEYS)
            p = jnp.exp2(nt(ka[h, at, :], qa[h]))
            ds = (p * nt(va[h, at, :], da[h])).astype(BF16)
            dv.append(nt(d_turned, p.astype(BF16)))
            dk.append(nt(q_turned, ds))
            more = nn(k_turned[:, t * KEYS : (t + 1) * KEYS], ds)
            dq = more if dq is None else dq + more
        dk = jnp.concatenate(dk, axis=1) * LN2
        grads.append((dq * SCALE, dk, jnp.concatenate(dv, axis=1)))
    (dq0, dk0, dv0), (dq1, dk1, dv1) = grads
    if chip is None:
        blank = jnp.zeros_like(dq0)
        stacks = ((blank, dq0), (dk0, dv0), (blank, dq1), (dk1, dv1))
    else:
        stacks = ((dq0, dq1), (dk0, dk1), (dv0, dv1))
    for i, stack in enumerate(stacks):
        both = jnp.transpose(jnp.concatenate(stack, axis=0))
        dqkv[:, i * LANES : (i + 1) * LANES] = both.astype(BF16)


def attend_back(info, dz, gathered, chip, saved):
    arrays, slots = gathered
    qa, ka, va, ctx = saved
    seq, width = dz.shape
    cols = 8 * HD if chip is None else 6 * HD
    return run(
        functools.partial(attend_back_kernel, slots, chip),
        "attend_back",
        (info, dz, qa, ka, va, ctx) + arrays,
        [smem()] + [vmem()] * (5 + len(arrays)),
        (array((seq, cols), BF16),),
        [vmem()],
        [
            pltpu.VMEM((width, 2 * LANES), BF16),
            pltpu.VMEM((width, 2 * LANES), BF16),
            pltpu.VMEM((2, seq, LANES), BF16),
        ],
    )[0]


def input_back_kernel(slots1, slots2, info, own, other, ends, dz, *rest):
    n1, n2 = len(slots1), len(slots2)
    refs1, refs2, (mine, *sent, w1, w2) = rest[:n1], rest[n1 : n1 + n2], rest[n1 + n2 :]
    place(info[0], refs1, slots1, w1)
    place(info[0], refs2, slots2, w2, 2 * HD, 6 * HD)
    per = len(sent) // 2
    height = sent[0].shape[0]
    for half in range(dz.shape[0] // TILE // 2):
        for whose in range(2):
            tile = 2 * half + (info[2] if whose == 0 else 1 - info[2])
            at = pl.ds(pl.multiple_of(tile * TILE, TILE), TILE)
            pairs = jnp.concatenate([own[at, :], other[at, :]], axis=1)
            back = nt(pairs, w1[...]) + nt(ends[at, :], w2[...])
            if whose == 0:
                mine[half] = back + dz[at, :].astype(F32)
                continue
            for k in range(per):
                part = back[k * height : (k + 1) * height]
                sent[half * per + k][...] = part.astype(BF16)


def input_back(info, own, other, ends, dz, gathered1, gathered2):
    seq, width = dz.shape
    arrays = gathered1[0] + gathered2[0]
    halves = (seq // TILE // 2, TILE, width)
    grads = (own, other, ends, dz)
    return run(
        functools.partial(input_back_kernel, gathered1[1], gathered2[1]),
        "input_back",
        (info,) + grads + arrays,
        [smem()] + [vmem()] * (len(grads) + len(arrays)),
        (array(halves, F32),) + (array((SENT, width), BF16),) * (seq // 2 // SENT),
        [vmem()] * (1 + seq // 2 // SENT),
        [pltpu.VMEM((width, 12 * HD), BF16), pltpu.VMEM((width, 8 * HD), BF16)],
    )


def center(z):
    mean = jnp.mean(z, axis=1, keepdims=True)
    moved = z - mean
    spread = jnp.mean(moved * moved, axis=1, keepdims=True)
    scale = lax.rsqrt(spread + EPSILON)
    return moved * scale, scale


def norm_back(n, scale, gy, gain):
    dn = gy * gain
    return scale * (
        dn - jnp.mean(dn, axis=1, keepdims=True) - n * jnp.mean(dn * n, axis=1, keepdims=True)
    )


def add_sums(gy, n, sums):
    more = [jnp.sum(v, axis=0, keepdims=True) for v in (gy * n, gy)]
    return more if sums is None else [a + b for a, b in zip(sums, more)]


def norm_one_kernel(tok, gain, bias, *rest):
    *parts, normal, scale, hn = rest
    count = len(parts) // 2
    for t, at in tile_rows(tok):
        value = tok[at, :].astype(F32) + get_sum(parts[:count], parts[count:], t)
        n, r = center(value)
        normal[at, :] = n.astype(BF16)
        scale[at, :] = r
        hn[at, :] = (n * gain[...] + bias[...]).astype(BF16)


def norm_one(tok, p0, p1, gain, bias):
    seq, width = tok.shape
    return run(
        norm_one_kernel,
        "norm_one",
        (tok, gain, bias, *p0, *p1),
        [vmem()] * (3 + len(p0) + len(p1)),
        (array((seq, width), BF16), array((seq, 1), F32), array((seq, width), BF16)),
        [vmem()] * 3,
    )


def norm_two_kernel(info, lengths, hn, own, got, core_own, core_got, gain, bias, *rest):
    *parts, own_out, send_out, dzb, sums, out = rest
    count = len(parts) // 2
    seq = hn.shape[0]
    total = None
    for t, at in tile_rows(hn):
        value = hn[at, :].astype(F32) + get_sum(parts[:count], parts[count:], t)
        n, scale = center(value)
        out[at, :] = (n * gain[...] + bias[...]).astype(BF16)
        position = lax.broadcasted_iota(jnp.int32, (TILE, 1), 0) + t * TILE + info[3]
        position = jnp.where(position >= seq, position - seq, position)
        valid = jnp.where(position < lengths[info[1]], 1.0, 0.0)
        mine, others = ((own, core_own), (got, core_got))[t // 2]
        cot = jnp.where(info[2] == t % 2, mine[1].astype(F32), others[1].astype(F32))
        gy = cot * valid
        dzb[at, :] = norm_back(n, scale, gy, gain[...]).astype(BF16)
        total = add_sums(gy, n, total)
    sums[...] = jnp.concatenate(total, axis=0)
    for half, ref in enumerate((own_out, send_out)):
        at = pl.multiple_of((2 * half + info[2]) * TILE, TILE)
        ref[...] = out[pl.ds(at, TILE), :]


def norm_two(info, lengths, hn, m0, m1, cot, gain, bias):
    seq, width = hn.shape
    return run(
        norm_two_kernel,
        "norm_two",
        (info, lengths, hn, *cot, gain, bias, *m0, *m1),
        [smem()] * 2 + [vmem()] * (3 + len(cot) + len(m0) + len(m1)),
        (
            array((TILE, width), BF16),
            array((TILE, width), BF16),
            array((seq, width), BF16),
            array((2, width), F32),
        ),
        [vmem()] * 4,
        [pltpu.VMEM((seq, width), BF16)],
    )


def norm_one_back_kernel(normal, scale, dz2, gain, *rest):
    *parts, dzb, sums = rest
    count = len(parts) // 2
    total = None
    for t, at in tile_rows(dz2):
        n = normal[at, :].astype(F32)
        gy = dz2[at, :].astype(F32) + get_sum(parts[:count], parts[count:], t)
        dzb[at, :] = norm_back(n, scale[at, :], gy, gain[...]).astype(BF16)
        total = add_sums(gy, n, total)
    sums[...] = jnp.concatenate(total, axis=0)


def norm_one_back(normal, scale, dz2, p0, p1, gain):
    seq, width = normal.shape
    return run(
        norm_one_back_kernel,
        "norm_one_back",
        (normal, scale, dz2, gain, *p0, *p1),
        [vmem()] * (4 + len(p0) + len(p1)),
        (array((seq, width), BF16), array((2, width), F32)),
        [vmem()] * 2,
    )


def gelu_pair(u):
    phi = 0.5 + 0.5 * lax.erf(u * 0.7071067811865476)
    return u * phi, phi + u * (jnp.exp(-0.5 * u * u) * 0.3989422804014327)


def feed_up_kernel(slots, info, hn, *rest):
    refs, (active, slope, wfull) = rest[: len(slots)], rest[len(slots) :]
    place(info[0], refs, slots, wfull)
    for _, at in tile_rows(hn):
        a, g = gelu_pair(nn(hn[at, :], wfull[...]))
        active[at, :] = a.astype(BF16)
        slope[at, :] = g.astype(BF16)


def feed_up(info, hn, gathered, units):
    arrays, slots = gathered
    seq, width = hn.shape
    return run(
        functools.partial(feed_up_kernel, slots),
        "feed_up",
        (info, hn) + arrays,
        [smem()] + [vmem()] * (1 + len(arrays)),
        (array((seq, units), BF16), array((seq, units), BF16)),
        [vmem()] * 2,
        [pltpu.VMEM((width, units), BF16)],
    )


def feed_down_kernel(slots, info, act1, act2, *rest):
    refs, parts, wfull = rest[: len(slots)], rest[len(slots) : -1], rest[-1]
    place(info[0], refs, slots, wfull)
    for t, at in tile_rows(act1):
        both = jnp.concatenate([act1[at, :], act2[at, :]], axis=1)
        put_rows(parts, t, nt(both, wfull[...]).astype(BF16))


def feed_down(info, act1, act2, gathered, width):
    seq, units = act1.shape
    arrays, slots = gathered
    return run(
        functools.partial(feed_down_kernel, slots),
        "feed_down",
        (info, act1, act2) + arrays,
        [smem()] + [vmem()] * (2 + len(arrays)),
        *tiles(seq, width, seq),
        [pltpu.VMEM((width, 2 * units), BF16)],
    )


def feed_back_kernel(slots_up, slots_down, info, dzb, slope1, slope2, *rest):
    n1, n2 = len(slots_up), len(slots_down)
    ups, downs, (du1, du2, *parts, up, down) = rest[:n1], rest[n1 : n1 + n2], rest[n1 + n2 :]
    place(info[0], ups, slots_up, up)
    place(info[0], downs, slots_down, down)
    units = du1.shape[1]
    for t, at in tile_rows(dzb):
        out = None
        for i, (slope, du) in enumerate(((slope1, du1), (slope2, du2))):
            cols = pl.ds(i * units, units)
            grad = (nn(dzb[at, :], down[:, cols]) * slope[at, :].astype(F32)).astype(BF16)
            du[at, :] = grad
            more = nt(grad, up[:, cols])
            out = more if out is None else out + more
        put_rows(parts, t, out.astype(BF16))


def feed_back(info, dzb, slope1, slope2, up, down):
    seq, width = dzb.shape
    units = slope1.shape[1]
    arrays = up[0] + down[0]
    parts, part_specs = tiles(seq, width, TILE)
    return run(
        functools.partial(feed_back_kernel, up[1], down[1]),
        "feed_back",
        (info, dzb, slope1, slope2) + arrays,
        [smem()] + [vmem()] * (3 + len(arrays)),
        (array((seq, units), BF16),) * 2 + parts,
        [vmem()] * 2 + part_specs,
        [pltpu.VMEM((width, 2 * units), BF16)] * 2,
    )


def turn_rows_kernel(order, info, first, second, out1, out2, full):
    count = len(order)
    height = full.shape[0] // count
    for values, out in ((first, out1), (second, out2)):
        for t, at in tile_rows(values):
            full[:, t * TILE : (t + 1) * TILE] = jnp.transpose(values[at, :])
        for e, j in enumerate(order):
            at = 0 if count == 1 else pl.multiple_of((info[0] ^ j) * height, height)
            out[pl.ds(e * height, height), :] = full[pl.ds(at, height), :]


def turn_rows(info, first, second, order):
    shape = first.shape[::-1]
    out = array(shape, BF16)
    return run(
        functools.partial(turn_rows_kernel, order),
        "turn_rows",
        (info, first, second),
        [smem()] + [vmem()] * 2,
        (out, out),
        [vmem()] * 2,
        [pltpu.VMEM(shape, BF16)],
    )


def feed_grad_kernel(turned, places, info, a, d1, d2, *rest):
    outs, full = rest[:4], rest[4]
    half = outs[0].shape[2]
    product = nn if turned else tn
    made = product(a[...], jnp.concatenate([d1[...], d2[...]], axis=1)).astype(BF16)
    if turned:
        height = outs[0].shape[1]
        order = [j for chip, j in places[0] if chip == 0]
        for i, out in enumerate(outs):
            for e, (chip, j) in enumerate(places[i]):
                row = order.index(j) * height
                first = 2 * chip * half + (i // 2) * half
                out[e] = made[row : row + height, first : first + half]
        return
    full[...] = made
    fulls = [full.at[:, pl.ds(2 * chip * half, 2 * half)] for chip in range(2)]
    for i, out in enumerate(outs):
        pick(info[0], fulls, out, places[i], (i // 2) * half)


def feed_grad(info, a, d1, d2, places, turned):
    seq, units = d1.shape
    width = a.shape[0] if turned else a.shape[1]
    count = len(places[0])
    out = array((count, width // count, units // 2), BF16)
    return run(
        functools.partial(feed_grad_kernel, turned, places),
        "feed_grad",
        (info, a, d1, d2),
        [smem()] + [vmem()] * 3,
        (out,) * 4,
        [vmem()] * 4,
        [pltpu.VMEM((width, 2 * units), BF16)],
    )


def pair_grad_kernel(tok_turned, d, out):
    made = nn(tok_turned[...], d[...]).astype(BF16)
    height = out.shape[1]
    for e in range(out.shape[0]):
        out[e] = made[e * height : (e + 1) * height]


def pair_grad(tok_turned, d, count):
    width = tok_turned.shape[0]
    cols = d.shape[1]
    return run(
        pair_grad_kernel,
        "pair_grad",
        (tok_turned, d),
        [vmem()] * 2,
        (array((count, width // count, cols), BF16),),
        [vmem()],
    )[0]


def encode(sums):
    hi = sums.astype(BF16).astype(F32)
    mid = (sums - hi).astype(BF16).astype(F32)
    low = sums - hi - mid
    return jnp.concatenate([hi, mid, low, jnp.zeros_like(low)], axis=0).astype(BF16)


def decode(coded):
    values = coded.astype(F32)
    n = values.shape[0] // 4
    return values[:n] + values[n : 2 * n] + values[2 * n : 3 * n]


def single_grad_kernel(
    order, info, tok_turned, d, dz, own, other, ends, sums_one, sums_two, keep, send, full
):
    mine = nn(tok_turned[...], d[...])
    full[...] = tn(dz[...], jnp.concatenate([ends[...], own[...], other[...]], axis=1))
    count = len(order)
    height = full.shape[0] // count
    width = keep.shape[1]
    blank = jnp.zeros((height, HD), F32)
    both = jnp.concatenate([sums_one[...], sums_two[...]], axis=0)
    both = encode(jnp.concatenate([both[:, :width], both[:, width:]], axis=0))
    half = max(1, count // 2)
    for e, j in enumerate(order):
        at = 0 if count == 1 else pl.multiple_of((info[0] ^ j) * height, height)
        heads = full[pl.ds(at, height), :]
        rows_in = mine[e * height : (e + 1) * height]
        for chip in range(2):
            first = chip * 4 * HD
            third = jnp.concatenate([heads[:, chip * HD : (chip + 1) * HD], blank], axis=1)
            made = [
                heads[:, (chip + 1) * LANES : (chip + 2) * LANES],
                third + rows_in[:, first : first + LANES],
                rows_in[:, first + LANES : first + 2 * LANES],
            ]
            if count == 1:
                out, row = (keep, send)[chip], 0
            else:
                out, row = (keep, send)[e // half], (chip * half + e % half) * height
            out[pl.ds(row, height), :] = jnp.concatenate(made, axis=1).astype(BF16)
    for out in (keep, send):
        out[pl.ds(out.shape[0] - TAIL, TAIL), :] = both


def single_grad(info, tok_turned, d, dz, contexts, sums_one, sums_two, order):
    width = tok_turned.shape[0]
    cols = 6 * HD
    out = array((width + TAIL, cols), BF16)
    return run(
        functools.partial(single_grad_kernel, order),
        "single_grad",
        (info, tok_turned, d, dz, *contexts, sums_one, sums_two),
        [smem()] + [vmem()] * 8,
        (out, out),
        [vmem()] * 2,
        [pltpu.VMEM((width, 3 * LANES), F32)],
    )


def across(values, axis, pairs):
    return lax.ppermute(values, axis, pairs)


def flip_chip(values):
    return across(values, "mp", CHIP_SWAP)


def flip_core(values):
    return across(values, "mp", CORE_SWAP)


def flip_cores(parts):
    return [flip_core(p) for p in parts]


def flip_dp(values, distance):
    size = lax.axis_size("dp")
    return across(values, "dp", [(i, i ^ distance) for i in range(size)])


def join_kernel(groups, *refs):
    count = sum(groups)
    parts, outs, sems = refs[:count], refs[count:-1], refs[-1]
    copies = []
    for out, number in zip(outs, groups):
        first = 0
        for part in parts[len(copies) : len(copies) + number]:
            to = out.at[pl.ds(first, part.shape[0])]
            copies.append(pltpu.make_async_copy(part, to, sems.at[len(copies)]))
            first += part.shape[0]
    for copy in copies:
        copy.start()
    for copy in copies:
        copy.wait()


def join(*groups):
    parts = sum((tuple(g) for g in groups), ())
    outs = [array((sum(p.shape[0] for p in g),) + g[0].shape[1:], g[0].dtype) for g in groups]
    return run(
        functools.partial(join_kernel, tuple(len(g) for g in groups)),
        "join",
        parts,
        [anywhere()] * len(parts),
        outs,
        [anywhere()] * len(outs),
        [pltpu.SemaphoreType.DMA((len(parts),))],
    )


def pack_kernel(w_query, w_key, w_value, w_out, out, rows_in, out_in, sems):
    copies = [
        pltpu.make_async_copy(w, rows_in.at[i], sems.at[i])
        for i, w in enumerate((w_query, w_key, w_value))
    ]
    copies.append(pltpu.make_async_copy(w_out, out_in, sems.at[3]))
    for copy in copies:
        copy.start()
    for copy in copies:
        copy.wait()
    for i in range(3):
        out[0, :, 2 * i * HD : 2 * (i + 1) * HD] = rows_in[i, :, : 2 * HD]
    parts = [jnp.transpose(out_in[...].astype(F32))]
    parts += [rows_in[i, :, 2 * HD :].astype(F32) for i in range(3)]
    out[0, :, 6 * HD :] = jnp.concatenate(parts, axis=1).astype(BF16)


def pack(w_query, w_key, w_value, w_out):
    height, span = w_query.shape
    return run(
        pack_kernel,
        "pack",
        in_hbm((w_query, w_key, w_value, w_out)),
        [anywhere()] * 4,
        (array((1, height, 4 * span), BF16),),
        [vmem()],
        [
            pltpu.VMEM((3, height, span), BF16),
            pltpu.VMEM(w_out.shape, BF16),
            pltpu.SemaphoreType.DMA((4,)),
        ],
    )[0]


def beside_kernel(first, second, out, sems):
    width = first.shape[1]
    copies = [
        pltpu.make_async_copy(ref, out.at[0, :, pl.ds(i * width, width)], sems.at[i])
        for i, ref in enumerate((first, second))
    ]
    for copy in copies:
        copy.start()
    for copy in copies:
        copy.wait()


def beside(first, second):
    height, width = first.shape
    return run(
        beside_kernel,
        "beside",
        in_hbm((first, second)),
        [anywhere()] * 2,
        (array((1, height, 2 * width), BF16),),
        [anywhere()],
        [pltpu.SemaphoreType.DMA((2,))],
    )[0]


def join_sides_kernel(count, *refs):
    parts, outs, sems = refs[:count], refs[count : count + 2], refs[count + 2]
    width = outs[0].shape[2]
    copies = []
    each = parts[0].shape[0]
    for i, part in enumerate(parts):
        for side, out in enumerate(outs):
            copies.append(
                pltpu.make_async_copy(
                    part.at[:, :, pl.ds(side * width, width)],
                    out.at[pl.ds(i * each, each)],
                    sems.at[2 * i + side],
                )
            )
    for copy in copies:
        copy.start()
    for copy in copies:
        copy.wait()


def join_sides(parts):
    count = len(parts)
    each, height, width = parts[0].shape
    out = array((count * each, height, width // 2), BF16)
    return run(
        functools.partial(join_sides_kernel, count),
        "join_sides",
        tuple(parts),
        [anywhere()] * count,
        (out, out),
        [anywhere()] * 2,
        [pltpu.SemaphoreType.DMA((2 * count,))],
    )


def fold_kernel(tail, own, got, *outs):
    body = own.shape[0] - tail
    each = body // len(outs)
    for i, out in enumerate(outs):
        at = pl.ds(i * each, each)
        total = (own[at].astype(F32) + got[at].astype(F32)).astype(BF16)
        if tail:
            out[:each] = total
        else:
            out[...] = total
    if tail:
        coded = encode(decode(own[body:]) + decode(got[body:]))
        for out in outs:
            out[each:] = coded


def fold(own, got, parts, tail=0):
    shape = ((own.shape[0] - tail) // parts + tail,) + own.shape[1:]
    return run(
        functools.partial(fold_kernel, tail),
        "fold",
        (own, got),
        [vmem()] * 2,
        (array(shape, BF16),) * parts,
        [vmem()] * parts,
    )


def fold_last_kernel(own1, got1, own2, got2, keep1, send1, keep2, send2):
    height = own2.shape[1]
    each = height + TAIL
    body = own1.shape[0] - TAIL
    coded = encode(decode(own1[body:]) + decode(got1[body:]))
    half = own2.shape[0] // 2
    for i in range(2 * half):
        out, first = (keep1, send1)[i // half], i % half * each
        at = pl.ds(i * height, height)
        out[first : first + height] = (own1[at].astype(F32) + got1[at].astype(F32)).astype(BF16)
        out[first + height : first + each] = coded
        total = own2[i].astype(F32) + got2[i].astype(F32)
        (keep2, send2)[i // half][i % half] = total.astype(BF16)


def fold_last(own1, got1, own2, got2):
    count, height, width = own2.shape
    first = array((count // 2 * (height + TAIL), width), BF16)
    second = array((count // 2, height, width), BF16)
    return run(
        fold_last_kernel,
        "fold_last",
        (own1, got1, own2, got2),
        [vmem()] * 4,
        (first, first, second, second),
        [vmem()] * 4,
    )


def fold_z_kernel(own1, got1, own2, got2, keep, send):
    height = own2.shape[1]
    each = height + TAIL
    for i, out in enumerate((keep, send)):
        at = pl.ds(i * each, height)
        out[:height] = (own1[at].astype(F32) + got1[at].astype(F32)).astype(BF16)
        at = pl.ds(i * each + height, TAIL)
        out[height:each] = encode(decode(own1[at]) + decode(got1[at]))
        out[each:] = (own2[i].astype(F32) + got2[i].astype(F32)).astype(BF16)


def fold_z(own1, got1, own2, got2):
    _, height, width = own2.shape
    out = array((2 * height + TAIL, width), BF16)
    return run(
        fold_z_kernel,
        "fold_z",
        (own1, got1, own2, got2),
        [vmem()] * 4,
        (out, out),
        [vmem()] * 2,
    )


def fold_add_kernel(own1, got1, own2, got2, out1, out2):
    for own, got, out in ((own1, got1, out1), (own2, got2, out2)):
        out[...] = (own[...].astype(F32) + got[...].astype(F32)).astype(BF16)


def fold_add(own1, got1, own2, got2):
    out = array(own1.shape, BF16)
    return run(
        fold_add_kernel,
        "fold_add",
        (own1, got1, own2, got2),
        [vmem()] * 4,
        (out, out),
        [vmem()] * 2,
    )


def fold_feed_kernel(first1, own1, got1, first2, own2, got2, keep1, send1, keep2, send2):
    width = own1.shape[2]
    half = keep1.shape[0]
    for first, own, got, outs in (
        (first1, own1, got1, (keep1, send1)),
        (first2, own2, got2, (keep2, send2)),
    ):
        for i, out in enumerate(outs):
            at = pl.ds(i * half, half)
            out[:, :, :width] = first[at]
            out[:, :, width:] = (own[at].astype(F32) + got[at].astype(F32)).astype(BF16)


def fold_feed(first1, own1, got1, first2, own2, got2):
    count, height, width = own1.shape
    out = array((count // 2, height, 2 * width), BF16)
    return run(
        fold_feed_kernel,
        "fold_feed",
        (first1, own1, got1, first2, own2, got2),
        [vmem()] * 6,
        (out,) * 4,
        [vmem()] * 4,
    )


def fold_sides_kernel(own1, got1, own2, got2, keep, send):
    width = own1.shape[2]
    half = keep.shape[0]
    for side, (own, got) in enumerate(((own1, got1), (own2, got2))):
        for i, out in enumerate((keep, send)):
            at = pl.ds(i * half, half)
            total = own[at].astype(F32) + got[at].astype(F32)
            out[:, :, side * width : (side + 1) * width] = total.astype(BF16)


def fold_sides(own1, got1, own2, got2):
    count, height, width = own1.shape
    out = array((count // 2, height, 2 * width), BF16)
    return run(
        fold_sides_kernel,
        "fold_sides",
        (own1, got1, own2, got2),
        [vmem()] * 4,
        (out, out),
        [vmem()] * 2,
    )


BY_Z = (0, 4, 2, 6)
Y_MAJOR = BY_Z + tuple(z + 1 for z in BY_Z)
OWN = tuple((0, j) for j in Y_MAJOR)
OTHER = tuple((1, j) for j in Y_MAJOR)
CHIP_NEAR = tuple((chip, z) for chip in range(2) for z in BY_Z)
CHIP_FAR = tuple((chip, z + 1) for chip in range(2) for z in BY_Z)


def split_kernel(other, info, first, second, out, sems):
    slot = 1 - info[1] if other else info[1]
    half = first.shape[1] // 2
    copies = []
    for i, values in enumerate((first, second)):
        for j in range(2):
            at = pl.ds(j * half, half)
            copies.append(
                pltpu.make_async_copy(values.at[slot, at], out.at[i, at], sems.at[2 * i + j])
            )
    for copy in copies:
        copy.start()
    for copy in copies:
        copy.wait()


def split(info, first, second, other):
    return run(
        functools.partial(split_kernel, other),
        "split",
        (info, *in_hbm((first, second))),
        [smem()] + [anywhere()] * 2,
        (array((2,) + first.shape[1:], first.dtype),),
        [vmem()],
        [pltpu.SemaphoreType.DMA((4,))],
    )[0]


def merge_kernel(info, own, got, core_own, core_got, out, sems):
    core = info[2]
    copies = []
    for half, (mine, other) in enumerate(((own, core_own), (got, core_got))):
        copies += [
            pltpu.make_async_copy(mine.at[0], out.at[half, core], sems.at[2 * half]),
            pltpu.make_async_copy(other.at[0], out.at[half, 1 - core], sems.at[2 * half + 1]),
        ]
    for copy in copies:
        copy.start()
    for copy in copies:
        copy.wait()


def merge(info, quarters):
    _, quarter, width = quarters[0].shape
    out = run(
        merge_kernel,
        "merge",
        (info, *quarters),
        [smem()] + [anywhere()] * 4,
        (array((2, 2, quarter, width), quarters[0].dtype),),
        [anywhere()],
        [pltpu.SemaphoreType.DMA((4,))],
    )[0]
    return out.reshape(4 * quarter, width)


def slots_kernel(info, own, other, out, sems):
    copies = [
        pltpu.make_async_copy(own, out.at[info[1]], sems.at[0]),
        pltpu.make_async_copy(other, out.at[1 - info[1]], sems.at[1]),
    ]
    for copy in copies:
        copy.start()
    for copy in copies:
        copy.wait()


def slots_of(info, own, other):
    return run(
        slots_kernel,
        "slots",
        (info, own, other),
        [smem()] + [anywhere()] * 2,
        (array((2,) + own.shape, own.dtype),),
        [anywhere()],
        [pltpu.SemaphoreType.DMA((2,))],
    )[0]


def tokens_add_kernel(count, mine, *rest):
    got, own, sends = rest[:count], rest[count], rest[count + 1 :]
    per = count // 2
    height = got[0].shape[0]
    for k, part in enumerate(got):
        at = k % per * height
        total = mine[k // per, pl.ds(at, height)] + part[...].astype(F32)
        if k < per:
            own[pl.ds(at, height)] = total
        else:
            each = sends[0].shape[0]
            for first in range(0, height, each):
                sends[(at + first) // each][...] = total[first : first + each].astype(BF16)


def tokens_add(mine, got):
    _, quarter, width = mine.shape
    send = array((quarter // 2, width), BF16)
    return run(
        functools.partial(tokens_add_kernel, len(got)),
        "tokens_add",
        (mine, *got),
        [vmem()] * (1 + len(got)),
        (array((quarter, width), F32), send, send),
        [vmem()] * 3,
    )


def tokens_out_kernel(info, own, *rest):
    *got, out = rest
    out[info[1]] = own[...]
    height = got[0].shape[0]
    for k, part in enumerate(got):
        out[1 - info[1], pl.ds(k * height, height), :] = part[...].astype(F32)


def tokens_out(info, own, got):
    return run(
        tokens_out_kernel,
        "tokens_out",
        (info, own, *got),
        [smem()] + [vmem()] * (1 + len(got)),
        (array((2,) + own.shape, F32),),
        [vmem()],
    )[0]


def feed_out_kernel(own, got, up, down):
    half = up.shape[1] // 2
    for i in range(4):
        at = pl.ds(i * half, half)
        total = own[0, :, at].astype(F32) + got[0, :, at].astype(F32)
        out = (down, up)[i % 2]
        out[:, pl.ds(i // 2 * half, half)] = total


def feed_out(own, got):
    _, height, width = own.shape
    out = array((height, width // 2), F32)
    return run(
        feed_out_kernel,
        "feed_out",
        (own, got),
        [vmem()] * 2,
        (out, out),
        [vmem()] * 2,
    )


def attend_out_kernel(a, b, query, key, value, out, gain1, bias1, gain2, bias2):
    height = query.shape[0]

    def both(first, last):
        return a[first:last].astype(F32) + b[first:last].astype(F32)

    one = both(0, height)
    two = both(height + TAIL, 2 * height + TAIL)
    at = pl.ds(height, TAIL)
    sums = decode(a[at]) + decode(b[at])
    for i, ref in enumerate((query, key, value)):
        ref[...] = jnp.concatenate(
            [two[:, 2 * i * HD : 2 * (i + 1) * HD], one[:, (3 + i) * HD : (4 + i) * HD]], axis=1
        )
    out[...] = jnp.transpose(one[:, : 3 * HD])
    for i, ref in enumerate((gain1, bias1, gain2, bias2)):
        ref[...] = jnp.concatenate([sums[i], sums[4 + i]], axis=0)


def attend_out(pieces, height):
    cols = pieces[0].shape[1]
    span = cols // 2
    return run(
        attend_out_kernel,
        "attend_out",
        tuple(pieces),
        [vmem()] * 2,
        (array((height, span), F32),) * 3
        + (array((span, height), F32),)
        + (array((2 * cols,), F32),) * 4,
        [vmem()] * 8,
    )


def fast_path(info, tokens, cotangent, weights, lengths, masks, norms):
    w_query, w_key, w_value, w_out, w_up, w_down = weights
    mask_own, mask_other, mask_ends = masks
    g_one, b_one, g_two, b_two = norms
    height, features, units = w_query.shape[0], tokens.shape[2], w_up.shape[1]
    flat = (tuple((0, j) for j in Y_MAJOR),)
    got_rows = flip_chip(split(info, tokens, cotangent, True))
    piece = pack(w_query, w_key, w_value, w_out)
    got_piece = flip_dp(piece, 4)
    own_rows = split(info, tokens, cotangent, False)
    (two_attn,) = join([piece, got_piece])
    got_attn = flip_dp(two_attn, 2)
    feed_piece = beside(w_up, w_down.T)
    got_feed = flip_dp(feed_piece, 4)
    z_pair, z_single = join_sides([two_attn, got_attn])
    y_pair, x_single = flip_dp(z_pair, 1), flip_chip(z_single)
    own_pair, near_single = join([z_pair, y_pair], [z_single, x_single])
    other_pair, far_single = flip_chip(own_pair), flip_dp(near_single, 1)
    single_w = ((near_single, far_single), (CHIP_NEAR, CHIP_FAR))
    two_up, two_down = join_sides([feed_piece, got_feed])
    got_up, got_down = flip_dp(two_up, 2), flip_dp(two_down, 2)
    quarters = (own_rows, got_rows, flip_core(own_rows), flip_core(got_rows))
    tok = merge(info, quarters)
    own01 = attend(info, lengths, tok, ((own_pair,), flat), True, mask_own[:2])
    z_up, z_down = join([two_up, got_up], [two_down, got_down])
    y_up, x_down = flip_dp(z_up, 1), flip_chip(z_down)
    other01 = attend(info, lengths, tok, ((other_pair,), flat), True, mask_other[:2])
    ends = attend(info, lengths, tok, single_w, False, mask_ends)
    own_up, near_down = join([z_up, y_up], [z_down, x_down])
    other_up, far_down = flip_chip(own_up), flip_dp(near_down, 1)
    up = ((own_up, other_up), (OWN, OTHER))
    down = ((near_down, far_down), (CHIP_NEAR, CHIP_FAR))
    contexts = (own01[3], other01[3], ends[3])
    attn_part = project(info, contexts, single_w, features)
    attn_got = flip_cores(attn_part)
    normal, scale_one, hn = norm_one(tok, attn_part, attn_got, g_one, b_one)
    act1, slope1 = feed_up(info, hn, ((own_up,), flat), units)
    tok_turned, hn_turned = turn_rows(info, tok, hn, Y_MAJOR)
    act2, slope2 = feed_up(info, hn, ((other_up,), flat), units)
    mixed = feed_down(info, act1, act2, down, features)
    mixed_got = flip_cores(mixed)
    own_out, send_out, dzb_two, sums_two = norm_two(
        info, lengths, hn, mixed, mixed_got, quarters, g_two, b_two
    )
    keep_d1, send_d1, keep_d2, send_d2 = feed_grad(
        info, dzb_two, act1, act2, (OWN, OTHER, CHIP_NEAR, CHIP_FAR), False
    )
    got_d1, got_d2 = flip_chip(send_d1), flip_dp(send_d2, 1)
    du1, du2, *back = feed_back(info, dzb_two, slope1, slope2, up, down)
    back_got = flip_cores(back)
    keep_u1, send_u1, keep_u2, send_u2 = feed_grad(
        info, hn_turned, du1, du2, (OWN, OTHER, CHIP_NEAR, CHIP_FAR), True
    )
    got_u1, got_u2 = flip_chip(send_u1), flip_dp(send_u2, 1)
    sum_d1, sum_d2 = fold_add(keep_d1, got_d1, keep_d2, got_d2)
    dzb_one, sums_one = norm_one_back(normal, scale_one, dzb_two, back, back_got, g_one)
    d_ends = attend_back(info, dzb_one, single_w, None, ends)
    keep_f1, send_f1, keep_f2, send_f2 = fold_feed(
        sum_d1, keep_u1, got_u1, sum_d2, keep_u2, got_u2
    )
    got_f1, got_f2 = flip_dp(send_f1, 1), flip_chip(send_f2)
    keep_s, send_s = single_grad(
        info, tok_turned, d_ends, dzb_one, contexts, sums_one, sums_two, Y_MAJOR
    )
    d_other = attend_back(info, dzb_one, single_w, 1, other01)
    grad_b = pair_grad(tok_turned, d_other, len(OWN))
    got_b = flip_chip(grad_b)
    (send_s1,) = join([send_s])
    got_s = flip_dp(send_s1, 1)
    keep_f, send_f = fold_sides(keep_f1, got_f1, keep_f2, got_f2)
    got_f = flip_dp(send_f, 2)
    d_own = attend_back(info, dzb_one, single_w, 0, own01)
    grad_a = pair_grad(tok_turned, d_own, len(OWN))
    keep_a, send_a = fold(grad_a, got_b, 2, 0)
    got_a = flip_dp(send_a, 1)
    keep_s2, send_s2 = fold(keep_s, got_s, 2, TAIL)
    got_s2 = flip_chip(send_s2)
    mine, *sent = input_back(
        info, d_own, d_other, d_ends, dzb_one, ((own_pair, other_pair), (OWN, OTHER)), single_w
    )
    keep_f3, send_f3 = fold(keep_f, got_f, 2, 0)
    got_f3 = flip_dp(send_f3, 4)
    keep_s3, send_s3, keep_a3, send_a3 = fold_last(keep_s2, got_s2, keep_a, got_a)
    got_s3, got_a3 = flip_dp(send_s3, 2), flip_dp(send_a3, 2)
    sent_parts = join(*[[v] for v in sent])
    sent_got = flip_cores(sent_parts)
    own_tok, *send_tok = tokens_add(mine, sent_got)
    got_tok = [flip_chip(v) for v in send_tok]
    got_out = flip_chip(send_out)
    keep_z, send_z = fold_z(keep_s3, got_s3, keep_a3, got_a3)
    got_z = flip_dp(send_z, 4)
    grad_tokens = tokens_out(info, own_tok, got_tok)
    output = slots_of(info, own_out, got_out)
    grad_up, grad_down = feed_out(keep_f3, got_f3)
    grads = attend_out((keep_z, got_z), height)
    return (output, grad_tokens, *grads[:4], grad_up, grad_down.T, *grads[4:])


def plain_path(info, tokens, cotangent, weights, lengths, masks, norms):
    w_query, w_key, w_value, w_out, w_up, w_down = weights
    mask_own, mask_other, mask_ends = masks
    g_one, b_one, g_two, b_two = norms
    features, units = tokens.shape[2], w_up.shape[1]
    flat = (((0, 0),),)
    two = (((0, 0),), ((1, 0),))

    def gathered(piece):
        own = lax.all_gather(piece, "dp", axis=0, tiled=True)[None]
        return own, flip_chip(own)

    got_rows = flip_chip(split(info, tokens, cotangent, True))
    own_rows = split(info, tokens, cotangent, False)
    quarters = (own_rows, got_rows, flip_core(own_rows), flip_core(got_rows))
    tok = merge(info, quarters)
    firsts = [w[:, : 2 * HD] for w in (w_query, w_key, w_value)]
    thirds = [w_out.T] + [w[:, 2 * HD :] for w in (w_query, w_key, w_value)]
    pair_w = (gathered(jnp.concatenate(firsts, axis=1)), two)
    single_w = (gathered(jnp.concatenate(thirds, axis=1)), two)
    up, down = (gathered(w_up), two), (gathered(w_down.T), two)
    own01 = attend(info, lengths, tok, ((pair_w[0][0],), flat), True, mask_own[:2])
    other01 = attend(info, lengths, tok, ((pair_w[0][1],), flat), True, mask_other[:2])
    ends = attend(info, lengths, tok, single_w, False, mask_ends)
    contexts = (own01[3], other01[3], ends[3])
    part = project(info, contexts, single_w, features)
    normal, scale_one, hn = norm_one(tok, part, flip_cores(part), g_one, b_one)
    act1, slope1 = feed_up(info, hn, ((up[0][0],), flat), units)
    act2, slope2 = feed_up(info, hn, ((up[0][1],), flat), units)
    tok_turned, hn_turned = turn_rows(info, tok, hn, (0,))
    part = feed_down(info, act1, act2, down, features)
    own_out, send_out, dzb_two, sums_two = norm_two(
        info, lengths, hn, part, flip_cores(part), quarters, g_two, b_two
    )
    places = (((0, 0),), ((1, 0),)) * 2
    grad_d = feed_grad(info, dzb_two, act1, act2, places, False)
    du1, du2, *part = feed_back(info, dzb_two, slope1, slope2, up, down)
    grad_u = feed_grad(info, hn_turned, du1, du2, places, True)
    dzb_one, sums_one = norm_one_back(
        normal, scale_one, dzb_two, part, flip_cores(part), g_one
    )
    d_ends = attend_back(info, dzb_one, single_w, None, ends)
    keep_s, send_s = single_grad(
        info, tok_turned, d_ends, dzb_one, contexts, sums_one, sums_two, (0,)
    )
    d_other = attend_back(info, dzb_one, single_w, 1, other01)
    grad_b = pair_grad(tok_turned, d_other, 1)
    d_own = attend_back(info, dzb_one, single_w, 0, own01)
    grad_a = pair_grad(tok_turned, d_own, 1)
    mine, *sent = input_back(info, d_own, d_other, d_ends, dzb_one, pair_w, single_w)
    own_tok, *send_tok = tokens_add(mine, flip_cores(sent))
    output = slots_of(info, own_out, flip_chip(send_out))
    grad_tokens = tokens_out(info, own_tok, [flip_chip(v) for v in send_tok])

    def summed(own, other):
        total = own.astype(F32) + flip_chip(other).astype(F32)
        return lax.psum_scatter(total, "dp", scatter_dimension=0, tiled=True)

    def wide(keep1, send1, keep2, send2):
        return jnp.concatenate([summed(keep1[0], send1[0]), summed(keep2[0], send2[0])], axis=1)

    single = summed(keep_s[:features], send_s[:features])
    pair = summed(grad_a[0], grad_b[0])
    grads = [
        jnp.concatenate(
            [pair[:, 2 * i * HD : 2 * (i + 1) * HD], single[:, (3 + i) * HD : (4 + i) * HD]],
            axis=1,
        )
        for i in range(3)
    ] + [single[:, : 3 * HD].T]
    sums = decode(keep_s[features:])
    sums = lax.psum(sums + flip_chip(sums), "dp")
    sums = [jnp.concatenate([sums[i], sums[4 + i]]) for i in range(4)]
    return (output, grad_tokens, *grads, wide(*grad_u), wide(*grad_d).T, *sums)


def local(
    tokens,
    w_query,
    w_key,
    w_value,
    w_out,
    w_up,
    w_down,
    gain_attn,
    bias_attn,
    gain_ffn,
    bias_ffn,
    lengths,
    random_blocks,
    cotangent,
):
    ORDER.clear()
    size = lax.axis_size("dp")
    rank = lax.axis_index("mp")
    me = lax.axis_index("dp")
    x, core = rank // 2, rank % 2
    quarter = tokens.shape[1]
    seq = 4 * quarter
    height = w_query.shape[0]
    span = w_query.shape[1]
    heads = span // HD
    nblocks = seq // BLOCK
    fast = size == 8 and height % 16 == 0

    shift = x * (seq // 2)
    info = jnp.stack([me, x, core, shift]).astype(jnp.int32)

    blocks = (jnp.arange(nblocks) + x * (nblocks // 2)) % nblocks
    near_blocks = jnp.abs(blocks[:, None] - blocks[None, :]) <= 1
    edge = (blocks == 0) | (blocks == nblocks - 1)
    fixed = near_blocks | edge[:, None] | edge[None, :]

    def table(shard):
        chosen = lax.dynamic_slice_in_dim(random_blocks, shard * heads, heads, 0)
        chosen = jnp.roll(chosen, -x * (nblocks // 2), axis=1)
        hit = jnp.any(chosen[:, None, :, :] == blocks[None, :, None, None], axis=3)
        bias = jnp.where(fixed.T[None] | hit, 0.0, NEGATIVE)
        return jnp.concatenate(
            [
                jnp.zeros((heads, nblocks, HD), F32),
                bias,
                jnp.full((heads, nblocks, 3), -1.0, F32),
                jnp.zeros((heads, nblocks, HD - 3 - nblocks), F32),
            ],
            axis=2,
        )

    mask_own, mask_other = table(rank), table(rank ^ 2)
    mask_ends = jnp.concatenate([mask_own[2:], mask_other[2:]], axis=0)
    g_one, b_one = gain_attn[None], bias_attn[None]
    g_two, b_two = gain_ffn[None], bias_ffn[None]

    path = fast_path if fast else plain_path
    return path(
        info,
        tokens,
        cotangent,
        (w_query, w_key, w_value, w_out, w_up, w_down),
        lengths,
        (mask_own, mask_other, mask_ends),
        (g_one, b_one, g_two, b_two),
    )


def solution(mesh):
    return jax.shard_map(
        local,
        mesh=mesh,
        in_specs=(
            P("dp", "mp", None),
            P("dp", "mp"),
            P("dp", "mp"),
            P("dp", "mp"),
            P("mp", "dp"),
            P("dp", "mp"),
            P("mp", "dp"),
            P(),
            P(),
            P(),
            P(),
            P("dp"),
            P(),
            P("dp", "mp", None),
        ),
        out_specs=(
            P("dp", "mp", None),
            P("dp", "mp", None),
            P("dp", "mp"),
            P("dp", "mp"),
            P("dp", "mp"),
            P("mp", "dp"),
            P("dp", "mp"),
            P("mp", "dp"),
            P(),
            P(),
            P(),
            P(),
        ),
        check_vma=False,
    )
```

```python
import functools

import jax
import jax.numpy as jnp
from jax import lax
from jax.experimental import pallas as pl
from jax.experimental.pallas import tpu as pltpu
from jax.sharding import PartitionSpec as P

HD = 64
BLOCK = 64
LANES = 128
TILE = 256
SENT = 256
EPSILON = 1e-12
TAIL = 32
TOKEN = (8, 128)
ROOM = {
    "attend": 28,
    "attend_back": 28,
    "project": 12,
    "input_back": 24,
    "norm_one": 12,
    "norm_two": 18,
    "norm_one_back": 14,
    "feed_up": 16,
    "feed_down": 18,
    "feed_back": 32,
    "turn_rows": 12,
    "feed_grad": 24,
    "pair_grad": 16,
    "single_grad": 24,
    "join": 1,
    "join_sides": 1,
    "beside": 1,
    "pack": 2,
    "split": 4,
    "merge": 1,
    "fold": 6,
    "fold_add": 8,
    "fold_feed": 10,
    "fold_sides": 8,
    "fold_last": 6,
    "fold_z": 4,
    "slots": 1,
    "tokens_add": 8,
    "tokens_out": 8,
    "feed_out": 6,
    "attend_out": 6,
}
SCALE = 0.125
LOG2E = 1.4426950408889634
LN2 = 0.6931471805599453
NEGATIVE = -1e30
F32 = jnp.float32
BF16 = jnp.bfloat16

CORE_SWAP = [(0, 1), (1, 0), (2, 3), (3, 2)]
CHIP_SWAP = [(0, 2), (2, 0), (1, 3), (3, 1)]


def nn(a, b):
    return lax.dot_general(a, b, (((1,), (0,)), ((), ())), preferred_element_type=F32)


def nt(a, b):
    return lax.dot_general(a, b, (((1,), (1,)), ((), ())), preferred_element_type=F32)


def tn(a, b):
    return lax.dot_general(a, b, (((0,), (0,)), ((), ())), preferred_element_type=F32)


def vmem():
    return pl.BlockSpec(memory_space=pltpu.VMEM)


def smem():
    return pl.BlockSpec(memory_space=pltpu.SMEM)


def anywhere():
    return pl.BlockSpec(memory_space=pl.ANY)


def in_hbm(values):
    return tuple(pltpu.with_memory_space_constraint(v, pltpu.HBM) for v in values)


def array(shape, dtype):
    return jax.ShapeDtypeStruct(shape, dtype)


ORDER = []


def run(kernel, name, args, specs, outs, out_specs, scratch=()):
    given, made = len(args), len(outs)
    extra = tuple(ORDER)

    def body(*refs):
        ins, rest = refs[:given], refs[given + len(extra) :]
        rest[made][...] = jnp.zeros(TOKEN, F32)
        kernel(*ins, *rest[:made], *rest[made + 1 :])

    results = pl.pallas_call(
        body,
        out_shape=tuple(outs) + (array(TOKEN, F32),),
        in_specs=list(specs) + [anywhere()] * len(extra),
        out_specs=tuple(out_specs) + (vmem(),),
        scratch_shapes=list(scratch),
        compiler_params=pltpu.CompilerParams(vmem_limit_bytes=ROOM[name] * 2**20),
        cost_estimate=pl.CostEstimate(flops=1, bytes_accessed=0, transcendentals=0),
        name=name,
    )(*args, *extra)
    ORDER[:] = [results[-1]]
    return results[:-1]


def put_rows(parts, t, value):
    height, tile = parts[0].shape[0], value.shape[0]
    if height <= tile:
        per = tile // height
        for k in range(per):
            parts[t * per + k][...] = value[k * height : (k + 1) * height]
    else:
        per = height // tile
        parts[t // per][pl.ds(t % per * tile, tile), :] = value


def get_sum(parts, more, t):
    height = parts[0].shape[0]
    if height <= TILE:
        per = TILE // height
        at = range(t * per, (t + 1) * per)
        pieces = [parts[k][...].astype(F32) + more[k][...].astype(F32) for k in at]
        return pieces[0] if per == 1 else jnp.concatenate(pieces, axis=0)
    per = height // TILE
    at = pl.ds(t % per * TILE, TILE)
    return parts[t // per][at, :].astype(F32) + more[t // per][at, :].astype(F32)


def tile_rows(ref, tile=TILE):
    return [(t, pl.ds(t * tile, tile)) for t in range(ref.shape[0] // tile)]


def far(shape, dtype):
    return pltpu.HBM(shape, dtype)


def tiles(seq, width, height):
    parts = (array((height, width), BF16),) * (seq // height)
    return parts, [vmem()] * len(parts)


def place(me, refs, slots, dst_ref, first=0, last=None, only=None, to=0):
    for ref, of in zip(refs, slots):
        height, width = ref.shape[1], ref.shape[2]
        end = width if last is None else last
        for e, (chip, j) in enumerate(of):
            if only is not None and chip != only:
                continue
            at = 0 if height == dst_ref.shape[0] else pl.multiple_of((me ^ j) * height, height)
            at_column = to + (0 if only is not None else chip * (end - first))
            dst_ref[pl.ds(at, height), pl.ds(at_column, end - first)] = ref[e, :, first:end]


def pick(me, fulls, out_ref, slots, first):
    _, height, width = out_ref.shape
    for e, (chip, j) in enumerate(slots):
        full = fulls[chip]
        at = 0 if height == full.shape[0] else pl.multiple_of((me ^ j) * height, height)
        out_ref[e] = full[pl.ds(at, height), pl.ds(first, width)]


def attend_kernel(slots, columns, only, places, info, lengths, tok, mask, *rest):
    refs, (qa, ka, va, ctx, wfull) = rest[: len(slots)], rest[len(slots) :]
    seq = tok.shape[0]
    place(info[0], refs, slots, wfull, *columns, only)
    lane = lax.broadcasted_iota(jnp.int32, (TILE, LANES), 1)
    row0 = lax.broadcasted_iota(jnp.int32, (TILE, LANES), 0)
    for t in range(seq // TILE):
        at = pl.ds(t * TILE, TILE)
        row = row0 + t * TILE
        made = nn(tok[at, :], wfull[...])
        onehot = jnp.where(lane - HD == row // BLOCK, 1.0, 0.0)[:, HD:]
        position = row + info[3]
        position = jnp.where(position >= seq, position - seq, position)
        dead = (position >= lengths[info[1]]) & (lane >= HD) & (lane < HD + 16)
        for h, (q_at, k_at, v_at) in enumerate(places):
            q = made[:, q_at : q_at + HD] * (SCALE * LOG2E)
            k = made[:, k_at : k_at + HD]
            v = made[:, v_at : v_at + HD]
            qa[h, at, :] = jnp.concatenate([q, onehot], axis=1).astype(BF16)
            per = TILE // BLOCK
            table = jnp.concatenate(
                [
                    jnp.broadcast_to(mask[h, t * per + b : t * per + b + 1, :], (BLOCK, LANES))
                    for b in range(per)
                ],
                axis=0,
            )
            table = jnp.where(dead, NEGATIVE, table)
            ka[h, at, :] = jnp.concatenate([k, table[:, HD:]], axis=1).astype(BF16)
            va[h, at, :] = jnp.concatenate([v, jnp.full((TILE, HD), -1.0, F32)], axis=1).astype(BF16)
    lane = lax.broadcasted_iota(jnp.int32, (2 * TILE, LANES), 1)
    for t in range(seq // TILE // 2):
        at = pl.ds(t * 2 * TILE, 2 * TILE)
        pieces = []
        for h in range(len(places)):
            q = qa[h, at, :]
            s = nt(q, ka[h])
            top = jnp.max(s, axis=1, keepdims=True)
            p = jnp.exp2(s - top).astype(BF16)
            got = nn(p, va[h])
            total = -got[:, HD:]
            pieces.append(got[:, :HD] / total)
            log = top + jnp.log2(-got)
            hi = log.astype(BF16).astype(F32)
            mid = (log - hi).astype(BF16).astype(F32)
            low = log - hi - mid
            new = jnp.where(
                lane == HD + 16,
                hi,
                jnp.where(lane == HD + 17, mid, jnp.where(lane == HD + 18, low, q.astype(F32))),
            )
            qa[h, at, :] = new.astype(BF16)
        ctx[at, :] = jnp.concatenate(pieces, axis=1).astype(BF16)


PAIR = ((0, 2 * HD, 4 * HD), (HD, 3 * HD, 5 * HD))
SINGLES = ((HD, 2 * HD, 3 * HD), (5 * HD, 6 * HD, 7 * HD))


def attend(info, lengths, tok, gathered, pair, mask):
    arrays, slots = gathered
    seq, width = tok.shape
    aug = far((2, seq, LANES), BF16)
    columns, only, cols = ((0, 6 * HD), 0, 6 * HD) if pair else ((2 * HD, 6 * HD), None, 8 * HD)
    return run(
        functools.partial(attend_kernel, slots, columns, only, PAIR if pair else SINGLES),
        "attend",
        (info, lengths, tok, mask) + arrays,
        [smem()] * 2 + [vmem()] * (2 + len(arrays)),
        (aug, aug, aug, array((seq, LANES), BF16)),
        [vmem()] * 4,
        [pltpu.VMEM((width, cols), BF16)],
    )


def place_out(me, refs, slots, pairs, ends):
    place(me, refs, slots, pairs, 0, 2 * HD)
    place(me, refs, slots, ends, 2 * HD, 4 * HD)
    both = ends[...]
    ends[:, :LANES] = jnp.concatenate([both[:, :HD], both[:, LANES : LANES + HD]], axis=1)


def project_kernel(slots, info, own, other, ends, *rest):
    refs, parts, (w1, w2) = rest[: len(slots)], rest[len(slots) : -2], rest[-2:]
    place_out(info[0], refs, slots, w1, w2)
    for t, at in tile_rows(own):
        both = jnp.concatenate([own[at, :], other[at, :]], axis=1)
        out = nt(both, w1[...]) + nt(ends[at, :], w2[:, :LANES])
        put_rows(parts, t, out.astype(BF16))


def project(info, contexts, gathered, width):
    arrays, slots = gathered
    seq = contexts[0].shape[0]
    return run(
        functools.partial(project_kernel, slots),
        "project",
        (info,) + contexts + arrays,
        [smem()] + [vmem()] * (3 + len(arrays)),
        *tiles(seq, width, 2 * TILE),
        [pltpu.VMEM((width, 2 * LANES), BF16)] * 2,
    )


def attend_back_kernel(slots, chip, info, dz, qa, ka, va, ctx, *rest):
    refs, (dqkv, pairs, ends, da) = rest[: len(slots)], rest[len(slots) :]
    seq = dz.shape[0]
    heads = qa.shape[0]
    if chip is None:
        place_out(info[0], refs, slots, pairs, ends)
        wfull = ends.at[:, pl.ds(0, LANES)]
    else:
        place(info[0], refs, slots, pairs, 0, 2 * HD, chip)
        wfull = pairs.at[:, pl.ds(0, LANES)]
    lane = lax.broadcasted_iota(jnp.int32, (TILE, LANES), 1)
    for t in range(seq // TILE):
        at = pl.ds(t * TILE, TILE)
        dctx = nn(dz[at, :], wfull[...]).astype(BF16).astype(F32)
        both = dctx * ctx[at, :].astype(F32)
        for h in range(heads):
            inner = jnp.sum(both[:, h * HD : (h + 1) * HD], axis=1, keepdims=True)
            hi = inner.astype(BF16).astype(F32)
            mid = (inner - hi).astype(BF16).astype(F32)
            low = inner - hi - mid
            one = jnp.concatenate(
                [dctx[:, h * HD : (h + 1) * HD], jnp.zeros((TILE, HD), F32)], axis=1
            )
            one = jnp.where(lane == HD, hi, one)
            one = jnp.where(lane == HD + 1, mid, one)
            one = jnp.where(lane == HD + 2, low, one)
            da[h, at, :] = one.astype(BF16)

    def turned(values):
        return jnp.transpose(values.astype(F32))[:HD].astype(BF16)

    grads = []
    for h in range(heads):
        k_turned, q_turned, d_turned = turned(ka[h]), turned(qa[h]), turned(da[h])
        dq, dk, dv = None, [], []
        for t in range(seq // TILE):
            at = pl.ds(t * TILE, TILE)
            p = jnp.exp2(nt(ka[h, at, :], qa[h]))
            ds = (p * nt(va[h, at, :], da[h])).astype(BF16)
            dv.append(nt(d_turned, p.astype(BF16)))
            dk.append(nt(q_turned, ds))
            more = nn(k_turned[:, t * TILE : (t + 1) * TILE], ds)
            dq = more if dq is None else dq + more
        dk = jnp.concatenate(dk, axis=1) * LN2
        grads.append((dq * SCALE, dk, jnp.concatenate(dv, axis=1)))
    (dq0, dk0, dv0), (dq1, dk1, dv1) = grads
    if chip is None:
        blank = jnp.zeros_like(dq0)
        stacks = ((blank, dq0), (dk0, dv0), (blank, dq1), (dk1, dv1))
    else:
        stacks = ((dq0, dq1), (dk0, dk1), (dv0, dv1))
    for i, stack in enumerate(stacks):
        both = jnp.transpose(jnp.concatenate(stack, axis=0))
        dqkv[:, i * LANES : (i + 1) * LANES] = both.astype(BF16)


def attend_back(info, dz, gathered, chip, saved):
    arrays, slots = gathered
    qa, ka, va, ctx = saved
    seq, width = dz.shape
    cols = 8 * HD if chip is None else 6 * HD
    return run(
        functools.partial(attend_back_kernel, slots, chip),
        "attend_back",
        (info, dz, qa, ka, va, ctx) + arrays,
        [smem()] + [vmem()] * (5 + len(arrays)),
        (array((seq, cols), BF16),),
        [vmem()],
        [
            pltpu.VMEM((width, 2 * LANES), BF16),
            pltpu.VMEM((width, 2 * LANES), BF16),
            pltpu.VMEM((2, seq, LANES), BF16),
        ],
    )[0]


def input_back_kernel(slots1, slots2, info, own, other, ends, dz, *rest):
    n1, n2 = len(slots1), len(slots2)
    refs1, refs2, (mine, *sent, w1, w2) = rest[:n1], rest[n1 : n1 + n2], rest[n1 + n2 :]
    place(info[0], refs1, slots1, w1)
    place(info[0], refs2, slots2, w2, 2 * HD, 6 * HD)
    per = len(sent) // 2
    height = sent[0].shape[0]
    for half in range(dz.shape[0] // TILE // 2):
        for whose in range(2):
            tile = 2 * half + (info[2] if whose == 0 else 1 - info[2])
            at = pl.ds(pl.multiple_of(tile * TILE, TILE), TILE)
            pairs = jnp.concatenate([own[at, :], other[at, :]], axis=1)
            back = nt(pairs, w1[...]) + nt(ends[at, :], w2[...])
            if whose == 0:
                mine[half] = back + dz[at, :].astype(F32)
                continue
            for k in range(per):
                part = back[k * height : (k + 1) * height]
                sent[half * per + k][...] = part.astype(BF16)


def input_back(info, own, other, ends, dz, gathered1, gathered2):
    seq, width = dz.shape
    arrays = gathered1[0] + gathered2[0]
    halves = (seq // TILE // 2, TILE, width)
    grads = (own, other, ends, dz)
    return run(
        functools.partial(input_back_kernel, gathered1[1], gathered2[1]),
        "input_back",
        (info,) + grads + arrays,
        [smem()] + [vmem()] * (len(grads) + len(arrays)),
        (array(halves, F32),) + (array((SENT, width), BF16),) * (seq // 2 // SENT),
        [vmem()] * (1 + seq // 2 // SENT),
        [pltpu.VMEM((width, 12 * HD), BF16), pltpu.VMEM((width, 8 * HD), BF16)],
    )


def center(z):
    mean = jnp.mean(z, axis=1, keepdims=True)
    moved = z - mean
    spread = jnp.mean(moved * moved, axis=1, keepdims=True)
    scale = lax.rsqrt(spread + EPSILON)
    return moved * scale, scale


def norm_back(n, scale, gy, gain):
    dn = gy * gain
    return scale * (
        dn - jnp.mean(dn, axis=1, keepdims=True) - n * jnp.mean(dn * n, axis=1, keepdims=True)
    )


def add_sums(gy, n, sums):
    more = [jnp.sum(v, axis=0, keepdims=True) for v in (gy * n, gy)]
    return more if sums is None else [a + b for a, b in zip(sums, more)]


def norm_one_kernel(tok, gain, bias, *rest):
    *parts, normal, scale, hn = rest
    count = len(parts) // 2
    for t, at in tile_rows(tok):
        value = tok[at, :].astype(F32) + get_sum(parts[:count], parts[count:], t)
        n, r = center(value)
        normal[at, :] = n.astype(BF16)
        scale[at, :] = r
        hn[at, :] = (n * gain[...] + bias[...]).astype(BF16)


def norm_one(tok, p0, p1, gain, bias):
    seq, width = tok.shape
    return run(
        norm_one_kernel,
        "norm_one",
        (tok, gain, bias, *p0, *p1),
        [vmem()] * (3 + len(p0) + len(p1)),
        (array((seq, width), BF16), array((seq, 1), F32), array((seq, width), BF16)),
        [vmem()] * 3,
    )


def norm_two_kernel(info, lengths, hn, own, got, core_own, core_got, gain, bias, *rest):
    *parts, own_out, send_out, dzb, sums, out = rest
    count = len(parts) // 2
    seq = hn.shape[0]
    total = None
    for t, at in tile_rows(hn):
        value = hn[at, :].astype(F32) + get_sum(parts[:count], parts[count:], t)
        n, scale = center(value)
        out[at, :] = (n * gain[...] + bias[...]).astype(BF16)
        position = lax.broadcasted_iota(jnp.int32, (TILE, 1), 0) + t * TILE + info[3]
        position = jnp.where(position >= seq, position - seq, position)
        valid = jnp.where(position < lengths[info[1]], 1.0, 0.0)
        mine, others = ((own, core_own), (got, core_got))[t // 2]
        cot = jnp.where(info[2] == t % 2, mine[1].astype(F32), others[1].astype(F32))
        gy = cot * valid
        dzb[at, :] = norm_back(n, scale, gy, gain[...]).astype(BF16)
        total = add_sums(gy, n, total)
    sums[...] = jnp.concatenate(total, axis=0)
    for half, ref in enumerate((own_out, send_out)):
        at = pl.multiple_of((2 * half + info[2]) * TILE, TILE)
        ref[...] = out[pl.ds(at, TILE), :]


def norm_two(info, lengths, hn, m0, m1, cot, gain, bias):
    seq, width = hn.shape
    return run(
        norm_two_kernel,
        "norm_two",
        (info, lengths, hn, *cot, gain, bias, *m0, *m1),
        [smem()] * 2 + [vmem()] * (3 + len(cot) + len(m0) + len(m1)),
        (
            array((TILE, width), BF16),
            array((TILE, width), BF16),
            array((seq, width), BF16),
            array((2, width), F32),
        ),
        [vmem()] * 4,
        [pltpu.VMEM((seq, width), BF16)],
    )


def norm_one_back_kernel(normal, scale, dz2, gain, *rest):
    *parts, dzb, sums = rest
    count = len(parts) // 2
    total = None
    for t, at in tile_rows(dz2):
        n = normal[at, :].astype(F32)
        gy = dz2[at, :].astype(F32) + get_sum(parts[:count], parts[count:], t)
        dzb[at, :] = norm_back(n, scale[at, :], gy, gain[...]).astype(BF16)
        total = add_sums(gy, n, total)
    sums[...] = jnp.concatenate(total, axis=0)


def norm_one_back(normal, scale, dz2, p0, p1, gain):
    seq, width = normal.shape
    return run(
        norm_one_back_kernel,
        "norm_one_back",
        (normal, scale, dz2, gain, *p0, *p1),
        [vmem()] * (4 + len(p0) + len(p1)),
        (array((seq, width), BF16), array((2, width), F32)),
        [vmem()] * 2,
    )


def gelu_pair(u):
    phi = 0.5 + 0.5 * lax.erf(u * 0.7071067811865476)
    return u * phi, phi + u * (jnp.exp(-0.5 * u * u) * 0.3989422804014327)


def feed_up_kernel(slots, info, hn, *rest):
    refs, (active, slope, wfull) = rest[: len(slots)], rest[len(slots) :]
    place(info[0], refs, slots, wfull)
    for _, at in tile_rows(hn):
        a, g = gelu_pair(nn(hn[at, :], wfull[...]))
        active[at, :] = a.astype(BF16)
        slope[at, :] = g.astype(BF16)


def feed_up(info, hn, gathered, units):
    arrays, slots = gathered
    seq, width = hn.shape
    return run(
        functools.partial(feed_up_kernel, slots),
        "feed_up",
        (info, hn) + arrays,
        [smem()] + [vmem()] * (1 + len(arrays)),
        (array((seq, units), BF16), array((seq, units), BF16)),
        [vmem()] * 2,
        [pltpu.VMEM((width, units), BF16)],
    )


def feed_down_kernel(slots, info, act1, act2, *rest):
    refs, parts, wfull = rest[: len(slots)], rest[len(slots) : -1], rest[-1]
    place(info[0], refs, slots, wfull)
    for t, at in tile_rows(act1):
        both = jnp.concatenate([act1[at, :], act2[at, :]], axis=1)
        put_rows(parts, t, nt(both, wfull[...]).astype(BF16))


def feed_down(info, act1, act2, gathered, width):
    seq, units = act1.shape
    arrays, slots = gathered
    return run(
        functools.partial(feed_down_kernel, slots),
        "feed_down",
        (info, act1, act2) + arrays,
        [smem()] + [vmem()] * (2 + len(arrays)),
        *tiles(seq, width, seq),
        [pltpu.VMEM((width, 2 * units), BF16)],
    )


def feed_back_kernel(slots_up, slots_down, info, dzb, slope1, slope2, *rest):
    n1, n2 = len(slots_up), len(slots_down)
    ups, downs, (du1, du2, *parts, up, down) = rest[:n1], rest[n1 : n1 + n2], rest[n1 + n2 :]
    place(info[0], ups, slots_up, up)
    place(info[0], downs, slots_down, down)
    units = du1.shape[1]
    for t, at in tile_rows(dzb):
        out = None
        for i, (slope, du) in enumerate(((slope1, du1), (slope2, du2))):
            cols = pl.ds(i * units, units)
            grad = (nn(dzb[at, :], down[:, cols]) * slope[at, :].astype(F32)).astype(BF16)
            du[at, :] = grad
            more = nt(grad, up[:, cols])
            out = more if out is None else out + more
        put_rows(parts, t, out.astype(BF16))


def feed_back(info, dzb, slope1, slope2, up, down):
    seq, width = dzb.shape
    units = slope1.shape[1]
    arrays = up[0] + down[0]
    parts, part_specs = tiles(seq, width, TILE)
    return run(
        functools.partial(feed_back_kernel, up[1], down[1]),
        "feed_back",
        (info, dzb, slope1, slope2) + arrays,
        [smem()] + [vmem()] * (3 + len(arrays)),
        (array((seq, units), BF16),) * 2 + parts,
        [vmem()] * 2 + part_specs,
        [pltpu.VMEM((width, 2 * units), BF16)] * 2,
    )


def turn_rows_kernel(order, info, first, second, out1, out2, full):
    count = len(order)
    height = full.shape[0] // count
    for values, out in ((first, out1), (second, out2)):
        for t, at in tile_rows(values):
            full[:, t * TILE : (t + 1) * TILE] = jnp.transpose(values[at, :])
        for e, j in enumerate(order):
            at = 0 if count == 1 else pl.multiple_of((info[0] ^ j) * height, height)
            out[pl.ds(e * height, height), :] = full[pl.ds(at, height), :]


def turn_rows(info, first, second, order):
    shape = first.shape[::-1]
    out = array(shape, BF16)
    return run(
        functools.partial(turn_rows_kernel, order),
        "turn_rows",
        (info, first, second),
        [smem()] + [vmem()] * 2,
        (out, out),
        [vmem()] * 2,
        [pltpu.VMEM(shape, BF16)],
    )


def feed_grad_kernel(turned, places, info, a, d1, d2, *rest):
    outs, full = rest[:4], rest[4]
    half = outs[0].shape[2]
    product = nn if turned else tn
    made = product(a[...], jnp.concatenate([d1[...], d2[...]], axis=1)).astype(BF16)
    if turned:
        height = outs[0].shape[1]
        order = [j for chip, j in places[0] if chip == 0]
        for i, out in enumerate(outs):
            for e, (chip, j) in enumerate(places[i]):
                row = order.index(j) * height
                first = 2 * chip * half + (i // 2) * half
                out[e] = made[row : row + height, first : first + half]
        return
    full[...] = made
    fulls = [full.at[:, pl.ds(2 * chip * half, 2 * half)] for chip in range(2)]
    for i, out in enumerate(outs):
        pick(info[0], fulls, out, places[i], (i // 2) * half)


def feed_grad(info, a, d1, d2, places, turned):
    seq, units = d1.shape
    width = a.shape[0] if turned else a.shape[1]
    count = len(places[0])
    out = array((count, width // count, units // 2), BF16)
    return run(
        functools.partial(feed_grad_kernel, turned, places),
        "feed_grad",
        (info, a, d1, d2),
        [smem()] + [vmem()] * 3,
        (out,) * 4,
        [vmem()] * 4,
        [pltpu.VMEM((width, 2 * units), BF16)],
    )


def pair_grad_kernel(tok_turned, d, out):
    made = nn(tok_turned[...], d[...]).astype(BF16)
    height = out.shape[1]
    for e in range(out.shape[0]):
        out[e] = made[e * height : (e + 1) * height]


def pair_grad(tok_turned, d, count):
    width = tok_turned.shape[0]
    cols = d.shape[1]
    return run(
        pair_grad_kernel,
        "pair_grad",
        (tok_turned, d),
        [vmem()] * 2,
        (array((count, width // count, cols), BF16),),
        [vmem()],
    )[0]


def encode(sums):
    hi = sums.astype(BF16).astype(F32)
    mid = (sums - hi).astype(BF16).astype(F32)
    low = sums - hi - mid
    return jnp.concatenate([hi, mid, low, jnp.zeros_like(low)], axis=0).astype(BF16)


def decode(coded):
    values = coded.astype(F32)
    n = values.shape[0] // 4
    return values[:n] + values[n : 2 * n] + values[2 * n : 3 * n]


def single_grad_kernel(
    order, info, tok_turned, d, dz, own, other, ends, sums_one, sums_two, keep, send, full
):
    mine = nn(tok_turned[...], d[...])
    full[...] = tn(dz[...], jnp.concatenate([ends[...], own[...], other[...]], axis=1))
    count = len(order)
    height = full.shape[0] // count
    width = keep.shape[1]
    blank = jnp.zeros((height, HD), F32)
    both = jnp.concatenate([sums_one[...], sums_two[...]], axis=0)
    both = encode(jnp.concatenate([both[:, :width], both[:, width:]], axis=0))
    half = max(1, count // 2)
    for e, j in enumerate(order):
        at = 0 if count == 1 else pl.multiple_of((info[0] ^ j) * height, height)
        heads = full[pl.ds(at, height), :]
        rows_in = mine[e * height : (e + 1) * height]
        for chip in range(2):
            first = chip * 4 * HD
            third = jnp.concatenate([heads[:, chip * HD : (chip + 1) * HD], blank], axis=1)
            made = [
                heads[:, (chip + 1) * LANES : (chip + 2) * LANES],
                third + rows_in[:, first : first + LANES],
                rows_in[:, first + LANES : first + 2 * LANES],
            ]
            if count == 1:
                out, row = (keep, send)[chip], 0
            else:
                out, row = (keep, send)[e // half], (chip * half + e % half) * height
            out[pl.ds(row, height), :] = jnp.concatenate(made, axis=1).astype(BF16)
    for out in (keep, send):
        out[pl.ds(out.shape[0] - TAIL, TAIL), :] = both


def single_grad(info, tok_turned, d, dz, contexts, sums_one, sums_two, order):
    width = tok_turned.shape[0]
    cols = 6 * HD
    out = array((width + TAIL, cols), BF16)
    return run(
        functools.partial(single_grad_kernel, order),
        "single_grad",
        (info, tok_turned, d, dz, *contexts, sums_one, sums_two),
        [smem()] + [vmem()] * 8,
        (out, out),
        [vmem()] * 2,
        [pltpu.VMEM((width, 3 * LANES), F32)],
    )


def across(values, axis, pairs):
    return lax.ppermute(values, axis, pairs)


def flip_chip(values):
    return across(values, "mp", CHIP_SWAP)


def flip_core(values):
    return across(values, "mp", CORE_SWAP)


def flip_cores(parts):
    return [flip_core(p) for p in parts]


def flip_dp(values, distance):
    size = lax.axis_size("dp")
    return across(values, "dp", [(i, i ^ distance) for i in range(size)])


def join_kernel(groups, *refs):
    count = sum(groups)
    parts, outs, sems = refs[:count], refs[count:-1], refs[-1]
    copies = []
    for out, number in zip(outs, groups):
        first = 0
        for part in parts[len(copies) : len(copies) + number]:
            to = out.at[pl.ds(first, part.shape[0])]
            copies.append(pltpu.make_async_copy(part, to, sems.at[len(copies)]))
            first += part.shape[0]
    for copy in copies:
        copy.start()
    for copy in copies:
        copy.wait()


def join(*groups):
    parts = sum((tuple(g) for g in groups), ())
    outs = [array((sum(p.shape[0] for p in g),) + g[0].shape[1:], g[0].dtype) for g in groups]
    return run(
        functools.partial(join_kernel, tuple(len(g) for g in groups)),
        "join",
        parts,
        [anywhere()] * len(parts),
        outs,
        [anywhere()] * len(outs),
        [pltpu.SemaphoreType.DMA((len(parts),))],
    )


def pack_kernel(w_query, w_key, w_value, w_out, out, rows_in, out_in, sems):
    copies = [
        pltpu.make_async_copy(w, rows_in.at[i], sems.at[i])
        for i, w in enumerate((w_query, w_key, w_value))
    ]
    copies.append(pltpu.make_async_copy(w_out, out_in, sems.at[3]))
    for copy in copies:
        copy.start()
    for copy in copies:
        copy.wait()
    for i in range(3):
        out[0, :, 2 * i * HD : 2 * (i + 1) * HD] = rows_in[i, :, : 2 * HD]
    parts = [jnp.transpose(out_in[...].astype(F32))]
    parts += [rows_in[i, :, 2 * HD :].astype(F32) for i in range(3)]
    out[0, :, 6 * HD :] = jnp.concatenate(parts, axis=1).astype(BF16)


def pack(w_query, w_key, w_value, w_out):
    height, span = w_query.shape
    return run(
        pack_kernel,
        "pack",
        in_hbm((w_query, w_key, w_value, w_out)),
        [anywhere()] * 4,
        (array((1, height, 4 * span), BF16),),
        [vmem()],
        [
            pltpu.VMEM((3, height, span), BF16),
            pltpu.VMEM(w_out.shape, BF16),
            pltpu.SemaphoreType.DMA((4,)),
        ],
    )[0]


def beside_kernel(first, second, out, sems):
    width = first.shape[1]
    copies = [
        pltpu.make_async_copy(ref, out.at[0, :, pl.ds(i * width, width)], sems.at[i])
        for i, ref in enumerate((first, second))
    ]
    for copy in copies:
        copy.start()
    for copy in copies:
        copy.wait()


def beside(first, second):
    height, width = first.shape
    return run(
        beside_kernel,
        "beside",
        in_hbm((first, second)),
        [anywhere()] * 2,
        (array((1, height, 2 * width), BF16),),
        [anywhere()],
        [pltpu.SemaphoreType.DMA((2,))],
    )[0]


def join_sides_kernel(count, *refs):
    parts, outs, sems = refs[:count], refs[count : count + 2], refs[count + 2]
    width = outs[0].shape[2]
    copies = []
    each = parts[0].shape[0]
    for i, part in enumerate(parts):
        for side, out in enumerate(outs):
            copies.append(
                pltpu.make_async_copy(
                    part.at[:, :, pl.ds(side * width, width)],
                    out.at[pl.ds(i * each, each)],
                    sems.at[2 * i + side],
                )
            )
    for copy in copies:
        copy.start()
    for copy in copies:
        copy.wait()


def join_sides(parts):
    count = len(parts)
    each, height, width = parts[0].shape
    out = array((count * each, height, width // 2), BF16)
    return run(
        functools.partial(join_sides_kernel, count),
        "join_sides",
        tuple(parts),
        [anywhere()] * count,
        (out, out),
        [anywhere()] * 2,
        [pltpu.SemaphoreType.DMA((2 * count,))],
    )


def fold_kernel(tail, own, got, *outs):
    body = own.shape[0] - tail
    each = body // len(outs)
    for i, out in enumerate(outs):
        at = pl.ds(i * each, each)
        total = (own[at].astype(F32) + got[at].astype(F32)).astype(BF16)
        if tail:
            out[:each] = total
        else:
            out[...] = total
    if tail:
        coded = encode(decode(own[body:]) + decode(got[body:]))
        for out in outs:
            out[each:] = coded


def fold(own, got, parts, tail=0):
    shape = ((own.shape[0] - tail) // parts + tail,) + own.shape[1:]
    return run(
        functools.partial(fold_kernel, tail),
        "fold",
        (own, got),
        [vmem()] * 2,
        (array(shape, BF16),) * parts,
        [vmem()] * parts,
    )


def fold_last_kernel(own1, got1, own2, got2, keep1, send1, keep2, send2):
    height = own2.shape[1]
    each = height + TAIL
    body = own1.shape[0] - TAIL
    coded = encode(decode(own1[body:]) + decode(got1[body:]))
    half = own2.shape[0] // 2
    for i in range(2 * half):
        out, first = (keep1, send1)[i // half], i % half * each
        at = pl.ds(i * height, height)
        out[first : first + height] = (own1[at].astype(F32) + got1[at].astype(F32)).astype(BF16)
        out[first + height : first + each] = coded
        total = own2[i].astype(F32) + got2[i].astype(F32)
        (keep2, send2)[i // half][i % half] = total.astype(BF16)


def fold_last(own1, got1, own2, got2):
    count, height, width = own2.shape
    first = array((count // 2 * (height + TAIL), width), BF16)
    second = array((count // 2, height, width), BF16)
    return run(
        fold_last_kernel,
        "fold_last",
        (own1, got1, own2, got2),
        [vmem()] * 4,
        (first, first, second, second),
        [vmem()] * 4,
    )


def fold_z_kernel(own1, got1, own2, got2, keep, send):
    height = own2.shape[1]
    each = height + TAIL
    for i, out in enumerate((keep, send)):
        at = pl.ds(i * each, height)
        out[:height] = (own1[at].astype(F32) + got1[at].astype(F32)).astype(BF16)
        at = pl.ds(i * each + height, TAIL)
        out[height:each] = encode(decode(own1[at]) + decode(got1[at]))
        out[each:] = (own2[i].astype(F32) + got2[i].astype(F32)).astype(BF16)


def fold_z(own1, got1, own2, got2):
    _, height, width = own2.shape
    out = array((2 * height + TAIL, width), BF16)
    return run(
        fold_z_kernel,
        "fold_z",
        (own1, got1, own2, got2),
        [vmem()] * 4,
        (out, out),
        [vmem()] * 2,
    )


def fold_add_kernel(own1, got1, own2, got2, out1, out2):
    for own, got, out in ((own1, got1, out1), (own2, got2, out2)):
        out[...] = (own[...].astype(F32) + got[...].astype(F32)).astype(BF16)


def fold_add(own1, got1, own2, got2):
    out = array(own1.shape, BF16)
    return run(
        fold_add_kernel,
        "fold_add",
        (own1, got1, own2, got2),
        [vmem()] * 4,
        (out, out),
        [vmem()] * 2,
    )


def fold_feed_kernel(first1, own1, got1, first2, own2, got2, keep1, send1, keep2, send2):
    width = own1.shape[2]
    half = keep1.shape[0]
    for first, own, got, outs in (
        (first1, own1, got1, (keep1, send1)),
        (first2, own2, got2, (keep2, send2)),
    ):
        for i, out in enumerate(outs):
            at = pl.ds(i * half, half)
            out[:, :, :width] = first[at]
            out[:, :, width:] = (own[at].astype(F32) + got[at].astype(F32)).astype(BF16)


def fold_feed(first1, own1, got1, first2, own2, got2):
    count, height, width = own1.shape
    out = array((count // 2, height, 2 * width), BF16)
    return run(
        fold_feed_kernel,
        "fold_feed",
        (first1, own1, got1, first2, own2, got2),
        [vmem()] * 6,
        (out,) * 4,
        [vmem()] * 4,
    )


def fold_sides_kernel(own1, got1, own2, got2, keep, send):
    width = own1.shape[2]
    half = keep.shape[0]
    for side, (own, got) in enumerate(((own1, got1), (own2, got2))):
        for i, out in enumerate((keep, send)):
            at = pl.ds(i * half, half)
            total = own[at].astype(F32) + got[at].astype(F32)
            out[:, :, side * width : (side + 1) * width] = total.astype(BF16)


def fold_sides(own1, got1, own2, got2):
    count, height, width = own1.shape
    out = array((count // 2, height, 2 * width), BF16)
    return run(
        fold_sides_kernel,
        "fold_sides",
        (own1, got1, own2, got2),
        [vmem()] * 4,
        (out, out),
        [vmem()] * 2,
    )


BY_Z = (0, 4, 2, 6)
Y_MAJOR = BY_Z + tuple(z + 1 for z in BY_Z)
OWN = tuple((0, j) for j in Y_MAJOR)
OTHER = tuple((1, j) for j in Y_MAJOR)
CHIP_NEAR = tuple((chip, z) for chip in range(2) for z in BY_Z)
CHIP_FAR = tuple((chip, z + 1) for chip in range(2) for z in BY_Z)


def split_kernel(other, info, first, second, out, sems):
    slot = 1 - info[1] if other else info[1]
    half = first.shape[1] // 2
    copies = []
    for i, values in enumerate((first, second)):
        for j in range(2):
            at = pl.ds(j * half, half)
            copies.append(
                pltpu.make_async_copy(values.at[slot, at], out.at[i, at], sems.at[2 * i + j])
            )
    for copy in copies:
        copy.start()
    for copy in copies:
        copy.wait()


def split(info, first, second, other):
    return run(
        functools.partial(split_kernel, other),
        "split",
        (info, *in_hbm((first, second))),
        [smem()] + [anywhere()] * 2,
        (array((2,) + first.shape[1:], first.dtype),),
        [vmem()],
        [pltpu.SemaphoreType.DMA((4,))],
    )[0]


def merge_kernel(info, own, got, core_own, core_got, out, sems):
    core = info[2]
    copies = []
    for half, (mine, other) in enumerate(((own, core_own), (got, core_got))):
        copies += [
            pltpu.make_async_copy(mine.at[0], out.at[half, core], sems.at[2 * half]),
            pltpu.make_async_copy(other.at[0], out.at[half, 1 - core], sems.at[2 * half + 1]),
        ]
    for copy in copies:
        copy.start()
    for copy in copies:
        copy.wait()


def merge(info, quarters):
    _, quarter, width = quarters[0].shape
    out = run(
        merge_kernel,
        "merge",
        (info, *quarters),
        [smem()] + [anywhere()] * 4,
        (array((2, 2, quarter, width), quarters[0].dtype),),
        [anywhere()],
        [pltpu.SemaphoreType.DMA((4,))],
    )[0]
    return out.reshape(4 * quarter, width)


def slots_kernel(info, own, other, out, sems):
    copies = [
        pltpu.make_async_copy(own, out.at[info[1]], sems.at[0]),
        pltpu.make_async_copy(other, out.at[1 - info[1]], sems.at[1]),
    ]
    for copy in copies:
        copy.start()
    for copy in copies:
        copy.wait()


def slots_of(info, own, other):
    return run(
        slots_kernel,
        "slots",
        (info, own, other),
        [smem()] + [anywhere()] * 2,
        (array((2,) + own.shape, own.dtype),),
        [anywhere()],
        [pltpu.SemaphoreType.DMA((2,))],
    )[0]


def tokens_add_kernel(count, mine, *rest):
    got, own, sends = rest[:count], rest[count], rest[count + 1 :]
    per = count // 2
    height = got[0].shape[0]
    for k, part in enumerate(got):
        at = k % per * height
        total = mine[k // per, pl.ds(at, height)] + part[...].astype(F32)
        if k < per:
            own[pl.ds(at, height)] = total
        else:
            each = sends[0].shape[0]
            for first in range(0, height, each):
                sends[(at + first) // each][...] = total[first : first + each].astype(BF16)


def tokens_add(mine, got):
    _, quarter, width = mine.shape
    send = array((quarter // 2, width), BF16)
    return run(
        functools.partial(tokens_add_kernel, len(got)),
        "tokens_add",
        (mine, *got),
        [vmem()] * (1 + len(got)),
        (array((quarter, width), F32), send, send),
        [vmem()] * 3,
    )


def tokens_out_kernel(info, own, *rest):
    *got, out = rest
    out[info[1]] = own[...]
    height = got[0].shape[0]
    for k, part in enumerate(got):
        out[1 - info[1], pl.ds(k * height, height), :] = part[...].astype(F32)


def tokens_out(info, own, got):
    return run(
        tokens_out_kernel,
        "tokens_out",
        (info, own, *got),
        [smem()] + [vmem()] * (1 + len(got)),
        (array((2,) + own.shape, F32),),
        [vmem()],
    )[0]


def feed_out_kernel(own, got, up, down):
    half = up.shape[1] // 2
    for i in range(4):
        at = pl.ds(i * half, half)
        total = own[0, :, at].astype(F32) + got[0, :, at].astype(F32)
        out = (down, up)[i % 2]
        out[:, pl.ds(i // 2 * half, half)] = total


def feed_out(own, got):
    _, height, width = own.shape
    out = array((height, width // 2), F32)
    return run(
        feed_out_kernel,
        "feed_out",
        (own, got),
        [vmem()] * 2,
        (out, out),
        [vmem()] * 2,
    )


def attend_out_kernel(a, b, query, key, value, out, gain1, bias1, gain2, bias2):
    height = query.shape[0]

    def both(first, last):
        return a[first:last].astype(F32) + b[first:last].astype(F32)

    one = both(0, height)
    two = both(height + TAIL, 2 * height + TAIL)
    at = pl.ds(height, TAIL)
    sums = decode(a[at]) + decode(b[at])
    for i, ref in enumerate((query, key, value)):
        ref[...] = jnp.concatenate(
            [two[:, 2 * i * HD : 2 * (i + 1) * HD], one[:, (3 + i) * HD : (4 + i) * HD]], axis=1
        )
    out[...] = jnp.transpose(one[:, : 3 * HD])
    for i, ref in enumerate((gain1, bias1, gain2, bias2)):
        ref[...] = jnp.concatenate([sums[i], sums[4 + i]], axis=0)


def attend_out(pieces, height):
    cols = pieces[0].shape[1]
    span = cols // 2
    return run(
        attend_out_kernel,
        "attend_out",
        tuple(pieces),
        [vmem()] * 2,
        (array((height, span), F32),) * 3
        + (array((span, height), F32),)
        + (array((2 * cols,), F32),) * 4,
        [vmem()] * 8,
    )


def fast_path(info, tokens, cotangent, weights, lengths, masks, norms):
    w_query, w_key, w_value, w_out, w_up, w_down = weights
    mask_own, mask_other, mask_ends = masks
    g_one, b_one, g_two, b_two = norms
    height, features, units = w_query.shape[0], tokens.shape[2], w_up.shape[1]
    flat = (tuple((0, j) for j in Y_MAJOR),)
    got_rows = flip_chip(split(info, tokens, cotangent, True))
    piece = pack(w_query, w_key, w_value, w_out)
    got_piece = flip_dp(piece, 4)
    own_rows = split(info, tokens, cotangent, False)
    (two_attn,) = join([piece, got_piece])
    got_attn = flip_dp(two_attn, 2)
    feed_piece = beside(w_up, w_down.T)
    got_feed = flip_dp(feed_piece, 4)
    z_pair, z_single = join_sides([two_attn, got_attn])
    y_pair, x_single = flip_dp(z_pair, 1), flip_chip(z_single)
    own_pair, near_single = join([z_pair, y_pair], [z_single, x_single])
    other_pair, far_single = flip_chip(own_pair), flip_dp(near_single, 1)
    single_w = ((near_single, far_single), (CHIP_NEAR, CHIP_FAR))
    two_up, two_down = join_sides([feed_piece, got_feed])
    got_up, got_down = flip_dp(two_up, 2), flip_dp(two_down, 2)
    quarters = (own_rows, got_rows, flip_core(own_rows), flip_core(got_rows))
    tok = merge(info, quarters)
    own01 = attend(info, lengths, tok, ((own_pair,), flat), True, mask_own[:2])
    z_up, z_down = join([two_up, got_up], [two_down, got_down])
    y_up, x_down = flip_dp(z_up, 1), flip_chip(z_down)
    other01 = attend(info, lengths, tok, ((other_pair,), flat), True, mask_other[:2])
    ends = attend(info, lengths, tok, single_w, False, mask_ends)
    own_up, near_down = join([z_up, y_up], [z_down, x_down])
    other_up, far_down = flip_chip(own_up), flip_dp(near_down, 1)
    up = ((own_up, other_up), (OWN, OTHER))
    down = ((near_down, far_down), (CHIP_NEAR, CHIP_FAR))
    contexts = (own01[3], other01[3], ends[3])
    attn_part = project(info, contexts, single_w, features)
    attn_got = flip_cores(attn_part)
    normal, scale_one, hn = norm_one(tok, attn_part, attn_got, g_one, b_one)
    act1, slope1 = feed_up(info, hn, ((own_up,), flat), units)
    tok_turned, hn_turned = turn_rows(info, tok, hn, Y_MAJOR)
    act2, slope2 = feed_up(info, hn, ((other_up,), flat), units)
    mixed = feed_down(info, act1, act2, down, features)
    mixed_got = flip_cores(mixed)
    own_out, send_out, dzb_two, sums_two = norm_two(
        info, lengths, hn, mixed, mixed_got, quarters, g_two, b_two
    )
    keep_d1, send_d1, keep_d2, send_d2 = feed_grad(
        info, dzb_two, act1, act2, (OWN, OTHER, CHIP_NEAR, CHIP_FAR), False
    )
    got_d1, got_d2 = flip_chip(send_d1), flip_dp(send_d2, 1)
    du1, du2, *back = feed_back(info, dzb_two, slope1, slope2, up, down)
    back_got = flip_cores(back)
    keep_u1, send_u1, keep_u2, send_u2 = feed_grad(
        info, hn_turned, du1, du2, (OWN, OTHER, CHIP_NEAR, CHIP_FAR), True
    )
    got_u1, got_u2 = flip_chip(send_u1), flip_dp(send_u2, 1)
    sum_d1, sum_d2 = fold_add(keep_d1, got_d1, keep_d2, got_d2)
    dzb_one, sums_one = norm_one_back(normal, scale_one, dzb_two, back, back_got, g_one)
    d_ends = attend_back(info, dzb_one, single_w, None, ends)
    keep_f1, send_f1, keep_f2, send_f2 = fold_feed(
        sum_d1, keep_u1, got_u1, sum_d2, keep_u2, got_u2
    )
    got_f1, got_f2 = flip_dp(send_f1, 1), flip_chip(send_f2)
    keep_s, send_s = single_grad(
        info, tok_turned, d_ends, dzb_one, contexts, sums_one, sums_two, Y_MAJOR
    )
    d_other = attend_back(info, dzb_one, single_w, 1, other01)
    grad_b = pair_grad(tok_turned, d_other, len(OWN))
    got_b = flip_chip(grad_b)
    (send_s1,) = join([send_s])
    got_s = flip_dp(send_s1, 1)
    keep_f, send_f = fold_sides(keep_f1, got_f1, keep_f2, got_f2)
    got_f = flip_dp(send_f, 2)
    d_own = attend_back(info, dzb_one, single_w, 0, own01)
    grad_a = pair_grad(tok_turned, d_own, len(OWN))
    keep_a, send_a = fold(grad_a, got_b, 2, 0)
    got_a = flip_dp(send_a, 1)
    keep_s2, send_s2 = fold(keep_s, got_s, 2, TAIL)
    got_s2 = flip_chip(send_s2)
    mine, *sent = input_back(
        info, d_own, d_other, d_ends, dzb_one, ((own_pair, other_pair), (OWN, OTHER)), single_w
    )
    keep_f3, send_f3 = fold(keep_f, got_f, 2, 0)
    got_f3 = flip_dp(send_f3, 4)
    keep_s3, send_s3, keep_a3, send_a3 = fold_last(keep_s2, got_s2, keep_a, got_a)
    got_s3, got_a3 = flip_dp(send_s3, 2), flip_dp(send_a3, 2)
    sent_parts = join(*[[v] for v in sent])
    sent_got = flip_cores(sent_parts)
    own_tok, *send_tok = tokens_add(mine, sent_got)
    got_tok = [flip_chip(v) for v in send_tok]
    got_out = flip_chip(send_out)
    keep_z, send_z = fold_z(keep_s3, got_s3, keep_a3, got_a3)
    got_z = flip_dp(send_z, 4)
    grad_tokens = tokens_out(info, own_tok, got_tok)
    output = slots_of(info, own_out, got_out)
    grad_up, grad_down = feed_out(keep_f3, got_f3)
    grads = attend_out((keep_z, got_z), height)
    return (output, grad_tokens, *grads[:4], grad_up, grad_down.T, *grads[4:])


def plain_path(info, tokens, cotangent, weights, lengths, masks, norms):
    w_query, w_key, w_value, w_out, w_up, w_down = weights
    mask_own, mask_other, mask_ends = masks
    g_one, b_one, g_two, b_two = norms
    features, units = tokens.shape[2], w_up.shape[1]
    flat = (((0, 0),),)
    two = (((0, 0),), ((1, 0),))

    def gathered(piece):
        own = lax.all_gather(piece, "dp", axis=0, tiled=True)[None]
        return own, flip_chip(own)

    got_rows = flip_chip(split(info, tokens, cotangent, True))
    own_rows = split(info, tokens, cotangent, False)
    quarters = (own_rows, got_rows, flip_core(own_rows), flip_core(got_rows))
    tok = merge(info, quarters)
    firsts = [w[:, : 2 * HD] for w in (w_query, w_key, w_value)]
    thirds = [w_out.T] + [w[:, 2 * HD :] for w in (w_query, w_key, w_value)]
    pair_w = (gathered(jnp.concatenate(firsts, axis=1)), two)
    single_w = (gathered(jnp.concatenate(thirds, axis=1)), two)
    up, down = (gathered(w_up), two), (gathered(w_down.T), two)
    own01 = attend(info, lengths, tok, ((pair_w[0][0],), flat), True, mask_own[:2])
    other01 = attend(info, lengths, tok, ((pair_w[0][1],), flat), True, mask_other[:2])
    ends = attend(info, lengths, tok, single_w, False, mask_ends)
    contexts = (own01[3], other01[3], ends[3])
    part = project(info, contexts, single_w, features)
    normal, scale_one, hn = norm_one(tok, part, flip_cores(part), g_one, b_one)
    act1, slope1 = feed_up(info, hn, ((up[0][0],), flat), units)
    act2, slope2 = feed_up(info, hn, ((up[0][1],), flat), units)
    tok_turned, hn_turned = turn_rows(info, tok, hn, (0,))
    part = feed_down(info, act1, act2, down, features)
    own_out, send_out, dzb_two, sums_two = norm_two(
        info, lengths, hn, part, flip_cores(part), quarters, g_two, b_two
    )
    places = (((0, 0),), ((1, 0),)) * 2
    grad_d = feed_grad(info, dzb_two, act1, act2, places, False)
    du1, du2, *part = feed_back(info, dzb_two, slope1, slope2, up, down)
    grad_u = feed_grad(info, hn_turned, du1, du2, places, True)
    dzb_one, sums_one = norm_one_back(
        normal, scale_one, dzb_two, part, flip_cores(part), g_one
    )
    d_ends = attend_back(info, dzb_one, single_w, None, ends)
    keep_s, send_s = single_grad(
        info, tok_turned, d_ends, dzb_one, contexts, sums_one, sums_two, (0,)
    )
    d_other = attend_back(info, dzb_one, single_w, 1, other01)
    grad_b = pair_grad(tok_turned, d_other, 1)
    d_own = attend_back(info, dzb_one, single_w, 0, own01)
    grad_a = pair_grad(tok_turned, d_own, 1)
    mine, *sent = input_back(info, d_own, d_other, d_ends, dzb_one, pair_w, single_w)
    own_tok, *send_tok = tokens_add(mine, flip_cores(sent))
    output = slots_of(info, own_out, flip_chip(send_out))
    grad_tokens = tokens_out(info, own_tok, [flip_chip(v) for v in send_tok])

    def summed(own, other):
        total = own.astype(F32) + flip_chip(other).astype(F32)
        return lax.psum_scatter(total, "dp", scatter_dimension=0, tiled=True)

    def wide(keep1, send1, keep2, send2):
        return jnp.concatenate([summed(keep1[0], send1[0]), summed(keep2[0], send2[0])], axis=1)

    single = summed(keep_s[:features], send_s[:features])
    pair = summed(grad_a[0], grad_b[0])
    grads = [
        jnp.concatenate(
            [pair[:, 2 * i * HD : 2 * (i + 1) * HD], single[:, (3 + i) * HD : (4 + i) * HD]],
            axis=1,
        )
        for i in range(3)
    ] + [single[:, : 3 * HD].T]
    sums = decode(keep_s[features:])
    sums = lax.psum(sums + flip_chip(sums), "dp")
    sums = [jnp.concatenate([sums[i], sums[4 + i]]) for i in range(4)]
    return (output, grad_tokens, *grads, wide(*grad_u), wide(*grad_d).T, *sums)


def local(
    tokens,
    w_query,
    w_key,
    w_value,
    w_out,
    w_up,
    w_down,
    gain_attn,
    bias_attn,
    gain_ffn,
    bias_ffn,
    lengths,
    random_blocks,
    cotangent,
):
    ORDER.clear()
    size = lax.axis_size("dp")
    rank = lax.axis_index("mp")
    me = lax.axis_index("dp")
    x, core = rank // 2, rank % 2
    quarter = tokens.shape[1]
    seq = 4 * quarter
    height = w_query.shape[0]
    span = w_query.shape[1]
    heads = span // HD
    nblocks = seq // BLOCK
    fast = size == 8 and height % 16 == 0

    shift = x * (seq // 2)
    info = jnp.stack([me, x, core, shift]).astype(jnp.int32)

    blocks = (jnp.arange(nblocks) + x * (nblocks // 2)) % nblocks
    near_blocks = jnp.abs(blocks[:, None] - blocks[None, :]) <= 1
    edge = (blocks == 0) | (blocks == nblocks - 1)
    fixed = near_blocks | edge[:, None] | edge[None, :]

    def table(shard):
        chosen = lax.dynamic_slice_in_dim(random_blocks, shard * heads, heads, 0)
        chosen = jnp.roll(chosen, -x * (nblocks // 2), axis=1)
        hit = jnp.any(chosen[:, None, :, :] == blocks[None, :, None, None], axis=3)
        bias = jnp.where(fixed.T[None] | hit, 0.0, NEGATIVE)
        return jnp.concatenate(
            [
                jnp.zeros((heads, nblocks, HD), F32),
                bias,
                jnp.full((heads, nblocks, 3), -1.0, F32),
                jnp.zeros((heads, nblocks, HD - 3 - nblocks), F32),
            ],
            axis=2,
        )

    mask_own, mask_other = table(rank), table(rank ^ 2)
    mask_ends = jnp.concatenate([mask_own[2:], mask_other[2:]], axis=0)
    g_one, b_one = gain_attn[None], bias_attn[None]
    g_two, b_two = gain_ffn[None], bias_ffn[None]

    path = fast_path if fast else plain_path
    return path(
        info,
        tokens,
        cotangent,
        (w_query, w_key, w_value, w_out, w_up, w_down),
        lengths,
        (mask_own, mask_other, mask_ends),
        (g_one, b_one, g_two, b_two),
    )


def solution(mesh):
    return jax.shard_map(
        local,
        mesh=mesh,
        in_specs=(
            P("dp", "mp", None),
            P("dp", "mp"),
            P("dp", "mp"),
            P("dp", "mp"),
            P("mp", "dp"),
            P("dp", "mp"),
            P("mp", "dp"),
            P(),
            P(),
            P(),
            P(),
            P("dp"),
            P(),
            P("dp", "mp", None),
        ),
        out_specs=(
            P("dp", "mp", None),
            P("dp", "mp", None),
            P("dp", "mp"),
            P("dp", "mp"),
            P("dp", "mp"),
            P("mp", "dp"),
            P("dp", "mp"),
            P("mp", "dp"),
            P(),
            P(),
            P(),
            P(),
        ),
        check_vma=False,
    )
```
